32 devices in a mesh: lat: 4 (over x, core), lon: 8 (over z, y).
Axes of the slice: x: 2, y: 2, z: 4, core: 2. Of those that a mesh axis runs over, the one named last changes fastest.
Arguments:
- features: bfloat16 [128, 128, 768], P('lat', 'lon'), may hold values from -6 to 6
- cotangent: bfloat16 [128, 128, 768], P('lat', 'lon'), may hold values from -6 to 6
- weight_first: bfloat16 [2, 8, 96, 96], replicated, may hold values from -1 to 1
- weight_second: bfloat16 [2, 8, 96, 96], replicated, may hold values from -1 to 1
Outputs:
- mixed_field: bfloat16 [128, 128, 768], P('lat', 'lon')
- feature_grad: bfloat16 [128, 128, 768], P('lat', 'lon')
- grad_first: float32 [2, 8, 96, 96], replicated
- grad_second: float32 [2, 8, 96, 96], replicated
The draws below stay inside these ranges and needn't reach their ends.
All inputs are finite; a program needn't handle non-finite values.
Results may differ from the reference program's by a relative error of at most 0.012.
The reference program's roundings to bfloat16 on the way count: a program that leaves them out, or rounds other values in their place, can miss the bound.
Values may be sent and summed in bfloat16 or wider, within the bound.
No kernel may reach another device: no remote copies, remote signals or barrier semaphores. Data moves between devices by JAX's collectives and lax.ppermute only.
A program may use at most 64 MiB of HBM per device.

```python
import math
import jax
import jax.numpy as jnp
from jax import lax

NB = 8
BS = 96
C = 768
HR = 32
H = 128
W = 128
KW = 32
N_LAT = 4


def draw_weight_first(key, part):
    sample = jax.random.normal(key, (2, NB, BS, BS), jnp.float32)
    column_norm = jnp.sqrt(jnp.sum(sample * sample, axis=(0, 2), keepdims=True))
    return (sample / column_norm).astype(jnp.bfloat16)


def draw_weight_second(key, part):
    sample = jnp.clip(jax.random.normal(key, (2, NB, BS, BS), jnp.float32), -6.0, 6.0)
    return ((sample - jnp.roll(sample, 1, axis=2)) / math.sqrt(4.0 * BS)).astype(jnp.bfloat16)


def shard_levels(own_key, dims, shards, least, largest):
    gain, own = 1.0, jax.random.fold_in(own_key, 6)
    for dim, shards_of in shards:
        steps = jnp.exp(jax.random.uniform(jax.random.fold_in(own, dim), (shards_of,), jnp.float32, least / len(shards), largest / len(shards)))
        gain = gain * jnp.repeat(steps, dims[dim] // shards_of).reshape([-1 if axis == dim else 1 for axis in range(len(dims))])
    return gain


def noise(stream_key, extent, width, reach, cuts=(), kind=jnp.bfloat16):
    level = shard_levels(stream_key, extent, cuts, -0.22, 0.18) if cuts else 1.0
    array = jax.random.normal(stream_key, extent, jnp.float32) * width * level
    return jnp.minimum(jnp.maximum(array, -reach), reach).astype(kind)


def setup_inputs(seed: int = 0) -> dict:
    key_list = jax.random.split(jax.random.key(seed), 5)
    return {
        "features": noise(key_list[0], (H, W, C), 1.0, 6.0, ((0, 4), (1, 8))),
        "cotangent": noise(key_list[1], (H, W, C), 1.0, 6.0, ((0, 4), (1, 8))),
        "weight_first": draw_weight_first(jax.random.fold_in(key_list[4], 71), 0),
        "weight_second": draw_weight_second(jax.random.fold_in(key_list[4], 71), 0),
    }


shrink_level = 0.01
gelu_coeff = 0.7978845608028654

def wave_table(first, second, length):
    product = first[:, None] * second[None, :] % length
    angle = 2.0 * math.pi / length * product.astype(jnp.float32)
    return (jnp.cos(angle) / math.sqrt(length), jnp.sin(angle) / math.sqrt(length))

def batch_product(left, weights):
    return jnp.einsum('mbi,bio->mbo', left.astype(jnp.float32), weights.astype(jnp.float32))

def batch_back(left, weights):
    return jnp.einsum('mbo,bio->mbi', left.astype(jnp.float32), weights.astype(jnp.float32))

def batch_outer(left, right):
    return jnp.einsum('mbi,mbo->bio', left.astype(jnp.float32), right.astype(jnp.float32))

def gelu_parts(values):
    squared = values * values
    tangent = jnp.tanh(gelu_coeff * (values + 0.044715 * squared * values))
    result = 0.5 * values * (1.0 + tangent)
    slope = 0.5 * (1.0 + tangent) + 0.5 * values * (1.0 - tangent * tangent) * gelu_coeff * (1.0 + 3.0 * 0.044715 * squared)
    return (result, slope)

def shrink_parts(values):
    ratio = jnp.tanh(values / shrink_level)
    return (values - shrink_level * ratio, ratio * ratio)

def spectral_block(real_in, imag_in, real_cot, imag_cot, mode_weight, weight_first, weight_second):
    first_re, first_im = (weight_first[0], weight_first[1])
    second_re, second_im = (weight_second[0], weight_second[1])
    pre_real = batch_product(real_in, first_re) - batch_product(imag_in, first_im)
    pre_imag = batch_product(real_in, first_im) + batch_product(imag_in, first_re)
    act_real, slope_real = gelu_parts(pre_real)
    act_imag, slope_imag = gelu_parts(pre_imag)
    hidden_real = act_real.astype(jnp.bfloat16)
    hidden_imag = act_imag.astype(jnp.bfloat16)
    post_real = batch_product(hidden_real, second_re) - batch_product(hidden_imag, second_im)
    post_imag = batch_product(hidden_real, second_im) + batch_product(hidden_imag, second_re)
    shr_real, pass_real = shrink_parts(post_real)
    shr_imag, pass_imag = shrink_parts(post_imag)
    out_real = shr_real.astype(jnp.bfloat16)
    out_imag = shr_imag.astype(jnp.bfloat16)
    grad_post_real = (mode_weight * real_cot.astype(jnp.float32) * pass_real).astype(jnp.bfloat16)
    grad_post_imag = (mode_weight * imag_cot.astype(jnp.float32) * pass_imag).astype(jnp.bfloat16)
    grad_hid_real = batch_back(grad_post_real, second_re) + batch_back(grad_post_imag, second_im)
    grad_hid_imag = batch_back(grad_post_imag, second_re) - batch_back(grad_post_real, second_im)
    grad_pre_real = (grad_hid_real * slope_real).astype(jnp.bfloat16)
    grad_pre_imag = (grad_hid_imag * slope_imag).astype(jnp.bfloat16)
    back_real = (batch_back(grad_pre_real, first_re) + batch_back(grad_pre_imag, first_im)).astype(jnp.bfloat16)
    back_imag = (batch_back(grad_pre_imag, first_re) - batch_back(grad_pre_real, first_im)).astype(jnp.bfloat16)
    grad_second = jnp.stack([batch_outer(hidden_real, grad_post_real) + batch_outer(hidden_imag, grad_post_imag), batch_outer(hidden_real, grad_post_imag) - batch_outer(hidden_imag, grad_post_real)])
    grad_first = jnp.stack([batch_outer(real_in, grad_pre_real) + batch_outer(imag_in, grad_pre_imag), batch_outer(real_in, grad_pre_imag) - batch_outer(imag_in, grad_pre_real)])
    return (out_real, out_imag, back_real, back_imag, grad_first, grad_second)

def lat_forward(coeffs, slab):
    rows_total = slab.shape[0]
    product = jnp.einsum('ah,hrkc->arkc', coeffs.astype(jnp.float32), slab.astype(jnp.float32))
    upper = product[:rows_total]
    lower = product[rows_total:]
    real_part = (upper[:, 0] + lower[:, 1]).astype(jnp.bfloat16)
    imag_part = (upper[:, 1] - lower[:, 0]).astype(jnp.bfloat16)
    return (real_part, imag_part)

def lat_inverse(coeffs, real_part, imag_part):
    rows_total = real_part.shape[0]
    slab = jnp.stack([real_part, imag_part], axis=1)
    product = jnp.einsum('ak,krbc->arbc', coeffs.astype(jnp.float32), slab.astype(jnp.float32))
    upper = product[:rows_total]
    lower = product[rows_total:]
    return jnp.stack([upper[:, 0] - lower[:, 1], lower[:, 0] + upper[:, 1]], axis=1).astype(jnp.bfloat16)

def reference(features, cotangent, weight_first, weight_second):
    kept_block = KW // 16
    lon_cos, lon_sin = wave_table(jnp.arange(KW, dtype=jnp.int32), jnp.arange(W, dtype=jnp.int32), W)
    lon_coeffs = jnp.concatenate([lon_cos, lon_sin]).astype(jnp.bfloat16)

    def lon_forward(band):
        product = jnp.einsum('aw,rwc->rac', lon_coeffs.astype(jnp.float32), band.astype(jnp.float32))
        return jnp.stack([product[:, :KW], -product[:, KW:]], axis=1).astype(jnp.bfloat16)
    spec_field = lax.map(lon_forward, features.reshape(N_LAT, HR, W, C)).reshape(H, 2, KW, C)
    spec_cot = lax.map(lon_forward, cotangent.reshape(N_LAT, HR, W, C)).reshape(H, 2, KW, C)
    lat_cos, lat_sin = wave_table(jnp.arange(H, dtype=jnp.int32), jnp.arange(H, dtype=jnp.int32), H)
    lat_coeffs = jnp.concatenate([lat_cos, lat_sin]).astype(jnp.bfloat16)
    doubled = jnp.where(jnp.arange(KW, dtype=jnp.int32) == 0, 1.0, 2.0).astype(jnp.float32)

    def step(totals, position):
        start = (position * kept_block).astype(jnp.int32)
        field_slab = lax.dynamic_slice_in_dim(spec_field, start, kept_block, 2)
        cot_slab = lax.dynamic_slice_in_dim(spec_cot, start, kept_block, 2)
        real_in, imag_in = lat_forward(lat_coeffs, field_slab)
        real_cot, imag_cot = lat_forward(lat_coeffs, cot_slab)
        modes = H * kept_block
        weight_slab = lax.dynamic_slice_in_dim(doubled, start, kept_block, 0)
        mode_weight = jnp.broadcast_to(weight_slab[None, :], (H, kept_block)).reshape(modes, 1, 1)
        results = spectral_block(real_in.reshape(modes, NB, BS), imag_in.reshape(modes, NB, BS), real_cot.reshape(modes, NB, BS), imag_cot.reshape(modes, NB, BS), mode_weight, weight_first, weight_second)
        out_real, out_imag, back_real, back_imag, grad_first, grad_second = results
        inv_out = lat_inverse(lat_coeffs, out_real.reshape(H, kept_block, C), out_imag.reshape(H, kept_block, C))
        inv_back = lat_inverse(lat_coeffs, back_real.reshape(H, kept_block, C), back_imag.reshape(H, kept_block, C))
        return ((totals[0] + grad_first, totals[1] + grad_second), (inv_out, inv_back))
    zeros_grad = jnp.zeros((2, NB, BS, BS), jnp.float32)
    totals, stacked = lax.scan(step, (zeros_grad, zeros_grad), jnp.arange(16, dtype=jnp.int32))
    inv_out, inv_back = stacked

    def regroup(blocks):
        return jnp.moveaxis(blocks, 0, 2).reshape(N_LAT, HR, 2 * KW, C)
    plain = jnp.concatenate([lon_cos, -lon_sin]).astype(jnp.bfloat16)
    scaled = (plain.astype(jnp.float32) * jnp.concatenate([doubled, doubled])[:, None]).astype(jnp.bfloat16)

    def lon_inverse(coeffs):

        def apply_rows(band):
            return jnp.einsum('aw,rac->rwc', coeffs.astype(jnp.float32), band.astype(jnp.float32)).astype(jnp.bfloat16)
        return apply_rows
    filtered = lax.map(lon_inverse(scaled), regroup(inv_out)).reshape(H, W, C)
    backward = lax.map(lon_inverse(plain), regroup(inv_back)).reshape(H, W, C)
    mixed_field = (features.astype(jnp.float32) + filtered.astype(jnp.float32)).astype(jnp.bfloat16)
    feature_grad = (cotangent.astype(jnp.float32) + backward.astype(jnp.float32)).astype(jnp.bfloat16)
    factor = 1.0 / math.sqrt(H * KW)
    return (mixed_field, feature_grad, totals[0] * factor, totals[1] * factor)
```

```python
import functools
import math

import jax
import jax.numpy as jnp
import ml_dtypes
import numpy as np
from jax import lax
from jax.experimental import pallas as pl
from jax.experimental.pallas import tpu as pltpu
from jax.sharding import PartitionSpec as P

NB = 8
BS = 96
KWD = 1
RQ = 4
PACK = RQ * BS

shrink_level = 0.01
gelu_coeff = 0.7978845608028654


def wave_table(first, second, length):
    product = (first[:, None] * second[None, :]) % length
    angle = np.float32(2.0 * math.pi / length) * product.astype(np.float32)
    scale = np.float32(math.sqrt(length))
    rounded = ml_dtypes.bfloat16
    cos = (np.cos(angle) / scale).astype(rounded).astype(np.float32)
    sin = (np.sin(angle) / scale).astype(rounded).astype(np.float32)
    return cos, sin


def lon_tables(kept, cols, lon_count, rows_sub):
    cos, sin = wave_table(np.arange(kept), np.arange(cols), cols)
    parts = np.stack([cos, -sin], axis=1).reshape(kept, 2, lon_count, cols // lon_count)
    eye = np.eye(rows_sub, dtype=np.float32)
    forward = np.einsum("kpgw,rs->kprgsw", parts, eye).reshape(2 * kept * rows_sub, -1)
    doubled = np.where(np.arange(kept) == 0, 1.0, 2.0).astype(np.float32)
    scaled = parts * doubled[:, None, None, None]
    inverse = np.einsum("kpgw,rs->gswkpr", scaled, eye).reshape(-1, 2 * kept * rows_sub)
    return forward, inverse, forward.T


def lat_tables(rows, lat_count, subs):
    cos, sin = wave_table(np.arange(rows), np.arange(rows), rows)
    forward = np.stack([np.stack([cos, sin], axis=1), np.stack([-sin, cos], axis=1)])
    split = forward.reshape(2, rows, 2, lat_count, RQ, subs, -1)
    forward = split.transpose(0, 1, 4, 3, 5, 2, 6).reshape(2 * rows, 2 * rows)
    return forward, forward.T


def constant(table):
    return jnp.asarray(table.astype(ml_dtypes.bfloat16))


def kernel_call(body, out_shape):
    return pl.pallas_call(
        body,
        out_shape=out_shape,
        compiler_params=pltpu.CompilerParams(vmem_limit_bytes=40 * 1024 * 1024),
    )


def pack_body(rows_sub, subs, source, packed):
    cols = source.shape[1]
    for sub in range(subs):
        for block in range(NB):
            pieces = []
            for group in range(RQ):
                row = (group * subs + sub) * rows_sub
                piece = source[row : row + rows_sub, :, block * BS : (block + 1) * BS]
                pieces.append(piece.reshape(rows_sub * cols, BS))
            packed[sub * NB + block] = jnp.concatenate(pieces, axis=1)


def unpack_body(rows_sub, subs, packed, base, result):
    cols = base.shape[1]
    for sub in range(subs):
        for group in range(RQ):
            row = (group * subs + sub) * rows_sub
            pieces = [
                packed[sub * NB + block, :, group * BS : (group + 1) * BS] for block in range(NB)
            ]
            update = jnp.concatenate(pieces, axis=1).reshape(rows_sub, cols, NB * BS)
            old = base[row : row + rows_sub]
            result[row : row + rows_sub] = (
                old.astype(jnp.float32) + update.astype(jnp.float32)
            ).astype(jnp.bfloat16)


def product(left, right):
    return jnp.dot(left, right, preferred_element_type=jnp.float32)


def product_back(left, right):
    return lax.dot_general(
        left, right, (((1,), (1,)), ((), ())), preferred_element_type=jnp.float32
    )


def product_outer(left, right):
    return lax.dot_general(
        left, right, (((0,), (0,)), ((), ())), preferred_element_type=jnp.float32
    )


def table_body(table, source, result):
    rows = source.shape[0] * source.shape[1]
    flat = source[...].reshape(rows, source.shape[2])
    result[...] = product(table[...], flat).astype(jnp.bfloat16).reshape(result.shape)


def lat_forward(table, received, index):
    slab = received[:, index]
    flat = slab.reshape(slab.shape[0] * slab.shape[1], PACK)
    stacked = jnp.concatenate(
        [flat[:, group * BS : (group + 1) * BS] for group in range(RQ)], axis=0
    )
    spectrum = product(table, stacked).astype(jnp.bfloat16)
    half = spectrum.shape[0] // 2
    return jnp.concatenate([spectrum[:half], spectrum[half:]], axis=1)


def lat_inverse(table, values):
    stacked = jnp.concatenate([values[:, :BS], values[:, BS:]], axis=0)
    rows = product(table, stacked).astype(jnp.bfloat16)
    each = rows.shape[0] // RQ
    return jnp.concatenate([rows[group * each : (group + 1) * each] for group in range(RQ)], axis=1)


def forward_body(lat_table, inv_table, first, second, received, sent, spec, hidden, slope, passed):
    for index in range(received.shape[1]):
        rows = pl.ds(index * spec.shape[1], spec.shape[1])
        values = lat_forward(lat_table[...], received, index)
        spec[index] = values
        pre = product(values, first[...])
        squared = pre * pre
        tangent = jnp.tanh(gelu_coeff * (pre + 0.044715 * squared * pre))
        act = (0.5 * pre * (1.0 + tangent)).astype(jnp.bfloat16)
        slope[index] = 0.5 * (1.0 + tangent) + 0.5 * pre * (1.0 - tangent * tangent) * gelu_coeff * (
            1.0 + 3.0 * 0.044715 * squared
        )
        hidden[index] = act
        post = product(act, second[...])
        ratio = jnp.tanh(post / shrink_level)
        passed[index] = ratio * ratio
        out = (post - shrink_level * ratio).astype(jnp.bfloat16)
        sent[:, index] = lat_inverse(inv_table[...], out).reshape(sent.shape[0], -1, PACK)


def backward_body(
    factor,
    lat_table,
    inv_table,
    first,
    second,
    weights,
    received,
    spec,
    hidden,
    slope,
    passed,
    sent,
    grads,
):
    total_first = None
    total_second = None
    for index in range(received.shape[1]):
        cot = lat_forward(lat_table[...], received, index).astype(jnp.float32)
        grad_post = (weights[index] * cot * passed[index]).astype(jnp.bfloat16)
        grad_hid = product_back(grad_post, second[...])
        grad_pre = (grad_hid * slope[index]).astype(jnp.bfloat16)
        back = product_back(grad_pre, first[...]).astype(jnp.bfloat16)
        sent[:, index] = lat_inverse(inv_table[...], back).reshape(sent.shape[0], -1, PACK)
        part_second = product_outer(hidden[index], grad_post)
        part_first = product_outer(spec[index], grad_pre)
        total_second = part_second if index == 0 else total_second + part_second
        total_first = part_first if index == 0 else total_first + part_first
    for slot, total in enumerate((total_first, total_second)):
        grads[2 * slot] = ((total[:BS, :BS] + total[BS:, BS:]) * factor).astype(jnp.bfloat16)
        grads[2 * slot + 1] = ((total[:BS, BS:] - total[BS:, :BS]) * factor).astype(jnp.bfloat16)


def complex_weights(weights, block):
    real, imag = lax.dynamic_index_in_dim(weights, block, 1, keepdims=False)
    return jnp.concatenate(
        [jnp.concatenate([real, imag], axis=1), jnp.concatenate([-imag, real], axis=1)], axis=0
    )


def exchange(source, axis, groups=None):
    return lax.all_to_all(
        source, axis, split_axis=0, concat_axis=0, tiled=True, axis_index_groups=groups
    )


def shards(features, cotangent, weight_first, weight_second):
    lat_count = lax.axis_size("lat")
    lon_count = lax.axis_size("lon")
    band_rows, band_cols, channels = features.shape
    rows_total = band_rows * lat_count
    cols_total = band_cols * lon_count
    kept_total = KWD * lat_count * lon_count
    subs = lon_count // NB
    rows_sub = band_rows // (RQ * subs)
    kept = kept_total // (lat_count * subs)
    lon_index = lax.axis_index("lon")
    block = lon_index % NB
    sub = lon_index // NB
    group = lax.axis_index("lat") * subs + sub
    sub_groups = [[s * NB + b for s in range(subs)] for b in range(NB)]
    bf16 = jnp.bfloat16

    lon_fwd, lon_inv, lon_adj = map(constant, lon_tables(kept_total, cols_total, lon_count, rows_sub))
    lat_fwd, lat_inv = map(constant, lat_tables(rows_total, lat_count, subs))
    first = complex_weights(weight_first, block)
    second = complex_weights(weight_second, block)

    pack = kernel_call(
        functools.partial(pack_body, rows_sub, subs),
        jax.ShapeDtypeStruct((lon_count, rows_sub * band_cols, PACK), bf16),
    )
    unpack = kernel_call(
        functools.partial(unpack_body, rows_sub, subs),
        jax.ShapeDtypeStruct(features.shape, bf16),
    )
    members = lat_count * subs
    deep = 2 * rows_sub
    to_spectra = kernel_call(
        table_body, jax.ShapeDtypeStruct((members, kept * deep, PACK), bf16)
    )
    to_columns = kernel_call(
        table_body, jax.ShapeDtypeStruct((lon_count, rows_sub * band_cols, PACK), bf16)
    )

    def swap(source):
        split = source.reshape(lat_count, subs, kept * deep, PACK)
        split = exchange(split, "lat")
        if subs > 1:
            split = exchange(jnp.swapaxes(split, 0, 1), "lon", sub_groups)
            split = jnp.swapaxes(split, 0, 1)
        return split.reshape(members, kept * deep, PACK)

    whole = deep % 16 == 0
    mid_shape = (members, kept, deep, PACK) if whole else (1, kept, members * deep, PACK)

    def gather_rows(source):
        split = source.reshape(members, kept, deep, PACK)
        return split if whole else jnp.swapaxes(split, 0, 1).reshape(mid_shape)

    def part_rows(source):
        if not whole:
            source = jnp.swapaxes(source.reshape(kept, members, deep, PACK), 0, 1)
        return source.reshape(members, kept * deep, PACK)

    mid = jax.ShapeDtypeStruct(mid_shape, bf16)
    modes = (kept, rows_total, 2 * BS)
    forward = kernel_call(
        forward_body,
        (
            mid,
            jax.ShapeDtypeStruct(modes, bf16),
            jax.ShapeDtypeStruct(modes, bf16),
            jax.ShapeDtypeStruct(modes, jnp.float32),
            jax.ShapeDtypeStruct(modes, jnp.float32),
        ),
    )
    factor = 1.0 / math.sqrt(rows_total * kept_total)
    backward = kernel_call(
        functools.partial(backward_body, factor),
        (mid, jax.ShapeDtypeStruct((4, BS, BS), bf16)),
    )
    held = group * kept + jnp.arange(kept, dtype=jnp.int32)
    mode_weight = jnp.broadcast_to(
        jnp.where(held == 0, 1.0, 2.0).astype(jnp.float32)[:, None, None], (kept, 1, 2 * BS)
    )

    field = exchange(pack(features), "lon")
    field_cot = exchange(pack(cotangent), "lon")
    spectra = swap(to_spectra(lon_fwd, field))
    sent, spec, hidden, slope, passed = forward(
        lat_fwd, lat_inv, first, second, gather_rows(spectra)
    )
    filtered = exchange(to_columns(lon_inv, swap(part_rows(sent))), "lon")

    spectra_cot = swap(to_spectra(lon_fwd, field_cot))
    sent_cot, grads = backward(
        lat_fwd,
        lat_inv,
        first,
        second,
        mode_weight,
        gather_rows(spectra_cot),
        spec,
        hidden,
        slope,
        passed,
    )
    returned = exchange(to_columns(lon_adj, swap(part_rows(sent_cot))), "lon")

    pieces = exchange(grads.reshape(lat_count, 4 * BS // lat_count, BS), "lat")
    piece = jnp.sum(pieces.astype(jnp.float32), axis=0).astype(bf16)
    blocks = lax.all_gather(piece, "lon")
    blocks = jnp.sum(
        blocks.reshape((subs, NB) + piece.shape).astype(jnp.float32), axis=0
    ).astype(bf16)
    total = lax.all_gather(blocks, "lat").astype(jnp.float32)
    total = jnp.moveaxis(total, 1, 0).reshape(NB, 2, 2, BS, BS).transpose(1, 2, 0, 3, 4)
    return (unpack(filtered, features), unpack(returned, cotangent), total[0], total[1])


def solution(mesh):
    in_specs = (P("lat", "lon", None), P("lat", "lon", None), P(), P())
    out_specs = (P("lat", "lon", None), P("lat", "lon", None), P(), P())
    return jax.shard_map(shards, mesh=mesh, in_specs=in_specs, out_specs=out_specs, check_vma=False)
```

```python
import functools
import math

import jax
import jax.numpy as jnp
import ml_dtypes
import numpy as np
from jax import lax
from jax.experimental import pallas as pl
from jax.experimental.pallas import tpu as pltpu
from jax.sharding import PartitionSpec as P

NB = 8
BS = 96
KWD = 1
RQ = 4
PACK = RQ * BS
VMEM_LIMIT = 24 * 1024 * 1024

shrink_level = 0.01
gelu_coeff = 0.7978845608028654


def wave_table(first, second, length):
    product = (first[:, None] * second[None, :]) % length
    angle = np.float32(2.0 * math.pi / length) * product.astype(np.float32)
    scale = np.float32(math.sqrt(length))
    rounded = ml_dtypes.bfloat16
    cos = (np.cos(angle) / scale).astype(rounded).astype(np.float32)
    sin = (np.sin(angle) / scale).astype(rounded).astype(np.float32)
    return cos, sin


def lon_tables(kept, cols, lon_count, rows_sub):
    cos, sin = wave_table(np.arange(kept), np.arange(cols), cols)
    parts = np.stack([cos, -sin], axis=1).reshape(kept, 2, lon_count, cols // lon_count)
    eye = np.eye(rows_sub, dtype=np.float32)
    forward = np.einsum("kpgw,rs->kprgsw", parts, eye).reshape(2 * kept * rows_sub, -1)
    return forward, forward.T


def lat_table(rows, lat_count, subs, rows_sub, pack_modes):
    cos, sin = wave_table(np.arange(rows), np.arange(rows), rows)
    forward = np.stack([np.stack([cos, sin], axis=1), np.stack([-sin, cos], axis=1)])
    split = forward.reshape(2, rows, 2, lat_count, RQ, subs, rows_sub)
    eye = np.eye(pack_modes, dtype=np.float32)
    return np.einsum("aqplgsr,jk->jaqglskpr", split, eye).reshape(2 * pack_modes * rows, -1)


def constant(table):
    return jnp.asarray(table.astype(ml_dtypes.bfloat16))


def kernel_call(body, out_shape, scalars, arrays, scratch=()):
    in_specs = [pl.BlockSpec(memory_space=pltpu.SMEM)] * len(scalars)
    in_specs += [pl.BlockSpec(memory_space=pltpu.VMEM)] * len(arrays)
    return pl.pallas_call(
        body,
        out_shape=out_shape,
        in_specs=in_specs,
        scratch_shapes=list(scratch),
        compiler_params=pltpu.CompilerParams(vmem_limit_bytes=VMEM_LIMIT),
    )(*[value.reshape(1).astype(jnp.int32) for value in scalars], *arrays)


def pack_body(rows_sub, subs, source, packed):
    cols = source.shape[1]
    for sub in range(subs):
        for block in range(NB):
            pieces = []
            for group in range(RQ):
                row = (group * subs + sub) * rows_sub
                piece = source[row : row + rows_sub, :, block * BS : (block + 1) * BS]
                pieces.append(piece.reshape(rows_sub * cols, BS))
            packed[sub * NB + block] = jnp.concatenate(pieces, axis=1)


def unpack_body(rows_sub, subs, packed, base, result):
    cols = base.shape[1]
    for sub in range(subs):
        for group in range(RQ):
            row = (group * subs + sub) * rows_sub
            pieces = [
                packed[sub * NB + block, :, group * BS : (group + 1) * BS] for block in range(NB)
            ]
            update = jnp.concatenate(pieces, axis=1).reshape(rows_sub, cols, NB * BS)
            old = base[row : row + rows_sub]
            result[row : row + rows_sub] = (
                old.astype(jnp.float32) + update.astype(jnp.float32)
            ).astype(jnp.bfloat16)


def product(left, right):
    return jnp.dot(left, right, preferred_element_type=jnp.float32)


def product_back(left, right):
    return lax.dot_general(
        left, right, (((1,), (1,)), ((), ())), preferred_element_type=jnp.float32
    )


def product_outer(left, right):
    return lax.dot_general(
        left, right, (((0,), (0,)), ((), ())), preferred_element_type=jnp.float32
    )


def place(slots, pieces, own):
    for offset, piece in enumerate(pieces):
        slots[jnp.bitwise_xor(own, offset)] = piece[...]


def deal(pieces, slots, own):
    for offset, piece in enumerate(pieces):
        piece[...] = slots[jnp.bitwise_xor(own, offset)]


def spectra_body(member, table, source, *rest):
    sent, slots = rest[:-1], rest[-1]
    flat = source[...].reshape(-1, PACK)
    slots[...] = product(table[...], flat).astype(jnp.bfloat16).reshape(slots.shape)
    deal(sent, slots, member[0])


def columns_body(member, table, *rest):
    received, result, slots = rest[:-2], rest[-2], rest[-1]
    place(slots, received, member[0])
    flat = slots[...].reshape(-1, PACK)
    result[...] = product(table[...], flat).astype(jnp.bfloat16).reshape(result.shape)


def lat_forward(table, slots, tile, deep, rows):
    slab = slots[:, tile * deep : (tile + 1) * deep]
    flat = slab.reshape(slab.shape[0] * deep, PACK)
    stacked = jnp.concatenate(
        [flat[:, group * BS : (group + 1) * BS] for group in range(RQ)], axis=0
    )
    spectrum = product(table, stacked).astype(jnp.bfloat16)
    return [
        jnp.concatenate([spectrum[at : at + rows], spectrum[at + rows : at + 2 * rows]], axis=1)
        for at in range(0, spectrum.shape[0], 2 * rows)
    ]


def lat_inverse(table, values, slots, tile, deep):
    stacked = jnp.concatenate(
        [part for value in values for part in (value[:, :BS], value[:, BS:])], axis=0
    )
    rows = product(table, stacked).astype(jnp.bfloat16)
    each = rows.shape[0] // RQ
    packed = jnp.concatenate([rows[at : at + each] for at in range(0, RQ * each, each)], axis=1)
    slots[:, tile * deep : (tile + 1) * deep] = packed.reshape(slots.shape[0], deep, PACK)


def mode_weight(first_mode, index):
    return jnp.where(first_mode + index == 0, 1.0, 2.0).astype(jnp.float32)


def forward_body(members, pack_modes, member, first_mode, table, first, second, *rest):
    received, rest = rest[:members], rest[members:]
    sent, (spec, hidden, slope, passed, slots) = rest[:members], rest[members:]
    own = member[0]
    kept, rows, _ = spec.shape
    deep = slots.shape[1] * pack_modes // kept
    place(slots, received, own)
    lat = table[...]
    inverse = lat.T
    for tile in range(kept // pack_modes):
        outs = []
        for inner, values in enumerate(lat_forward(lat, slots, tile, deep, rows)):
            index = tile * pack_modes + inner
            spec[index] = values
            pre = product(values, first[...])
            squared = pre * pre
            tangent = jnp.tanh(gelu_coeff * (pre + 0.044715 * squared * pre))
            act = (0.5 * pre * (1.0 + tangent)).astype(jnp.bfloat16)
            slope[index] = 0.5 * (1.0 + tangent) + 0.5 * pre * (
                1.0 - tangent * tangent
            ) * gelu_coeff * (1.0 + 3.0 * 0.044715 * squared)
            hidden[index] = act
            post = product(act, second[...])
            ratio = jnp.tanh(post / shrink_level)
            weight = mode_weight(first_mode[0], index)
            passed[index] = weight * (ratio * ratio)
            outs.append((weight * (post - shrink_level * ratio)).astype(jnp.bfloat16))
        lat_inverse(inverse, outs, slots, tile, deep)
    deal(sent, slots, own)


def backward_body(members, pack_modes, factor, member, lat_own, table, first, second, *rest):
    received, rest = rest[:members], rest[members:]
    (spec, hidden, slope, passed), rest = rest[:4], rest[4:]
    sent, rest = rest[:members], rest[members:]
    shares, (slots, grads) = rest[:-2], rest[-2:]
    own = member[0]
    kept, rows, _ = spec.shape
    deep = slots.shape[1] * pack_modes // kept
    place(slots, received, own)
    lat = table[...]
    inverse = lat.T
    total_first = jnp.zeros((2 * BS, 2 * BS), jnp.float32)
    total_second = jnp.zeros((2 * BS, 2 * BS), jnp.float32)
    for tile in range(kept // pack_modes):
        backs = []
        for inner, values in enumerate(lat_forward(lat, slots, tile, deep, rows)):
            index = tile * pack_modes + inner
            grad_post = (values.astype(jnp.float32) * passed[index]).astype(jnp.bfloat16)
            grad_hid = product_back(grad_post, second[...])
            grad_pre = (grad_hid * slope[index]).astype(jnp.bfloat16)
            backs.append(product_back(grad_pre, first[...]).astype(jnp.bfloat16))
            total_second += product_outer(hidden[index], grad_post)
            total_first += product_outer(spec[index], grad_pre)
        lat_inverse(inverse, backs, slots, tile, deep)
    deal(sent, slots, own)
    share = grads.shape[1]
    for slot, total in enumerate((total_first, total_second)):
        real = (total[:BS, :BS] + total[BS:, BS:]) * factor
        imag = (total[:BS, BS:] - total[BS:, :BS]) * factor
        for part, value in enumerate((real, imag)):
            for at in range(0, BS, share):
                piece = ((2 * slot + part) * BS + at) // share
                grads[piece] = value[at : at + share].astype(jnp.bfloat16)
    deal(shares, grads, lat_own[0])


def weights_body(block, first, second, first_full, second_full):
    for weights, full in ((first, first_full), (second, second_full)):
        real, imag = weights[0, block[0]], weights[1, block[0]]
        full[:BS] = jnp.concatenate([real, imag], axis=1)
        full[BS:] = jnp.concatenate([-imag, real], axis=1)


def assemble_body(lat_count, subs, lat_own, lon_own, *rest):
    gathered, (first, second, slots) = rest[:lat_count], rest[lat_count:]
    rows = gathered[0].shape[1]
    for offset, pieces in enumerate(gathered):
        start = jnp.bitwise_xor(lat_own[0], offset) * rows
        matrix, row = start // BS, pl.multiple_of(start % BS, 16)
        for block in range(NB):
            total = None
            for sub in range(subs):
                value = pieces[jnp.bitwise_xor(lon_own[0], sub * NB + block)].astype(jnp.float32)
                total = value if total is None else total + value
            slots[matrix, block, pl.ds(row, rows)] = total
    first[...] = slots[:2]
    second[...] = slots[2:]


def exchange(source):
    return lax.all_to_all(source, "lon", split_axis=0, concat_axis=0, tiled=True)


def swap(pieces, axes, partners):
    return [pieces[0]] + [
        lax.ppermute(piece, axes, partners(offset))
        for offset, piece in enumerate(pieces)
        if offset
    ]


def shards(features, cotangent, weight_first, weight_second):
    lat_count = lax.axis_size("lat")
    lon_count = lax.axis_size("lon")
    band_rows, band_cols, channels = features.shape
    rows_total = band_rows * lat_count
    cols_total = band_cols * lon_count
    kept_total = KWD * lat_count * lon_count
    subs = lon_count // NB
    members = lat_count * subs
    rows_sub = band_rows // (RQ * subs)
    kept = kept_total // members
    deep = 2 * rows_sub
    pack_modes = max(1, 16 // deep)
    lat_index = lax.axis_index("lat")
    lon_index = lax.axis_index("lon")
    block = lon_index % NB
    member = lat_index * subs + lon_index // NB
    bf16, f32 = jnp.bfloat16, jnp.float32
    array = jax.ShapeDtypeStruct

    def member_pairs(offset):
        pairs = []
        for lat in range(lat_count):
            for lon in range(lon_count):
                other = (lat * subs + lon // NB) ^ offset
                lon_other = other % subs * NB + lon % NB
                pairs.append((lat * lon_count + lon, other // subs * lon_count + lon_other))
        return pairs

    def line_pairs(count):
        return lambda offset: [(place, place ^ offset) for place in range(count)]

    lon_fwd, lon_inv = map(constant, lon_tables(kept_total, cols_total, lon_count, rows_sub))
    lat_both = constant(lat_table(rows_total, lat_count, subs, rows_sub, pack_modes))
    first, second = kernel_call(
        weights_body,
        [array((2 * BS, 2 * BS), bf16)] * 2,
        [block],
        [weight_first, weight_second],
    )

    packed = array((lon_count, rows_sub * band_cols, PACK), bf16)
    piece = array((kept * deep, PACK), bf16)
    slots = pltpu.VMEM((members, kept * deep, PACK), bf16)

    def pack(source):
        return kernel_call(functools.partial(pack_body, rows_sub, subs), packed, [], [source])

    def unpack(source, base):
        body = functools.partial(unpack_body, rows_sub, subs)
        return kernel_call(body, array(base.shape, bf16), [], [source, base])

    def to_spectra(source):
        pieces = kernel_call(
            spectra_body, [piece] * members, [member], [lon_fwd, source], [slots]
        )
        return swap(pieces, ("lat", "lon"), member_pairs)

    def to_columns(pieces):
        received = swap(pieces, ("lat", "lon"), member_pairs)
        return kernel_call(columns_body, packed, [member], [lon_inv, *received], [slots])

    modes = (kept, rows_total, 2 * BS)
    state = [array(modes, bf16), array(modes, bf16), array(modes, f32), array(modes, f32)]
    share = 4 * BS // lat_count

    field = exchange(pack(features))
    field_cot = exchange(pack(cotangent))
    results = kernel_call(
        functools.partial(forward_body, members, pack_modes),
        [piece] * members + state,
        [member, member * kept],
        [lat_both, first, second, *to_spectra(field)],
        [slots],
    )
    filtered = exchange(to_columns(results[:members]))
    cot_results = kernel_call(
        functools.partial(
            backward_body, members, pack_modes, 1.0 / math.sqrt(rows_total * kept_total)
        ),
        [piece] * members + [array((share, BS), bf16)] * lat_count,
        [member, lat_index],
        [lat_both, first, second, *to_spectra(field_cot), *results[members:]],
        [slots, pltpu.VMEM((lat_count, share, BS), bf16)],
    )
    returned = exchange(to_columns(cot_results[:members]))

    shares = swap(cot_results[members:], "lat", line_pairs(lat_count))
    own_share = sum(value.astype(f32) for value in shares).astype(bf16)
    blocks = jnp.stack(swap([own_share] * lon_count, "lon", line_pairs(lon_count)))
    gathered = swap([blocks] * lat_count, "lat", line_pairs(lat_count))
    full = array((2, NB, BS, BS), f32)
    grad_first, grad_second = kernel_call(
        functools.partial(assemble_body, lat_count, subs),
        [full, full],
        [lat_index, lon_index],
        gathered,
        [pltpu.VMEM((4, NB, BS, BS), f32)],
    )
    return (unpack(filtered, features), unpack(returned, cotangent), grad_first, grad_second)


def solution(mesh):
    in_specs = (P("lat", "lon", None), P("lat", "lon", None), P(), P())
    out_specs = (P("lat", "lon", None), P("lat", "lon", None), P(), P())
    return jax.shard_map(shards, mesh=mesh, in_specs=in_specs, out_specs=out_specs, check_vma=False)
```

```python
import functools
import math

import jax
import jax.numpy as jnp
import ml_dtypes
import numpy as np
from jax import lax
from jax.experimental import pallas as pl
from jax.experimental.pallas import tpu as pltpu
from jax.sharding import PartitionSpec as P

NB = 8
BS = 96
KWD = 1
RQ = 4
PACK = RQ * BS
VMEM_LIMIT = 32 * 1024 * 1024

shrink_level = 0.01
gelu_coeff = 0.7978845608028654


def wave_table(first, second, length):
    product = (first[:, None] * second[None, :]) % length
    angle = np.float32(2.0 * math.pi / length) * product.astype(np.float32)
    scale = np.float32(math.sqrt(length))
    rounded = ml_dtypes.bfloat16
    cos = (np.cos(angle) / scale).astype(rounded).astype(np.float32)
    sin = (np.sin(angle) / scale).astype(rounded).astype(np.float32)
    return cos, sin


def lon_tables(kept, cols, lon_count, rows_sub):
    cos, sin = wave_table(np.arange(kept), np.arange(cols), cols)
    parts = np.stack([cos, -sin], axis=1).reshape(kept, 2, lon_count, cols // lon_count)
    eye = np.eye(rows_sub, dtype=np.float32)
    forward = np.einsum("kpgw,rs->kprgsw", parts, eye).reshape(2 * kept * rows_sub, -1)
    return forward, forward.T


def lat_table(rows, lat_count, subs, rows_sub, pack_modes):
    cos, sin = wave_table(np.arange(rows), np.arange(rows), rows)
    forward = np.stack([np.stack([cos, sin], axis=1), np.stack([-sin, cos], axis=1)])
    split = forward.reshape(2, rows, 2, lat_count, RQ, subs, rows_sub)
    eye = np.eye(pack_modes, dtype=np.float32)
    return np.einsum("aqplgsr,jk->jaqglskpr", split, eye).reshape(2 * pack_modes * rows, -1)


def constant(table):
    return jnp.asarray(table.astype(ml_dtypes.bfloat16))


def kernel_call(body, out_shape, scalars, arrays, scratch=(), far=(), far_out=()):
    near, hbm = pl.BlockSpec(memory_space=pltpu.VMEM), pl.BlockSpec(memory_space=pltpu.HBM)
    in_specs = [pl.BlockSpec(memory_space=pltpu.SMEM)] * len(scalars)
    in_specs += [near] * len(arrays) + [hbm] * len(far)
    return pl.pallas_call(
        body,
        out_shape=[*out_shape, *far_out],
        in_specs=in_specs,
        out_specs=[near] * len(out_shape) + [hbm] * len(far_out),
        scratch_shapes=list(scratch),
        compiler_params=pltpu.CompilerParams(vmem_limit_bytes=VMEM_LIMIT),
    )(*[value.reshape(1).astype(jnp.int32) for value in scalars], *arrays, *far)


def pack_body(rows_sub, subs, source, packed):
    cols = source.shape[1]
    for sub in range(subs):
        for block in range(NB):
            pieces = []
            for group in range(RQ):
                row = (group * subs + sub) * rows_sub
                piece = source[row : row + rows_sub, :, block * BS : (block + 1) * BS]
                pieces.append(piece.reshape(rows_sub * cols, BS))
            packed[sub * NB + block] = jnp.concatenate(pieces, axis=1)


def unpack_body(rows_sub, subs, packed, base, result):
    cols = base.shape[1]
    for sub in range(subs):
        for group in range(RQ):
            row = (group * subs + sub) * rows_sub
            pieces = [
                packed[sub * NB + block, :, group * BS : (group + 1) * BS] for block in range(NB)
            ]
            update = jnp.concatenate(pieces, axis=1).reshape(rows_sub, cols, NB * BS)
            old = base[row : row + rows_sub]
            result[row : row + rows_sub] = (
                old.astype(jnp.float32) + update.astype(jnp.float32)
            ).astype(jnp.bfloat16)


def product(left, right):
    return jnp.dot(left, right, preferred_element_type=jnp.float32)


def product_back(left, right):
    return lax.dot_general(
        left, right, (((1,), (1,)), ((), ())), preferred_element_type=jnp.float32
    )


def product_outer(left, right):
    return lax.dot_general(
        left, right, (((0,), (0,)), ((), ())), preferred_element_type=jnp.float32
    )


def place(slots, pieces, own):
    for offset, piece in enumerate(pieces):
        slots[jnp.bitwise_xor(own, offset)] = piece[...]


def deal(pieces, slots, own, sems):
    copies = [
        pltpu.make_async_copy(slots.at[jnp.bitwise_xor(own, offset)], piece, sems.at[offset])
        for offset, piece in enumerate(pieces)
    ]
    for copy in copies:
        copy.start()
    return copies


def finish(copies):
    for copy in copies:
        copy.wait()


def spectra_body(member, table, source, anchor, *rest):
    sent, slots, sems = rest[:-2], rest[-2], rest[-1]
    flat = source[...].reshape(-1, PACK)
    slots[...] = product(table[...], flat).astype(jnp.bfloat16).reshape(slots.shape)
    finish(deal(sent, slots, member[0], sems))


def columns_body(member, table, *rest):
    received, (result, anchor, slots) = rest[:-3], rest[-3:]
    place(slots, received, member[0])
    flat = slots[...].reshape(-1, PACK)
    result[...] = product(table[...], flat).astype(jnp.bfloat16).reshape(result.shape)
    anchor[...] = jnp.zeros_like(anchor)


def lat_forward(table, slots, tile, deep, rows):
    slab = slots[:, tile * deep : (tile + 1) * deep]
    flat = slab.reshape(slab.shape[0] * deep, PACK)
    stacked = jnp.concatenate(
        [flat[:, group * BS : (group + 1) * BS] for group in range(RQ)], axis=0
    )
    spectrum = product(table, stacked).astype(jnp.bfloat16)
    return [
        jnp.concatenate([spectrum[at : at + rows], spectrum[at + rows : at + 2 * rows]], axis=1)
        for at in range(0, spectrum.shape[0], 2 * rows)
    ]


def lat_inverse(table, values, slots, tile, deep):
    stacked = jnp.concatenate(
        [part for value in values for part in (value[:, :BS], value[:, BS:])], axis=0
    )
    rows = product(table, stacked).astype(jnp.bfloat16)
    each = rows.shape[0] // RQ
    packed = jnp.concatenate([rows[at : at + each] for at in range(0, RQ * each, each)], axis=1)
    slots[:, tile * deep : (tile + 1) * deep] = packed.reshape(slots.shape[0], deep, PACK)


def mode_weight(first_mode, index):
    return jnp.where(first_mode + index == 0, 1.0, 2.0).astype(jnp.float32)


def forward_body(members, pack_modes, member, first_mode, table, first, second, *rest):
    received, rest = rest[:members], rest[members:]
    sent, rest = rest[:members], rest[members:]
    saved, (slots, spec, hidden, slope, passed, send_sems, save_sems) = rest[:4], rest[4:]
    own = member[0]
    kept, rows, _ = spec.shape
    deep = slots.shape[1] * pack_modes // kept
    place(slots, received, own)
    lat = table[...]
    inverse = lat.T
    for tile in range(kept // pack_modes):
        outs = []
        for inner, values in enumerate(lat_forward(lat, slots, tile, deep, rows)):
            index = tile * pack_modes + inner
            spec[index] = values
            pre = product(values, first[...])
            squared = pre * pre
            tangent = jnp.tanh(gelu_coeff * (pre + 0.044715 * squared * pre))
            act = (0.5 * pre * (1.0 + tangent)).astype(jnp.bfloat16)
            slope[index] = 0.5 * (1.0 + tangent) + 0.5 * pre * (
                1.0 - tangent * tangent
            ) * gelu_coeff * (1.0 + 3.0 * 0.044715 * squared)
            hidden[index] = act
            post = product(act, second[...])
            ratio = jnp.tanh(post / shrink_level)
            weight = mode_weight(first_mode[0], index)
            passed[index] = weight * (ratio * ratio)
            outs.append((weight * (post - shrink_level * ratio)).astype(jnp.bfloat16))
        lat_inverse(inverse, outs, slots, tile, deep)
    copies = deal(sent, slots, own, send_sems)
    for slot, (near, distant) in enumerate(zip((spec, hidden, slope, passed), saved)):
        copies.append(pltpu.make_async_copy(near, distant, save_sems.at[slot]))
        copies[-1].start()
    finish(copies)


def backward_body(members, shares, pack_modes, factor, member, lat_own, table, first, second, *rest):
    received, rest = rest[:members], rest[members:]
    saved, rest = rest[:4], rest[4:]
    sent, rest = rest[:members], rest[members:]
    parts, (slots, grads, spec, hidden, slope, passed) = rest[:shares], rest[shares:-3]
    send_sems, load_sems, part_sems = rest[-3:]
    own = member[0]
    kept, rows, _ = spec.shape
    deep = slots.shape[1] * pack_modes // kept
    loads = [
        [
            pltpu.make_async_copy(distant.at[index], near.at[index], load_sems.at[slot, index])
            for slot, (near, distant) in enumerate(zip((spec, hidden, slope, passed), saved))
        ]
        for index in range(kept)
    ]
    for group in loads:
        for copy in group:
            copy.start()
    place(slots, received, own)
    lat = table[...]
    inverse = lat.T
    total_first = jnp.zeros((2 * BS, 2 * BS), jnp.float32)
    total_second = jnp.zeros((2 * BS, 2 * BS), jnp.float32)
    for tile in range(kept // pack_modes):
        backs = []
        for inner, values in enumerate(lat_forward(lat, slots, tile, deep, rows)):
            index = tile * pack_modes + inner
            finish(loads[index])
            grad_post = (values.astype(jnp.float32) * passed[index]).astype(jnp.bfloat16)
            grad_hid = product_back(grad_post, second[...])
            grad_pre = (grad_hid * slope[index]).astype(jnp.bfloat16)
            backs.append(product_back(grad_pre, first[...]).astype(jnp.bfloat16))
            total_second += product_outer(hidden[index], grad_post)
            total_first += product_outer(spec[index], grad_pre)
        lat_inverse(inverse, backs, slots, tile, deep)
    copies = deal(sent, slots, own, send_sems)
    share = grads.shape[1]
    for slot, total in enumerate((total_first, total_second)):
        real = (total[:BS, :BS] + total[BS:, BS:]) * factor
        imag = (total[:BS, BS:] - total[BS:, :BS]) * factor
        for part, value in enumerate((real, imag)):
            for at in range(0, BS, share):
                piece = ((2 * slot + part) * BS + at) // share
                grads[piece] = value[at : at + share].astype(jnp.bfloat16)
    finish(copies + deal(parts, grads, lat_own[0], part_sems))


def weights_body(block, first, second, first_full, second_full):
    for weights, full in ((first, first_full), (second, second_full)):
        real, imag = weights[0, block[0]], weights[1, block[0]]
        full[:BS] = jnp.concatenate([real, imag], axis=1)
        full[BS:] = jnp.concatenate([-imag, real], axis=1)


def assemble_body(subs, lat_own, lon_own, near, other, first, second, slots):
    count, rows, _ = near.shape
    lon_count = subs * NB
    for offset in range(2 * count // lon_count):
        half = near if offset * lon_count < count else other
        start = jnp.bitwise_xor(lat_own[0], offset) * rows
        matrix, row = start // BS, pl.multiple_of(start % BS, 16)
        for block in range(NB):
            total = None
            for sub in range(subs):
                place_of = jnp.bitwise_xor(lon_own[0], sub * NB + block)
                value = half[offset * lon_count % count + place_of].astype(jnp.float32)
                total = value if total is None else total + value
            slots[matrix, block, pl.ds(row, rows)] = total
    first[...] = slots[:2]
    second[...] = slots[2:]


def exchange(source):
    return lax.all_to_all(source, "lon", split_axis=0, concat_axis=0, tiled=True)


def swap(pieces, axes, partners):
    return [pieces[0]] + [
        lax.ppermute(piece, axes, partners(offset))
        for offset, piece in enumerate(pieces)
        if offset
    ]


def shards(features, cotangent, weight_first, weight_second):
    lat_count = lax.axis_size("lat")
    lon_count = lax.axis_size("lon")
    band_rows, band_cols, channels = features.shape
    rows_total = band_rows * lat_count
    cols_total = band_cols * lon_count
    kept_total = KWD * lat_count * lon_count
    subs = lon_count // NB
    members = lat_count * subs
    rows_sub = band_rows // (RQ * subs)
    kept = kept_total // members
    deep = 2 * rows_sub
    pack_modes = max(1, 16 // deep)
    lat_index = lax.axis_index("lat")
    lon_index = lax.axis_index("lon")
    block = lon_index % NB
    member = lat_index * subs + lon_index // NB
    bf16, f32 = jnp.bfloat16, jnp.float32
    array = jax.ShapeDtypeStruct

    def member_pairs(offset):
        pairs = []
        for lat in range(lat_count):
            for lon in range(lon_count):
                other = (lat * subs + lon // NB) ^ offset
                lon_other = other % subs * NB + lon % NB
                pairs.append((lat * lon_count + lon, other // subs * lon_count + lon_other))
        return pairs

    def line_pairs(count):
        return lambda offset: [(place, place ^ offset) for place in range(count)]

    lon_fwd, lon_inv = map(constant, lon_tables(kept_total, cols_total, lon_count, rows_sub))
    lat_both = constant(lat_table(rows_total, lat_count, subs, rows_sub, pack_modes))
    first, second = kernel_call(
        weights_body,
        [array((2 * BS, 2 * BS), bf16)] * 2,
        [block],
        [weight_first, weight_second],
    )

    packed = array((lon_count, rows_sub * band_cols, PACK), bf16)
    piece = array((kept * deep, PACK), bf16)
    anchor_shape = array((8, 128), f32)
    slots = pltpu.VMEM((members, kept * deep, PACK), bf16)
    send_sems = pltpu.SemaphoreType.DMA((members,))

    def pack(source):
        body = functools.partial(pack_body, rows_sub, subs)
        return kernel_call(body, [packed], [], [source])[0]

    def unpack(source, base):
        body = functools.partial(unpack_body, rows_sub, subs)
        return kernel_call(body, [array(base.shape, bf16)], [], [source, base])[0]

    def to_spectra(source, anchor):
        pieces = kernel_call(
            spectra_body,
            [],
            [member],
            [lon_fwd, source],
            [slots, send_sems],
            [anchor],
            [piece] * members,
        )
        return swap(pieces, ("lat", "lon"), member_pairs)

    def to_columns(pieces):
        received = swap(pieces, ("lat", "lon"), member_pairs)
        return kernel_call(
            columns_body, [packed, anchor_shape], [member], [lon_inv, *received], [slots]
        )

    modes = (kept, rows_total, 2 * BS)
    types = (bf16, bf16, f32, f32)
    saved = [array(modes, kind) for kind in types]
    state = [pltpu.VMEM(modes, kind) for kind in types]
    share = 4 * BS // lat_count

    field = exchange(pack(features))
    field_cot = exchange(pack(cotangent))
    results = kernel_call(
        functools.partial(forward_body, members, pack_modes),
        [],
        [member, member * kept],
        [lat_both, first, second, *to_spectra(field, jnp.zeros((8, 128), f32))],
        [slots, *state, send_sems, pltpu.SemaphoreType.DMA((4,))],
        [],
        [piece] * members + saved,
    )
    columns, anchor = to_columns(results[:members])
    filtered = exchange(columns)
    cot_results = kernel_call(
        functools.partial(
            backward_body, members, lat_count, pack_modes, 1.0 / math.sqrt(rows_total * kept_total)
        ),
        [],
        [member, lat_index],
        [lat_both, first, second, *to_spectra(field_cot, anchor)],
        [
            slots,
            pltpu.VMEM((lat_count, share, BS), bf16),
            *state,
            send_sems,
            pltpu.SemaphoreType.DMA((4, kept)),
            pltpu.SemaphoreType.DMA((lat_count,)),
        ],
        results[members:],
        [piece] * members + [array((share, BS), bf16)] * lat_count,
    )
    returned = exchange(to_columns(cot_results[:members])[0])

    shares = swap(cot_results[members:], "lat", line_pairs(lat_count))
    gathered = sum(value.astype(f32) for value in shares).astype(bf16)[None]
    halves = None
    for axis, count in (("lon", lon_count), ("lat", lat_count)):
        step = 1
        while step < count:
            if halves is not None:
                gathered = jnp.concatenate(halves)
            halves = (gathered, lax.ppermute(gathered, axis, line_pairs(count)(step)))
            step *= 2
    full = array((2, NB, BS, BS), f32)
    grad_first, grad_second = kernel_call(
        functools.partial(assemble_body, subs),
        [full, full],
        [lat_index, lon_index],
        list(halves),
        [pltpu.VMEM((4, NB, BS, BS), f32)],
    )
    return (unpack(filtered, features), unpack(returned, cotangent), grad_first, grad_second)


def solution(mesh):
    in_specs = (P("lat", "lon", None), P("lat", "lon", None), P(), P())
    out_specs = (P("lat", "lon", None), P("lat", "lon", None), P(), P())
    return jax.shard_map(shards, mesh=mesh, in_specs=in_specs, out_specs=out_specs, check_vma=False)
```

```python
import functools
import math

import jax
import jax.numpy as jnp
import ml_dtypes
import numpy as np
from jax import lax
from jax.experimental import pallas as pl
from jax.experimental.pallas import tpu as pltpu
from jax.sharding import PartitionSpec as P

NB = 8
BS = 96
KWD = 1
RQ = 4
PACK = RQ * BS
MIB = 1024 * 1024

shrink_level = 0.01
gelu_coeff = 0.7978845608028654


def wave_table(first, second, length):
    product = (first[:, None] * second[None, :]) % length
    angle = np.float32(2.0 * math.pi / length) * product.astype(np.float32)
    scale = np.float32(math.sqrt(length))
    rounded = ml_dtypes.bfloat16
    cos = (np.cos(angle) / scale).astype(rounded).astype(np.float32)
    sin = (np.sin(angle) / scale).astype(rounded).astype(np.float32)
    return cos, sin


def lon_tables(kept, cols, lon_count, rows_sub):
    cos, sin = wave_table(np.arange(kept), np.arange(cols), cols)
    parts = np.stack([cos, -sin], axis=1).reshape(kept, 2, lon_count, cols // lon_count)
    eye = np.eye(rows_sub, dtype=np.float32)
    forward = np.einsum("kpgw,rs->kprgsw", parts, eye).reshape(2 * kept * rows_sub, -1)
    return forward, forward.T


def lat_table(rows, lat_count, subs, rows_sub, pack_modes):
    cos, sin = wave_table(np.arange(rows), np.arange(rows), rows)
    forward = np.stack([np.stack([cos, sin], axis=1), np.stack([-sin, cos], axis=1)])
    split = forward.reshape(2, rows, 2, lat_count, RQ, subs, rows_sub)
    eye = np.eye(pack_modes, dtype=np.float32)
    return np.einsum("aqplgsr,jk->jaqglskpr", split, eye).reshape(2 * pack_modes * rows, -1)


def constant(table):
    return jnp.asarray(table.astype(ml_dtypes.bfloat16))


def kernel_call(body, out_shape, scalars, arrays, scratch=(), anchors=(), limit=8 * MIB):
    near, anywhere = pl.BlockSpec(memory_space=pltpu.VMEM), pl.BlockSpec(memory_space=pl.ANY)
    in_specs = [pl.BlockSpec(memory_space=pltpu.SMEM)] * len(scalars)
    in_specs += [near] * len(arrays) + [anywhere] * len(anchors)
    return pl.pallas_call(
        body,
        out_shape=out_shape,
        in_specs=in_specs,
        out_specs=[near] * len(out_shape),
        scratch_shapes=list(scratch),
        compiler_params=pltpu.CompilerParams(vmem_limit_bytes=limit),
    )(*[value.reshape(1).astype(jnp.int32) for value in scalars], *arrays, *anchors)


def pack_body(rows_sub, subs, own, source, *rest):
    sent, slots = rest[:-1], rest[-1]
    cols = source.shape[1]
    for sub in range(subs):
        for block in range(NB):
            pieces = []
            for group in range(RQ):
                row = (group * subs + sub) * rows_sub
                piece = source[row : row + rows_sub, :, block * BS : (block + 1) * BS]
                pieces.append(piece.reshape(rows_sub * cols, BS))
            slots[sub * NB + block] = jnp.concatenate(pieces, axis=1)
    deal(sent, slots, own[0])


def unpack_body(rows_sub, subs, own, base, *rest):
    received, (result, slots) = rest[:-2], rest[-2:]
    cols = base.shape[1]
    place(slots, received, own[0])
    for sub in range(subs):
        for group in range(RQ):
            row = (group * subs + sub) * rows_sub
            pieces = [
                slots[sub * NB + block, :, group * BS : (group + 1) * BS] for block in range(NB)
            ]
            update = jnp.concatenate(pieces, axis=1).reshape(rows_sub, cols, NB * BS)
            old = base[row : row + rows_sub]
            result[row : row + rows_sub] = (
                old.astype(jnp.float32) + update.astype(jnp.float32)
            ).astype(jnp.bfloat16)


def product(left, right):
    return jnp.dot(left, right, preferred_element_type=jnp.float32)


def product_back(left, right):
    return lax.dot_general(
        left, right, (((1,), (1,)), ((), ())), preferred_element_type=jnp.float32
    )


def product_outer(left, right):
    return lax.dot_general(
        left, right, (((0,), (0,)), ((), ())), preferred_element_type=jnp.float32
    )


def place(slots, pieces, own):
    for offset, piece in enumerate(pieces):
        slots[jnp.bitwise_xor(own, offset)] = piece[...]


def deal(pieces, slots, own):
    for offset, piece in enumerate(pieces):
        piece[...] = slots[jnp.bitwise_xor(own, offset)]


def table_body(count, extra, own_in, own_out, table, *rest):
    received, (rest, slots_in, slots_out) = rest[:count], (rest[count:-2], rest[-2], rest[-1])
    place(slots_in, received, own_in[0])
    flat = slots_in[...].reshape(-1, PACK)
    slots_out[...] = product(table[...], flat).astype(jnp.bfloat16).reshape(slots_out.shape)
    deal(rest[extra : extra + slots_out.shape[0]], slots_out, own_out[0])
    for anchor in rest[extra + slots_out.shape[0] :]:
        anchor[...] = jnp.zeros_like(anchor)


def lat_forward(table, slots, tile, deep, rows):
    slab = slots[:, tile * deep : (tile + 1) * deep]
    flat = slab.reshape(slab.shape[0] * deep, PACK)
    stacked = jnp.concatenate(
        [flat[:, group * BS : (group + 1) * BS] for group in range(RQ)], axis=0
    )
    spectrum = product(table, stacked).astype(jnp.bfloat16)
    return [
        jnp.concatenate([spectrum[at : at + rows], spectrum[at + rows : at + 2 * rows]], axis=1)
        for at in range(0, spectrum.shape[0], 2 * rows)
    ]


def lat_inverse(table, values, slots, tile, deep):
    stacked = jnp.concatenate(
        [part for value in values for part in (value[:, :BS], value[:, BS:])], axis=0
    )
    rows = product(table, stacked).astype(jnp.bfloat16)
    each = rows.shape[0] // RQ
    packed = jnp.concatenate([rows[at : at + each] for at in range(0, RQ * each, each)], axis=1)
    slots[:, tile * deep : (tile + 1) * deep] = packed.reshape(slots.shape[0], deep, PACK)


def mode_weight(first_mode, index):
    return jnp.where(first_mode + index == 0, 1.0, 2.0).astype(jnp.float32)


def forward_body(members, pack_modes, member, first_mode, table, first, second, *rest):
    received, rest = rest[:members], rest[members:]
    sent, (spec, hidden, slope, passed, slots) = rest[:members], rest[members:]
    own = member[0]
    kept, rows, _ = spec.shape
    deep = slots.shape[1] * pack_modes // kept
    place(slots, received, own)
    lat = table[...]
    inverse = lat.T
    for tile in range(kept // pack_modes):
        outs = []
        for inner, values in enumerate(lat_forward(lat, slots, tile, deep, rows)):
            index = tile * pack_modes + inner
            spec[index] = values
            pre = product(values, first[...])
            squared = pre * pre
            tangent = jnp.tanh(gelu_coeff * (pre + 0.044715 * squared * pre))
            act = (0.5 * pre * (1.0 + tangent)).astype(jnp.bfloat16)
            slope[index] = 0.5 * (1.0 + tangent) + 0.5 * pre * (
                1.0 - tangent * tangent
            ) * gelu_coeff * (1.0 + 3.0 * 0.044715 * squared)
            hidden[index] = act
            post = product(act, second[...])
            ratio = jnp.tanh(post / shrink_level)
            weight = mode_weight(first_mode[0], index)
            passed[index] = weight * (ratio * ratio)
            outs.append((weight * (post - shrink_level * ratio)).astype(jnp.bfloat16))
        lat_inverse(inverse, outs, slots, tile, deep)
    deal(sent, slots, own)


def backward_body(members, pack_modes, factor, member, lat_own, table, first, second, *rest):
    received, rest = rest[:members], rest[members:]
    (spec, hidden, slope, passed), rest = rest[:4], rest[4:]
    sent, rest = rest[:members], rest[members:]
    shares, (slots, grads) = rest[:-2], rest[-2:]
    own = member[0]
    kept, rows, _ = spec.shape
    deep = slots.shape[1] * pack_modes // kept
    place(slots, received, own)
    lat = table[...]
    inverse = lat.T
    total_first = jnp.zeros((2 * BS, 2 * BS), jnp.float32)
    total_second = jnp.zeros((2 * BS, 2 * BS), jnp.float32)
    for tile in range(kept // pack_modes):
        backs = []
        for inner, values in enumerate(lat_forward(lat, slots, tile, deep, rows)):
            index = tile * pack_modes + inner
            grad_post = (values.astype(jnp.float32) * passed[index]).astype(jnp.bfloat16)
            grad_hid = product_back(grad_post, second[...])
            grad_pre = (grad_hid * slope[index]).astype(jnp.bfloat16)
            backs.append(product_back(grad_pre, first[...]).astype(jnp.bfloat16))
            total_second += product_outer(hidden[index], grad_post)
            total_first += product_outer(spec[index], grad_pre)
        lat_inverse(inverse, backs, slots, tile, deep)
    deal(sent, slots, own)
    share = grads.shape[1]
    for slot, total in enumerate((total_first, total_second)):
        real = (total[:BS, :BS] + total[BS:, BS:]) * factor
        imag = (total[:BS, BS:] - total[BS:, :BS]) * factor
        for part, value in enumerate((real, imag)):
            for at in range(0, BS, share):
                piece = ((2 * slot + part) * BS + at) // share
                grads[piece] = value[at : at + share].astype(jnp.bfloat16)
    deal(shares, grads, lat_own[0])


def weights_body(block, first, second, first_full, second_full):
    for weights, full in ((first, first_full), (second, second_full)):
        real, imag = weights[0, block[0]], weights[1, block[0]]
        full[:BS] = jnp.concatenate([real, imag], axis=1)
        full[BS:] = jnp.concatenate([-imag, real], axis=1)


def assemble_body(lat_count, subs, lat_own, lon_own, *rest):
    gathered, (first, second, slots) = rest[:lat_count], rest[lat_count:]
    rows = gathered[0].shape[1]
    for offset, pieces in enumerate(gathered):
        start = jnp.bitwise_xor(lat_own[0], offset) * rows
        matrix, row = start // BS, pl.multiple_of(start % BS, 16)
        for block in range(NB):
            total = None
            for sub in range(subs):
                value = pieces[jnp.bitwise_xor(lon_own[0], sub * NB + block)].astype(jnp.float32)
                total = value if total is None else total + value
            slots[matrix, block, pl.ds(row, rows)] = total
    first[...] = slots[:2]
    second[...] = slots[2:]


def swap(pieces, axes, partners):
    return [pieces[0]] + [
        lax.ppermute(piece, axes, partners(offset))
        for offset, piece in enumerate(pieces)
        if offset
    ]


def shards(features, cotangent, weight_first, weight_second):
    lat_count = lax.axis_size("lat")
    lon_count = lax.axis_size("lon")
    band_rows, band_cols, channels = features.shape
    rows_total = band_rows * lat_count
    cols_total = band_cols * lon_count
    kept_total = KWD * lat_count * lon_count
    subs = lon_count // NB
    members = lat_count * subs
    rows_sub = band_rows // (RQ * subs)
    kept = kept_total // members
    deep = 2 * rows_sub
    pack_modes = max(1, 16 // deep)
    lat_index = lax.axis_index("lat")
    lon_index = lax.axis_index("lon")
    block = lon_index % NB
    member = lat_index * subs + lon_index // NB
    bf16, f32 = jnp.bfloat16, jnp.float32
    array = jax.ShapeDtypeStruct

    def member_pairs(offset):
        pairs = []
        for lat in range(lat_count):
            for lon in range(lon_count):
                other = (lat * subs + lon // NB) ^ offset
                lon_other = other % subs * NB + lon % NB
                pairs.append((lat * lon_count + lon, other // subs * lon_count + lon_other))
        return pairs

    def line_pairs(count):
        return lambda offset: [(place, place ^ offset) for place in range(count)]

    lon_fwd, lon_inv = map(constant, lon_tables(kept_total, cols_total, lon_count, rows_sub))
    lat_both = constant(lat_table(rows_total, lat_count, subs, rows_sub, pack_modes))
    first, second = kernel_call(
        weights_body,
        [array((2 * BS, 2 * BS), bf16)] * 2,
        [block],
        [weight_first, weight_second],
    )

    lon_piece = array((rows_sub * band_cols, PACK), bf16)
    mid_piece = array((kept * deep, PACK), bf16)
    lon_slots = pltpu.VMEM((lon_count, rows_sub * band_cols, PACK), bf16)
    mid_slots = pltpu.VMEM((members, kept * deep, PACK), bf16)
    anchor_shape = array((8, 128), f32)
    mid_limit = 12 * MIB + 4 * lat_both.size

    def lon_swap(pieces):
        return swap(pieces, "lon", line_pairs(lon_count))

    def mid_swap(pieces):
        return swap(pieces, ("lat", "lon"), member_pairs)

    def pack(source):
        body = functools.partial(pack_body, rows_sub, subs)
        return kernel_call(body, [lon_piece] * lon_count, [lon_index], [source], [lon_slots])

    def unpack(pieces, base):
        body = functools.partial(unpack_body, rows_sub, subs)
        result = array(base.shape, bf16)
        return kernel_call(body, [result], [lon_index], [base, *pieces], [lon_slots])[0]

    def to_spectra(pieces, anchors=()):
        return kernel_call(
            functools.partial(table_body, lon_count, len(anchors)),
            [mid_piece] * members,
            [lon_index, member],
            [lon_fwd, *pieces],
            [lon_slots, mid_slots],
            anchors,
        )

    def to_columns(pieces):
        results = kernel_call(
            functools.partial(table_body, members, 0),
            [lon_piece] * lon_count + [anchor_shape],
            [member, lon_index],
            [lon_inv, *pieces],
            [mid_slots, lon_slots],
        )
        return results[:-1], results[-1:]

    modes = (kept, rows_total, 2 * BS)
    state = [array(modes, kind) for kind in (bf16, bf16, f32, f32)]
    share = 4 * BS // lat_count

    field = lon_swap(pack(features))
    field_cot = lon_swap(pack(cotangent))
    results = kernel_call(
        functools.partial(forward_body, members, pack_modes),
        [mid_piece] * members + state,
        [member, member * kept],
        [lat_both, first, second, *mid_swap(to_spectra(field))],
        [mid_slots],
        limit=mid_limit,
    )
    columns, anchors = to_columns(mid_swap(results[:members]))
    filtered = lon_swap(columns)
    cot_results = kernel_call(
        functools.partial(
            backward_body, members, pack_modes, 1.0 / math.sqrt(rows_total * kept_total)
        ),
        [mid_piece] * members + [array((share, BS), bf16)] * lat_count,
        [member, lat_index],
        [lat_both, first, second, *mid_swap(to_spectra(field_cot, anchors)), *results[members:]],
        [mid_slots, pltpu.VMEM((lat_count, share, BS), bf16)],
        limit=mid_limit,
    )
    shares = swap(cot_results[members:], "lat", line_pairs(lat_count))
    own_share = sum(value.astype(f32) for value in shares).astype(bf16)
    blocks = jnp.stack(lon_swap([own_share] * lon_count))
    returned = lon_swap(to_columns(mid_swap(cot_results[:members]))[0])

    gathered = swap([blocks] * lat_count, "lat", line_pairs(lat_count))
    full = array((2, NB, BS, BS), f32)
    grad_first, grad_second = kernel_call(
        functools.partial(assemble_body, lat_count, subs),
        [full, full],
        [lat_index, lon_index],
        gathered,
        [pltpu.VMEM((4, NB, BS, BS), f32)],
    )
    return (unpack(filtered, features), unpack(returned, cotangent), grad_first, grad_second)


def solution(mesh):
    in_specs = (P("lat", "lon", None), P("lat", "lon", None), P(), P())
    out_specs = (P("lat", "lon", None), P("lat", "lon", None), P(), P())
    return jax.shard_map(shards, mesh=mesh, in_specs=in_specs, out_specs=out_specs, check_vma=False)
```

```python
import functools
import math

import jax
import jax.numpy as jnp
import ml_dtypes
import numpy as np
from jax import lax
from jax.experimental import pallas as pl
from jax.experimental.pallas import tpu as pltpu
from jax.sharding import PartitionSpec as P

NB = 8
BS = 96
KWD = 1
RQ = 4
PACK = RQ * BS
MIB = 1024 * 1024

shrink_level = 0.01
gelu_coeff = 0.7978845608028654


def wave_table(first, second, length):
    product = (first[:, None] * second[None, :]) % length
    angle = np.float32(2.0 * math.pi / length) * product.astype(np.float32)
    scale = np.float32(math.sqrt(length))
    rounded = ml_dtypes.bfloat16
    cos = (np.cos(angle) / scale).astype(rounded).astype(np.float32)
    sin = (np.sin(angle) / scale).astype(rounded).astype(np.float32)
    return cos, sin


def lon_tables(kept, cols, lon_count, rows_sub):
    cos, sin = wave_table(np.arange(kept), np.arange(cols), cols)
    parts = np.stack([cos, -sin], axis=1).reshape(kept, 2, lon_count, cols // lon_count)
    eye = np.eye(rows_sub, dtype=np.float32)
    forward = np.einsum("kpgw,rs->kprgsw", parts, eye).reshape(2 * kept * rows_sub, -1)
    return forward, forward.T


def lat_table(rows, lat_count, subs, rows_sub, pack_modes):
    cos, sin = wave_table(np.arange(rows), np.arange(rows), rows)
    forward = np.stack([np.stack([cos, sin], axis=1), np.stack([-sin, cos], axis=1)])
    split = forward.reshape(2, rows, 2, lat_count, RQ, subs, rows_sub)
    eye = np.eye(pack_modes, dtype=np.float32)
    return np.einsum("aqplgsr,jk->jaqglskpr", split, eye).reshape(2 * pack_modes * rows, -1)


def constant(table):
    return jnp.asarray(table.astype(ml_dtypes.bfloat16))


def kernel_call(body, out_shape, scalars, arrays, scratch=(), anchors=(), limit=8 * MIB):
    near, anywhere = pl.BlockSpec(memory_space=pltpu.VMEM), pl.BlockSpec(memory_space=pl.ANY)
    in_specs = [pl.BlockSpec(memory_space=pltpu.SMEM)] * len(scalars)
    in_specs += [near] * len(arrays) + [anywhere] * len(anchors)
    return pl.pallas_call(
        body,
        out_shape=out_shape,
        in_specs=in_specs,
        out_specs=[near] * len(out_shape),
        scratch_shapes=list(scratch),
        compiler_params=pltpu.CompilerParams(vmem_limit_bytes=limit),
    )(*[value.reshape(1).astype(jnp.int32) for value in scalars], *arrays, *anchors)


def pack_body(rows_sub, subs, own, source, *rest):
    sent, slots = rest[:-1], rest[-1]
    cols = source.shape[1]
    for sub in range(subs):
        for block in range(NB):
            pieces = []
            for group in range(RQ):
                row = (group * subs + sub) * rows_sub
                piece = source[row : row + rows_sub, :, block * BS : (block + 1) * BS]
                pieces.append(piece.reshape(rows_sub * cols, BS))
            slots[sub * NB + block] = jnp.concatenate(pieces, axis=1)
    deal(sent, slots, own[0])


def unpack_body(rows_sub, subs, own, base, *rest):
    received, (result, slots) = rest[:-2], rest[-2:]
    cols = base.shape[1]
    place(slots, received, own[0])
    for sub in range(subs):
        for group in range(RQ):
            row = (group * subs + sub) * rows_sub
            pieces = [
                slots[sub * NB + block, :, group * BS : (group + 1) * BS] for block in range(NB)
            ]
            update = jnp.concatenate(pieces, axis=1).reshape(rows_sub, cols, NB * BS)
            old = base[row : row + rows_sub]
            result[row : row + rows_sub] = (
                old.astype(jnp.float32) + update.astype(jnp.float32)
            ).astype(jnp.bfloat16)


def product(left, right):
    return jnp.dot(left, right, preferred_element_type=jnp.float32)


def product_back(left, right):
    return lax.dot_general(
        left, right, (((1,), (1,)), ((), ())), preferred_element_type=jnp.float32
    )


def product_outer(left, right):
    return lax.dot_general(
        left, right, (((0,), (0,)), ((), ())), preferred_element_type=jnp.float32
    )


def place(slots, pieces, own):
    if len(pieces) == 1:
        slots[...] = pieces[0][...]
        return
    for offset, piece in enumerate(pieces):
        slots[jnp.bitwise_xor(own, offset)] = piece[...]


def deal(pieces, slots, own):
    if len(pieces) == 1:
        pieces[0][...] = slots[...]
        return
    for offset, piece in enumerate(pieces):
        piece[...] = slots[jnp.bitwise_xor(own, offset)]


def table_body(count, extra, own_in, own_out, table, *rest):
    received, (sent, slots_in, slots_out) = rest[:count], (rest[count + extra : -2], *rest[-2:])
    place(slots_in, received, own_in[0])
    flat = slots_in[...].reshape(-1, PACK)
    slots_out[...] = product(table[...], flat).astype(jnp.bfloat16).reshape(slots_out.shape)
    deal(sent, slots_out, own_out[0])


def lat_forward(table, slots, tile, deep, rows):
    slab = slots[:, tile * deep : (tile + 1) * deep]
    flat = slab.reshape(slab.shape[0] * deep, PACK)
    stacked = jnp.concatenate(
        [flat[:, group * BS : (group + 1) * BS] for group in range(RQ)], axis=0
    )
    spectrum = product(table, stacked).astype(jnp.bfloat16)
    return [
        jnp.concatenate([spectrum[at : at + rows], spectrum[at + rows : at + 2 * rows]], axis=1)
        for at in range(0, spectrum.shape[0], 2 * rows)
    ]


def lat_inverse(table, values, slots, tile, deep):
    stacked = jnp.concatenate(
        [part for value in values for part in (value[:, :BS], value[:, BS:])], axis=0
    )
    rows = product(table, stacked).astype(jnp.bfloat16)
    each = rows.shape[0] // RQ
    packed = jnp.concatenate([rows[at : at + each] for at in range(0, RQ * each, each)], axis=1)
    slots[:, tile * deep : (tile + 1) * deep] = packed.reshape(slots.shape[0], deep, PACK)


def mode_weight(first_mode, index):
    return jnp.where(first_mode + index == 0, 1.0, 2.0).astype(jnp.float32)


def forward_body(members, pack_modes, member, first_mode, table, first, second, *rest):
    received, rest = rest[:members], rest[members:]
    sent, (spec, hidden, slope, passed, anchor, slots) = rest[:members], rest[members:]
    anchor[...] = jnp.zeros_like(anchor)
    own = member[0]
    kept, rows, _ = spec.shape
    deep = slots.shape[1] * pack_modes // kept
    place(slots, received, own)
    lat = table[...]
    inverse = lat.T
    for tile in range(kept // pack_modes):
        outs = []
        for inner, values in enumerate(lat_forward(lat, slots, tile, deep, rows)):
            index = tile * pack_modes + inner
            spec[index] = values
            pre = product(values, first[...])
            squared = pre * pre
            tangent = jnp.tanh(gelu_coeff * (pre + 0.044715 * squared * pre))
            act = (0.5 * pre * (1.0 + tangent)).astype(jnp.bfloat16)
            slope[index] = 0.5 * (1.0 + tangent) + 0.5 * pre * (
                1.0 - tangent * tangent
            ) * gelu_coeff * (1.0 + 3.0 * 0.044715 * squared)
            hidden[index] = act
            post = product(act, second[...])
            ratio = jnp.tanh(post / shrink_level)
            weight = mode_weight(first_mode[0], index)
            passed[index] = weight * (ratio * ratio)
            outs.append((weight * (post - shrink_level * ratio)).astype(jnp.bfloat16))
        lat_inverse(inverse, outs, slots, tile, deep)
    deal(sent, slots, own)


def backward_body(members, pack_modes, factor, member, lat_own, table, first, second, *rest):
    received, rest = rest[:members], rest[members:]
    (spec, hidden, slope, passed), rest = rest[:4], rest[4:]
    sent, rest = rest[:members], rest[members:]
    shares, (slots, grads) = rest[:-2], rest[-2:]
    own = member[0]
    kept, rows, _ = spec.shape
    deep = slots.shape[1] * pack_modes // kept
    place(slots, received, own)
    lat = table[...]
    inverse = lat.T
    total_first = jnp.zeros((2 * BS, 2 * BS), jnp.float32)
    total_second = jnp.zeros((2 * BS, 2 * BS), jnp.float32)
    for tile in range(kept // pack_modes):
        backs = []
        for inner, values in enumerate(lat_forward(lat, slots, tile, deep, rows)):
            index = tile * pack_modes + inner
            grad_post = (values.astype(jnp.float32) * passed[index]).astype(jnp.bfloat16)
            grad_hid = product_back(grad_post, second[...])
            grad_pre = (grad_hid * slope[index]).astype(jnp.bfloat16)
            backs.append(product_back(grad_pre, first[...]).astype(jnp.bfloat16))
            total_second += product_outer(hidden[index], grad_post)
            total_first += product_outer(spec[index], grad_pre)
        lat_inverse(inverse, backs, slots, tile, deep)
    deal(sent, slots, own)
    share = grads.shape[1]
    for slot, total in enumerate((total_first, total_second)):
        real = (total[:BS, :BS] + total[BS:, BS:]) * factor
        imag = (total[:BS, BS:] - total[BS:, :BS]) * factor
        for part, value in enumerate((real, imag)):
            for at in range(0, BS, share):
                piece = ((2 * slot + part) * BS + at) // share
                grads[piece] = value[at : at + share].astype(jnp.bfloat16)
    deal(shares, grads, lat_own[0])


def weights_body(block, first, second, first_full, second_full):
    for weights, full in ((first, first_full), (second, second_full)):
        real, imag = weights[0, block[0]], weights[1, block[0]]
        full[:BS] = jnp.concatenate([real, imag], axis=1)
        full[BS:] = jnp.concatenate([-imag, real], axis=1)


def assemble_body(lat_count, subs, lat_own, *rest):
    gathered, (first, second, slots) = rest[:lat_count], rest[lat_count:]
    rows = gathered[0].shape[1]
    for offset, pieces in enumerate(gathered):
        start = jnp.bitwise_xor(lat_own[0], offset) * rows
        matrix, row = start // BS, pl.multiple_of(start % BS, 16)
        for block in range(NB):
            total = None
            for sub in range(subs):
                value = pieces[sub * NB + block].astype(jnp.float32)
                total = value if total is None else total + value
            slots[matrix, block, pl.ds(row, rows)] = total
    first[...] = slots[:2]
    second[...] = slots[2:]


def exchange(source):
    return lax.all_to_all(source, "lon", split_axis=0, concat_axis=0, tiled=True)


def swap(pieces, axes, partners):
    return [pieces[0]] + [
        lax.ppermute(piece, axes, partners(offset))
        for offset, piece in enumerate(pieces)
        if offset
    ]


def shards(features, cotangent, weight_first, weight_second):
    lat_count = lax.axis_size("lat")
    lon_count = lax.axis_size("lon")
    band_rows, band_cols, channels = features.shape
    rows_total = band_rows * lat_count
    cols_total = band_cols * lon_count
    kept_total = KWD * lat_count * lon_count
    subs = lon_count // NB
    members = lat_count * subs
    rows_sub = band_rows // (RQ * subs)
    kept = kept_total // members
    deep = 2 * rows_sub
    pack_modes = max(1, 16 // deep)
    lat_index = lax.axis_index("lat")
    lon_index = lax.axis_index("lon")
    block = lon_index % NB
    member = lat_index * subs + lon_index // NB
    bf16, f32 = jnp.bfloat16, jnp.float32
    array = jax.ShapeDtypeStruct

    def member_pairs(offset):
        pairs = []
        for lat in range(lat_count):
            for lon in range(lon_count):
                other = (lat * subs + lon // NB) ^ offset
                lon_other = other % subs * NB + lon % NB
                pairs.append((lat * lon_count + lon, other // subs * lon_count + lon_other))
        return pairs

    def line_pairs(count):
        return lambda offset: [(place, place ^ offset) for place in range(count)]

    lon_fwd, lon_inv = map(constant, lon_tables(kept_total, cols_total, lon_count, rows_sub))
    lat_both = constant(lat_table(rows_total, lat_count, subs, rows_sub, pack_modes))
    first, second = kernel_call(
        weights_body,
        [array((2 * BS, 2 * BS), bf16)] * 2,
        [block],
        [weight_first, weight_second],
    )

    lon_piece = array((rows_sub * band_cols, PACK), bf16)
    lon_whole = array((lon_count, rows_sub * band_cols, PACK), bf16)
    mid_piece = array((kept * deep, PACK), bf16)
    lon_slots = pltpu.VMEM(lon_whole.shape, bf16)
    mid_slots = pltpu.VMEM((members, kept * deep, PACK), bf16)
    mid_limit = 12 * MIB + 4 * lat_both.size

    def lon_swap(pieces):
        if len(pieces) == 1:
            return [exchange(pieces[0])]
        return swap(pieces, "lon", line_pairs(lon_count))

    def mid_swap(pieces):
        return swap(pieces, ("lat", "lon"), member_pairs)

    def pack(source, sent):
        body = functools.partial(pack_body, rows_sub, subs)
        return kernel_call(body, sent, [lon_index], [source], [lon_slots])

    def unpack(pieces, base):
        body = functools.partial(unpack_body, rows_sub, subs)
        result = array(base.shape, bf16)
        return kernel_call(body, [result], [lon_index], [base, *pieces], [lon_slots])[0]

    def to_spectra(pieces, anchors=()):
        return kernel_call(
            functools.partial(table_body, len(pieces), len(anchors)),
            [mid_piece] * members,
            [lon_index, member],
            [lon_fwd, *pieces],
            [lon_slots, mid_slots],
            anchors,
        )

    def to_columns(pieces, sent):
        return kernel_call(
            functools.partial(table_body, members, 0),
            sent,
            [member, lon_index],
            [lon_inv, *pieces],
            [mid_slots, lon_slots],
        )

    modes = (kept, rows_total, 2 * BS)
    state = [array(modes, kind) for kind in (bf16, bf16, f32, f32)]
    share = 4 * BS // lat_count

    in_one, in_pieces = [lon_whole], [lon_piece] * lon_count
    field = lon_swap(pack(features, in_pieces))
    field_cot = lon_swap(pack(cotangent, in_one))
    results = kernel_call(
        functools.partial(forward_body, members, pack_modes),
        [mid_piece] * members + state + [array((8, 128), f32)],
        [member, member * kept],
        [lat_both, first, second, *mid_swap(to_spectra(field))],
        [mid_slots],
        limit=mid_limit,
    )
    saved, anchors = results[members:-1], results[-1:]
    filtered = lon_swap(to_columns(mid_swap(results[:members]), in_one))
    cot_results = kernel_call(
        functools.partial(
            backward_body, members, pack_modes, 1.0 / math.sqrt(rows_total * kept_total)
        ),
        [mid_piece] * members + [array((share, BS), bf16)] * lat_count,
        [member, lat_index],
        [lat_both, first, second, *mid_swap(to_spectra(field_cot, anchors)), *saved],
        [mid_slots, pltpu.VMEM((lat_count, share, BS), bf16)],
        limit=mid_limit,
    )
    returned = lon_swap(to_columns(mid_swap(cot_results[:members]), in_pieces))
    shares = swap(cot_results[members:], "lat", line_pairs(lat_count))
    own_share = sum(value.astype(f32) for value in shares).astype(bf16)
    blocks = exchange(jnp.broadcast_to(own_share, (lon_count, share, BS)))

    gathered = swap([blocks] * lat_count, "lat", line_pairs(lat_count))
    full = array((2, NB, BS, BS), f32)
    grad_first, grad_second = kernel_call(
        functools.partial(assemble_body, lat_count, subs),
        [full, full],
        [lat_index],
        gathered,
        [pltpu.VMEM((4, NB, BS, BS), f32)],
    )
    return (unpack(filtered, features), unpack(returned, cotangent), grad_first, grad_second)


def solution(mesh):
    in_specs = (P("lat", "lon", None), P("lat", "lon", None), P(), P())
    out_specs = (P("lat", "lon", None), P("lat", "lon", None), P(), P())
    return jax.shard_map(shards, mesh=mesh, in_specs=in_specs, out_specs=out_specs, check_vma=False)
```

```python
import functools
import math

import jax
import jax.numpy as jnp
import ml_dtypes
import numpy as np
from jax import lax
from jax.experimental import pallas as pl
from jax.experimental.pallas import tpu as pltpu
from jax.sharding import PartitionSpec as P

NB = 8
BS = 96
KWD = 1
RQ = 4
PACK = RQ * BS
MIB = 1024 * 1024

shrink_level = 0.01
gelu_coeff = 0.7978845608028654


def wave_table(first, second, length):
    product = (first[:, None] * second[None, :]) % length
    angle = np.float32(2.0 * math.pi / length) * product.astype(np.float32)
    scale = np.float32(math.sqrt(length))
    rounded = ml_dtypes.bfloat16
    cos = (np.cos(angle) / scale).astype(rounded).astype(np.float32)
    sin = (np.sin(angle) / scale).astype(rounded).astype(np.float32)
    return cos, sin


def lon_tables(kept, cols, lon_count, rows_sub):
    cos, sin = wave_table(np.arange(kept), np.arange(cols), cols)
    parts = np.stack([cos, -sin], axis=1).reshape(kept, 2, lon_count, cols // lon_count)
    eye = np.eye(rows_sub, dtype=np.float32)
    forward = np.einsum("kpgw,rs->kprgsw", parts, eye).reshape(2 * kept * rows_sub, -1)
    return forward, forward.T


def lat_table(rows, lat_count, subs, rows_sub, pack_modes):
    cos, sin = wave_table(np.arange(rows), np.arange(rows), rows)
    forward = np.stack([np.stack([cos, sin], axis=1), np.stack([-sin, cos], axis=1)])
    split = forward.reshape(2, rows, 2, lat_count, RQ, subs, rows_sub)
    eye = np.eye(pack_modes, dtype=np.float32)
    return np.einsum("aqplgsr,jk->jaqglskpr", split, eye).reshape(2 * pack_modes * rows, -1)


def constant(table):
    return jnp.asarray(table.astype(ml_dtypes.bfloat16))


def kernel_call(body, out_shape, scalars, arrays, scratch=(), anchors=(), limit=8 * MIB):
    near, anywhere = pl.BlockSpec(memory_space=pltpu.VMEM), pl.BlockSpec(memory_space=pl.ANY)
    in_specs = [pl.BlockSpec(memory_space=pltpu.SMEM)] * len(scalars)
    in_specs += [near] * len(arrays) + [anywhere] * len(anchors)
    return pl.pallas_call(
        body,
        out_shape=out_shape,
        in_specs=in_specs,
        out_specs=[near] * len(out_shape),
        scratch_shapes=list(scratch),
        compiler_params=pltpu.CompilerParams(vmem_limit_bytes=limit),
    )(*[value.reshape(1).astype(jnp.int32) for value in scalars], *arrays, *anchors)


def pinned(arrays):
    return [pltpu.with_memory_space_constraint(value, pltpu.VMEM) for value in arrays]


def pack_body(rows_sub, subs, extra, own, source, *rest):
    sent, slots = rest[extra:-1], rest[-1]
    cols = source.shape[1]
    for sub in range(subs):
        for block in range(NB):
            pieces = []
            for group in range(RQ):
                row = (group * subs + sub) * rows_sub
                piece = source[row : row + rows_sub, :, block * BS : (block + 1) * BS]
                pieces.append(piece.reshape(rows_sub * cols, BS))
            slots[sub * NB + block] = jnp.concatenate(pieces, axis=1)
    deal(sent, slots, own[0])


def unpack_body(rows_sub, subs, own, base, *rest):
    received, (result, slots) = rest[:-2], rest[-2:]
    cols = base.shape[1]
    place(slots, received, own[0])
    for sub in range(subs):
        for group in range(RQ):
            row = (group * subs + sub) * rows_sub
            pieces = [
                slots[sub * NB + block, :, group * BS : (group + 1) * BS] for block in range(NB)
            ]
            update = jnp.concatenate(pieces, axis=1).reshape(rows_sub, cols, NB * BS)
            old = base[row : row + rows_sub]
            result[row : row + rows_sub] = (
                old.astype(jnp.float32) + update.astype(jnp.float32)
            ).astype(jnp.bfloat16)


def product(left, right):
    return jnp.dot(left, right, preferred_element_type=jnp.float32)


def product_back(left, right):
    return lax.dot_general(
        left, right, (((1,), (1,)), ((), ())), preferred_element_type=jnp.float32
    )


def product_outer(left, right):
    return lax.dot_general(
        left, right, (((0,), (0,)), ((), ())), preferred_element_type=jnp.float32
    )


def place(slots, pieces, own):
    if len(pieces) == 1:
        slots[...] = pieces[0][...]
        return
    for offset, piece in enumerate(pieces):
        slots[jnp.bitwise_xor(own, offset)] = piece[...]


def deal(pieces, slots, own):
    if len(pieces) == 1:
        pieces[0][...] = slots[...]
        return
    for offset, piece in enumerate(pieces):
        piece[...] = slots[jnp.bitwise_xor(own, offset)]


def table_body(count, extra, own_in, own_out, table, *rest):
    received, (sent, anchor, slots_in, slots_out) = (
        rest[:count],
        (rest[count + extra : -3], *rest[-3:]),
    )
    anchor[...] = jnp.zeros_like(anchor)
    place(slots_in, received, own_in[0])
    flat = slots_in[...].reshape(-1, PACK)
    slots_out[...] = product(table[...], flat).astype(jnp.bfloat16).reshape(slots_out.shape)
    deal(sent, slots_out, own_out[0])


def lat_forward(table, slots, tile, deep, rows):
    slab = slots[:, tile * deep : (tile + 1) * deep]
    flat = slab.reshape(slab.shape[0] * deep, PACK)
    stacked = jnp.concatenate(
        [flat[:, group * BS : (group + 1) * BS] for group in range(RQ)], axis=0
    )
    spectrum = product(table, stacked).astype(jnp.bfloat16)
    return [
        jnp.concatenate([spectrum[at : at + rows], spectrum[at + rows : at + 2 * rows]], axis=1)
        for at in range(0, spectrum.shape[0], 2 * rows)
    ]


def lat_inverse(table, values, slots, tile, deep):
    stacked = jnp.concatenate(
        [part for value in values for part in (value[:, :BS], value[:, BS:])], axis=0
    )
    rows = product(table, stacked).astype(jnp.bfloat16)
    each = rows.shape[0] // RQ
    packed = jnp.concatenate([rows[at : at + each] for at in range(0, RQ * each, each)], axis=1)
    slots[:, tile * deep : (tile + 1) * deep] = packed.reshape(slots.shape[0], deep, PACK)


def mode_weight(first_mode, index):
    return jnp.where(first_mode + index == 0, 1.0, 2.0).astype(jnp.float32)


def forward_body(members, pack_modes, member, first_mode, table, first, second, *rest):
    received, rest = rest[:members], rest[members:]
    sent, (spec, hidden, slope, passed, slots) = rest[:members], rest[members:]
    own = member[0]
    kept, rows, _ = spec.shape
    deep = slots.shape[1] * pack_modes // kept
    place(slots, received, own)
    lat = table[...]
    inverse = lat.T
    for tile in range(kept // pack_modes):
        outs = []
        for inner, values in enumerate(lat_forward(lat, slots, tile, deep, rows)):
            index = tile * pack_modes + inner
            spec[index] = values
            pre = product(values, first[...])
            squared = pre * pre
            tangent = jnp.tanh(gelu_coeff * (pre + 0.044715 * squared * pre))
            act = (0.5 * pre * (1.0 + tangent)).astype(jnp.bfloat16)
            slope[index] = 0.5 * (1.0 + tangent) + 0.5 * pre * (
                1.0 - tangent * tangent
            ) * gelu_coeff * (1.0 + 3.0 * 0.044715 * squared)
            hidden[index] = act
            post = product(act, second[...])
            ratio = jnp.tanh(post / shrink_level)
            weight = mode_weight(first_mode[0], index)
            passed[index] = weight * (ratio * ratio)
            outs.append((weight * (post - shrink_level * ratio)).astype(jnp.bfloat16))
        lat_inverse(inverse, outs, slots, tile, deep)
    deal(sent, slots, own)


def backward_body(members, pack_modes, factor, member, lat_own, table, first, second, *rest):
    received, rest = rest[:members], rest[members:]
    (spec, hidden, slope, passed), rest = rest[:4], rest[4:]
    sent, rest = rest[:members], rest[members:]
    shares, (slots, grads) = rest[:-2], rest[-2:]
    own = member[0]
    kept, rows, _ = spec.shape
    deep = slots.shape[1] * pack_modes // kept
    place(slots, received, own)
    lat = table[...]
    inverse = lat.T
    total_first = jnp.zeros((2 * BS, 2 * BS), jnp.float32)
    total_second = jnp.zeros((2 * BS, 2 * BS), jnp.float32)
    for tile in range(kept // pack_modes):
        backs = []
        for inner, values in enumerate(lat_forward(lat, slots, tile, deep, rows)):
            index = tile * pack_modes + inner
            grad_post = (values.astype(jnp.float32) * passed[index]).astype(jnp.bfloat16)
            grad_hid = product_back(grad_post, second[...])
            grad_pre = (grad_hid * slope[index]).astype(jnp.bfloat16)
            backs.append(product_back(grad_pre, first[...]).astype(jnp.bfloat16))
            total_second += product_outer(hidden[index], grad_post)
            total_first += product_outer(spec[index], grad_pre)
        lat_inverse(inverse, backs, slots, tile, deep)
    deal(sent, slots, own)
    share = grads.shape[1]
    for slot, total in enumerate((total_first, total_second)):
        real = (total[:BS, :BS] + total[BS:, BS:]) * factor
        imag = (total[:BS, BS:] - total[BS:, :BS]) * factor
        for part, value in enumerate((real, imag)):
            for at in range(0, BS, share):
                piece = ((2 * slot + part) * BS + at) // share
                grads[piece] = value[at : at + share].astype(jnp.bfloat16)
    deal(shares, grads, lat_own[0])


def weights_body(block, first, second, first_full, second_full):
    for weights, full in ((first, first_full), (second, second_full)):
        real, imag = weights[0, block[0]], weights[1, block[0]]
        full[:BS] = jnp.concatenate([real, imag], axis=1)
        full[BS:] = jnp.concatenate([-imag, real], axis=1)


def assemble_body(lat_count, subs, lat_own, *rest):
    gathered, (first, second, slots) = rest[:lat_count], rest[lat_count:]
    rows = gathered[0].shape[1]
    for offset, pieces in enumerate(gathered):
        start = jnp.bitwise_xor(lat_own[0], offset) * rows
        matrix, row = start // BS, pl.multiple_of(start % BS, 16)
        for block in range(NB):
            total = None
            for sub in range(subs):
                value = pieces[sub * NB + block].astype(jnp.float32)
                total = value if total is None else total + value
            slots[matrix, block, pl.ds(row, rows)] = total
    first[...] = slots[:2]
    second[...] = slots[2:]


def exchange(source):
    return lax.all_to_all(source, "lon", split_axis=0, concat_axis=0, tiled=True)


def swap(pieces, axes, partners):
    return [pieces[0]] + [
        lax.ppermute(piece, axes, partners(offset))
        for offset, piece in enumerate(pieces)
        if offset
    ]


def shards(features, cotangent, weight_first, weight_second):
    lat_count = lax.axis_size("lat")
    lon_count = lax.axis_size("lon")
    band_rows, band_cols, channels = features.shape
    rows_total = band_rows * lat_count
    cols_total = band_cols * lon_count
    kept_total = KWD * lat_count * lon_count
    subs = lon_count // NB
    members = lat_count * subs
    rows_sub = band_rows // (RQ * subs)
    kept = kept_total // members
    deep = 2 * rows_sub
    pack_modes = max(1, 16 // deep)
    lat_index = lax.axis_index("lat")
    lon_index = lax.axis_index("lon")
    block = lon_index % NB
    member = lat_index * subs + lon_index // NB
    bf16, f32 = jnp.bfloat16, jnp.float32
    array = jax.ShapeDtypeStruct

    def member_pairs(offset):
        pairs = []
        for lat in range(lat_count):
            for lon in range(lon_count):
                other = (lat * subs + lon // NB) ^ offset
                lon_other = other % subs * NB + lon % NB
                pairs.append((lat * lon_count + lon, other // subs * lon_count + lon_other))
        return pairs

    def line_pairs(count):
        return lambda offset: [(place, place ^ offset) for place in range(count)]

    lon_fwd, lon_inv = map(constant, lon_tables(kept_total, cols_total, lon_count, rows_sub))
    lat_both = constant(lat_table(rows_total, lat_count, subs, rows_sub, pack_modes))
    first, second = kernel_call(
        weights_body,
        [array((2 * BS, 2 * BS), bf16)] * 2,
        [block],
        [weight_first, weight_second],
    )

    lon_piece = pltpu.VMEM((rows_sub * band_cols, PACK), bf16)
    lon_whole = array((lon_count, rows_sub * band_cols, PACK), bf16)
    mid_piece = pltpu.VMEM((kept * deep, PACK), bf16)
    lon_slots = pltpu.VMEM(lon_whole.shape, bf16)
    mid_slots = pltpu.VMEM((members, kept * deep, PACK), bf16)
    mid_limit = 12 * MIB + 4 * lat_both.size

    def lon_swap(pieces):
        if len(pieces) == 1:
            return [exchange(pieces[0])]
        return pinned(swap(pieces, "lon", line_pairs(lon_count)))

    def mid_swap(pieces):
        return pinned(swap(pieces, ("lat", "lon"), member_pairs))

    def pack(source, sent, anchors=()):
        body = functools.partial(pack_body, rows_sub, subs, len(anchors))
        return kernel_call(body, sent, [lon_index], [source], [lon_slots], anchors)

    def unpack(pieces, base):
        body = functools.partial(unpack_body, rows_sub, subs)
        result = array(base.shape, bf16)
        return kernel_call(body, [result], [lon_index], [base, *pieces], [lon_slots])[0]

    def to_spectra(pieces, anchors=()):
        return kernel_call(
            functools.partial(table_body, len(pieces), len(anchors)),
            [mid_piece] * members + [array((8, 128), f32)],
            [lon_index, member],
            [lon_fwd, *pieces],
            [lon_slots, mid_slots],
            anchors,
        )

    def to_columns(pieces, sent):
        return kernel_call(
            functools.partial(table_body, members, 0),
            sent + [array((8, 128), f32)],
            [member, lon_index],
            [lon_inv, *pieces],
            [mid_slots, lon_slots],
        )

    modes = (kept, rows_total, 2 * BS)
    state = [pltpu.VMEM(modes, kind) for kind in (bf16, bf16, f32, f32)]
    share = 4 * BS // lat_count

    in_one, in_pieces = [lon_whole], [lon_piece] * lon_count
    field = lon_swap(pack(features, in_pieces))
    field_cot = lon_swap(pack(cotangent, in_one, field[2:3]))
    results = kernel_call(
        functools.partial(forward_body, members, pack_modes),
        [mid_piece] * members + state,
        [member, member * kept],
        [lat_both, first, second, *mid_swap(to_spectra(field)[:members])],
        [mid_slots],
        limit=mid_limit,
    )
    columns = to_columns(mid_swap(results[:members]), in_one)
    filtered = lon_swap(columns[:1])
    spectra_cot = mid_swap(to_spectra(field_cot, columns[1:])[:members])
    cot_results = kernel_call(
        functools.partial(
            backward_body, members, pack_modes, 1.0 / math.sqrt(rows_total * kept_total)
        ),
        [mid_piece] * members + [array((share, BS), bf16)] * lat_count,
        [member, lat_index],
        [lat_both, first, second, *spectra_cot, *pinned(results[members:])],
        [mid_slots, pltpu.VMEM((lat_count, share, BS), bf16)],
        limit=mid_limit,
    )
    returned = lon_swap(to_columns(mid_swap(cot_results[:members]), in_pieces)[:-1])
    shares = swap(cot_results[members:], "lat", line_pairs(lat_count))
    own_share = sum(value.astype(f32) for value in shares).astype(bf16)
    blocks = exchange(jnp.broadcast_to(own_share, (lon_count, share, BS)))

    gathered = {0: blocks}
    step = lat_count // 2
    while step:
        for offset in sorted(gathered):
            moved = lax.ppermute(gathered[offset], "lat", line_pairs(lat_count)(step))
            gathered[offset | step] = moved
        step //= 2
    gathered = [gathered[offset] for offset in range(lat_count)]
    full = array((2, NB, BS, BS), f32)
    grad_first, grad_second = kernel_call(
        functools.partial(assemble_body, lat_count, subs),
        [full, full],
        [lat_index],
        gathered,
        [pltpu.VMEM((4, NB, BS, BS), f32)],
    )
    return (unpack(filtered, features), unpack(returned, cotangent), grad_first, grad_second)


def solution(mesh):
    in_specs = (P("lat", "lon", None), P("lat", "lon", None), P(), P())
    out_specs = (P("lat", "lon", None), P("lat", "lon", None), P(), P())
    return jax.shard_map(shards, mesh=mesh, in_specs=in_specs, out_specs=out_specs, check_vma=False)
```

```python
import functools
import math

import jax
import jax.numpy as jnp
import ml_dtypes
import numpy as np
from jax import lax
from jax.experimental import pallas as pl
from jax.experimental.pallas import tpu as pltpu
from jax.sharding import PartitionSpec as P

NB = 8
BS = 96
KWD = 1
RQ = 4
PACK = RQ * BS
MIB = 1024 * 1024

shrink_level = 0.01
gelu_coeff = 0.7978845608028654


def wave_table(first, second, length):
    product = (first[:, None] * second[None, :]) % length
    angle = np.float32(2.0 * math.pi / length) * product.astype(np.float32)
    scale = np.float32(math.sqrt(length))
    rounded = ml_dtypes.bfloat16
    cos = (np.cos(angle) / scale).astype(rounded).astype(np.float32)
    sin = (np.sin(angle) / scale).astype(rounded).astype(np.float32)
    return cos, sin


def lon_tables(kept, cols, lon_count, rows):
    cos, sin = wave_table(np.arange(kept), np.arange(cols), cols)
    parts = np.stack([cos, -sin], axis=1).reshape(kept, 2, lon_count, cols // lon_count)
    eye = np.eye(rows, dtype=np.float32)
    forward = np.einsum("kpgw,rs->kprgsw", parts, eye).reshape(2 * kept * rows, -1)
    return forward, forward.T


def lat_table(rows, lat_count, subs, rows_sub, rows_cut, pack_modes):
    cos, sin = wave_table(np.arange(rows), np.arange(rows), rows)
    forward = np.stack([np.stack([cos, sin], axis=1), np.stack([-sin, cos], axis=1)])
    split = forward.reshape(2, rows, 2, lat_count, RQ, subs, rows_sub // rows_cut, rows_cut)
    eye = np.eye(pack_modes, dtype=np.float32)
    return np.einsum("aqplgshr,jk->jaqglskhpr", split, eye).reshape(2 * pack_modes * rows, -1)


def constant(table):
    return jnp.asarray(table.astype(ml_dtypes.bfloat16))


def kernel_call(body, out_shape, scalars, arrays, scratch=(), anchors=(), limit=8 * MIB):
    near, anywhere = pl.BlockSpec(memory_space=pltpu.VMEM), pl.BlockSpec(memory_space=pl.ANY)
    in_specs = [pl.BlockSpec(memory_space=pltpu.SMEM)] * len(scalars)
    in_specs += [near] * len(arrays) + [anywhere] * len(anchors)
    return pl.pallas_call(
        body,
        out_shape=out_shape,
        in_specs=in_specs,
        out_specs=[near] * len(out_shape),
        scratch_shapes=list(scratch),
        compiler_params=pltpu.CompilerParams(vmem_limit_bytes=limit),
    )(*[value.reshape(1).astype(jnp.int32) for value in scalars], *arrays, *anchors)


def gate(source, anchors):
    anywhere = pl.BlockSpec(memory_space=pl.ANY)
    return pl.pallas_call(
        lambda *refs: None,
        out_shape=jax.ShapeDtypeStruct(source.shape, source.dtype),
        in_specs=[anywhere] * (1 + len(anchors)),
        out_specs=anywhere,
        input_output_aliases={0: 0},
    )(source, *anchors)


def pack_body(rows_sub, subs, own, source, *rest):
    sent, slots = rest[:-1], rest[-1]
    cols = source.shape[1]
    for sub in range(subs):
        for block in range(NB):
            pieces = []
            for group in range(RQ):
                row = (group * subs + sub) * rows_sub
                piece = source[row : row + rows_sub, :, block * BS : (block + 1) * BS]
                pieces.append(piece.reshape(rows_sub * cols, BS))
            slots[sub * NB + block] = jnp.concatenate(pieces, axis=1)
    deal(sent, slots, own[0])


def unpack_body(rows_sub, subs, own, base, *rest):
    received, (result, slots) = rest[:-2], rest[-2:]
    cols = base.shape[1]
    place(slots, received, own[0])
    for sub in range(subs):
        for group in range(RQ):
            row = (group * subs + sub) * rows_sub
            pieces = [
                slots[sub * NB + block, :, group * BS : (group + 1) * BS] for block in range(NB)
            ]
            update = jnp.concatenate(pieces, axis=1).reshape(rows_sub, cols, NB * BS)
            old = base[row : row + rows_sub]
            result[row : row + rows_sub] = (
                old.astype(jnp.float32) + update.astype(jnp.float32)
            ).astype(jnp.bfloat16)


def product(left, right):
    return jnp.dot(left, right, preferred_element_type=jnp.float32)


def product_back(left, right):
    return lax.dot_general(
        left, right, (((1,), (1,)), ((), ())), preferred_element_type=jnp.float32
    )


def product_outer(left, right):
    return lax.dot_general(
        left, right, (((0,), (0,)), ((), ())), preferred_element_type=jnp.float32
    )


def place(slots, pieces, own):
    if len(pieces) == 1:
        slots[...] = pieces[0][...]
        return
    for offset, piece in enumerate(pieces):
        slots[jnp.bitwise_xor(own, offset)] = piece[...]


def deal(pieces, slots, own):
    if len(pieces) == 1:
        pieces[0][...] = slots[...]
        return
    for offset, piece in enumerate(pieces):
        piece[...] = slots[jnp.bitwise_xor(own, offset)]


def spectra_body(count, extra, cuts, kept, own_in, own_out, table, *rest):
    received, (sent, slots_in, slots_out) = rest[:count], (rest[count + extra : -2], *rest[-2:])
    place(slots_in, received, own_in[0])
    each = slots_in.shape[1] // cuts
    parts = []
    for cut in range(cuts):
        flat = slots_in[:, cut * each : (cut + 1) * each].reshape(-1, PACK)
        parts.append(product(table[...], flat).reshape(slots_out.shape[0] * kept, -1, PACK))
    joined = jnp.stack(parts, axis=1) if cuts > 1 else parts[0]
    slots_out[...] = joined.reshape(slots_out.shape).astype(jnp.bfloat16)
    deal(sent, slots_out, own_out[0])


def columns_body(count, shares, cuts, kept, own_in, own_out, table, *rest):
    received, shared, rest = rest[:count], rest[count : count + shares], rest[count + shares :]
    sent, (last, slots_in, slots_out) = rest[:-3], rest[-3:]
    if shares:
        last[...] = sum(value[...].astype(jnp.float32) for value in shared).astype(jnp.bfloat16)
    else:
        last[...] = jnp.zeros_like(last)
    place(slots_in, received, own_in[0])
    each = slots_out.shape[1] // cuts
    modes = slots_in.shape[0] * kept
    split = slots_in[...].astype(jnp.float32).reshape(modes, cuts, -1, PACK)
    for cut in range(cuts):
        flat = split[:, cut].reshape(-1, PACK).astype(jnp.bfloat16)
        part = product(table[...], flat).astype(jnp.bfloat16)
        slots_out[:, cut * each : (cut + 1) * each] = part.reshape(slots_out.shape[0], each, PACK)
    deal(sent, slots_out, own_out[0])


def lat_forward(table, slots, tile, deep, rows):
    slab = slots[:, tile * deep : (tile + 1) * deep]
    flat = slab.reshape(slab.shape[0] * deep, PACK)
    stacked = jnp.concatenate(
        [flat[:, group * BS : (group + 1) * BS] for group in range(RQ)], axis=0
    )
    spectrum = product(table, stacked).astype(jnp.bfloat16)
    return [
        jnp.concatenate([spectrum[at : at + rows], spectrum[at + rows : at + 2 * rows]], axis=1)
        for at in range(0, spectrum.shape[0], 2 * rows)
    ]


def lat_inverse(table, values, slots, tile, deep):
    stacked = jnp.concatenate(
        [part for value in values for part in (value[:, :BS], value[:, BS:])], axis=0
    )
    rows = product(table, stacked).astype(jnp.bfloat16)
    each = rows.shape[0] // RQ
    packed = jnp.concatenate([rows[at : at + each] for at in range(0, RQ * each, each)], axis=1)
    slots[:, tile * deep : (tile + 1) * deep] = packed.reshape(slots.shape[0], deep, PACK)


def mode_weight(first_mode, index):
    return jnp.where(first_mode + index == 0, 1.0, 2.0).astype(jnp.float32)


def forward_body(members, pack_modes, member, first_mode, table, first, second, *rest):
    received, rest = rest[:members], rest[members:]
    sent, (spec, hidden, slope, passed, slots) = rest[:members], rest[members:]
    own = member[0]
    kept, rows, _ = spec.shape
    deep = slots.shape[1] * pack_modes // kept
    place(slots, received, own)
    lat = table[...]
    inverse = lat.T
    for tile in range(kept // pack_modes):
        outs = []
        for inner, values in enumerate(lat_forward(lat, slots, tile, deep, rows)):
            index = tile * pack_modes + inner
            spec[index] = values
            pre = product(values, first[...])
            squared = pre * pre
            tangent = jnp.tanh(gelu_coeff * (pre + 0.044715 * squared * pre))
            act = (0.5 * pre * (1.0 + tangent)).astype(jnp.bfloat16)
            slope[index] = 0.5 * (1.0 + tangent) + 0.5 * pre * (
                1.0 - tangent * tangent
            ) * gelu_coeff * (1.0 + 3.0 * 0.044715 * squared)
            hidden[index] = act
            post = product(act, second[...])
            ratio = jnp.tanh(post / shrink_level)
            weight = mode_weight(first_mode[0], index)
            passed[index] = weight * (ratio * ratio)
            outs.append((weight * (post - shrink_level * ratio)).astype(jnp.bfloat16))
        lat_inverse(inverse, outs, slots, tile, deep)
    deal(sent, slots, own)


def backward_body(members, pack_modes, factor, member, lat_own, table, first, second, *rest):
    received, rest = rest[:members], rest[members:]
    (spec, hidden, slope, passed), rest = rest[:4], rest[4:]
    sent, rest = rest[:members], rest[members:]
    shares, (slots, grads) = rest[:-2], rest[-2:]
    own = member[0]
    kept, rows, _ = spec.shape
    deep = slots.shape[1] * pack_modes // kept
    place(slots, received, own)
    lat = table[...]
    inverse = lat.T
    total_first = jnp.zeros((2 * BS, 2 * BS), jnp.float32)
    total_second = jnp.zeros((2 * BS, 2 * BS), jnp.float32)
    for tile in range(kept // pack_modes):
        backs = []
        for inner, values in enumerate(lat_forward(lat, slots, tile, deep, rows)):
            index = tile * pack_modes + inner
            grad_post = (values.astype(jnp.float32) * passed[index]).astype(jnp.bfloat16)
            grad_hid = product_back(grad_post, second[...])
            grad_pre = (grad_hid * slope[index]).astype(jnp.bfloat16)
            backs.append(product_back(grad_pre, first[...]).astype(jnp.bfloat16))
            total_second += product_outer(hidden[index], grad_post)
            total_first += product_outer(spec[index], grad_pre)
        lat_inverse(inverse, backs, slots, tile, deep)
    deal(sent, slots, own)
    share = grads.shape[1]
    for slot, total in enumerate((total_first, total_second)):
        real = (total[:BS, :BS] + total[BS:, BS:]) * factor
        imag = (total[:BS, BS:] - total[BS:, :BS]) * factor
        for part, value in enumerate((real, imag)):
            for at in range(0, BS, share):
                piece = ((2 * slot + part) * BS + at) // share
                grads[piece] = value[at : at + share].astype(jnp.bfloat16)
    deal(shares, grads, lat_own[0])


def weights_body(block, first, second, first_full, second_full):
    for weights, full in ((first, first_full), (second, second_full)):
        real, imag = weights[0, block[0]], weights[1, block[0]]
        full[:BS] = jnp.concatenate([real, imag], axis=1)
        full[BS:] = jnp.concatenate([-imag, real], axis=1)


def assemble_body(lat_count, subs, lat_own, lon_own, *rest):
    gathered, (first, second, slots) = rest[:lat_count], rest[lat_count:]
    rows = gathered[0].shape[1]
    for offset, pieces in enumerate(gathered):
        start = jnp.bitwise_xor(lat_own[0], offset) * rows
        matrix, row = start // BS, pl.multiple_of(start % BS, 16)
        for block in range(NB):
            total = None
            for sub in range(subs):
                value = pieces[jnp.bitwise_xor(lon_own[0], sub * NB + block)].astype(jnp.float32)
                total = value if total is None else total + value
            slots[matrix, block, pl.ds(row, rows)] = total
    first[...] = slots[:2]
    second[...] = slots[2:]


def exchange(source):
    return lax.all_to_all(source, "lon", split_axis=0, concat_axis=0, tiled=True)


def swap(pieces, axes, partners):
    return [pieces[0]] + [
        lax.ppermute(piece, axes, partners(offset))
        for offset, piece in enumerate(pieces)
        if offset
    ]


def shards(features, cotangent, weight_first, weight_second):
    lat_count = lax.axis_size("lat")
    lon_count = lax.axis_size("lon")
    band_rows, band_cols, channels = features.shape
    rows_total = band_rows * lat_count
    cols_total = band_cols * lon_count
    kept_total = KWD * lat_count * lon_count
    subs = lon_count // NB
    members = lat_count * subs
    rows_sub = band_rows // (RQ * subs)
    rows_cut = min(rows_sub, 4)
    cuts = rows_sub // rows_cut
    kept = kept_total // members
    deep = 2 * rows_sub
    pack_modes = max(1, 16 // deep)
    lat_index = lax.axis_index("lat")
    lon_index = lax.axis_index("lon")
    block = lon_index % NB
    member = lat_index * subs + lon_index // NB
    bf16, f32 = jnp.bfloat16, jnp.float32
    array = jax.ShapeDtypeStruct

    def member_pairs(offset):
        pairs = []
        for lat in range(lat_count):
            for lon in range(lon_count):
                other = (lat * subs + lon // NB) ^ offset
                lon_other = other % subs * NB + lon % NB
                pairs.append((lat * lon_count + lon, other // subs * lon_count + lon_other))
        return pairs

    def line_pairs(count):
        return lambda offset: [(place, place ^ offset) for place in range(count)]

    lon_fwd, lon_inv = map(constant, lon_tables(kept_total, cols_total, lon_count, rows_cut))
    lat_both = constant(lat_table(rows_total, lat_count, subs, rows_sub, rows_cut, pack_modes))
    first, second = kernel_call(
        weights_body,
        [array((2 * BS, 2 * BS), bf16)] * 2,
        [block],
        [weight_first, weight_second],
    )

    lon_piece = array((rows_sub * band_cols, PACK), bf16)
    lon_whole = array((lon_count, rows_sub * band_cols, PACK), bf16)
    mid_piece = array((kept * deep, PACK), bf16)
    lon_slots = pltpu.VMEM(lon_whole.shape, bf16)
    mid_slots = pltpu.VMEM((members, kept * deep, PACK), bf16)
    mid_limit = 12 * MIB + 4 * lat_both.size
    share = 4 * BS // lat_count

    def mid_swap(pieces):
        return swap(pieces, ("lat", "lon"), member_pairs)

    def pack(source, sent):
        body = functools.partial(pack_body, rows_sub, subs)
        return kernel_call(body, sent, [lon_index], [source], [lon_slots])

    def unpack(source, base):
        body = functools.partial(unpack_body, rows_sub, subs)
        result = array(base.shape, bf16)
        return kernel_call(body, [result], [lon_index], [base, source], [lon_slots])[0]

    def to_spectra(pieces, anchors=()):
        return kernel_call(
            functools.partial(spectra_body, len(pieces), len(anchors), cuts, kept),
            [mid_piece] * members,
            [lon_index, member],
            [lon_fwd, *pieces],
            [lon_slots, mid_slots],
            anchors,
        )

    def to_columns(pieces, shares, last):
        return kernel_call(
            functools.partial(columns_body, members, len(shares), cuts, kept),
            [lon_whole, last],
            [member, lon_index],
            [lon_inv, *pieces, *shares],
            [mid_slots, lon_slots],
        )

    modes = (kept, rows_total, 2 * BS)
    state = [array(modes, kind) for kind in (bf16, bf16, f32, f32)]

    field = swap(pack(features, [lon_piece] * lon_count), "lon", line_pairs(lon_count))
    field_cot = exchange(gate(pack(cotangent, [lon_whole])[0], field))
    results = kernel_call(
        functools.partial(forward_body, members, pack_modes),
        [mid_piece] * members + state,
        [member, member * kept],
        [lat_both, first, second, *mid_swap(to_spectra(field))],
        [mid_slots],
        limit=mid_limit,
    )
    columns, anchor = to_columns(mid_swap(results[:members]), [], array((8, 128), f32))
    filtered = exchange(columns)
    cot_results = kernel_call(
        functools.partial(
            backward_body, members, pack_modes, 1.0 / math.sqrt(rows_total * kept_total)
        ),
        [mid_piece] * members + [array((share, BS), bf16)] * lat_count,
        [member, lat_index],
        [lat_both, first, second, *mid_swap(to_spectra([field_cot], [anchor])), *results[members:]],
        [mid_slots, pltpu.VMEM((lat_count, share, BS), bf16)],
        limit=mid_limit,
    )
    shares = swap(cot_results[members:], "lat", line_pairs(lat_count))
    columns, own_share = to_columns(
        mid_swap(cot_results[:members]), shares, array((share, BS), bf16)
    )
    returned = exchange(columns)

    pair = jnp.stack([own_share, lax.ppermute(own_share, "lon", line_pairs(lon_count)(1))])
    blocks = jnp.concatenate(
        [pair]
        + [
            lax.ppermute(pair, "lon", line_pairs(lon_count)(offset))
            for offset in range(2, lon_count, 2)
        ]
    )
    gathered = {0: blocks}
    step = lat_count // 2
    while step:
        for offset in sorted(gathered):
            moved = lax.ppermute(gathered[offset], "lat", line_pairs(lat_count)(step))
            gathered[offset | step] = moved
        step //= 2
    gathered = [gathered[offset] for offset in range(lat_count)]
    full = array((2, NB, BS, BS), f32)
    grad_first, grad_second = kernel_call(
        functools.partial(assemble_body, lat_count, subs),
        [full, full],
        [lat_index, lon_index],
        gathered,
        [pltpu.VMEM((4, NB, BS, BS), f32)],
    )
    return (unpack(filtered, features), unpack(returned, cotangent), grad_first, grad_second)


def solution(mesh):
    in_specs = (P("lat", "lon", None), P("lat", "lon", None), P(), P())
    out_specs = (P("lat", "lon", None), P("lat", "lon", None), P(), P())
    return jax.shard_map(shards, mesh=mesh, in_specs=in_specs, out_specs=out_specs, check_vma=False)
```

```python
import functools
import math

import jax
import jax.numpy as jnp
import ml_dtypes
import numpy as np
from jax import lax
from jax.experimental import pallas as pl
from jax.experimental.pallas import tpu as pltpu
from jax.sharding import PartitionSpec as P

NB = 8
BS = 96
KWD = 1
RQ = 4
PACK = RQ * BS
MIB = 1024 * 1024

shrink_level = 0.01
gelu_coeff = 0.7978845608028654


def wave_table(first, second, length):
    product = (first[:, None] * second[None, :]) % length
    angle = np.float32(2.0 * math.pi / length) * product.astype(np.float32)
    scale = np.float32(math.sqrt(length))
    rounded = ml_dtypes.bfloat16
    cos = (np.cos(angle) / scale).astype(rounded).astype(np.float32)
    sin = (np.sin(angle) / scale).astype(rounded).astype(np.float32)
    return cos, sin


def lon_tables(kept, cols, lon_count, rows):
    cos, sin = wave_table(np.arange(kept), np.arange(cols), cols)
    parts = np.stack([cos, -sin], axis=1).reshape(kept, 2, lon_count, cols // lon_count)
    eye = np.eye(rows, dtype=np.float32)
    forward = np.einsum("kpgw,rs->kprgsw", parts, eye).reshape(2 * kept * rows, -1)
    return forward, forward.T


def lat_table(rows, lat_count, subs, rows_sub, rows_cut, pack_modes):
    cos, sin = wave_table(np.arange(rows), np.arange(rows), rows)
    forward = np.stack([np.stack([cos, sin], axis=1), np.stack([-sin, cos], axis=1)])
    split = forward.reshape(2, rows, 2, lat_count, RQ, subs, rows_sub // rows_cut, rows_cut)
    eye = np.eye(pack_modes, dtype=np.float32)
    return np.einsum("aqplgshr,jk->jaqglskhpr", split, eye).reshape(2 * pack_modes * rows, -1)


def constant(table):
    return jnp.asarray(table.astype(ml_dtypes.bfloat16))


def kernel_call(body, out_shape, scalars, arrays, scratch=(), anchors=(), far=(), limit=8 * MIB):
    specs = {
        space: pl.BlockSpec(memory_space=space)
        for space in (pltpu.VMEM, pltpu.SMEM, pltpu.HBM, pl.ANY)
    }
    far = [pltpu.with_memory_space_constraint(value, pltpu.HBM) for value in far]
    in_specs = [specs[pltpu.SMEM]] * len(scalars) + [specs[pltpu.VMEM]] * len(arrays)
    in_specs += [specs[pltpu.HBM]] * len(far) + [specs[pl.ANY]] * len(anchors)
    is_far = [getattr(shape, "memory_space", None) is pltpu.HBM for shape in out_shape]
    return pl.pallas_call(
        body,
        out_shape=out_shape,
        in_specs=in_specs,
        out_specs=[specs[pltpu.HBM if distant else pltpu.VMEM] for distant in is_far],
        scratch_shapes=list(scratch),
        compiler_params=pltpu.CompilerParams(vmem_limit_bytes=limit),
    )(*[value.reshape(1).astype(jnp.int32) for value in scalars], *arrays, *far, *anchors)


def gate(source, anchors):
    anywhere = pl.BlockSpec(memory_space=pl.ANY)
    return pl.pallas_call(
        lambda *refs: None,
        out_shape=jax.ShapeDtypeStruct(source.shape, source.dtype),
        in_specs=[anywhere] * (1 + len(anchors)),
        out_specs=anywhere,
        input_output_aliases={0: 0},
    )(source, *anchors)


def pack_body(rows_sub, subs, own, source, *rest):
    sent, slots = rest[:-1], rest[-1]
    cols = source.shape[1]
    for sub in range(subs):
        for block in range(NB):
            pieces = []
            for group in range(RQ):
                row = (group * subs + sub) * rows_sub
                piece = source[row : row + rows_sub, :, block * BS : (block + 1) * BS]
                pieces.append(piece.reshape(rows_sub * cols, BS))
            slots[sub * NB + block] = jnp.concatenate(pieces, axis=1)
    deal(sent, slots, own[0])


def unpack_body(rows_sub, subs, own, base, *rest):
    received, (result, slots) = rest[:-2], rest[-2:]
    cols = base.shape[1]
    place(slots, received, own[0])
    for sub in range(subs):
        for group in range(RQ):
            row = (group * subs + sub) * rows_sub
            pieces = [
                slots[sub * NB + block, :, group * BS : (group + 1) * BS] for block in range(NB)
            ]
            update = jnp.concatenate(pieces, axis=1).reshape(rows_sub, cols, NB * BS)
            old = base[row : row + rows_sub]
            result[row : row + rows_sub] = (
                old.astype(jnp.float32) + update.astype(jnp.float32)
            ).astype(jnp.bfloat16)


def product(left, right):
    return jnp.dot(left, right, preferred_element_type=jnp.float32)


def product_back(left, right):
    return lax.dot_general(
        left, right, (((1,), (1,)), ((), ())), preferred_element_type=jnp.float32
    )


def product_outer(left, right):
    return lax.dot_general(
        left, right, (((0,), (0,)), ((), ())), preferred_element_type=jnp.float32
    )


def place(slots, pieces, own):
    if len(pieces) == 1:
        slots[...] = pieces[0][...]
        return
    for offset, piece in enumerate(pieces):
        slots[jnp.bitwise_xor(own, offset)] = piece[...]


def deal(pieces, slots, own):
    if len(pieces) == 1:
        pieces[0][...] = slots[...]
        return
    for offset, piece in enumerate(pieces):
        piece[...] = slots[jnp.bitwise_xor(own, offset)]


def spectra_body(count, extra, cuts, kept, own_in, own_out, table, *rest):
    received, (sent, slots_in, slots_out) = rest[:count], (rest[count + extra : -2], *rest[-2:])
    place(slots_in, received, own_in[0])
    each = slots_in.shape[1] // cuts
    parts = []
    for cut in range(cuts):
        flat = slots_in[:, cut * each : (cut + 1) * each].reshape(-1, PACK)
        parts.append(product(table[...], flat).reshape(slots_out.shape[0] * kept, -1, PACK))
    joined = jnp.stack(parts, axis=1) if cuts > 1 else parts[0]
    slots_out[...] = joined.reshape(slots_out.shape).astype(jnp.bfloat16)
    deal(sent, slots_out, own_out[0])


def columns_body(count, cuts, kept, own_in, table, *rest):
    received, (result, anchor, slots_in, slots_out, sems) = rest[:count], rest[count:]
    anchor[...] = jnp.zeros_like(anchor)
    place(slots_in, received, own_in[0])
    each = slots_out.shape[1] // cuts
    modes = slots_in.shape[0] * kept
    split = slots_in[...].astype(jnp.float32).reshape(modes, cuts, -1, PACK)
    flats = [split[:, cut].reshape(-1, PACK).astype(jnp.bfloat16) for cut in range(cuts)]
    copies = []
    for cut, flat in enumerate(flats):
        part = product(table[...], flat).astype(jnp.bfloat16)
        rows = pl.ds(cut * each, each)
        slots_out[:, rows] = part.reshape(slots_out.shape[0], each, PACK)
        copies.append(
            pltpu.make_async_copy(slots_out.at[:, rows], result.at[:, rows], sems.at[cut])
        )
        copies[-1].start()
    finish(copies)


def finish(copies):
    for copy in copies:
        copy.wait()


def load_weights(block, weights, real_imag, sems):
    copies = [
        pltpu.make_async_copy(source.at[part, block], real_imag.at[slot, part], sems.at[slot, part])
        for slot, source in enumerate(weights)
        for part in range(2)
    ]
    for copy in copies:
        copy.start()
    return copies


def complex_weights(real_imag, full):
    for slot in range(2):
        real, imag = real_imag[slot, 0], real_imag[slot, 1]
        full[slot, :BS] = jnp.concatenate([real, imag], axis=1)
        full[slot, BS:] = jnp.concatenate([-imag, real], axis=1)


def lat_forward(table, slots, tile, deep, rows):
    slab = slots[:, tile * deep : (tile + 1) * deep]
    flat = slab.reshape(slab.shape[0] * deep, PACK)
    stacked = jnp.concatenate(
        [flat[:, group * BS : (group + 1) * BS] for group in range(RQ)], axis=0
    )
    spectrum = product(table, stacked).astype(jnp.bfloat16)
    return [
        jnp.concatenate([spectrum[at : at + rows], spectrum[at + rows : at + 2 * rows]], axis=1)
        for at in range(0, spectrum.shape[0], 2 * rows)
    ]


def lat_inverse(table, values, slots, tile, deep):
    stacked = jnp.concatenate(
        [part for value in values for part in (value[:, :BS], value[:, BS:])], axis=0
    )
    rows = product(table, stacked).astype(jnp.bfloat16)
    each = rows.shape[0] // RQ
    packed = jnp.concatenate([rows[at : at + each] for at in range(0, RQ * each, each)], axis=1)
    slots[:, tile * deep : (tile + 1) * deep] = packed.reshape(slots.shape[0], deep, PACK)


def mode_weight(first_mode, index):
    return jnp.where(first_mode + index == 0, 1.0, 2.0).astype(jnp.float32)


def forward_body(members, pack_modes, member, first_mode, block, table, *rest):
    received, weights, sent = rest[:members], rest[members : members + 2], rest[members + 2 :]
    sent, rest = sent[:members], sent[members:]
    saved, (slots, spec, hidden, slope, passed, real_imag, full, weight_sems, save_sems) = (
        rest[:4],
        rest[4:],
    )
    loads = load_weights(block[0], weights, real_imag, weight_sems)
    own = member[0]
    kept, rows, _ = spec.shape
    deep = slots.shape[1] * pack_modes // kept
    place(slots, received, own)
    lat = table[...]
    inverse = lat.T
    finish(loads)
    complex_weights(real_imag, full)
    copies = []
    for tile in range(kept // pack_modes):
        outs = []
        for inner, values in enumerate(lat_forward(lat, slots, tile, deep, rows)):
            index = tile * pack_modes + inner
            spec[index] = values
            pre = product(values, full[0])
            squared = pre * pre
            tangent = jnp.tanh(gelu_coeff * (pre + 0.044715 * squared * pre))
            act = (0.5 * pre * (1.0 + tangent)).astype(jnp.bfloat16)
            slope[index] = 0.5 * (1.0 + tangent) + 0.5 * pre * (
                1.0 - tangent * tangent
            ) * gelu_coeff * (1.0 + 3.0 * 0.044715 * squared)
            hidden[index] = act
            post = product(act, full[1])
            ratio = jnp.tanh(post / shrink_level)
            weight = mode_weight(first_mode[0], index)
            passed[index] = weight * (ratio * ratio)
            outs.append((weight * (post - shrink_level * ratio)).astype(jnp.bfloat16))
            for slot, (near, distant) in enumerate(zip((spec, hidden, slope, passed), saved)):
                copy = pltpu.make_async_copy(
                    near.at[index], distant.at[index], save_sems.at[slot, index]
                )
                copy.start()
                copies.append(copy)
        lat_inverse(inverse, outs, slots, tile, deep)
    deal(sent, slots, own)
    finish(copies)


def backward_body(members, shares, pack_modes, factor, member, lat_own, block, table, *rest):
    received, rest = rest[:members], rest[members:]
    weights, saved, rest = rest[:2], rest[2:6], rest[6:]
    sent, parts, rest = rest[:members], rest[members : members + shares], rest[members + shares :]
    slots, grads, spec, hidden, slope, passed, real_imag, full, weight_sems, load_sems = rest
    weight_loads = load_weights(block[0], weights, real_imag, weight_sems)
    own = member[0]
    kept, rows, _ = spec.shape
    deep = slots.shape[1] * pack_modes // kept
    loads = [
        [
            pltpu.make_async_copy(distant.at[index], near.at[index], load_sems.at[slot, index])
            for slot, (near, distant) in enumerate(zip((spec, hidden, slope, passed), saved))
        ]
        for index in range(kept)
    ]
    for group in loads:
        for copy in group:
            copy.start()
    place(slots, received, own)
    lat = table[...]
    inverse = lat.T
    finish(weight_loads)
    complex_weights(real_imag, full)
    total_first = jnp.zeros((2 * BS, 2 * BS), jnp.float32)
    total_second = jnp.zeros((2 * BS, 2 * BS), jnp.float32)
    for tile in range(kept // pack_modes):
        backs = []
        for inner, values in enumerate(lat_forward(lat, slots, tile, deep, rows)):
            index = tile * pack_modes + inner
            finish(loads[index])
            grad_post = (values.astype(jnp.float32) * passed[index]).astype(jnp.bfloat16)
            grad_hid = product_back(grad_post, full[1])
            grad_pre = (grad_hid * slope[index]).astype(jnp.bfloat16)
            backs.append(product_back(grad_pre, full[0]).astype(jnp.bfloat16))
            total_second += product_outer(hidden[index], grad_post)
            total_first += product_outer(spec[index], grad_pre)
        lat_inverse(inverse, backs, slots, tile, deep)
    deal(sent, slots, own)
    share = grads.shape[1]
    for slot, total in enumerate((total_first, total_second)):
        real = (total[:BS, :BS] + total[BS:, BS:]) * factor
        imag = (total[:BS, BS:] - total[BS:, :BS]) * factor
        for part, value in enumerate((real, imag)):
            for at in range(0, BS, share):
                piece = ((2 * slot + part) * BS + at) // share
                grads[piece] = value[at : at + share].astype(jnp.bfloat16)
    deal(parts, grads, lat_own[0])


def sum_body(*refs):
    refs[-1][...] = sum(value[...].astype(jnp.float32) for value in refs[:-1]).astype(jnp.bfloat16)


def stack_body(own, *refs):
    place(refs[-1], refs[:-1], own[0])


def assemble_body(lat_count, subs, lat_own, *rest):
    gathered, (first, second, slots) = rest[:lat_count], rest[lat_count:]
    rows = gathered[0].shape[1]
    for offset, pieces in enumerate(gathered):
        start = jnp.bitwise_xor(lat_own[0], offset) * rows
        matrix, row = start // BS, pl.multiple_of(start % BS, 16)
        for block in range(NB):
            total = None
            for sub in range(subs):
                value = pieces[sub * NB + block].astype(jnp.float32)
                total = value if total is None else total + value
            slots[matrix, block, pl.ds(row, rows)] = total
    first[...] = slots[:2]
    second[...] = slots[2:]


def exchange(source):
    return lax.all_to_all(source, "lon", split_axis=0, concat_axis=0, tiled=True)


def swap(pieces, axes, partners):
    return [pieces[0]] + [
        lax.ppermute(piece, axes, partners(offset))
        for offset, piece in enumerate(pieces)
        if offset
    ]


def shards(features, cotangent, weight_first, weight_second):
    lat_count = lax.axis_size("lat")
    lon_count = lax.axis_size("lon")
    band_rows, band_cols, channels = features.shape
    rows_total = band_rows * lat_count
    cols_total = band_cols * lon_count
    kept_total = KWD * lat_count * lon_count
    subs = lon_count // NB
    members = lat_count * subs
    rows_sub = band_rows // (RQ * subs)
    rows_cut = min(rows_sub, 4)
    cuts = rows_sub // rows_cut
    kept = kept_total // members
    deep = 2 * rows_sub
    pack_modes = max(1, 16 // deep)
    lat_index = lax.axis_index("lat")
    lon_index = lax.axis_index("lon")
    block = lon_index % NB
    member = lat_index * subs + lon_index // NB
    bf16, f32 = jnp.bfloat16, jnp.float32
    array = jax.ShapeDtypeStruct

    def member_pairs(offset):
        pairs = []
        for lat in range(lat_count):
            for lon in range(lon_count):
                other = (lat * subs + lon // NB) ^ offset
                lon_other = other % subs * NB + lon % NB
                pairs.append((lat * lon_count + lon, other // subs * lon_count + lon_other))
        return pairs

    def line_pairs(count):
        return lambda offset: [(place, place ^ offset) for place in range(count)]

    lon_fwd, lon_inv = map(constant, lon_tables(kept_total, cols_total, lon_count, rows_cut))
    lat_both = constant(lat_table(rows_total, lat_count, subs, rows_sub, rows_cut, pack_modes))
    lon_piece = array((rows_sub * band_cols, PACK), bf16)
    lon_whole = array((lon_count, rows_sub * band_cols, PACK), bf16)
    mid_piece = array((kept * deep, PACK), bf16)
    lon_slots = pltpu.VMEM(lon_whole.shape, bf16)
    mid_slots = pltpu.VMEM((members, kept * deep, PACK), bf16)
    mid_limit = 14 * MIB + 5 * lat_both.size
    share = 4 * BS // lat_count

    def mid_swap(pieces):
        return swap(pieces, ("lat", "lon"), member_pairs)

    def pack(source, sent):
        body = functools.partial(pack_body, rows_sub, subs)
        return kernel_call(body, sent, [lon_index], [source], [lon_slots])

    def unpack(source, base):
        body = functools.partial(unpack_body, rows_sub, subs)
        result = array(base.shape, bf16)
        return kernel_call(body, [result], [lon_index], [base, source], [lon_slots])[0]

    def to_spectra(pieces, anchors=()):
        return kernel_call(
            functools.partial(spectra_body, len(pieces), len(anchors), cuts, kept),
            [mid_piece] * members,
            [lon_index, member],
            [lon_fwd, *pieces],
            [lon_slots, mid_slots],
            anchors,
        )

    def to_columns(pieces):
        return kernel_call(
            functools.partial(columns_body, members, cuts, kept),
            [pltpu.HBM(lon_whole.shape, bf16), array((8, 128), f32)],
            [member],
            [lon_inv, *pieces],
            [mid_slots, lon_slots, pltpu.SemaphoreType.DMA((cuts,))],
        )

    modes = (kept, rows_total, 2 * BS)
    types = (bf16, bf16, f32, f32)
    weights = [weight_first, weight_second]
    mid_scratch = [
        *[pltpu.VMEM(modes, kind) for kind in types],
        pltpu.VMEM((2, 2, BS, BS), bf16),
        pltpu.VMEM((2, 2 * BS, 2 * BS), bf16),
        pltpu.SemaphoreType.DMA((2, 2)),
        pltpu.SemaphoreType.DMA((4, kept)),
    ]

    field = swap(pack(features, [lon_piece] * lon_count), "lon", line_pairs(lon_count))
    field_cot = exchange(gate(pack(cotangent, [lon_whole])[0], field))
    results = kernel_call(
        functools.partial(forward_body, members, pack_modes),
        [mid_piece] * members + [pltpu.HBM(modes, kind) for kind in types],
        [member, member * kept, block],
        [lat_both, *mid_swap(to_spectra(field))],
        [mid_slots, *mid_scratch],
        far=weights,
        limit=mid_limit,
    )
    columns, anchor = to_columns(mid_swap(results[:members]))
    filtered = exchange(columns)
    cot_results = kernel_call(
        functools.partial(
            backward_body, members, lat_count, pack_modes, 1.0 / math.sqrt(rows_total * kept_total)
        ),
        [mid_piece] * members + [array((share, BS), bf16)] * lat_count,
        [member, lat_index, block],
        [lat_both, *mid_swap(to_spectra([field_cot], [anchor]))],
        [mid_slots, pltpu.VMEM((lat_count, share, BS), bf16), *mid_scratch],
        far=weights + list(results[members:]),
        limit=mid_limit,
    )
    returned = exchange(to_columns(mid_swap(cot_results[:members]))[0])

    shares = swap(cot_results[members:], "lat", line_pairs(lat_count))
    own_share = kernel_call(sum_body, [array((share, BS), bf16)], [], shares)[0]
    blocks = kernel_call(
        stack_body,
        [array((lon_count, share, BS), bf16)],
        [lon_index],
        swap([own_share] * lon_count, "lon", line_pairs(lon_count)),
    )[0]
    gathered = {0: blocks}
    step = lat_count // 2
    while step:
        for offset in sorted(gathered):
            moved = lax.ppermute(gathered[offset], "lat", line_pairs(lat_count)(step))
            gathered[offset | step] = moved
        step //= 2
    gathered = [gathered[offset] for offset in range(lat_count)]
    full = array((2, NB, BS, BS), f32)
    grad_first, grad_second = kernel_call(
        functools.partial(assemble_body, lat_count, subs),
        [full, full],
        [lat_index],
        gathered,
        [pltpu.VMEM((4, NB, BS, BS), f32)],
    )
    return (unpack(filtered, features), unpack(returned, cotangent), grad_first, grad_second)


def solution(mesh):
    in_specs = (P("lat", "lon", None), P("lat", "lon", None), P(), P())
    out_specs = (P("lat", "lon", None), P("lat", "lon", None), P(), P())
    return jax.shard_map(shards, mesh=mesh, in_specs=in_specs, out_specs=out_specs, check_vma=False)
```

```python
import functools
import math

import jax
import jax.numpy as jnp
import ml_dtypes
import numpy as np
from jax import lax
from jax.experimental import pallas as pl
from jax.experimental.pallas import tpu as pltpu
from jax.sharding import PartitionSpec as P

NB = 8
BS = 96
KWD = 1
RQ = 4
PACK = RQ * BS
WIDE = 2 * BS
STATE = -(-WIDE // 128) * 128
MIB = 1024 * 1024

shrink_level = 0.01
gelu_coeff = 0.7978845608028654


def wave_table(first, second, length):
    product = (first[:, None] * second[None, :]) % length
    angle = np.float32(2.0 * math.pi / length) * product.astype(np.float32)
    scale = np.float32(math.sqrt(length))
    rounded = ml_dtypes.bfloat16
    cos = (np.cos(angle) / scale).astype(rounded).astype(np.float32)
    sin = (np.sin(angle) / scale).astype(rounded).astype(np.float32)
    return cos, sin


def lon_tables(kept, cols, lon_count, rows):
    cos, sin = wave_table(np.arange(kept), np.arange(cols), cols)
    parts = np.stack([cos, -sin], axis=1).reshape(kept, 2, lon_count, cols // lon_count)
    eye = np.eye(rows, dtype=np.float32)
    forward = np.einsum("kpgw,rs->kprgsw", parts, eye).reshape(2 * kept * rows, -1)
    return forward, forward.T


def lat_table(rows, lat_count, subs, rows_sub, rows_cut, pack_modes):
    cos, sin = wave_table(np.arange(rows), np.arange(rows), rows)
    forward = np.stack([np.stack([cos, sin], axis=1), np.stack([-sin, cos], axis=1)])
    split = forward.reshape(2, rows, 2, lat_count, RQ, subs, rows_sub // rows_cut, rows_cut)
    eye = np.eye(pack_modes, dtype=np.float32)
    return np.einsum("aqplgshr,jk->jaqglskhpr", split, eye).reshape(2 * pack_modes * rows, -1)


def constant(table):
    return jnp.asarray(table.astype(ml_dtypes.bfloat16))


def kernel_call(body, out_shape, scalars, arrays, scratch=(), anchors=(), far=(), limit=8 * MIB):
    specs = {
        space: pl.BlockSpec(memory_space=space)
        for space in (pltpu.VMEM, pltpu.SMEM, pltpu.HBM, pl.ANY)
    }
    far = [pltpu.with_memory_space_constraint(value, pltpu.HBM) for value in far]
    in_specs = [specs[pltpu.SMEM]] * len(scalars) + [specs[pltpu.VMEM]] * len(arrays)
    in_specs += [specs[pltpu.HBM]] * len(far) + [specs[pl.ANY]] * len(anchors)
    is_far = [getattr(shape, "memory_space", None) is pltpu.HBM for shape in out_shape]
    return pl.pallas_call(
        body,
        out_shape=out_shape,
        in_specs=in_specs,
        out_specs=[specs[pltpu.HBM if distant else pltpu.VMEM] for distant in is_far],
        scratch_shapes=list(scratch),
        compiler_params=pltpu.CompilerParams(vmem_limit_bytes=limit),
    )(*[value.reshape(1).astype(jnp.int32) for value in scalars], *arrays, *far, *anchors)


def gate(source, anchors):
    anywhere = pl.BlockSpec(memory_space=pl.ANY)
    return pl.pallas_call(
        lambda *refs: None,
        out_shape=jax.ShapeDtypeStruct(source.shape, source.dtype),
        in_specs=[anywhere] * (1 + len(anchors)),
        out_specs=anywhere,
        input_output_aliases={0: 0},
    )(source, *anchors)


def pack_body(rows_sub, subs, own, source, *rest):
    sent, slots = rest[:-1], rest[-1]
    cols = source.shape[1]
    for sub in range(subs):
        for block in range(NB):
            pieces = []
            for group in range(RQ):
                row = (group * subs + sub) * rows_sub
                piece = source[row : row + rows_sub, :, block * BS : (block + 1) * BS]
                pieces.append(piece.reshape(rows_sub * cols, BS))
            slots[sub * NB + block] = jnp.concatenate(pieces, axis=1)
    deal(sent, slots, own[0])


def unpack_body(rows_sub, subs, own, base, *rest):
    received, (result, slots) = rest[:-2], rest[-2:]
    cols = base.shape[1]
    place(slots, received, own[0])
    for sub in range(subs):
        for group in range(RQ):
            row = (group * subs + sub) * rows_sub
            pieces = [
                slots[sub * NB + block, :, group * BS : (group + 1) * BS] for block in range(NB)
            ]
            update = jnp.concatenate(pieces, axis=1).reshape(rows_sub, cols, NB * BS)
            old = base[row : row + rows_sub]
            result[row : row + rows_sub] = (
                old.astype(jnp.float32) + update.astype(jnp.float32)
            ).astype(jnp.bfloat16)


def product(left, right):
    return jnp.dot(left, right, preferred_element_type=jnp.float32)


def product_back(left, right):
    return lax.dot_general(
        left, right, (((1,), (1,)), ((), ())), preferred_element_type=jnp.float32
    )


def product_outer(left, right):
    return lax.dot_general(
        left, right, (((0,), (0,)), ((), ())), preferred_element_type=jnp.float32
    )


def place(slots, pieces, own):
    if len(pieces) == 1:
        slots[...] = pieces[0][...]
        return
    for offset, piece in enumerate(pieces):
        slots[jnp.bitwise_xor(own, offset)] = piece[...]


def deal(pieces, slots, own):
    if len(pieces) == 1:
        pieces[0][...] = slots[...]
        return
    for offset, piece in enumerate(pieces):
        piece[...] = slots[jnp.bitwise_xor(own, offset)]


def spectra_body(count, extra, cuts, kept, own_in, own_out, table, *rest):
    received, (sent, slots_in, slots_out) = rest[:count], (rest[count + extra : -2], *rest[-2:])
    place(slots_in, received, own_in[0])
    each = slots_in.shape[1] // cuts
    parts = []
    for cut in range(cuts):
        flat = slots_in[:, cut * each : (cut + 1) * each].reshape(-1, PACK)
        parts.append(product(table[...], flat).reshape(slots_out.shape[0] * kept, -1, PACK))
    joined = jnp.stack(parts, axis=1) if cuts > 1 else parts[0]
    slots_out[...] = joined.reshape(slots_out.shape).astype(jnp.bfloat16)
    deal(sent, slots_out, own_out[0])


def columns_body(count, extra, cuts, kept, own_in, table, *rest):
    received, (result, slots_in, slots_out, sems) = rest[:count], rest[count + extra :]
    place(slots_in, received, own_in[0])
    each = slots_out.shape[1] // cuts
    modes = slots_in.shape[0] * kept
    split = slots_in[...].astype(jnp.float32).reshape(modes, cuts, -1, PACK)
    flats = [split[:, cut].reshape(-1, PACK).astype(jnp.bfloat16) for cut in range(cuts)]
    copies = []
    for cut, flat in enumerate(flats):
        part = product(table[...], flat).astype(jnp.bfloat16)
        rows = pl.ds(cut * each, each)
        slots_out[:, rows] = part.reshape(slots_out.shape[0], each, PACK)
        copies.append(
            pltpu.make_async_copy(slots_out.at[:, rows], result.at[:, rows], sems.at[cut])
        )
        copies[-1].start()
    finish(copies)


def finish(copies):
    for copy in copies:
        copy.wait()


def load_weights(block, weights, real_imag, sems):
    copies = [
        pltpu.make_async_copy(source.at[part, block], real_imag.at[slot, part], sems.at[slot, part])
        for slot, source in enumerate(weights)
        for part in range(2)
    ]
    for copy in copies:
        copy.start()
    return copies


def complex_weights(real_imag, full):
    for slot in range(2):
        real, imag = real_imag[slot, 0], real_imag[slot, 1]
        full[slot, :BS] = jnp.concatenate([real, imag], axis=1)
        full[slot, BS:] = jnp.concatenate([-imag, real], axis=1)


def lat_forward(table, slots, tile, deep, rows):
    slab = slots[:, tile * deep : (tile + 1) * deep]
    flat = slab.reshape(slab.shape[0] * deep, PACK)
    stacked = jnp.concatenate(
        [flat[:, group * BS : (group + 1) * BS] for group in range(RQ)], axis=0
    )
    spectrum = product(table, stacked).astype(jnp.bfloat16)
    return [
        jnp.concatenate([spectrum[at : at + rows], spectrum[at + rows : at + 2 * rows]], axis=1)
        for at in range(0, spectrum.shape[0], 2 * rows)
    ]


def lat_inverse(table, values, slots, tile, deep):
    stacked = jnp.concatenate(
        [part for value in values for part in (value[:, :BS], value[:, BS:])], axis=0
    )
    rows = product(table, stacked).astype(jnp.bfloat16)
    each = rows.shape[0] // RQ
    packed = jnp.concatenate([rows[at : at + each] for at in range(0, RQ * each, each)], axis=1)
    slots[:, tile * deep : (tile + 1) * deep] = packed.reshape(slots.shape[0], deep, PACK)


def mode_weight(first_mode, index):
    return jnp.where(first_mode + index == 0, 1.0, 2.0).astype(jnp.float32)


def forward_body(members, pack_modes, member, first_mode, block, table, *rest):
    received, weights, sent = rest[:members], rest[members : members + 2], rest[members + 2 :]
    sent, rest = sent[:members], sent[members:]
    saved, anchor, slots = rest[:4], rest[4], rest[5]
    spec, hidden, slope, passed, real_imag, full, weight_sems, save_sems = rest[6:]
    anchor[...] = jnp.zeros_like(anchor)
    loads = load_weights(block[0], weights, real_imag, weight_sems)
    own = member[0]
    kept, rows, _ = spec.shape
    deep = slots.shape[1] * pack_modes // kept
    place(slots, received, own)
    lat = table[...]
    inverse = lat.T
    finish(loads)
    complex_weights(real_imag, full)
    copies = []
    for tile in range(kept // pack_modes):
        outs = []
        for inner, values in enumerate(lat_forward(lat, slots, tile, deep, rows)):
            index = tile * pack_modes + inner
            spec[index, :, :WIDE] = values
            pre = product(values, full[0])
            squared = pre * pre
            tangent = jnp.tanh(gelu_coeff * (pre + 0.044715 * squared * pre))
            act = (0.5 * pre * (1.0 + tangent)).astype(jnp.bfloat16)
            slope[index, :, :WIDE] = 0.5 * (1.0 + tangent) + 0.5 * pre * (
                1.0 - tangent * tangent
            ) * gelu_coeff * (1.0 + 3.0 * 0.044715 * squared)
            hidden[index, :, :WIDE] = act
            post = product(act, full[1])
            ratio = jnp.tanh(post / shrink_level)
            weight = mode_weight(first_mode[0], index)
            passed[index, :, :WIDE] = weight * (ratio * ratio)
            outs.append((weight * (post - shrink_level * ratio)).astype(jnp.bfloat16))
            for slot, (near, distant) in enumerate(zip((spec, hidden, slope, passed), saved)):
                copy = pltpu.make_async_copy(
                    near.at[index], distant.at[index], save_sems.at[slot, index]
                )
                copy.start()
                copies.append(copy)
        lat_inverse(inverse, outs, slots, tile, deep)
    deal(sent, slots, own)
    finish(copies)


def backward_body(members, shares, pack_modes, factor, member, lat_own, block, table, *rest):
    received, rest = rest[:members], rest[members:]
    weights, saved, rest = rest[:2], rest[2:6], rest[6:]
    sent, parts, rest = rest[:members], rest[members : members + shares], rest[members + shares :]
    slots, grads, spec, hidden, slope, passed, real_imag, full, weight_sems, load_sems = rest
    weight_loads = load_weights(block[0], weights, real_imag, weight_sems)
    own = member[0]
    kept, rows, _ = spec.shape
    deep = slots.shape[1] * pack_modes // kept
    loads = [
        [
            pltpu.make_async_copy(distant.at[index], near.at[index], load_sems.at[slot, index])
            for slot, (near, distant) in enumerate(zip((spec, hidden, slope, passed), saved))
        ]
        for index in range(kept)
    ]
    for group in loads:
        for copy in group:
            copy.start()
    place(slots, received, own)
    lat = table[...]
    inverse = lat.T
    finish(weight_loads)
    complex_weights(real_imag, full)
    total_first = jnp.zeros((2 * BS, 2 * BS), jnp.float32)
    total_second = jnp.zeros((2 * BS, 2 * BS), jnp.float32)
    for tile in range(kept // pack_modes):
        backs = []
        for inner, values in enumerate(lat_forward(lat, slots, tile, deep, rows)):
            index = tile * pack_modes + inner
            finish(loads[index])
            grad_post = (values.astype(jnp.float32) * passed[index, :, :WIDE]).astype(jnp.bfloat16)
            grad_hid = product_back(grad_post, full[1])
            grad_pre = (grad_hid * slope[index, :, :WIDE]).astype(jnp.bfloat16)
            backs.append(product_back(grad_pre, full[0]).astype(jnp.bfloat16))
            total_second += product_outer(hidden[index, :, :WIDE], grad_post)
            total_first += product_outer(spec[index, :, :WIDE], grad_pre)
        lat_inverse(inverse, backs, slots, tile, deep)
    deal(sent, slots, own)
    share = grads.shape[1]
    for slot, total in enumerate((total_first, total_second)):
        real = (total[:BS, :BS] + total[BS:, BS:]) * factor
        imag = (total[:BS, BS:] - total[BS:, :BS]) * factor
        for part, value in enumerate((real, imag)):
            for at in range(0, BS, share):
                piece = ((2 * slot + part) * BS + at) // share
                grads[piece] = value[at : at + share].astype(jnp.bfloat16)
    deal(parts, grads, lat_own[0])


def sum_body(*refs):
    refs[-1][...] = sum(value[...].astype(jnp.float32) for value in refs[:-1]).astype(jnp.bfloat16)


def stack_body(own, *refs):
    place(refs[-1], refs[:-1], own[0])


def assemble_body(lat_count, subs, lat_own, *rest):
    gathered, (first, second, slots) = rest[:lat_count], rest[lat_count:]
    rows = gathered[0].shape[1]
    for offset, pieces in enumerate(gathered):
        start = jnp.bitwise_xor(lat_own[0], offset) * rows
        matrix, row = start // BS, pl.multiple_of(start % BS, 16)
        for block in range(NB):
            total = None
            for sub in range(subs):
                value = pieces[sub * NB + block].astype(jnp.float32)
                total = value if total is None else total + value
            slots[matrix, block, pl.ds(row, rows)] = total
    first[...] = slots[:2]
    second[...] = slots[2:]


def exchange(source):
    return lax.all_to_all(source, "lon", split_axis=0, concat_axis=0, tiled=True)


def swap(pieces, axes, partners):
    return [pieces[0]] + [
        lax.ppermute(piece, axes, partners(offset))
        for offset, piece in enumerate(pieces)
        if offset
    ]


def shards(features, cotangent, weight_first, weight_second):
    lat_count = lax.axis_size("lat")
    lon_count = lax.axis_size("lon")
    band_rows, band_cols, channels = features.shape
    rows_total = band_rows * lat_count
    cols_total = band_cols * lon_count
    kept_total = KWD * lat_count * lon_count
    subs = lon_count // NB
    members = lat_count * subs
    rows_sub = band_rows // (RQ * subs)
    rows_cut = min(rows_sub, 4)
    cuts = rows_sub // rows_cut
    kept = kept_total // members
    deep = 2 * rows_sub
    pack_modes = max(1, 16 // deep)
    lat_index = lax.axis_index("lat")
    lon_index = lax.axis_index("lon")
    block = lon_index % NB
    member = lat_index * subs + lon_index // NB
    bf16, f32 = jnp.bfloat16, jnp.float32
    array = jax.ShapeDtypeStruct

    def member_pairs(offset):
        pairs = []
        for lat in range(lat_count):
            for lon in range(lon_count):
                other = (lat * subs + lon // NB) ^ offset
                lon_other = other % subs * NB + lon % NB
                pairs.append((lat * lon_count + lon, other // subs * lon_count + lon_other))
        return pairs

    def line_pairs(count):
        return lambda offset: [(place, place ^ offset) for place in range(count)]

    lon_fwd, lon_inv = map(constant, lon_tables(kept_total, cols_total, lon_count, rows_cut))
    lat_both = constant(lat_table(rows_total, lat_count, subs, rows_sub, rows_cut, pack_modes))
    lon_piece = array((rows_sub * band_cols, PACK), bf16)
    lon_whole = array((lon_count, rows_sub * band_cols, PACK), bf16)
    mid_piece = array((kept * deep, PACK), bf16)
    lon_slots = pltpu.VMEM(lon_whole.shape, bf16)
    mid_slots = pltpu.VMEM((members, kept * deep, PACK), bf16)
    mid_limit = 14 * MIB + 5 * lat_both.size
    share = 4 * BS // lat_count

    def mid_swap(pieces):
        return swap(pieces, ("lat", "lon"), member_pairs)

    def pack(source, sent):
        body = functools.partial(pack_body, rows_sub, subs)
        return kernel_call(body, sent, [lon_index], [source], [lon_slots])

    def unpack(source, base):
        body = functools.partial(unpack_body, rows_sub, subs)
        result = array(base.shape, bf16)
        return kernel_call(body, [result], [lon_index], [base, source], [lon_slots])[0]

    def to_spectra(pieces, anchors=()):
        return kernel_call(
            functools.partial(spectra_body, len(pieces), len(anchors), cuts, kept),
            [mid_piece] * members,
            [lon_index, member],
            [lon_fwd, *pieces],
            [lon_slots, mid_slots],
            anchors,
        )

    def to_columns(pieces, anchors=()):
        return kernel_call(
            functools.partial(columns_body, members, len(anchors), cuts, kept),
            [pltpu.HBM(lon_whole.shape, bf16)],
            [member],
            [lon_inv, *pieces],
            [mid_slots, lon_slots, pltpu.SemaphoreType.DMA((cuts,))],
            anchors,
        )[0]

    modes = (kept, rows_total, STATE)
    types = (bf16, bf16, f32, f32)
    weights = [weight_first, weight_second]
    mid_scratch = [
        *[pltpu.VMEM(modes, kind) for kind in types],
        pltpu.VMEM((2, 2, BS, BS), bf16),
        pltpu.VMEM((2, 2 * BS, 2 * BS), bf16),
        pltpu.SemaphoreType.DMA((2, 2)),
        pltpu.SemaphoreType.DMA((4, kept)),
    ]

    field = swap(pack(features, [lon_piece] * lon_count), "lon", line_pairs(lon_count))
    field_cot = exchange(gate(pack(cotangent, [lon_whole])[0], field))
    results = kernel_call(
        functools.partial(forward_body, members, pack_modes),
        [mid_piece] * members
        + [pltpu.HBM(modes, kind) for kind in types]
        + [array((8, 128), f32)],
        [member, member * kept, block],
        [lat_both, *mid_swap(to_spectra(field))],
        [mid_slots, *mid_scratch],
        far=weights,
        limit=mid_limit,
    )
    saved, anchor = results[members:-1], results[-1]
    filtered = exchange(to_columns(mid_swap(results[:members])))
    cot_results = kernel_call(
        functools.partial(
            backward_body, members, lat_count, pack_modes, 1.0 / math.sqrt(rows_total * kept_total)
        ),
        [mid_piece] * members + [array((share, BS), bf16)] * lat_count,
        [member, lat_index, block],
        [lat_both, *mid_swap(to_spectra([field_cot], [anchor]))],
        [mid_slots, pltpu.VMEM((lat_count, share, BS), bf16), *mid_scratch],
        far=weights + list(saved),
        limit=mid_limit,
    )
    shares = swap(cot_results[members:], "lat", line_pairs(lat_count))
    own_share = kernel_call(sum_body, [array((share, BS), bf16)], [], shares)[0]
    blocks = kernel_call(
        stack_body,
        [array((lon_count, share, BS), bf16)],
        [lon_index],
        swap([own_share] * lon_count, "lon", line_pairs(lon_count)),
    )[0]
    returned = exchange(to_columns(mid_swap(cot_results[:members]), [blocks]))

    gathered = {0: blocks}
    step = lat_count // 2
    while step:
        for offset in sorted(gathered):
            moved = lax.ppermute(gathered[offset], "lat", line_pairs(lat_count)(step))
            gathered[offset | step] = moved
        step //= 2
    gathered = [gathered[offset] for offset in range(lat_count)]
    full = array((2, NB, BS, BS), f32)
    grad_first, grad_second = kernel_call(
        functools.partial(assemble_body, lat_count, subs),
        [full, full],
        [lat_index],
        gathered,
        [pltpu.VMEM((4, NB, BS, BS), f32)],
    )
    return (unpack(filtered, features), unpack(returned, cotangent), grad_first, grad_second)


def solution(mesh):
    in_specs = (P("lat", "lon", None), P("lat", "lon", None), P(), P())
    out_specs = (P("lat", "lon", None), P("lat", "lon", None), P(), P())
    return jax.shard_map(shards, mesh=mesh, in_specs=in_specs, out_specs=out_specs, check_vma=False)
```

```python
import functools
import math

import jax
import jax.numpy as jnp
import ml_dtypes
import numpy as np
from jax import lax
from jax.experimental import pallas as pl
from jax.experimental.pallas import tpu as pltpu
from jax.sharding import PartitionSpec as P

NB = 8
BS = 96
KWD = 1
RQ = 4
PACK = RQ * BS
WIDE = 2 * BS
STATE = -(-WIDE // 128) * 128
MIB = 1024 * 1024

shrink_level = 0.01
gelu_coeff = 0.7978845608028654


def wave_table(first, second, length):
    product = (first[:, None] * second[None, :]) % length
    angle = np.float32(2.0 * math.pi / length) * product.astype(np.float32)
    scale = np.float32(math.sqrt(length))
    rounded = ml_dtypes.bfloat16
    cos = (np.cos(angle) / scale).astype(rounded).astype(np.float32)
    sin = (np.sin(angle) / scale).astype(rounded).astype(np.float32)
    return cos, sin


def lon_tables(kept, cols, lon_count, rows):
    cos, sin = wave_table(np.arange(kept), np.arange(cols), cols)
    parts = np.stack([cos, -sin], axis=1).reshape(kept, 2, lon_count, cols // lon_count)
    eye = np.eye(rows, dtype=np.float32)
    forward = np.einsum("kpgw,rs->kprgsw", parts, eye).reshape(2 * kept * rows, -1)
    return forward, forward.T


def lat_table(rows, lat_count, subs, rows_sub, rows_cut, pack_modes):
    cos, sin = wave_table(np.arange(rows), np.arange(rows), rows)
    forward = np.stack([np.stack([cos, sin], axis=1), np.stack([-sin, cos], axis=1)])
    split = forward.reshape(2, rows, 2, lat_count, RQ, subs, rows_sub // rows_cut, rows_cut)
    eye = np.eye(pack_modes, dtype=np.float32)
    return np.einsum("aqplgshr,jk->jaqglskhpr", split, eye).reshape(2 * pack_modes * rows, -1)


def constant(table):
    return jnp.asarray(table.astype(ml_dtypes.bfloat16))


def kernel_call(body, out_shape, scalars, arrays, scratch=(), anchors=(), far=(), limit=8 * MIB):
    specs = {
        space: pl.BlockSpec(memory_space=space)
        for space in (pltpu.VMEM, pltpu.SMEM, pltpu.HBM, pl.ANY)
    }
    far = [pltpu.with_memory_space_constraint(value, pltpu.HBM) for value in far]
    in_specs = [specs[pltpu.SMEM]] * len(scalars) + [specs[pltpu.VMEM]] * len(arrays)
    in_specs += [specs[pltpu.HBM]] * len(far) + [specs[pl.ANY]] * len(anchors)
    is_far = [getattr(shape, "memory_space", None) is pltpu.HBM for shape in out_shape]
    return pl.pallas_call(
        body,
        out_shape=out_shape,
        in_specs=in_specs,
        out_specs=[specs[pltpu.HBM if distant else pltpu.VMEM] for distant in is_far],
        scratch_shapes=list(scratch),
        compiler_params=pltpu.CompilerParams(vmem_limit_bytes=limit),
    )(*[value.reshape(1).astype(jnp.int32) for value in scalars], *arrays, *far, *anchors)


def gate(source, anchors):
    anywhere = pl.BlockSpec(memory_space=pl.ANY)
    return pl.pallas_call(
        lambda *refs: None,
        out_shape=jax.ShapeDtypeStruct(source.shape, source.dtype),
        in_specs=[anywhere] * (1 + len(anchors)),
        out_specs=anywhere,
        input_output_aliases={0: 0},
    )(source, *anchors)


def pack_body(rows_sub, subs, own, source, *rest):
    sent, slots = rest[:-1], rest[-1]
    cols = source.shape[1]
    for sub in range(subs):
        for block in range(NB):
            pieces = []
            for group in range(RQ):
                row = (group * subs + sub) * rows_sub
                piece = source[row : row + rows_sub, :, block * BS : (block + 1) * BS]
                pieces.append(piece.reshape(rows_sub * cols, BS))
            slots[sub * NB + block] = jnp.concatenate(pieces, axis=1)
    deal(sent, slots, own[0])


def unpack_body(rows_sub, subs, own, base, *rest):
    received, (result, slots) = rest[:-2], rest[-2:]
    cols = base.shape[1]
    place(slots, received, own[0])
    for sub in range(subs):
        for group in range(RQ):
            row = (group * subs + sub) * rows_sub
            pieces = [
                slots[sub * NB + block, :, group * BS : (group + 1) * BS] for block in range(NB)
            ]
            update = jnp.concatenate(pieces, axis=1).reshape(rows_sub, cols, NB * BS)
            old = base[row : row + rows_sub]
            result[row : row + rows_sub] = (
                old.astype(jnp.float32) + update.astype(jnp.float32)
            ).astype(jnp.bfloat16)


def product(left, right):
    return jnp.dot(left, right, preferred_element_type=jnp.float32)


def product_back(left, right):
    return lax.dot_general(
        left, right, (((1,), (1,)), ((), ())), preferred_element_type=jnp.float32
    )


def product_outer(left, right):
    return lax.dot_general(
        left, right, (((0,), (0,)), ((), ())), preferred_element_type=jnp.float32
    )


def place(slots, pieces, own):
    if len(pieces) == 1:
        slots[...] = pieces[0][...]
        return
    for offset, piece in enumerate(pieces):
        slots[jnp.bitwise_xor(own, offset)] = piece[...]


def deal(pieces, slots, own):
    if len(pieces) == 1:
        pieces[0][...] = slots[...]
        return
    for offset, piece in enumerate(pieces):
        piece[...] = slots[jnp.bitwise_xor(own, offset)]


def spectra_body(count, extra, cuts, kept, own_in, own_out, table, *rest):
    received, (sent, slots_in, slots_out) = rest[:count], (rest[count + extra : -2], *rest[-2:])
    place(slots_in, received, own_in[0])
    each = slots_in.shape[1] // cuts
    parts = []
    for cut in range(cuts):
        flat = slots_in[:, cut * each : (cut + 1) * each].reshape(-1, PACK)
        parts.append(product(table[...], flat).reshape(slots_out.shape[0] * kept, -1, PACK))
    joined = jnp.stack(parts, axis=1) if cuts > 1 else parts[0]
    slots_out[...] = joined.reshape(slots_out.shape).astype(jnp.bfloat16)
    deal(sent, slots_out, own_out[0])


def columns_body(count, extra, cuts, kept, own_in, table, *rest):
    received, (result, slots_in, slots_out, sems) = rest[:count], rest[count + extra :]
    place(slots_in, received, own_in[0])
    each = slots_out.shape[1] // cuts
    modes = slots_in.shape[0] * kept
    split = slots_in[...].astype(jnp.float32).reshape(modes, cuts, -1, PACK)
    flats = [split[:, cut].reshape(-1, PACK).astype(jnp.bfloat16) for cut in range(cuts)]
    copies = []
    for cut, flat in enumerate(flats):
        part = product(table[...], flat).astype(jnp.bfloat16)
        rows = pl.ds(cut * each, each)
        slots_out[:, rows] = part.reshape(slots_out.shape[0], each, PACK)
        copies.append(
            pltpu.make_async_copy(slots_out.at[:, rows], result.at[:, rows], sems.at[cut])
        )
        copies[-1].start()
    finish(copies)


def finish(copies):
    for copy in copies:
        copy.wait()


def load_weights(block, weights, real_imag, sems):
    copies = [
        pltpu.make_async_copy(source.at[part, block], real_imag.at[slot, part], sems.at[slot, part])
        for slot, source in enumerate(weights)
        for part in range(2)
    ]
    for copy in copies:
        copy.start()
    return copies


def complex_weights(real_imag, full):
    for slot in range(full.shape[0]):
        real, imag = real_imag[slot, 0], real_imag[slot, 1]
        full[slot, :BS] = jnp.concatenate([real, imag], axis=1)
        full[slot, BS:] = jnp.concatenate([-imag, real], axis=1)


def lat_forward(table, slots, tile, deep, rows):
    slab = slots[:, tile * deep : (tile + 1) * deep]
    flat = slab.reshape(slab.shape[0] * deep, PACK)
    stacked = jnp.concatenate(
        [flat[:, group * BS : (group + 1) * BS] for group in range(RQ)], axis=0
    )
    spectrum = product(table, stacked).astype(jnp.bfloat16)
    return [
        jnp.concatenate([spectrum[at : at + rows], spectrum[at + rows : at + 2 * rows]], axis=1)
        for at in range(0, spectrum.shape[0], 2 * rows)
    ]


def lat_inverse(table, values, slots, tile, deep):
    stacked = jnp.concatenate(
        [part for value in values for part in (value[:, :BS], value[:, BS:])], axis=0
    )
    rows = product(table, stacked).astype(jnp.bfloat16)
    each = rows.shape[0] // RQ
    packed = jnp.concatenate([rows[at : at + each] for at in range(0, RQ * each, each)], axis=1)
    slots[:, tile * deep : (tile + 1) * deep] = packed.reshape(slots.shape[0], deep, PACK)


def mode_weight(first_mode, index):
    return jnp.where(first_mode + index == 0, 1.0, 2.0).astype(jnp.float32)


def gelu(pre):
    squared = pre * pre
    tangent = jnp.tanh(gelu_coeff * (pre + 0.044715 * squared * pre))
    act = (0.5 * pre * (1.0 + tangent)).astype(jnp.bfloat16)
    return act, squared, tangent


def forward_body(members, pack_modes, member, first_mode, block, table, *rest):
    received, weights, sent = rest[:members], rest[members : members + 2], rest[members + 2 :]
    sent, rest = sent[:members], sent[members:]
    saved, anchor, slots, spec, real_imag, full, weight_sems, save_sems = rest
    anchor[...] = jnp.zeros_like(anchor)
    loads = load_weights(block[0], weights, real_imag, weight_sems)
    own = member[0]
    kept, rows, _ = spec.shape
    deep = slots.shape[1] * pack_modes // kept
    place(slots, received, own)
    lat = table[...]
    inverse = lat.T
    finish(loads)
    complex_weights(real_imag, full)
    copies = []
    for tile in range(kept // pack_modes):
        outs = []
        for inner, values in enumerate(lat_forward(lat, slots, tile, deep, rows)):
            index = tile * pack_modes + inner
            spec[index, :, :WIDE] = values
            copies.append(
                pltpu.make_async_copy(spec.at[index], saved.at[index], save_sems.at[index])
            )
            copies[-1].start()
            act, _, _ = gelu(product(values, full[0]))
            post = product(act, full[1])
            weight = mode_weight(first_mode[0], index)
            shrunk = post - shrink_level * jnp.tanh(post / shrink_level)
            outs.append((weight * shrunk).astype(jnp.bfloat16))
        lat_inverse(inverse, outs, slots, tile, deep)
    deal(sent, slots, own)
    finish(copies)


def backward_body(
    members, shares, pack_modes, factor, member, first_mode, lat_own, block, table, *rest
):
    received, rest = rest[:members], rest[members:]
    weights, saved, result, rest = rest[:2], rest[2], rest[3], rest[4:]
    parts, (slots, grads, spec, real_imag, full, weight_sems, load_sems) = rest[:shares], rest[shares:]
    loads = load_weights(block[0], weights, real_imag, weight_sems)
    kept, rows, _ = spec.shape
    deep = slots.shape[1] * pack_modes // kept
    spec_loads = [
        pltpu.make_async_copy(saved.at[index], spec.at[index], load_sems.at[index])
        for index in range(kept)
    ]
    for copy in spec_loads:
        copy.start()
    place(slots, received, member[0])
    lat = table[...]
    finish(loads)
    complex_weights(real_imag, full)
    total_first = jnp.zeros((WIDE, WIDE), jnp.float32)
    total_second = jnp.zeros((WIDE, WIDE), jnp.float32)
    for tile in range(kept // pack_modes):
        for inner, cot in enumerate(lat_forward(lat, slots, tile, deep, rows)):
            index = tile * pack_modes + inner
            spec_loads[index].wait()
            values = spec[index, :, :WIDE]
            pre = product(values, full[0])
            act, squared, tangent = gelu(pre)
            slope = 0.5 * (1.0 + tangent) + 0.5 * pre * (1.0 - tangent * tangent) * gelu_coeff * (
                1.0 + 3.0 * 0.044715 * squared
            )
            ratio = jnp.tanh(product(act, full[1]) / shrink_level)
            weight = mode_weight(first_mode[0], index)
            grad_post = (weight * cot.astype(jnp.float32) * (ratio * ratio)).astype(jnp.bfloat16)
            grad_pre = (product_back(grad_post, full[1]) * slope).astype(jnp.bfloat16)
            result[index] = grad_pre
            total_second += product_outer(act, grad_post)
            total_first += product_outer(values, grad_pre)
    share = grads.shape[1]
    for slot, total in enumerate((total_first, total_second)):
        real = (total[:BS, :BS] + total[BS:, BS:]) * factor
        imag = (total[:BS, BS:] - total[BS:, :BS]) * factor
        for part, value in enumerate((real, imag)):
            for at in range(0, BS, share):
                piece = ((2 * slot + part) * BS + at) // share
                grads[piece] = value[at : at + share].astype(jnp.bfloat16)
    deal(parts, grads, lat_own[0])


def input_grad_body(pack_modes, member, block, table, grad_pre, weights, *rest):
    sent, (slots, real_imag, full, weight_sems) = rest[:-4], rest[-4:]
    loads = load_weights(block[0], [weights], real_imag, weight_sems)
    kept = grad_pre.shape[0]
    deep = slots.shape[1] * pack_modes // kept
    inverse = table[...].T
    finish(loads)
    complex_weights(real_imag, full)
    for tile in range(kept // pack_modes):
        backs = [
            product_back(grad_pre[tile * pack_modes + inner], full[0]).astype(jnp.bfloat16)
            for inner in range(pack_modes)
        ]
        lat_inverse(inverse, backs, slots, tile, deep)
    deal(sent, slots, member[0])


def sum_body(*refs):
    refs[-1][...] = sum(value[...].astype(jnp.float32) for value in refs[:-1]).astype(jnp.bfloat16)


def stack_body(*refs):
    for slot, piece in enumerate(refs[:-1]):
        refs[-1][slot] = piece[...]


def blocks_body(own, near, other, blocks):
    for slot in range(near.shape[0]):
        blocks[jnp.bitwise_xor(own[0], 2 * slot)] = near[slot]
        blocks[jnp.bitwise_xor(own[0], 2 * slot + 1)] = other[slot]


def assemble_body(lat_count, subs, lat_own, *rest):
    gathered, (first, second, slots) = rest[:lat_count], rest[lat_count:]
    rows = gathered[0].shape[1]
    for offset, pieces in enumerate(gathered):
        start = jnp.bitwise_xor(lat_own[0], offset) * rows
        matrix, row = start // BS, pl.multiple_of(start % BS, 16)
        for block in range(NB):
            total = None
            for sub in range(subs):
                value = pieces[sub * NB + block].astype(jnp.float32)
                total = value if total is None else total + value
            slots[matrix, block, pl.ds(row, rows)] = total
    first[...] = slots[:2]
    second[...] = slots[2:]


def exchange(source):
    return lax.all_to_all(source, "lon", split_axis=0, concat_axis=0, tiled=True)


def swap(pieces, axes, partners):
    return [pieces[0]] + [
        lax.ppermute(piece, axes, partners(offset))
        for offset, piece in enumerate(pieces)
        if offset
    ]


def shards(features, cotangent, weight_first, weight_second):
    lat_count = lax.axis_size("lat")
    lon_count = lax.axis_size("lon")
    band_rows, band_cols, channels = features.shape
    rows_total = band_rows * lat_count
    cols_total = band_cols * lon_count
    kept_total = KWD * lat_count * lon_count
    subs = lon_count // NB
    members = lat_count * subs
    rows_sub = band_rows // (RQ * subs)
    rows_cut = min(rows_sub, 4)
    cuts = rows_sub // rows_cut
    kept = kept_total // members
    deep = 2 * rows_sub
    pack_modes = max(1, 16 // deep)
    lat_index = lax.axis_index("lat")
    lon_index = lax.axis_index("lon")
    block = lon_index % NB
    member = lat_index * subs + lon_index // NB
    bf16, f32 = jnp.bfloat16, jnp.float32
    array = jax.ShapeDtypeStruct

    def member_pairs(offset):
        pairs = []
        for lat in range(lat_count):
            for lon in range(lon_count):
                other = (lat * subs + lon // NB) ^ offset
                lon_other = other % subs * NB + lon % NB
                pairs.append((lat * lon_count + lon, other // subs * lon_count + lon_other))
        return pairs

    def line_pairs(count):
        return lambda offset: [(place, place ^ offset) for place in range(count)]

    lon_fwd, lon_inv = map(constant, lon_tables(kept_total, cols_total, lon_count, rows_cut))
    lat_both = constant(lat_table(rows_total, lat_count, subs, rows_sub, rows_cut, pack_modes))
    lon_piece = array((rows_sub * band_cols, PACK), bf16)
    lon_whole = array((lon_count, rows_sub * band_cols, PACK), bf16)
    mid_piece = array((kept * deep, PACK), bf16)
    lon_slots = pltpu.VMEM(lon_whole.shape, bf16)
    mid_slots = pltpu.VMEM((members, kept * deep, PACK), bf16)
    mid_limit = 14 * MIB + 5 * lat_both.size
    share = 4 * BS // lat_count

    def mid_swap(pieces):
        return swap(pieces, ("lat", "lon"), member_pairs)

    def pack(source, sent):
        body = functools.partial(pack_body, rows_sub, subs)
        return kernel_call(body, sent, [lon_index], [source], [lon_slots])

    def unpack(source, base):
        body = functools.partial(unpack_body, rows_sub, subs)
        result = array(base.shape, bf16)
        return kernel_call(body, [result], [lon_index], [base, source], [lon_slots])[0]

    def to_spectra(pieces, anchors=()):
        return kernel_call(
            functools.partial(spectra_body, len(pieces), len(anchors), cuts, kept),
            [mid_piece] * members,
            [lon_index, member],
            [lon_fwd, *pieces],
            [lon_slots, mid_slots],
            anchors,
        )

    def to_columns(pieces, anchors=()):
        return kernel_call(
            functools.partial(columns_body, members, len(anchors), cuts, kept),
            [pltpu.HBM(lon_whole.shape, bf16)],
            [member],
            [lon_inv, *pieces],
            [mid_slots, lon_slots, pltpu.SemaphoreType.DMA((cuts,))],
            anchors,
        )[0]

    modes = (kept, rows_total, STATE)
    weights = [weight_first, weight_second]
    mid_scratch = [
        pltpu.VMEM(modes, bf16),
        pltpu.VMEM((2, 2, BS, BS), bf16),
        pltpu.VMEM((2, WIDE, WIDE), bf16),
        pltpu.SemaphoreType.DMA((2, 2)),
        pltpu.SemaphoreType.DMA((kept,)),
    ]

    field = swap(pack(features, [lon_piece] * lon_count), "lon", line_pairs(lon_count))
    field_cot = exchange(gate(pack(cotangent, [lon_whole])[0], field))
    results = kernel_call(
        functools.partial(forward_body, members, pack_modes),
        [mid_piece] * members + [pltpu.HBM(modes, bf16), array((8, 128), f32)],
        [member, member * kept, block],
        [lat_both, *mid_swap(to_spectra(field))],
        [mid_slots, *mid_scratch],
        far=weights,
        limit=mid_limit,
    )
    saved, anchor = results[members:]
    spectra_cot = to_spectra([field_cot], [anchor])
    filtered = exchange(to_columns(mid_swap(results[:members]), spectra_cot[:1]))
    grad_pre, *parts = kernel_call(
        functools.partial(
            backward_body, members, lat_count, pack_modes, 1.0 / math.sqrt(rows_total * kept_total)
        ),
        [array((kept, rows_total, WIDE), bf16)] + [array((share, BS), bf16)] * lat_count,
        [member, member * kept, lat_index, block],
        [lat_both, *mid_swap(spectra_cot)],
        [mid_slots, pltpu.VMEM((lat_count, share, BS), bf16), *mid_scratch],
        far=weights + [saved],
        limit=mid_limit,
    )
    own_share = kernel_call(
        sum_body, [array((share, BS), bf16)], [], swap(parts, "lat", line_pairs(lat_count))
    )[0]
    back = kernel_call(
        functools.partial(input_grad_body, pack_modes),
        [mid_piece] * members,
        [member, block],
        [lat_both, grad_pre],
        [
            mid_slots,
            pltpu.VMEM((1, 2, BS, BS), bf16),
            pltpu.VMEM((1, WIDE, WIDE), bf16),
            pltpu.SemaphoreType.DMA((1, 2)),
        ],
        far=weights[:1],
        limit=mid_limit,
    )
    lon_pairs = line_pairs(lon_count)
    near = kernel_call(
        stack_body,
        [array((lon_count // 2, share, BS), bf16)],
        [],
        [own_share]
        + [lax.ppermute(own_share, "lon", lon_pairs(far)) for far in range(2, lon_count, 2)],
    )[0]
    returned = exchange(to_columns(mid_swap(back), [near]))
    blocks = kernel_call(
        blocks_body,
        [array((lon_count, share, BS), bf16)],
        [lon_index],
        [near, lax.ppermute(near, "lon", lon_pairs(1))],
    )[0]

    gathered = {0: blocks}
    step = lat_count // 2
    while step:
        for offset in sorted(gathered):
            moved = lax.ppermute(gathered[offset], "lat", line_pairs(lat_count)(step))
            gathered[offset | step] = moved
        step //= 2
    gathered = [gathered[offset] for offset in range(lat_count)]
    full = array((2, NB, BS, BS), f32)
    grad_first, grad_second = kernel_call(
        functools.partial(assemble_body, lat_count, subs),
        [full, full],
        [lat_index],
        gathered,
        [pltpu.VMEM((4, NB, BS, BS), f32)],
    )
    return (unpack(filtered, features), unpack(returned, cotangent), grad_first, grad_second)


def solution(mesh):
    in_specs = (P("lat", "lon", None), P("lat", "lon", None), P(), P())
    out_specs = (P("lat", "lon", None), P("lat", "lon", None), P(), P())
    return jax.shard_map(shards, mesh=mesh, in_specs=in_specs, out_specs=out_specs, check_vma=False)
```

```python
import functools
import math

import jax
import jax.numpy as jnp
import ml_dtypes
import numpy as np
from jax import lax
from jax.experimental import pallas as pl
from jax.experimental.pallas import tpu as pltpu
from jax.sharding import PartitionSpec as P

NB = 8
BS = 96
KWD = 1
RQ = 4
PACK = RQ * BS
WIDE = 2 * BS
STATE = -(-WIDE // 128) * 128
MIB = 1024 * 1024

shrink_level = 0.01
gelu_coeff = 0.7978845608028654


def wave_table(first, second, length):
    product = (first[:, None] * second[None, :]) % length
    angle = np.float32(2.0 * math.pi / length) * product.astype(np.float32)
    scale = np.float32(math.sqrt(length))
    rounded = ml_dtypes.bfloat16
    cos = (np.cos(angle) / scale).astype(rounded).astype(np.float32)
    sin = (np.sin(angle) / scale).astype(rounded).astype(np.float32)
    return cos, sin


def lon_tables(kept, cols, lon_count, rows):
    cos, sin = wave_table(np.arange(kept), np.arange(cols), cols)
    parts = np.stack([cos, -sin], axis=1).reshape(kept, 2, lon_count, cols // lon_count)
    eye = np.eye(rows, dtype=np.float32)
    forward = np.einsum("kpgw,rs->kprgsw", parts, eye).reshape(2 * kept * rows, -1)
    return forward, forward.T


def lat_table(rows, lat_count, subs, rows_sub, rows_cut, pack_modes):
    cos, sin = wave_table(np.arange(rows), np.arange(rows), rows)
    forward = np.stack([np.stack([cos, sin], axis=1), np.stack([-sin, cos], axis=1)])
    split = forward.reshape(2, rows, 2, lat_count, RQ, subs, rows_sub // rows_cut, rows_cut)
    eye = np.eye(pack_modes, dtype=np.float32)
    return np.einsum("aqplgshr,jk->jaqglskhpr", split, eye).reshape(2 * pack_modes * rows, -1)


def constant(table):
    return jnp.asarray(table.astype(ml_dtypes.bfloat16))


def kernel_call(body, out_shape, scalars, arrays, scratch=(), anchors=(), far=(), limit=8 * MIB):
    specs = {
        space: pl.BlockSpec(memory_space=space)
        for space in (pltpu.VMEM, pltpu.SMEM, pltpu.HBM, pl.ANY)
    }
    far = [pltpu.with_memory_space_constraint(value, pltpu.HBM) for value in far]
    in_specs = [specs[pltpu.SMEM]] * len(scalars) + [specs[pltpu.VMEM]] * len(arrays)
    in_specs += [specs[pltpu.HBM]] * len(far) + [specs[pl.ANY]] * len(anchors)
    is_far = [getattr(shape, "memory_space", None) is pltpu.HBM for shape in out_shape]
    return pl.pallas_call(
        body,
        out_shape=out_shape,
        in_specs=in_specs,
        out_specs=[specs[pltpu.HBM if distant else pltpu.VMEM] for distant in is_far],
        scratch_shapes=list(scratch),
        compiler_params=pltpu.CompilerParams(vmem_limit_bytes=limit),
    )(*[value.reshape(1).astype(jnp.int32) for value in scalars], *arrays, *far, *anchors)


def gate(source, anchors):
    anywhere = pl.BlockSpec(memory_space=pl.ANY)
    return pl.pallas_call(
        lambda *refs: None,
        out_shape=jax.ShapeDtypeStruct(source.shape, source.dtype),
        in_specs=[anywhere] * (1 + len(anchors)),
        out_specs=anywhere,
        input_output_aliases={0: 0},
    )(source, *anchors)


def pack_body(rows_sub, subs, own, source, *rest):
    sent, slots = rest[:-1], rest[-1]
    cols = source.shape[1]
    for sub in range(subs):
        for block in range(NB):
            pieces = []
            for group in range(RQ):
                row = (group * subs + sub) * rows_sub
                piece = source[row : row + rows_sub, :, block * BS : (block + 1) * BS]
                pieces.append(piece.reshape(rows_sub * cols, BS))
            slots[sub * NB + block] = jnp.concatenate(pieces, axis=1)
    deal(sent, slots, own[0])


def unpack_body(rows_sub, subs, own, base, *rest):
    received, (result, slots) = rest[:-2], rest[-2:]
    cols = base.shape[1]
    place(slots, received, own[0])
    for sub in range(subs):
        for group in range(RQ):
            row = (group * subs + sub) * rows_sub
            pieces = [
                slots[sub * NB + block, :, group * BS : (group + 1) * BS] for block in range(NB)
            ]
            update = jnp.concatenate(pieces, axis=1).reshape(rows_sub, cols, NB * BS)
            old = base[row : row + rows_sub]
            result[row : row + rows_sub] = (
                old.astype(jnp.float32) + update.astype(jnp.float32)
            ).astype(jnp.bfloat16)


def product(left, right):
    return jnp.dot(left, right, preferred_element_type=jnp.float32)


def product_back(left, right):
    return lax.dot_general(
        left, right, (((1,), (1,)), ((), ())), preferred_element_type=jnp.float32
    )


def product_outer(left, right):
    return lax.dot_general(
        left, right, (((0,), (0,)), ((), ())), preferred_element_type=jnp.float32
    )


def place(slots, pieces, own):
    if len(pieces) == 1:
        slots[...] = pieces[0][...]
        return
    for offset, piece in enumerate(pieces):
        slots[jnp.bitwise_xor(own, offset)] = piece[...]


def deal(pieces, slots, own):
    if len(pieces) == 1:
        pieces[0][...] = slots[...]
        return
    for offset, piece in enumerate(pieces):
        piece[...] = slots[jnp.bitwise_xor(own, offset)]


def spectra_body(count, extra, cuts, kept, own_in, own_out, table, *rest):
    received, (sent, slots_in, slots_out) = rest[:count], (rest[count + extra : -2], *rest[-2:])
    place(slots_in, received, own_in[0])
    each = slots_in.shape[1] // cuts
    parts = []
    for cut in range(cuts):
        flat = slots_in[:, cut * each : (cut + 1) * each].reshape(-1, PACK)
        parts.append(product(table[...], flat).reshape(slots_out.shape[0] * kept, -1, PACK))
    joined = jnp.stack(parts, axis=1) if cuts > 1 else parts[0]
    slots_out[...] = joined.reshape(slots_out.shape).astype(jnp.bfloat16)
    deal(sent, slots_out, own_out[0])


def columns_body(count, extra, cuts, kept, own_in, table, *rest):
    received, (result, slots_in, slots_out, sems) = rest[:count], rest[count + extra :]
    place(slots_in, received, own_in[0])
    each = slots_out.shape[1] // cuts
    modes = slots_in.shape[0] * kept
    split = slots_in[...].astype(jnp.float32).reshape(modes, cuts, -1, PACK)
    flats = [split[:, cut].reshape(-1, PACK).astype(jnp.bfloat16) for cut in range(cuts)]
    copies = []
    for cut, flat in enumerate(flats):
        part = product(table[...], flat).astype(jnp.bfloat16)
        rows = pl.ds(cut * each, each)
        slots_out[:, rows] = part.reshape(slots_out.shape[0], each, PACK)
        copies.append(
            pltpu.make_async_copy(slots_out.at[:, rows], result.at[:, rows], sems.at[cut])
        )
        copies[-1].start()
    finish(copies)


def finish(copies):
    for copy in copies:
        copy.wait()


def load_weights(block, weights, real_imag, sems):
    copies = [
        pltpu.make_async_copy(source.at[part, block], real_imag.at[slot, part], sems.at[slot, part])
        for slot, source in enumerate(weights)
        for part in range(2)
    ]
    for copy in copies:
        copy.start()
    return copies


def complex_weights(real_imag, full):
    for slot in range(full.shape[0]):
        real, imag = real_imag[slot, 0], real_imag[slot, 1]
        full[slot, :BS] = jnp.concatenate([real, imag], axis=1)
        full[slot, BS:] = jnp.concatenate([-imag, real], axis=1)


def lat_forward(table, slots, tile, deep, rows):
    slab = slots[:, tile * deep : (tile + 1) * deep]
    flat = slab.reshape(slab.shape[0] * deep, PACK)
    stacked = jnp.concatenate(
        [flat[:, group * BS : (group + 1) * BS] for group in range(RQ)], axis=0
    )
    spectrum = product(table, stacked).astype(jnp.bfloat16)
    return [
        jnp.concatenate([spectrum[at : at + rows], spectrum[at + rows : at + 2 * rows]], axis=1)
        for at in range(0, spectrum.shape[0], 2 * rows)
    ]


def lat_inverse(table, values, slots, tile, deep):
    stacked = jnp.concatenate(
        [part for value in values for part in (value[:, :BS], value[:, BS:])], axis=0
    )
    rows = product(table, stacked).astype(jnp.bfloat16)
    each = rows.shape[0] // RQ
    packed = jnp.concatenate([rows[at : at + each] for at in range(0, RQ * each, each)], axis=1)
    slots[:, tile * deep : (tile + 1) * deep] = packed.reshape(slots.shape[0], deep, PACK)


def mode_weight(first_mode, index):
    return jnp.where(first_mode + index == 0, 1.0, 2.0).astype(jnp.float32)


def gelu(pre):
    squared = pre * pre
    tangent = jnp.tanh(gelu_coeff * (pre + 0.044715 * squared * pre))
    act = (0.5 * pre * (1.0 + tangent)).astype(jnp.bfloat16)
    return act, squared, tangent


def forward_body(members, pack_modes, member, first_mode, block, table, *rest):
    received, weights, sent = rest[:members], rest[members : members + 2], rest[members + 2 :]
    sent, rest = sent[:members], sent[members:]
    saved, anchor, slots, spec, real_imag, full, weight_sems, save_sems = rest
    anchor[...] = jnp.zeros_like(anchor)
    loads = load_weights(block[0], weights, real_imag, weight_sems)
    own = member[0]
    kept, rows, _ = spec.shape
    deep = slots.shape[1] * pack_modes // kept
    place(slots, received, own)
    lat = table[...]
    inverse = lat.T
    copies = []
    for tile in range(kept // pack_modes):
        for inner, values in enumerate(lat_forward(lat, slots, tile, deep, rows)):
            index = tile * pack_modes + inner
            spec[index, :, :WIDE] = values
            copies.append(
                pltpu.make_async_copy(spec.at[index], saved.at[index], save_sems.at[index])
            )
            copies[-1].start()
    finish(loads)
    complex_weights(real_imag, full)
    for tile in range(kept // pack_modes):
        outs = []
        for index in range(tile * pack_modes, (tile + 1) * pack_modes):
            act, _, _ = gelu(product(spec[index, :, :WIDE], full[0]))
            post = product(act, full[1])
            weight = mode_weight(first_mode[0], index)
            shrunk = post - shrink_level * jnp.tanh(post / shrink_level)
            outs.append((weight * shrunk).astype(jnp.bfloat16))
        lat_inverse(inverse, outs, slots, tile, deep)
    deal(sent, slots, own)
    finish(copies)


def backward_body(
    members, shares, pack_modes, factor, member, first_mode, lat_own, block, table, *rest
):
    received, rest = rest[:members], rest[members:]
    weights, saved, result, combined, rest = rest[:2], rest[2], rest[3], rest[4], rest[5:]
    parts, (slots, grads, cots, spec, real_imag, full, weight_sems, load_sems) = (
        rest[:shares],
        rest[shares:],
    )
    loads = load_weights(block[0], weights, real_imag, weight_sems)
    kept, rows, _ = spec.shape
    deep = slots.shape[1] * pack_modes // kept
    spec_loads = [
        pltpu.make_async_copy(saved.at[index], spec.at[index], load_sems.at[index])
        for index in range(kept)
    ]
    for copy in spec_loads:
        copy.start()
    place(slots, received, member[0])
    lat = table[...]
    for tile in range(kept // pack_modes):
        for inner, cot in enumerate(lat_forward(lat, slots, tile, deep, rows)):
            cots[tile * pack_modes + inner] = cot
    finish(loads)
    complex_weights(real_imag, full)
    combined[...] = full[0]
    total_first = jnp.zeros((WIDE, WIDE), jnp.float32)
    total_second = jnp.zeros((WIDE, WIDE), jnp.float32)
    for index in range(kept):
        spec_loads[index].wait()
        values = spec[index, :, :WIDE]
        pre = product(values, full[0])
        act, squared, tangent = gelu(pre)
        slope = 0.5 * (1.0 + tangent) + 0.5 * pre * (1.0 - tangent * tangent) * gelu_coeff * (
            1.0 + 3.0 * 0.044715 * squared
        )
        ratio = jnp.tanh(product(act, full[1]) / shrink_level)
        weight = mode_weight(first_mode[0], index)
        cot = cots[index].astype(jnp.float32)
        grad_post = (weight * cot * (ratio * ratio)).astype(jnp.bfloat16)
        grad_pre = (product_back(grad_post, full[1]) * slope).astype(jnp.bfloat16)
        result[index] = grad_pre
        total_second += product_outer(act, grad_post)
        total_first += product_outer(values, grad_pre)
    share = grads.shape[1]
    for slot, total in enumerate((total_first, total_second)):
        real = (total[:BS, :BS] + total[BS:, BS:]) * factor
        imag = (total[:BS, BS:] - total[BS:, :BS]) * factor
        for part, value in enumerate((real, imag)):
            for at in range(0, BS, share):
                piece = ((2 * slot + part) * BS + at) // share
                grads[piece] = value[at : at + share].astype(jnp.bfloat16)
    deal(parts, grads, lat_own[0])


def input_grad_body(pack_modes, extra, member, table, grad_pre, combined, *rest):
    sent, slots = rest[extra:-1], rest[-1]
    kept = grad_pre.shape[0]
    deep = slots.shape[1] * pack_modes // kept
    inverse = table[...].T
    for tile in range(kept // pack_modes):
        backs = [
            product_back(grad_pre[index], combined[...]).astype(jnp.bfloat16)
            for index in range(tile * pack_modes, (tile + 1) * pack_modes)
        ]
        lat_inverse(inverse, backs, slots, tile, deep)
    deal(sent, slots, member[0])


def sum_body(*refs):
    refs[-1][...] = sum(value[...].astype(jnp.float32) for value in refs[:-1]).astype(jnp.bfloat16)


def stack_body(*refs):
    for slot, piece in enumerate(refs[:-1]):
        refs[-1][slot] = piece[...]


def blocks_body(own, near, other, blocks):
    for slot in range(near.shape[0]):
        blocks[jnp.bitwise_xor(own[0], 2 * slot)] = near[slot]
        blocks[jnp.bitwise_xor(own[0], 2 * slot + 1)] = other[slot]


def assemble_body(lat_count, subs, lat_own, *rest):
    gathered, (first, second, slots) = rest[:lat_count], rest[lat_count:]
    rows = gathered[0].shape[1]
    for offset, pieces in enumerate(gathered):
        start = jnp.bitwise_xor(lat_own[0], offset) * rows
        matrix, row = start // BS, pl.multiple_of(start % BS, 16)
        for block in range(NB):
            total = None
            for sub in range(subs):
                value = pieces[sub * NB + block].astype(jnp.float32)
                total = value if total is None else total + value
            slots[matrix, block, pl.ds(row, rows)] = total
    first[...] = slots[:2]
    second[...] = slots[2:]


def exchange(source):
    return lax.all_to_all(source, "lon", split_axis=0, concat_axis=0, tiled=True)


def swap(pieces, axes, partners):
    return [pieces[0]] + [
        lax.ppermute(piece, axes, partners(offset))
        for offset, piece in enumerate(pieces)
        if offset
    ]


def shards(features, cotangent, weight_first, weight_second):
    lat_count = lax.axis_size("lat")
    lon_count = lax.axis_size("lon")
    band_rows, band_cols, channels = features.shape
    rows_total = band_rows * lat_count
    cols_total = band_cols * lon_count
    kept_total = KWD * lat_count * lon_count
    subs = lon_count // NB
    members = lat_count * subs
    rows_sub = band_rows // (RQ * subs)
    rows_cut = min(rows_sub, 4)
    cuts = rows_sub // rows_cut
    kept = kept_total // members
    deep = 2 * rows_sub
    pack_modes = max(1, 16 // deep)
    lat_index = lax.axis_index("lat")
    lon_index = lax.axis_index("lon")
    block = lon_index % NB
    member = lat_index * subs + lon_index // NB
    bf16, f32 = jnp.bfloat16, jnp.float32
    array = jax.ShapeDtypeStruct

    def member_pairs(offset):
        pairs = []
        for lat in range(lat_count):
            for lon in range(lon_count):
                other = (lat * subs + lon // NB) ^ offset
                lon_other = other % subs * NB + lon % NB
                pairs.append((lat * lon_count + lon, other // subs * lon_count + lon_other))
        return pairs

    def line_pairs(count):
        return lambda offset: [(place, place ^ offset) for place in range(count)]

    lon_fwd, lon_inv = map(constant, lon_tables(kept_total, cols_total, lon_count, rows_cut))
    lat_both = constant(lat_table(rows_total, lat_count, subs, rows_sub, rows_cut, pack_modes))
    lon_piece = array((rows_sub * band_cols, PACK), bf16)
    lon_whole = array((lon_count, rows_sub * band_cols, PACK), bf16)
    mid_piece = array((kept * deep, PACK), bf16)
    lon_slots = pltpu.VMEM(lon_whole.shape, bf16)
    mid_slots = pltpu.VMEM((members, kept * deep, PACK), bf16)
    mid_limit = 14 * MIB + 5 * lat_both.size
    share = 4 * BS // lat_count

    def mid_swap(pieces):
        return swap(pieces, ("lat", "lon"), member_pairs)

    def pack(source, sent):
        body = functools.partial(pack_body, rows_sub, subs)
        return kernel_call(body, sent, [lon_index], [source], [lon_slots])

    def unpack(source, base):
        body = functools.partial(unpack_body, rows_sub, subs)
        result = array(base.shape, bf16)
        return kernel_call(body, [result], [lon_index], [base, source], [lon_slots])[0]

    def to_spectra(pieces, anchors=()):
        return kernel_call(
            functools.partial(spectra_body, len(pieces), len(anchors), cuts, kept),
            [mid_piece] * members,
            [lon_index, member],
            [lon_fwd, *pieces],
            [lon_slots, mid_slots],
            anchors,
        )

    def to_columns(pieces, anchors=()):
        return kernel_call(
            functools.partial(columns_body, members, len(anchors), cuts, kept),
            [pltpu.HBM(lon_whole.shape, bf16)],
            [member],
            [lon_inv, *pieces],
            [mid_slots, lon_slots, pltpu.SemaphoreType.DMA((cuts,))],
            anchors,
        )[0]

    modes = (kept, rows_total, STATE)
    weights = [weight_first, weight_second]
    mid_scratch = [
        pltpu.VMEM(modes, bf16),
        pltpu.VMEM((2, 2, BS, BS), bf16),
        pltpu.VMEM((2, WIDE, WIDE), bf16),
        pltpu.SemaphoreType.DMA((2, 2)),
        pltpu.SemaphoreType.DMA((kept,)),
    ]

    field = swap(pack(features, [lon_piece] * lon_count), "lon", line_pairs(lon_count))
    field_cot = exchange(gate(pack(cotangent, [lon_whole])[0], field))
    results = kernel_call(
        functools.partial(forward_body, members, pack_modes),
        [mid_piece] * members + [pltpu.HBM(modes, bf16), array((8, 128), f32)],
        [member, member * kept, block],
        [lat_both, *mid_swap(to_spectra(field))],
        [mid_slots, *mid_scratch],
        far=weights,
        limit=mid_limit,
    )
    saved, anchor = results[members:]
    spectra_cot = to_spectra([field_cot], [anchor])
    filtered = exchange(to_columns(mid_swap(results[:members]), spectra_cot[:1]))
    wide = (kept, rows_total, WIDE)
    grad_pre, combined, *parts = kernel_call(
        functools.partial(
            backward_body, members, lat_count, pack_modes, 1.0 / math.sqrt(rows_total * kept_total)
        ),
        [array(wide, bf16), array((WIDE, WIDE), bf16)] + [array((share, BS), bf16)] * lat_count,
        [member, member * kept, lat_index, block],
        [lat_both, *mid_swap(spectra_cot)],
        [
            mid_slots,
            pltpu.VMEM((lat_count, share, BS), bf16),
            pltpu.VMEM(wide, bf16),
            *mid_scratch,
        ],
        far=weights + [saved],
        limit=mid_limit,
    )
    own_share = kernel_call(
        sum_body, [array((share, BS), bf16)], [], swap(parts, "lat", line_pairs(lat_count))
    )[0]
    back = kernel_call(
        functools.partial(input_grad_body, pack_modes, 1),
        [mid_piece] * members,
        [member],
        [lat_both, grad_pre, combined],
        [mid_slots],
        [own_share],
        limit=mid_limit,
    )
    lon_pairs = line_pairs(lon_count)
    near = kernel_call(
        stack_body,
        [array((lon_count // 2, share, BS), bf16)],
        [],
        [own_share]
        + [lax.ppermute(own_share, "lon", lon_pairs(far)) for far in range(2, lon_count, 2)],
    )[0]
    returned = exchange(to_columns(mid_swap(back), [near]))
    blocks = kernel_call(
        blocks_body,
        [array((lon_count, share, BS), bf16)],
        [lon_index],
        [near, lax.ppermute(near, "lon", lon_pairs(1))],
    )[0]

    gathered = {0: blocks}
    step = lat_count // 2
    while step:
        for offset in sorted(gathered):
            moved = lax.ppermute(gathered[offset], "lat", line_pairs(lat_count)(step))
            gathered[offset | step] = moved
        step //= 2
    gathered = [gathered[offset] for offset in range(lat_count)]
    full = array((2, NB, BS, BS), f32)
    grad_first, grad_second = kernel_call(
        functools.partial(assemble_body, lat_count, subs),
        [full, full],
        [lat_index],
        gathered,
        [pltpu.VMEM((4, NB, BS, BS), f32)],
    )
    return (unpack(filtered, features), unpack(returned, cotangent), grad_first, grad_second)


def solution(mesh):
    in_specs = (P("lat", "lon", None), P("lat", "lon", None), P(), P())
    out_specs = (P("lat", "lon", None), P("lat", "lon", None), P(), P())
    return jax.shard_map(shards, mesh=mesh, in_specs=in_specs, out_specs=out_specs, check_vma=False)
```

```python
import functools
import math

import jax
import jax.numpy as jnp
import ml_dtypes
import numpy as np
from jax import lax
from jax.experimental import pallas as pl
from jax.experimental.pallas import tpu as pltpu
from jax.sharding import PartitionSpec as P

NB = 8
BS = 96
KWD = 1
RQ = 4
PACK = RQ * BS
WIDE = 2 * BS
STATE = -(-WIDE // 128) * 128
MIB = 1024 * 1024

shrink_level = 0.01
gelu_coeff = 0.7978845608028654


def wave_table(first, second, length):
    product = (first[:, None] * second[None, :]) % length
    angle = np.float32(2.0 * math.pi / length) * product.astype(np.float32)
    scale = np.float32(math.sqrt(length))
    rounded = ml_dtypes.bfloat16
    cos = (np.cos(angle) / scale).astype(rounded).astype(np.float32)
    sin = (np.sin(angle) / scale).astype(rounded).astype(np.float32)
    return cos, sin


def lon_tables(kept, cols, lon_count, rows):
    cos, sin = wave_table(np.arange(kept), np.arange(cols), cols)
    parts = np.stack([cos, -sin], axis=1).reshape(kept, 2, lon_count, cols // lon_count)
    eye = np.eye(rows, dtype=np.float32)
    forward = np.einsum("kpgw,rs->kprgsw", parts, eye).reshape(2 * kept * rows, -1)
    return forward, forward.T


def lat_table(rows, lat_count, subs, rows_sub, rows_cut, pack_modes):
    cos, sin = wave_table(np.arange(rows), np.arange(rows), rows)
    forward = np.stack([np.stack([cos, sin], axis=1), np.stack([-sin, cos], axis=1)])
    split = forward.reshape(2, rows, 2, lat_count, RQ, subs, rows_sub // rows_cut, rows_cut)
    eye = np.eye(pack_modes, dtype=np.float32)
    return np.einsum("aqplgshr,jk->jaqglskhpr", split, eye).reshape(2 * pack_modes * rows, -1)


def constant(table):
    return jnp.asarray(table.astype(ml_dtypes.bfloat16))


def kernel_call(body, out_shape, scalars, arrays, scratch=(), anchors=(), far=(), limit=8 * MIB):
    specs = {
        space: pl.BlockSpec(memory_space=space)
        for space in (pltpu.VMEM, pltpu.SMEM, pltpu.HBM, pl.ANY)
    }
    far = [pltpu.with_memory_space_constraint(value, pltpu.HBM) for value in far]
    in_specs = [specs[pltpu.SMEM]] * len(scalars) + [specs[pltpu.VMEM]] * len(arrays)
    in_specs += [specs[pltpu.HBM]] * len(far) + [specs[pl.ANY]] * len(anchors)
    is_far = [getattr(shape, "memory_space", None) is pltpu.HBM for shape in out_shape]
    return pl.pallas_call(
        body,
        out_shape=out_shape,
        in_specs=in_specs,
        out_specs=[specs[pltpu.HBM if distant else pltpu.VMEM] for distant in is_far],
        scratch_shapes=list(scratch),
        compiler_params=pltpu.CompilerParams(vmem_limit_bytes=limit),
    )(*[value.reshape(1).astype(jnp.int32) for value in scalars], *arrays, *far, *anchors)


def gate(source, anchors):
    anywhere = pl.BlockSpec(memory_space=pl.ANY)
    return pl.pallas_call(
        lambda *refs: None,
        out_shape=jax.ShapeDtypeStruct(source.shape, source.dtype),
        in_specs=[anywhere] * (1 + len(anchors)),
        out_specs=anywhere,
        input_output_aliases={0: 0},
    )(source, *anchors)


def pack_body(rows_sub, subs, own, source, *rest):
    sent, slots = rest[:-1], rest[-1]
    cols = source.shape[1]
    for sub in range(subs):
        for block in range(NB):
            pieces = []
            for group in range(RQ):
                row = (group * subs + sub) * rows_sub
                piece = source[row : row + rows_sub, :, block * BS : (block + 1) * BS]
                pieces.append(piece.reshape(rows_sub * cols, BS))
            slots[sub * NB + block] = jnp.concatenate(pieces, axis=1)
    deal(sent, slots, own[0])


def unpack_body(rows_sub, subs, own, base, *rest):
    received, (result, slots) = rest[:-2], rest[-2:]
    cols = base.shape[1]
    place(slots, received, own[0])
    for sub in range(subs):
        for group in range(RQ):
            row = (group * subs + sub) * rows_sub
            pieces = [
                slots[sub * NB + block, :, group * BS : (group + 1) * BS] for block in range(NB)
            ]
            update = jnp.concatenate(pieces, axis=1).reshape(rows_sub, cols, NB * BS)
            old = base[row : row + rows_sub]
            result[row : row + rows_sub] = (
                old.astype(jnp.float32) + update.astype(jnp.float32)
            ).astype(jnp.bfloat16)


def product(left, right):
    return jnp.dot(left, right, preferred_element_type=jnp.float32)


def product_back(left, right):
    return lax.dot_general(
        left, right, (((1,), (1,)), ((), ())), preferred_element_type=jnp.float32
    )


def product_outer(left, right):
    return lax.dot_general(
        left, right, (((0,), (0,)), ((), ())), preferred_element_type=jnp.float32
    )


def place(slots, pieces, own):
    if len(pieces) == 1:
        slots[...] = pieces[0][...]
        return
    for offset, piece in enumerate(pieces):
        slots[jnp.bitwise_xor(own, offset)] = piece[...]


def deal(pieces, slots, own):
    if len(pieces) == 1:
        pieces[0][...] = slots[...]
        return
    for offset, piece in enumerate(pieces):
        piece[...] = slots[jnp.bitwise_xor(own, offset)]


def spectra_body(count, extra, cuts, kept, own_in, own_out, table, *rest):
    received, (sent, slots_in, slots_out) = rest[:count], (rest[count + extra : -2], *rest[-2:])
    place(slots_in, received, own_in[0])
    each = slots_in.shape[1] // cuts
    parts = []
    for cut in range(cuts):
        flat = slots_in[:, cut * each : (cut + 1) * each].reshape(-1, PACK)
        parts.append(product(table[...], flat).reshape(slots_out.shape[0] * kept, -1, PACK))
    joined = jnp.stack(parts, axis=1) if cuts > 1 else parts[0]
    slots_out[...] = joined.reshape(slots_out.shape).astype(jnp.bfloat16)
    deal(sent, slots_out, own_out[0])


def columns_body(count, extra, cuts, kept, own_in, own_out, table, *rest):
    received, results, (slots_in, slots_out, sems) = (
        rest[:count],
        rest[count + extra : -3],
        rest[-3:],
    )
    place(slots_in, received, own_in[0])
    each = slots_out.shape[1] // cuts
    modes = slots_in.shape[0] * kept
    split = slots_in[...].astype(jnp.float32).reshape(modes, cuts, -1, PACK)
    flats = [split[:, cut].reshape(-1, PACK).astype(jnp.bfloat16) for cut in range(cuts)]
    copies = []
    for cut, flat in enumerate(flats):
        part = product(table[...], flat).astype(jnp.bfloat16)
        rows = pl.ds(cut * each, each)
        slots_out[:, rows] = part.reshape(slots_out.shape[0], each, PACK)
        if len(results) == 1:
            copies.append(
                pltpu.make_async_copy(slots_out.at[:, rows], results[0].at[:, rows], sems.at[cut])
            )
            copies[-1].start()
    if len(results) > 1:
        deal(results, slots_out, own_out[0])
    finish(copies)


def finish(copies):
    for copy in copies:
        copy.wait()


def load_weights(block, weights, real_imag, sems):
    copies = [
        pltpu.make_async_copy(source.at[part, block], real_imag.at[slot, part], sems.at[slot, part])
        for slot, source in enumerate(weights)
        for part in range(2)
    ]
    for copy in copies:
        copy.start()
    return copies


def complex_weights(real_imag, full):
    for slot in range(full.shape[0]):
        real, imag = real_imag[slot, 0], real_imag[slot, 1]
        full[slot, :BS] = jnp.concatenate([real, imag], axis=1)
        full[slot, BS:] = jnp.concatenate([-imag, real], axis=1)


def lat_forward(table, slots, tile, deep, rows):
    slab = slots[:, tile * deep : (tile + 1) * deep]
    flat = slab.reshape(slab.shape[0] * deep, PACK)
    stacked = jnp.concatenate(
        [flat[:, group * BS : (group + 1) * BS] for group in range(RQ)], axis=0
    )
    spectrum = product(table, stacked).astype(jnp.bfloat16)
    return [
        jnp.concatenate([spectrum[at : at + rows], spectrum[at + rows : at + 2 * rows]], axis=1)
        for at in range(0, spectrum.shape[0], 2 * rows)
    ]


def lat_inverse(table, values, slots, tile, deep):
    stacked = jnp.concatenate(
        [part for value in values for part in (value[:, :BS], value[:, BS:])], axis=0
    )
    rows = product(table, stacked).astype(jnp.bfloat16)
    each = rows.shape[0] // RQ
    packed = jnp.concatenate([rows[at : at + each] for at in range(0, RQ * each, each)], axis=1)
    slots[:, tile * deep : (tile + 1) * deep] = packed.reshape(slots.shape[0], deep, PACK)


def mode_weight(first_mode, index):
    return jnp.where(first_mode + index == 0, 1.0, 2.0).astype(jnp.float32)


def gelu(pre):
    squared = pre * pre
    tangent = jnp.tanh(gelu_coeff * (pre + 0.044715 * squared * pre))
    act = (0.5 * pre * (1.0 + tangent)).astype(jnp.bfloat16)
    return act, squared, tangent


def forward_body(members, pack_modes, member, first_mode, block, table, *rest):
    received, weights, sent = rest[:members], rest[members : members + 2], rest[members + 2 :]
    sent, rest = sent[:members], sent[members:]
    saved, anchor, slots, spec, real_imag, full, weight_sems, save_sems = rest
    anchor[...] = jnp.zeros_like(anchor)
    loads = load_weights(block[0], weights, real_imag, weight_sems)
    own = member[0]
    kept, rows, _ = spec.shape
    deep = slots.shape[1] * pack_modes // kept
    place(slots, received, own)
    lat = table[...]
    inverse = lat.T
    copies = []
    for tile in range(kept // pack_modes):
        for inner, values in enumerate(lat_forward(lat, slots, tile, deep, rows)):
            index = tile * pack_modes + inner
            spec[index, :, :WIDE] = values
            copies.append(
                pltpu.make_async_copy(spec.at[index], saved.at[index], save_sems.at[index])
            )
            copies[-1].start()
    finish(loads)
    complex_weights(real_imag, full)
    for tile in range(kept // pack_modes):
        outs = []
        for index in range(tile * pack_modes, (tile + 1) * pack_modes):
            act, _, _ = gelu(product(spec[index, :, :WIDE], full[0]))
            post = product(act, full[1])
            weight = mode_weight(first_mode[0], index)
            shrunk = post - shrink_level * jnp.tanh(post / shrink_level)
            outs.append((weight * shrunk).astype(jnp.bfloat16))
        lat_inverse(inverse, outs, slots, tile, deep)
    deal(sent, slots, own)
    finish(copies)


def backward_body(
    members, shares, pack_modes, factor, member, first_mode, lat_own, block, table, *rest
):
    received, rest = rest[:members], rest[members:]
    weights, saved, result, combined, rest = rest[:2], rest[2], rest[3], rest[4], rest[5:]
    parts, (slots, grads, cots, spec, real_imag, full, weight_sems, load_sems) = (
        rest[:shares],
        rest[shares:],
    )
    loads = load_weights(block[0], weights, real_imag, weight_sems)
    kept, rows, _ = spec.shape
    deep = slots.shape[1] * pack_modes // kept
    spec_loads = [
        pltpu.make_async_copy(saved.at[index], spec.at[index], load_sems.at[index])
        for index in range(kept)
    ]
    for copy in spec_loads:
        copy.start()
    place(slots, received, member[0])
    lat = table[...]
    for tile in range(kept // pack_modes):
        for inner, cot in enumerate(lat_forward(lat, slots, tile, deep, rows)):
            cots[tile * pack_modes + inner] = cot
    finish(loads)
    complex_weights(real_imag, full)
    combined[...] = full[0]
    total_first = jnp.zeros((WIDE, WIDE), jnp.float32)
    total_second = jnp.zeros((WIDE, WIDE), jnp.float32)
    for index in range(kept):
        spec_loads[index].wait()
        values = spec[index, :, :WIDE]
        pre = product(values, full[0])
        act, squared, tangent = gelu(pre)
        slope = 0.5 * (1.0 + tangent) + 0.5 * pre * (1.0 - tangent * tangent) * gelu_coeff * (
            1.0 + 3.0 * 0.044715 * squared
        )
        ratio = jnp.tanh(product(act, full[1]) / shrink_level)
        weight = mode_weight(first_mode[0], index)
        cot = cots[index].astype(jnp.float32)
        grad_post = (weight * cot * (ratio * ratio)).astype(jnp.bfloat16)
        grad_pre = (product_back(grad_post, full[1]) * slope).astype(jnp.bfloat16)
        result[index] = grad_pre
        total_second += product_outer(act, grad_post)
        total_first += product_outer(values, grad_pre)
    share = grads.shape[1]
    for slot, total in enumerate((total_first, total_second)):
        real = (total[:BS, :BS] + total[BS:, BS:]) * factor
        imag = (total[:BS, BS:] - total[BS:, :BS]) * factor
        for part, value in enumerate((real, imag)):
            for at in range(0, BS, share):
                piece = ((2 * slot + part) * BS + at) // share
                grads[piece] = value[at : at + share].astype(jnp.bfloat16)
    deal(parts, grads, lat_own[0])


def input_grad_body(pack_modes, member, table, grad_pre, combined, *rest):
    sent, slots = rest[:-1], rest[-1]
    kept = grad_pre.shape[0]
    deep = slots.shape[1] * pack_modes // kept
    inverse = table[...].T
    for tile in range(kept // pack_modes):
        backs = [
            product_back(grad_pre[index], combined[...]).astype(jnp.bfloat16)
            for index in range(tile * pack_modes, (tile + 1) * pack_modes)
        ]
        lat_inverse(inverse, backs, slots, tile, deep)
    deal(sent, slots, member[0])


def sum_body(*refs):
    refs[-1][...] = sum(value[...].astype(jnp.float32) for value in refs[:-1]).astype(jnp.bfloat16)


def stack_body(*refs):
    for slot, piece in enumerate(refs[:-1]):
        refs[-1][slot] = piece[...]


def blocks_body(own, near, other, blocks):
    for slot in range(near.shape[0]):
        blocks[jnp.bitwise_xor(own[0], 2 * slot)] = near[slot]
        blocks[jnp.bitwise_xor(own[0], 2 * slot + 1)] = other[slot]


def assemble_body(lat_count, subs, lat_own, *rest):
    gathered, (first, second, slots) = rest[:lat_count], rest[lat_count:]
    rows = gathered[0].shape[1]
    for offset, pieces in enumerate(gathered):
        start = jnp.bitwise_xor(lat_own[0], offset) * rows
        matrix, row = start // BS, pl.multiple_of(start % BS, 16)
        for block in range(NB):
            total = None
            for sub in range(subs):
                value = pieces[sub * NB + block].astype(jnp.float32)
                total = value if total is None else total + value
            slots[matrix, block, pl.ds(row, rows)] = total
    first[...] = slots[:2]
    second[...] = slots[2:]


def exchange(source):
    return lax.all_to_all(source, "lon", split_axis=0, concat_axis=0, tiled=True)


def swap(pieces, axes, partners):
    return [pieces[0]] + [
        lax.ppermute(piece, axes, partners(offset))
        for offset, piece in enumerate(pieces)
        if offset
    ]


def shards(features, cotangent, weight_first, weight_second):
    lat_count = lax.axis_size("lat")
    lon_count = lax.axis_size("lon")
    band_rows, band_cols, channels = features.shape
    rows_total = band_rows * lat_count
    cols_total = band_cols * lon_count
    kept_total = KWD * lat_count * lon_count
    subs = lon_count // NB
    members = lat_count * subs
    rows_sub = band_rows // (RQ * subs)
    rows_cut = min(rows_sub, 4)
    cuts = rows_sub // rows_cut
    kept = kept_total // members
    deep = 2 * rows_sub
    pack_modes = max(1, 16 // deep)
    lat_index = lax.axis_index("lat")
    lon_index = lax.axis_index("lon")
    block = lon_index % NB
    member = lat_index * subs + lon_index // NB
    bf16, f32 = jnp.bfloat16, jnp.float32
    array = jax.ShapeDtypeStruct

    def member_pairs(offset):
        pairs = []
        for lat in range(lat_count):
            for lon in range(lon_count):
                other = (lat * subs + lon // NB) ^ offset
                lon_other = other % subs * NB + lon % NB
                pairs.append((lat * lon_count + lon, other // subs * lon_count + lon_other))
        return pairs

    def line_pairs(count):
        return lambda offset: [(place, place ^ offset) for place in range(count)]

    lon_fwd, lon_inv = map(constant, lon_tables(kept_total, cols_total, lon_count, rows_cut))
    lat_both = constant(lat_table(rows_total, lat_count, subs, rows_sub, rows_cut, pack_modes))
    lon_piece = array((rows_sub * band_cols, PACK), bf16)
    lon_whole = array((lon_count, rows_sub * band_cols, PACK), bf16)
    mid_piece = array((kept * deep, PACK), bf16)
    lon_slots = pltpu.VMEM(lon_whole.shape, bf16)
    mid_slots = pltpu.VMEM((members, kept * deep, PACK), bf16)
    mid_limit = 14 * MIB + 5 * lat_both.size
    share = 4 * BS // lat_count

    def mid_swap(pieces):
        return swap(pieces, ("lat", "lon"), member_pairs)

    def pack(source, sent):
        body = functools.partial(pack_body, rows_sub, subs)
        return kernel_call(body, sent, [lon_index], [source], [lon_slots])

    def unpack(pieces, base):
        body = functools.partial(unpack_body, rows_sub, subs)
        result = array(base.shape, bf16)
        return kernel_call(body, [result], [lon_index], [base, *pieces], [lon_slots])[0]

    def to_spectra(pieces, anchors=()):
        return kernel_call(
            functools.partial(spectra_body, len(pieces), len(anchors), cuts, kept),
            [mid_piece] * members,
            [lon_index, member],
            [lon_fwd, *pieces],
            [lon_slots, mid_slots],
            anchors,
        )

    def to_columns(pieces, sent, anchors=()):
        return kernel_call(
            functools.partial(columns_body, members, len(anchors), cuts, kept),
            sent,
            [member, lon_index],
            [lon_inv, *pieces],
            [mid_slots, lon_slots, pltpu.SemaphoreType.DMA((cuts,))],
            anchors,
        )

    modes = (kept, rows_total, STATE)
    weights = [weight_first, weight_second]
    mid_scratch = [
        pltpu.VMEM(modes, bf16),
        pltpu.VMEM((2, 2, BS, BS), bf16),
        pltpu.VMEM((2, WIDE, WIDE), bf16),
        pltpu.SemaphoreType.DMA((2, 2)),
        pltpu.SemaphoreType.DMA((kept,)),
    ]

    field = swap(pack(features, [lon_piece] * lon_count), "lon", line_pairs(lon_count))
    field_cot = exchange(gate(pack(cotangent, [lon_whole])[0], field))
    results = kernel_call(
        functools.partial(forward_body, members, pack_modes),
        [mid_piece] * members + [pltpu.HBM(modes, bf16), array((8, 128), f32)],
        [member, member * kept, block],
        [lat_both, *mid_swap(to_spectra(field))],
        [mid_slots, *mid_scratch],
        far=weights,
        limit=mid_limit,
    )
    saved, anchor = results[members:]
    spectra_cot = to_spectra([field_cot], [anchor])
    columns = to_columns(
        mid_swap(results[:members]), [pltpu.HBM(lon_whole.shape, bf16)], spectra_cot[:1]
    )
    filtered = exchange(columns[0])
    wide = (kept, rows_total, WIDE)
    grad_pre, combined, *parts = kernel_call(
        functools.partial(
            backward_body, members, lat_count, pack_modes, 1.0 / math.sqrt(rows_total * kept_total)
        ),
        [array(wide, bf16), array((WIDE, WIDE), bf16)] + [array((share, BS), bf16)] * lat_count,
        [member, member * kept, lat_index, block],
        [lat_both, *mid_swap(spectra_cot)],
        [
            mid_slots,
            pltpu.VMEM((lat_count, share, BS), bf16),
            pltpu.VMEM(wide, bf16),
            *mid_scratch,
        ],
        far=weights + [saved],
        limit=mid_limit,
    )
    own_share = kernel_call(
        sum_body, [array((share, BS), bf16)], [], swap(parts, "lat", line_pairs(lat_count))
    )[0]
    back = kernel_call(
        functools.partial(input_grad_body, pack_modes),
        [mid_piece] * members,
        [member],
        [lat_both, grad_pre, combined],
        [mid_slots],
        limit=mid_limit,
    )
    lon_pairs = line_pairs(lon_count)
    near = kernel_call(
        stack_body,
        [array((lon_count // 2, share, BS), bf16)],
        [],
        [own_share]
        + [lax.ppermute(own_share, "lon", lon_pairs(far)) for far in range(2, lon_count, 2)],
    )[0]
    returned = swap(to_columns(mid_swap(back), [lon_piece] * lon_count), "lon", lon_pairs)
    blocks = kernel_call(
        blocks_body,
        [array((lon_count, share, BS), bf16)],
        [lon_index],
        [near, lax.ppermute(near, "lon", lon_pairs(1))],
    )[0]

    gathered = {0: blocks}
    step = lat_count // 2
    while step:
        for offset in sorted(gathered):
            moved = lax.ppermute(gathered[offset], "lat", line_pairs(lat_count)(step))
            gathered[offset | step] = moved
        step //= 2
    gathered = [gathered[offset] for offset in range(lat_count)]
    full = array((2, NB, BS, BS), f32)
    grad_first, grad_second = kernel_call(
        functools.partial(assemble_body, lat_count, subs),
        [full, full],
        [lat_index],
        gathered,
        [pltpu.VMEM((4, NB, BS, BS), f32)],
    )
    return (unpack([filtered], features), unpack(returned, cotangent), grad_first, grad_second)


def solution(mesh):
    in_specs = (P("lat", "lon", None), P("lat", "lon", None), P(), P())
    out_specs = (P("lat", "lon", None), P("lat", "lon", None), P(), P())
    return jax.shard_map(shards, mesh=mesh, in_specs=in_specs, out_specs=out_specs, check_vma=False)
```

```python
import functools
import math

import jax
import jax.numpy as jnp
import ml_dtypes
import numpy as np
from jax import lax
from jax.experimental import pallas as pl
from jax.experimental.pallas import tpu as pltpu
from jax.sharding import PartitionSpec as P

NB = 8
BS = 96
KWD = 1
RQ = 4
PACK = RQ * BS
WIDE = 2 * BS
STATE = -(-WIDE // 128) * 128
MIB = 1024 * 1024

shrink_level = 0.01
gelu_coeff = 0.7978845608028654


def wave_table(first, second, length):
    product = (first[:, None] * second[None, :]) % length
    angle = np.float32(2.0 * math.pi / length) * product.astype(np.float32)
    scale = np.float32(math.sqrt(length))
    rounded = ml_dtypes.bfloat16
    cos = (np.cos(angle) / scale).astype(rounded).astype(np.float32)
    sin = (np.sin(angle) / scale).astype(rounded).astype(np.float32)
    return cos, sin


def lon_tables(kept, cols, lon_count, rows):
    cos, sin = wave_table(np.arange(kept), np.arange(cols), cols)
    parts = np.stack([cos, -sin], axis=1).reshape(kept, 2, lon_count, cols // lon_count)
    eye = np.eye(rows, dtype=np.float32)
    forward = np.einsum("kpgw,rs->kprgsw", parts, eye).reshape(2 * kept * rows, -1)
    return forward, forward.T


def lat_table(rows, lat_count, subs, rows_sub, rows_cut, pack_modes):
    cos, sin = wave_table(np.arange(rows), np.arange(rows), rows)
    forward = np.stack([np.stack([cos, sin], axis=1), np.stack([-sin, cos], axis=1)])
    split = forward.reshape(2, rows, 2, lat_count, RQ, subs, rows_sub // rows_cut, rows_cut)
    eye = np.eye(pack_modes, dtype=np.float32)
    return np.einsum("aqplgshr,jk->jaqglskhpr", split, eye).reshape(2 * pack_modes * rows, -1)


def constant(table):
    return jnp.asarray(table.astype(ml_dtypes.bfloat16))


def kernel_call(body, out_shape, scalars, arrays, scratch=(), anchors=(), far=(), limit=8 * MIB):
    specs = {
        space: pl.BlockSpec(memory_space=space)
        for space in (pltpu.VMEM, pltpu.SMEM, pltpu.HBM, pl.ANY)
    }
    far = [pltpu.with_memory_space_constraint(value, pltpu.HBM) for value in far]
    in_specs = [specs[pltpu.SMEM]] * len(scalars) + [specs[pltpu.VMEM]] * len(arrays)
    in_specs += [specs[pltpu.HBM]] * len(far) + [specs[pl.ANY]] * len(anchors)
    is_far = [getattr(shape, "memory_space", None) is pltpu.HBM for shape in out_shape]
    return pl.pallas_call(
        body,
        out_shape=out_shape,
        in_specs=in_specs,
        out_specs=[specs[pltpu.HBM if distant else pltpu.VMEM] for distant in is_far],
        scratch_shapes=list(scratch),
        compiler_params=pltpu.CompilerParams(vmem_limit_bytes=limit),
    )(*[value.reshape(1).astype(jnp.int32) for value in scalars], *arrays, *far, *anchors)


def gate(source, anchors):
    anywhere = pl.BlockSpec(memory_space=pl.ANY)
    return pl.pallas_call(
        lambda *refs: None,
        out_shape=jax.ShapeDtypeStruct(source.shape, source.dtype),
        in_specs=[anywhere] * (1 + len(anchors)),
        out_specs=anywhere,
        input_output_aliases={0: 0},
    )(source, *anchors)


def pack_body(rows_sub, subs, own, source, *rest):
    sent, slots = rest[:-1], rest[-1]
    cols = source.shape[1]
    for sub in range(subs):
        for block in range(NB):
            pieces = []
            for group in range(RQ):
                row = (group * subs + sub) * rows_sub
                piece = source[row : row + rows_sub, :, block * BS : (block + 1) * BS]
                pieces.append(piece.reshape(rows_sub * cols, BS))
            slots[sub * NB + block] = jnp.concatenate(pieces, axis=1)
    deal(sent, slots, own[0])


def unpack_body(rows_sub, subs, extra, own, base, *rest):
    received, (result, slots) = rest[: len(rest) - 2 - extra], rest[-2:]
    cols = base.shape[1]
    place(slots, received, own[0])
    for sub in range(subs):
        for group in range(RQ):
            row = (group * subs + sub) * rows_sub
            pieces = [
                slots[sub * NB + block, :, group * BS : (group + 1) * BS] for block in range(NB)
            ]
            update = jnp.concatenate(pieces, axis=1).reshape(rows_sub, cols, NB * BS)
            old = base[row : row + rows_sub]
            result[row : row + rows_sub] = (
                old.astype(jnp.float32) + update.astype(jnp.float32)
            ).astype(jnp.bfloat16)


def product(left, right):
    return jnp.dot(left, right, preferred_element_type=jnp.float32)


def product_back(left, right):
    return lax.dot_general(
        left, right, (((1,), (1,)), ((), ())), preferred_element_type=jnp.float32
    )


def product_outer(left, right):
    return lax.dot_general(
        left, right, (((0,), (0,)), ((), ())), preferred_element_type=jnp.float32
    )


def place(slots, pieces, own):
    if len(pieces) == 1:
        slots[...] = pieces[0][...]
        return
    for offset, piece in enumerate(pieces):
        slots[jnp.bitwise_xor(own, offset)] = piece[...]


def deal(pieces, slots, own):
    if len(pieces) == 1:
        pieces[0][...] = slots[...]
        return
    for offset, piece in enumerate(pieces):
        piece[...] = slots[jnp.bitwise_xor(own, offset)]


def spectra_body(count, extra, cuts, kept, own_in, own_out, table, *rest):
    received, (sent, slots_in, slots_out) = rest[:count], (rest[count + extra : -2], *rest[-2:])
    place(slots_in, received, own_in[0])
    each = slots_in.shape[1] // cuts
    parts = []
    for cut in range(cuts):
        flat = slots_in[:, cut * each : (cut + 1) * each].reshape(-1, PACK)
        parts.append(product(table[...], flat).reshape(slots_out.shape[0] * kept, -1, PACK))
    joined = jnp.stack(parts, axis=1) if cuts > 1 else parts[0]
    slots_out[...] = joined.reshape(slots_out.shape).astype(jnp.bfloat16)
    deal(sent, slots_out, own_out[0])


def columns_body(count, extra, cuts, kept, own_in, own_out, table, *rest):
    received, results, (slots_in, slots_out, sems) = (
        rest[:count],
        rest[count + extra : -3],
        rest[-3:],
    )
    place(slots_in, received, own_in[0])
    each = slots_out.shape[1] // cuts
    modes = slots_in.shape[0] * kept
    split = slots_in[...].astype(jnp.float32).reshape(modes, cuts, -1, PACK)
    flats = [split[:, cut].reshape(-1, PACK).astype(jnp.bfloat16) for cut in range(cuts)]
    copies = []
    for cut, flat in enumerate(flats):
        part = product(table[...], flat).astype(jnp.bfloat16)
        rows = pl.ds(cut * each, each)
        slots_out[:, rows] = part.reshape(slots_out.shape[0], each, PACK)
        if len(results) == 1:
            copies.append(
                pltpu.make_async_copy(slots_out.at[:, rows], results[0].at[:, rows], sems.at[cut])
            )
            copies[-1].start()
    if len(results) > 1:
        deal(results, slots_out, own_out[0])
    finish(copies)


def finish(copies):
    for copy in copies:
        copy.wait()


def load_weights(block, weights, real_imag, sems):
    copies = [
        pltpu.make_async_copy(source.at[part, block], real_imag.at[slot, part], sems.at[slot, part])
        for slot, source in enumerate(weights)
        for part in range(2)
    ]
    for copy in copies:
        copy.start()
    return copies


def complex_weights(real_imag, full):
    for slot in range(full.shape[0]):
        real, imag = real_imag[slot, 0], real_imag[slot, 1]
        full[slot, :BS] = jnp.concatenate([real, imag], axis=1)
        full[slot, BS:] = jnp.concatenate([-imag, real], axis=1)


def lat_forward(table, slots, tile, deep, rows):
    slab = slots[:, tile * deep : (tile + 1) * deep]
    flat = slab.reshape(slab.shape[0] * deep, PACK)
    stacked = jnp.concatenate(
        [flat[:, group * BS : (group + 1) * BS] for group in range(RQ)], axis=0
    )
    spectrum = product(table, stacked).astype(jnp.bfloat16)
    return [
        jnp.concatenate([spectrum[at : at + rows], spectrum[at + rows : at + 2 * rows]], axis=1)
        for at in range(0, spectrum.shape[0], 2 * rows)
    ]


def lat_inverse(table, values, slots, tile, deep):
    stacked = jnp.concatenate(
        [part for value in values for part in (value[:, :BS], value[:, BS:])], axis=0
    )
    rows = product(table, stacked).astype(jnp.bfloat16)
    each = rows.shape[0] // RQ
    packed = jnp.concatenate([rows[at : at + each] for at in range(0, RQ * each, each)], axis=1)
    slots[:, tile * deep : (tile + 1) * deep] = packed.reshape(slots.shape[0], deep, PACK)


def mode_weight(first_mode, index):
    return jnp.where(first_mode + index == 0, 1.0, 2.0).astype(jnp.float32)


def gelu(pre):
    squared = pre * pre
    tangent = jnp.tanh(gelu_coeff * (pre + 0.044715 * squared * pre))
    act = (0.5 * pre * (1.0 + tangent)).astype(jnp.bfloat16)
    return act, squared, tangent


def forward_body(members, pack_modes, member, first_mode, block, table, *rest):
    received, weights, sent = rest[:members], rest[members : members + 2], rest[members + 2 :]
    sent, rest = sent[:members], sent[members:]
    saved, anchor, slots, spec, real_imag, full, weight_sems, save_sems = rest
    anchor[...] = jnp.zeros_like(anchor)
    loads = load_weights(block[0], weights, real_imag, weight_sems)
    own = member[0]
    kept, rows, _ = spec.shape
    deep = slots.shape[1] * pack_modes // kept
    place(slots, received, own)
    lat = table[...]
    inverse = lat.T
    copies = []
    for tile in range(kept // pack_modes):
        for inner, values in enumerate(lat_forward(lat, slots, tile, deep, rows)):
            index = tile * pack_modes + inner
            spec[index, :, :WIDE] = values
            copies.append(
                pltpu.make_async_copy(spec.at[index], saved.at[index], save_sems.at[index])
            )
            copies[-1].start()
    finish(loads)
    complex_weights(real_imag, full)
    for tile in range(kept // pack_modes):
        outs = []
        for index in range(tile * pack_modes, (tile + 1) * pack_modes):
            act, _, _ = gelu(product(spec[index, :, :WIDE], full[0]))
            post = product(act, full[1])
            weight = mode_weight(first_mode[0], index)
            shrunk = post - shrink_level * jnp.tanh(post / shrink_level)
            outs.append((weight * shrunk).astype(jnp.bfloat16))
        lat_inverse(inverse, outs, slots, tile, deep)
    deal(sent, slots, own)
    finish(copies)


def backward_body(members, pack_modes, factor, member, first_mode, block, table, *rest):
    received, rest = rest[:members], rest[members:]
    weights, saved, (result, combined, grads) = rest[:2], rest[2], rest[3:6]
    slots, cots, spec, real_imag, full, weight_sems, load_sems = rest[6:]
    loads = load_weights(block[0], weights, real_imag, weight_sems)
    kept, rows, _ = spec.shape
    deep = slots.shape[1] * pack_modes // kept
    spec_loads = [
        pltpu.make_async_copy(saved.at[index], spec.at[index], load_sems.at[index])
        for index in range(kept)
    ]
    for copy in spec_loads:
        copy.start()
    place(slots, received, member[0])
    lat = table[...]
    for tile in range(kept // pack_modes):
        for inner, cot in enumerate(lat_forward(lat, slots, tile, deep, rows)):
            cots[tile * pack_modes + inner] = cot
    finish(loads)
    complex_weights(real_imag, full)
    combined[...] = full[0]
    total_first = jnp.zeros((WIDE, WIDE), jnp.float32)
    total_second = jnp.zeros((WIDE, WIDE), jnp.float32)
    for index in range(kept):
        spec_loads[index].wait()
        values = spec[index, :, :WIDE]
        pre = product(values, full[0])
        act, squared, tangent = gelu(pre)
        slope = 0.5 * (1.0 + tangent) + 0.5 * pre * (1.0 - tangent * tangent) * gelu_coeff * (
            1.0 + 3.0 * 0.044715 * squared
        )
        ratio = jnp.tanh(product(act, full[1]) / shrink_level)
        weight = mode_weight(first_mode[0], index)
        cot = cots[index].astype(jnp.float32)
        grad_post = (weight * cot * (ratio * ratio)).astype(jnp.bfloat16)
        grad_pre = (product_back(grad_post, full[1]) * slope).astype(jnp.bfloat16)
        result[index] = grad_pre
        total_second += product_outer(act, grad_post)
        total_first += product_outer(values, grad_pre)
    share = grads.shape[1]
    for slot, total in enumerate((total_first, total_second)):
        real = (total[:BS, :BS] + total[BS:, BS:]) * factor
        imag = (total[:BS, BS:] - total[BS:, :BS]) * factor
        for part, value in enumerate((real, imag)):
            for at in range(0, BS, share):
                piece = ((2 * slot + part) * BS + at) // share
                grads[piece] = value[at : at + share].astype(jnp.bfloat16)


def input_grad_body(members, pack_modes, member, lat_own, table, grad_pre, combined, grads, *rest):
    sent, parts, slots = rest[:members], rest[members:-1], rest[-1]
    deal(parts, grads, lat_own[0])
    kept = grad_pre.shape[0]
    deep = slots.shape[1] * pack_modes // kept
    inverse = table[...].T
    for tile in range(kept // pack_modes):
        backs = [
            product_back(grad_pre[index], combined[...]).astype(jnp.bfloat16)
            for index in range(tile * pack_modes, (tile + 1) * pack_modes)
        ]
        lat_inverse(inverse, backs, slots, tile, deep)
    deal(sent, slots, member[0])


def sum_body(count, *refs):
    total = sum(value[...].astype(jnp.float32) for value in refs[:count])
    refs[-1][...] = total.astype(jnp.bfloat16)


def stack_body(*refs):
    for slot, piece in enumerate(refs[:-1]):
        refs[-1][slot] = piece[...]


def blocks_body(own, near, other, blocks):
    for slot in range(near.shape[0]):
        blocks[jnp.bitwise_xor(own[0], 2 * slot)] = near[slot]
        blocks[jnp.bitwise_xor(own[0], 2 * slot + 1)] = other[slot]


def assemble_body(lat_count, subs, lat_own, *rest):
    gathered, (first, second, slots) = rest[:lat_count], rest[lat_count:]
    rows = gathered[0].shape[1]
    for offset, pieces in enumerate(gathered):
        start = jnp.bitwise_xor(lat_own[0], offset) * rows
        matrix, row = start // BS, pl.multiple_of(start % BS, 16)
        for block in range(NB):
            total = None
            for sub in range(subs):
                value = pieces[sub * NB + block].astype(jnp.float32)
                total = value if total is None else total + value
            slots[matrix, block, pl.ds(row, rows)] = total
    first[...] = slots[:2]
    second[...] = slots[2:]


def exchange(source):
    return lax.all_to_all(source, "lon", split_axis=0, concat_axis=0, tiled=True)


def swap(pieces, axes, partners):
    return [pieces[0]] + [
        lax.ppermute(piece, axes, partners(offset))
        for offset, piece in enumerate(pieces)
        if offset
    ]


def shards(features, cotangent, weight_first, weight_second):
    lat_count = lax.axis_size("lat")
    lon_count = lax.axis_size("lon")
    band_rows, band_cols, channels = features.shape
    rows_total = band_rows * lat_count
    cols_total = band_cols * lon_count
    kept_total = KWD * lat_count * lon_count
    subs = lon_count // NB
    members = lat_count * subs
    rows_sub = band_rows // (RQ * subs)
    rows_cut = min(rows_sub, 4)
    cuts = rows_sub // rows_cut
    kept = kept_total // members
    deep = 2 * rows_sub
    pack_modes = max(1, 16 // deep)
    lat_index = lax.axis_index("lat")
    lon_index = lax.axis_index("lon")
    block = lon_index % NB
    member = lat_index * subs + lon_index // NB
    bf16, f32 = jnp.bfloat16, jnp.float32
    array = jax.ShapeDtypeStruct

    def member_pairs(offset):
        pairs = []
        for lat in range(lat_count):
            for lon in range(lon_count):
                other = (lat * subs + lon // NB) ^ offset
                lon_other = other % subs * NB + lon % NB
                pairs.append((lat * lon_count + lon, other // subs * lon_count + lon_other))
        return pairs

    def line_pairs(count):
        return lambda offset: [(place, place ^ offset) for place in range(count)]

    lon_fwd, lon_inv = map(constant, lon_tables(kept_total, cols_total, lon_count, rows_cut))
    lat_both = constant(lat_table(rows_total, lat_count, subs, rows_sub, rows_cut, pack_modes))
    lon_piece = array((rows_sub * band_cols, PACK), bf16)
    lon_whole = array((lon_count, rows_sub * band_cols, PACK), bf16)
    mid_piece = array((kept * deep, PACK), bf16)
    lon_slots = pltpu.VMEM(lon_whole.shape, bf16)
    mid_slots = pltpu.VMEM((members, kept * deep, PACK), bf16)
    mid_limit = 14 * MIB + 5 * lat_both.size
    share = 4 * BS // lat_count

    def mid_swap(pieces):
        return swap(pieces, ("lat", "lon"), member_pairs)

    def pack(source, sent):
        body = functools.partial(pack_body, rows_sub, subs)
        return kernel_call(body, sent, [lon_index], [source], [lon_slots])

    def unpack(pieces, base, anchors=()):
        body = functools.partial(unpack_body, rows_sub, subs, len(anchors))
        result = array(base.shape, bf16)
        return kernel_call(body, [result], [lon_index], [base, *pieces], [lon_slots], anchors)[0]

    def to_spectra(pieces, anchors=()):
        return kernel_call(
            functools.partial(spectra_body, len(pieces), len(anchors), cuts, kept),
            [mid_piece] * members,
            [lon_index, member],
            [lon_fwd, *pieces],
            [lon_slots, mid_slots],
            anchors,
        )

    def to_columns(pieces, sent, anchors=()):
        return kernel_call(
            functools.partial(columns_body, members, len(anchors), cuts, kept),
            sent,
            [member, lon_index],
            [lon_inv, *pieces],
            [mid_slots, lon_slots, pltpu.SemaphoreType.DMA((cuts,))],
            anchors,
        )

    modes = (kept, rows_total, STATE)
    weights = [weight_first, weight_second]
    mid_scratch = [
        pltpu.VMEM(modes, bf16),
        pltpu.VMEM((2, 2, BS, BS), bf16),
        pltpu.VMEM((2, WIDE, WIDE), bf16),
        pltpu.SemaphoreType.DMA((2, 2)),
        pltpu.SemaphoreType.DMA((kept,)),
    ]

    field = swap(pack(features, [lon_piece] * lon_count), "lon", line_pairs(lon_count))
    field_cot = exchange(gate(pack(cotangent, [lon_whole])[0], field))
    results = kernel_call(
        functools.partial(forward_body, members, pack_modes),
        [mid_piece] * members + [pltpu.HBM(modes, bf16), array((8, 128), f32)],
        [member, member * kept, block],
        [lat_both, *mid_swap(to_spectra(field))],
        [mid_slots, *mid_scratch],
        far=weights,
        limit=mid_limit,
    )
    saved, anchor = results[members:]
    spectra_cot = to_spectra([field_cot], [anchor])
    columns = to_columns(
        mid_swap(results[:members]), [pltpu.HBM(lon_whole.shape, bf16)], spectra_cot[:1]
    )
    filtered = exchange(columns[0])
    wide = (kept, rows_total, WIDE)
    grad_pre, combined, grads = kernel_call(
        functools.partial(
            backward_body, members, pack_modes, 1.0 / math.sqrt(rows_total * kept_total)
        ),
        [array(wide, bf16), array((WIDE, WIDE), bf16), array((lat_count, share, BS), bf16)],
        [member, member * kept, block],
        [lat_both, *mid_swap(spectra_cot)],
        [mid_slots, pltpu.VMEM(wide, bf16), *mid_scratch],
        far=weights + [saved],
        limit=mid_limit,
    )
    back = kernel_call(
        functools.partial(input_grad_body, members, pack_modes),
        [mid_piece] * members + [array((share, BS), bf16)] * lat_count,
        [member, lat_index],
        [lat_both, grad_pre, combined, grads],
        [mid_slots],
        limit=mid_limit,
    )
    lon_pairs = line_pairs(lon_count)
    columns = to_columns(mid_swap(back[:members]), [lon_piece] * lon_count)
    returned = swap(columns, "lon", lon_pairs)
    own_share = kernel_call(
        functools.partial(sum_body, lat_count),
        [array((share, BS), bf16)],
        [],
        swap(back[members:], "lat", line_pairs(lat_count)),
        anchors=columns[:1],
    )[0]
    near = kernel_call(
        stack_body,
        [array((lon_count // 2, share, BS), bf16)],
        [],
        [own_share]
        + [lax.ppermute(own_share, "lon", lon_pairs(far)) for far in range(2, lon_count, 2)],
    )[0]
    blocks = kernel_call(
        blocks_body,
        [array((lon_count, share, BS), bf16)],
        [lon_index],
        [near, lax.ppermute(near, "lon", lon_pairs(1))],
    )[0]

    gathered = {0: blocks}
    step = lat_count // 2
    while step:
        for offset in sorted(gathered):
            moved = lax.ppermute(gathered[offset], "lat", line_pairs(lat_count)(step))
            gathered[offset | step] = moved
        step //= 2
    gathered = [gathered[offset] for offset in range(lat_count)]
    full = array((2, NB, BS, BS), f32)
    grad_first, grad_second = kernel_call(
        functools.partial(assemble_body, lat_count, subs),
        [full, full],
        [lat_index],
        gathered,
        [pltpu.VMEM((4, NB, BS, BS), f32)],
    )
    mixed_field = unpack([filtered], features)
    feature_grad = unpack(returned, cotangent, [mixed_field])
    return (mixed_field, feature_grad, grad_first, grad_second)


def solution(mesh):
    in_specs = (P("lat", "lon", None), P("lat", "lon", None), P(), P())
    out_specs = (P("lat", "lon", None), P("lat", "lon", None), P(), P())
    return jax.shard_map(shards, mesh=mesh, in_specs=in_specs, out_specs=out_specs, check_vma=False)
```

```python
import functools
import math

import jax
import jax.numpy as jnp
import ml_dtypes
import numpy as np
from jax import lax
from jax.experimental import pallas as pl
from jax.experimental.pallas import tpu as pltpu
from jax.sharding import PartitionSpec as P

NB = 8
BS = 96
KWD = 1
RQ = 4
PACK = RQ * BS
WIDE = 2 * BS
STATE = -(-WIDE // 128) * 128
MIB = 1024 * 1024

shrink_level = 0.01
gelu_coeff = 0.7978845608028654


def wave_table(first, second, length):
    product = (first[:, None] * second[None, :]) % length
    angle = np.float32(2.0 * math.pi / length) * product.astype(np.float32)
    scale = np.float32(math.sqrt(length))
    rounded = ml_dtypes.bfloat16
    cos = (np.cos(angle) / scale).astype(rounded).astype(np.float32)
    sin = (np.sin(angle) / scale).astype(rounded).astype(np.float32)
    return cos, sin


def lon_tables(kept, cols, lon_count, rows):
    cos, sin = wave_table(np.arange(kept), np.arange(cols), cols)
    parts = np.stack([cos, -sin], axis=1).reshape(kept, 2, lon_count, cols // lon_count)
    eye = np.eye(rows, dtype=np.float32)
    forward = np.einsum("kpgw,rs->kprgsw", parts, eye).reshape(2 * kept * rows, -1)
    return forward, forward.T


def lat_table(rows, lat_count, subs, rows_sub, rows_cut, pack_modes):
    cos, sin = wave_table(np.arange(rows), np.arange(rows), rows)
    forward = np.stack([np.stack([cos, sin], axis=1), np.stack([-sin, cos], axis=1)])
    split = forward.reshape(2, rows, 2, lat_count, RQ, subs, rows_sub // rows_cut, rows_cut)
    eye = np.eye(pack_modes, dtype=np.float32)
    return np.einsum("aqplgshr,jk->jaqglskhpr", split, eye).reshape(2 * pack_modes * rows, -1)


def constant(table):
    return jnp.asarray(table.astype(ml_dtypes.bfloat16))


def kernel_call(body, out_shape, scalars, arrays, scratch=(), anchors=(), far=(), limit=8 * MIB):
    specs = {
        space: pl.BlockSpec(memory_space=space)
        for space in (pltpu.VMEM, pltpu.SMEM, pltpu.HBM, pl.ANY)
    }
    far = [pltpu.with_memory_space_constraint(value, pltpu.HBM) for value in far]
    in_specs = [specs[pltpu.SMEM]] * len(scalars) + [specs[pltpu.VMEM]] * len(arrays)
    in_specs += [specs[pltpu.HBM]] * len(far) + [specs[pl.ANY]] * len(anchors)
    is_far = [getattr(shape, "memory_space", None) is pltpu.HBM for shape in out_shape]
    return pl.pallas_call(
        body,
        out_shape=out_shape,
        in_specs=in_specs,
        out_specs=[specs[pltpu.HBM if distant else pltpu.VMEM] for distant in is_far],
        scratch_shapes=list(scratch),
        compiler_params=pltpu.CompilerParams(vmem_limit_bytes=limit),
    )(*[value.reshape(1).astype(jnp.int32) for value in scalars], *arrays, *far, *anchors)


def gate(source, anchors):
    anywhere = pl.BlockSpec(memory_space=pl.ANY)
    return pl.pallas_call(
        lambda *refs: None,
        out_shape=jax.ShapeDtypeStruct(source.shape, source.dtype),
        in_specs=[anywhere] * (1 + len(anchors)),
        out_specs=anywhere,
        input_output_aliases={0: 0},
    )(source, *anchors)


def pack_body(rows_sub, subs, own, source, *rest):
    sent, slots = rest[:-1], rest[-1]
    cols = source.shape[1]
    for sub in range(subs):
        for block in range(NB):
            pieces = []
            for group in range(RQ):
                row = (group * subs + sub) * rows_sub
                piece = source[row : row + rows_sub, :, block * BS : (block + 1) * BS]
                pieces.append(piece.reshape(rows_sub * cols, BS))
            slots[sub * NB + block] = jnp.concatenate(pieces, axis=1)
    deal(sent, slots, own[0])


def unpack_body(rows_sub, subs, extra, own, base, *rest):
    received, (result, slots) = rest[: len(rest) - 2 - extra], rest[-2:]
    cols = base.shape[1]
    place(slots, received, own[0])
    for sub in range(subs):
        for group in range(RQ):
            row = (group * subs + sub) * rows_sub
            pieces = [
                slots[sub * NB + block, :, group * BS : (group + 1) * BS] for block in range(NB)
            ]
            update = jnp.concatenate(pieces, axis=1).reshape(rows_sub, cols, NB * BS)
            old = base[row : row + rows_sub]
            result[row : row + rows_sub] = (
                old.astype(jnp.float32) + update.astype(jnp.float32)
            ).astype(jnp.bfloat16)


def product(left, right):
    return jnp.dot(left, right, preferred_element_type=jnp.float32)


def product_back(left, right):
    return lax.dot_general(
        left, right, (((1,), (1,)), ((), ())), preferred_element_type=jnp.float32
    )


def product_outer(left, right):
    return lax.dot_general(
        left, right, (((0,), (0,)), ((), ())), preferred_element_type=jnp.float32
    )


def place(slots, pieces, own):
    if len(pieces) == 1:
        slots[...] = pieces[0][...]
        return
    for offset, piece in enumerate(pieces):
        slots[jnp.bitwise_xor(own, offset)] = piece[...]


def deal(pieces, slots, own):
    if len(pieces) == 1:
        pieces[0][...] = slots[...]
        return
    for offset, piece in enumerate(pieces):
        piece[...] = slots[jnp.bitwise_xor(own, offset)]


def spectra_body(count, extra, cuts, kept, own_in, own_out, table, *rest):
    received, (sent, slots_in, slots_out) = rest[:count], (rest[count + extra : -2], *rest[-2:])
    place(slots_in, received, own_in[0])
    each = slots_in.shape[1] // cuts
    parts = []
    for cut in range(cuts):
        flat = slots_in[:, cut * each : (cut + 1) * each].reshape(-1, PACK)
        parts.append(product(table[...], flat).reshape(slots_out.shape[0] * kept, -1, PACK))
    joined = jnp.stack(parts, axis=1) if cuts > 1 else parts[0]
    slots_out[...] = joined.reshape(slots_out.shape).astype(jnp.bfloat16)
    deal(sent, slots_out, own_out[0])


def columns_body(count, extra, cuts, kept, own_in, own_out, table, *rest):
    received, results, (slots_in, slots_out, sems) = (
        rest[:count],
        rest[count + extra : -3],
        rest[-3:],
    )
    place(slots_in, received, own_in[0])
    each = slots_out.shape[1] // cuts
    modes = slots_in.shape[0] * kept
    split = slots_in[...].astype(jnp.float32).reshape(modes, cuts, -1, PACK)
    flats = [split[:, cut].reshape(-1, PACK).astype(jnp.bfloat16) for cut in range(cuts)]
    copies = []
    for cut, flat in enumerate(flats):
        part = product(table[...], flat).astype(jnp.bfloat16)
        rows = pl.ds(cut * each, each)
        slots_out[:, rows] = part.reshape(slots_out.shape[0], each, PACK)
        if len(results) == 1:
            copies.append(
                pltpu.make_async_copy(slots_out.at[:, rows], results[0].at[:, rows], sems.at[cut])
            )
            copies[-1].start()
    if len(results) > 1:
        deal(results, slots_out, own_out[0])
    finish(copies)


def finish(copies):
    for copy in copies:
        copy.wait()


def load_weights(block, weights, real_imag, sems):
    copies = [
        pltpu.make_async_copy(source.at[part, block], real_imag.at[slot, part], sems.at[slot, part])
        for slot, source in enumerate(weights)
        for part in range(2)
    ]
    for copy in copies:
        copy.start()
    return copies


def complex_weights(real_imag, full):
    for slot in range(full.shape[0]):
        real, imag = real_imag[slot, 0], real_imag[slot, 1]
        full[slot, :BS] = jnp.concatenate([real, imag], axis=1)
        full[slot, BS:] = jnp.concatenate([-imag, real], axis=1)


def lat_forward(table, slots, tile, deep, rows):
    slab = slots[:, tile * deep : (tile + 1) * deep]
    flat = slab.reshape(slab.shape[0] * deep, PACK)
    stacked = jnp.concatenate(
        [flat[:, group * BS : (group + 1) * BS] for group in range(RQ)], axis=0
    )
    spectrum = product(table, stacked).astype(jnp.bfloat16)
    return [
        jnp.concatenate([spectrum[at : at + rows], spectrum[at + rows : at + 2 * rows]], axis=1)
        for at in range(0, spectrum.shape[0], 2 * rows)
    ]


def lat_inverse(table, values, slots, tile, deep):
    stacked = jnp.concatenate(
        [part for value in values for part in (value[:, :BS], value[:, BS:])], axis=0
    )
    rows = product(table, stacked).astype(jnp.bfloat16)
    each = rows.shape[0] // RQ
    packed = jnp.concatenate([rows[at : at + each] for at in range(0, RQ * each, each)], axis=1)
    slots[:, tile * deep : (tile + 1) * deep] = packed.reshape(slots.shape[0], deep, PACK)


def mode_weight(first_mode, index):
    return jnp.where(first_mode + index == 0, 1.0, 2.0).astype(jnp.float32)


def gelu(pre):
    squared = pre * pre
    tangent = jnp.tanh(gelu_coeff * (pre + 0.044715 * squared * pre))
    act = (0.5 * pre * (1.0 + tangent)).astype(jnp.bfloat16)
    return act, squared, tangent


def forward_body(members, pack_modes, member, first_mode, block, table, *rest):
    received, weights, sent = rest[:members], rest[members : members + 2], rest[members + 2 :]
    sent, rest = sent[:members], sent[members:]
    saved, anchor, slots, spec, real_imag, full, weight_sems, save_sems = rest
    anchor[...] = jnp.zeros_like(anchor)
    loads = load_weights(block[0], weights, real_imag, weight_sems)
    own = member[0]
    kept, rows, _ = spec.shape
    deep = slots.shape[1] * pack_modes // kept
    place(slots, received, own)
    lat = table[...]
    inverse = lat.T
    copies = []
    for tile in range(kept // pack_modes):
        for inner, values in enumerate(lat_forward(lat, slots, tile, deep, rows)):
            index = tile * pack_modes + inner
            spec[index, :, :WIDE] = values
            copies.append(
                pltpu.make_async_copy(spec.at[index], saved.at[index], save_sems.at[index])
            )
            copies[-1].start()
    finish(loads)
    complex_weights(real_imag, full)
    for tile in range(kept // pack_modes):
        outs = []
        for index in range(tile * pack_modes, (tile + 1) * pack_modes):
            act, _, _ = gelu(product(spec[index, :, :WIDE], full[0]))
            post = product(act, full[1])
            weight = mode_weight(first_mode[0], index)
            shrunk = post - shrink_level * jnp.tanh(post / shrink_level)
            outs.append((weight * shrunk).astype(jnp.bfloat16))
        lat_inverse(inverse, outs, slots, tile, deep)
    deal(sent, slots, own)
    finish(copies)


def backward_body(members, pack_modes, factor, member, first_mode, block, table, *rest):
    received, rest = rest[:members], rest[members:]
    weights, saved, (result, combined, grads) = rest[:2], rest[2], rest[3:6]
    slots, cots, spec, real_imag, full, weight_sems, load_sems = rest[6:]
    loads = load_weights(block[0], weights, real_imag, weight_sems)
    kept, rows, _ = spec.shape
    deep = slots.shape[1] * pack_modes // kept
    spec_loads = [
        pltpu.make_async_copy(saved.at[index], spec.at[index], load_sems.at[index])
        for index in range(kept)
    ]
    for copy in spec_loads:
        copy.start()
    place(slots, received, member[0])
    lat = table[...]
    for tile in range(kept // pack_modes):
        for inner, cot in enumerate(lat_forward(lat, slots, tile, deep, rows)):
            cots[tile * pack_modes + inner] = cot
    finish(loads)
    complex_weights(real_imag, full)
    combined[...] = full[0]
    total_first = jnp.zeros((WIDE, WIDE), jnp.float32)
    total_second = jnp.zeros((WIDE, WIDE), jnp.float32)
    for index in range(kept):
        spec_loads[index].wait()
        values = spec[index, :, :WIDE]
        pre = product(values, full[0])
        act, squared, tangent = gelu(pre)
        slope = 0.5 * (1.0 + tangent) + 0.5 * pre * (1.0 - tangent * tangent) * gelu_coeff * (
            1.0 + 3.0 * 0.044715 * squared
        )
        ratio = jnp.tanh(product(act, full[1]) / shrink_level)
        weight = mode_weight(first_mode[0], index)
        cot = cots[index].astype(jnp.float32)
        grad_post = (weight * cot * (ratio * ratio)).astype(jnp.bfloat16)
        grad_pre = (product_back(grad_post, full[1]) * slope).astype(jnp.bfloat16)
        result[index] = grad_pre
        total_second += product_outer(act, grad_post)
        total_first += product_outer(values, grad_pre)
    share = grads.shape[1]
    for slot, total in enumerate((total_first, total_second)):
        real = (total[:BS, :BS] + total[BS:, BS:]) * factor
        imag = (total[:BS, BS:] - total[BS:, :BS]) * factor
        for part, value in enumerate((real, imag)):
            for at in range(0, BS, share):
                piece = ((2 * slot + part) * BS + at) // share
                grads[piece] = value[at : at + share].astype(jnp.bfloat16)


def input_grad_body(members, pack_modes, member, lat_own, table, grad_pre, combined, grads, *rest):
    sent, parts, slots = rest[:members], rest[members:-1], rest[-1]
    deal(parts, grads, lat_own[0])
    kept = grad_pre.shape[0]
    deep = slots.shape[1] * pack_modes // kept
    inverse = table[...].T
    for tile in range(kept // pack_modes):
        backs = [
            product_back(grad_pre[index], combined[...]).astype(jnp.bfloat16)
            for index in range(tile * pack_modes, (tile + 1) * pack_modes)
        ]
        lat_inverse(inverse, backs, slots, tile, deep)
    deal(sent, slots, member[0])


def sum_body(count, *refs):
    total = sum(value[...].astype(jnp.float32) for value in refs[:count])
    refs[-1][...] = total.astype(jnp.bfloat16)


def stack_body(*refs):
    for slot, piece in enumerate(refs[:-1]):
        refs[-1][slot] = piece[...]


def blocks_body(own, near, other, blocks):
    for slot in range(near.shape[0]):
        blocks[jnp.bitwise_xor(own[0], 2 * slot)] = near[slot]
        blocks[jnp.bitwise_xor(own[0], 2 * slot + 1)] = other[slot]


def assemble_body(lat_count, subs, lat_own, *rest):
    gathered, (first, second, slots) = rest[:lat_count], rest[lat_count:]
    rows = gathered[0].shape[1]
    for offset, pieces in enumerate(gathered):
        start = jnp.bitwise_xor(lat_own[0], offset) * rows
        matrix, row = start // BS, pl.multiple_of(start % BS, 16)
        for block in range(NB):
            total = None
            for sub in range(subs):
                value = pieces[sub * NB + block].astype(jnp.float32)
                total = value if total is None else total + value
            slots[matrix, block, pl.ds(row, rows)] = total
    first[...] = slots[:2]
    second[...] = slots[2:]


def exchange(source):
    return lax.all_to_all(source, "lon", split_axis=0, concat_axis=0, tiled=True)


def swap(pieces, axes, partners):
    return [pieces[0]] + [
        lax.ppermute(piece, axes, partners(offset))
        for offset, piece in enumerate(pieces)
        if offset
    ]


def shards(features, cotangent, weight_first, weight_second):
    lat_count = lax.axis_size("lat")
    lon_count = lax.axis_size("lon")
    band_rows, band_cols, channels = features.shape
    rows_total = band_rows * lat_count
    cols_total = band_cols * lon_count
    kept_total = KWD * lat_count * lon_count
    subs = lon_count // NB
    members = lat_count * subs
    rows_sub = band_rows // (RQ * subs)
    rows_cut = min(rows_sub, 4)
    cuts = rows_sub // rows_cut
    kept = kept_total // members
    deep = 2 * rows_sub
    pack_modes = max(1, 16 // deep)
    lat_index = lax.axis_index("lat")
    lon_index = lax.axis_index("lon")
    block = lon_index % NB
    member = lat_index * subs + lon_index // NB
    bf16, f32 = jnp.bfloat16, jnp.float32
    array = jax.ShapeDtypeStruct

    def member_pairs(offset):
        pairs = []
        for lat in range(lat_count):
            for lon in range(lon_count):
                other = (lat * subs + lon // NB) ^ offset
                lon_other = other % subs * NB + lon % NB
                pairs.append((lat * lon_count + lon, other // subs * lon_count + lon_other))
        return pairs

    def line_pairs(count):
        return lambda offset: [(place, place ^ offset) for place in range(count)]

    lon_fwd, lon_inv = map(constant, lon_tables(kept_total, cols_total, lon_count, rows_cut))
    lat_both = constant(lat_table(rows_total, lat_count, subs, rows_sub, rows_cut, pack_modes))
    lon_piece = array((rows_sub * band_cols, PACK), bf16)
    lon_whole = array((lon_count, rows_sub * band_cols, PACK), bf16)
    mid_piece = array((kept * deep, PACK), bf16)
    lon_slots = pltpu.VMEM(lon_whole.shape, bf16)
    mid_slots = pltpu.VMEM((members, kept * deep, PACK), bf16)
    mid_limit = 14 * MIB + 5 * lat_both.size
    share = 4 * BS // lat_count

    def mid_swap(pieces):
        return swap(pieces, ("lat", "lon"), member_pairs)

    def pack(source, sent):
        body = functools.partial(pack_body, rows_sub, subs)
        return kernel_call(body, sent, [lon_index], [source], [lon_slots])

    def unpack(pieces, base, anchors=()):
        body = functools.partial(unpack_body, rows_sub, subs, len(anchors))
        result = array(base.shape, bf16)
        return kernel_call(body, [result], [lon_index], [base, *pieces], [lon_slots], anchors)[0]

    def to_spectra(pieces, anchors=()):
        return kernel_call(
            functools.partial(spectra_body, len(pieces), len(anchors), cuts, kept),
            [mid_piece] * members,
            [lon_index, member],
            [lon_fwd, *pieces],
            [lon_slots, mid_slots],
            anchors,
        )

    def to_columns(pieces, sent, anchors=()):
        return kernel_call(
            functools.partial(columns_body, members, len(anchors), cuts, kept),
            sent,
            [member, lon_index],
            [lon_inv, *pieces],
            [mid_slots, lon_slots, pltpu.SemaphoreType.DMA((cuts,))],
            anchors,
        )

    modes = (kept, rows_total, STATE)
    weights = [weight_first, weight_second]
    mid_scratch = [
        pltpu.VMEM(modes, bf16),
        pltpu.VMEM((2, 2, BS, BS), bf16),
        pltpu.VMEM((2, WIDE, WIDE), bf16),
        pltpu.SemaphoreType.DMA((2, 2)),
        pltpu.SemaphoreType.DMA((kept,)),
    ]

    field = swap(pack(features, [lon_piece] * lon_count), "lon", line_pairs(lon_count))
    field_cot = exchange(gate(pack(cotangent, [lon_whole])[0], field[1:]))
    results = kernel_call(
        functools.partial(forward_body, members, pack_modes),
        [mid_piece] * members + [pltpu.HBM(modes, bf16), array((8, 128), f32)],
        [member, member * kept, block],
        [lat_both, *mid_swap(to_spectra(field))],
        [mid_slots, *mid_scratch],
        far=weights,
        limit=mid_limit,
    )
    saved, anchor = results[members:]
    spectra_cot = to_spectra([field_cot], [anchor])
    columns = to_columns(
        mid_swap(results[:members]), [pltpu.HBM(lon_whole.shape, bf16)], spectra_cot[:1]
    )
    filtered = exchange(columns[0])
    wide = (kept, rows_total, WIDE)
    grad_pre, combined, grads = kernel_call(
        functools.partial(
            backward_body, members, pack_modes, 1.0 / math.sqrt(rows_total * kept_total)
        ),
        [array(wide, bf16), array((WIDE, WIDE), bf16), array((lat_count, share, BS), bf16)],
        [member, member * kept, block],
        [lat_both, *mid_swap(spectra_cot)],
        [mid_slots, pltpu.VMEM(wide, bf16), *mid_scratch],
        far=weights + [saved],
        limit=mid_limit,
    )
    back = kernel_call(
        functools.partial(input_grad_body, members, pack_modes),
        [mid_piece] * members + [array((share, BS), bf16)] * lat_count,
        [member, lat_index],
        [lat_both, grad_pre, combined, grads],
        [mid_slots],
        limit=mid_limit,
    )
    lon_pairs = line_pairs(lon_count)
    columns = to_columns(mid_swap(back[:members]), [pltpu.HBM(lon_whole.shape, bf16)])
    own_share = kernel_call(
        functools.partial(sum_body, lat_count),
        [array((share, BS), bf16)],
        [],
        swap(back[members:], "lat", line_pairs(lat_count)),
        anchors=columns[:1],
    )[0]
    near = kernel_call(
        stack_body,
        [array((lon_count // 2, share, BS), bf16)],
        [],
        [own_share]
        + [lax.ppermute(own_share, "lon", lon_pairs(far)) for far in range(2, lon_count, 2)],
    )[0]
    returned = exchange(gate(columns[0], [near]))
    blocks = kernel_call(
        blocks_body,
        [array((lon_count, share, BS), bf16)],
        [lon_index],
        [near, lax.ppermute(near, "lon", lon_pairs(1))],
    )[0]

    gathered = {0: blocks}
    step = lat_count // 2
    while step:
        for offset in sorted(gathered):
            moved = lax.ppermute(gathered[offset], "lat", line_pairs(lat_count)(step))
            gathered[offset | step] = moved
        step //= 2
    gathered = [gathered[offset] for offset in range(lat_count)]
    full = array((2, NB, BS, BS), f32)
    grad_first, grad_second = kernel_call(
        functools.partial(assemble_body, lat_count, subs),
        [full, full],
        [lat_index],
        gathered,
        [pltpu.VMEM((4, NB, BS, BS), f32)],
    )
    mixed_field = unpack([filtered], features)
    feature_grad = unpack([returned], cotangent, [mixed_field])
    return (mixed_field, feature_grad, grad_first, grad_second)


def solution(mesh):
    in_specs = (P("lat", "lon", None), P("lat", "lon", None), P(), P())
    out_specs = (P("lat", "lon", None), P("lat", "lon", None), P(), P())
    return jax.shard_map(shards, mesh=mesh, in_specs=in_specs, out_specs=out_specs, check_vma=False)
```

```python
import functools
import math

import jax
import jax.numpy as jnp
import ml_dtypes
import numpy as np
from jax import lax
from jax.experimental import pallas as pl
from jax.experimental.pallas import tpu as pltpu
from jax.sharding import PartitionSpec as P

NB = 8
BS = 96
KWD = 1
RQ = 4
PACK = RQ * BS
WIDE = 2 * BS
STATE = -(-WIDE // 128) * 128
MIB = 1024 * 1024

shrink_level = 0.01
gelu_coeff = 0.7978845608028654


def wave_table(first, second, length):
    product = (first[:, None] * second[None, :]) % length
    angle = np.float32(2.0 * math.pi / length) * product.astype(np.float32)
    scale = np.float32(math.sqrt(length))
    rounded = ml_dtypes.bfloat16
    cos = (np.cos(angle) / scale).astype(rounded).astype(np.float32)
    sin = (np.sin(angle) / scale).astype(rounded).astype(np.float32)
    return cos, sin


def lon_tables(kept, cols, lon_count, rows):
    cos, sin = wave_table(np.arange(kept), np.arange(cols), cols)
    parts = np.stack([cos, -sin], axis=1).reshape(kept, 2, lon_count, cols // lon_count)
    eye = np.eye(rows, dtype=np.float32)
    forward = np.einsum("kpgw,rs->kprgsw", parts, eye).reshape(2 * kept * rows, -1)
    return forward, forward.T


def lat_table(rows, lat_count, subs, rows_sub, rows_cut, pack_modes):
    cos, sin = wave_table(np.arange(rows), np.arange(rows), rows)
    forward = np.stack([np.stack([cos, sin], axis=1), np.stack([-sin, cos], axis=1)])
    split = forward.reshape(2, rows, 2, lat_count, RQ, subs, rows_sub // rows_cut, rows_cut)
    eye = np.eye(pack_modes, dtype=np.float32)
    return np.einsum("aqplgshr,jk->jaqglskhpr", split, eye).reshape(2 * pack_modes * rows, -1)


def constant(table):
    return jnp.asarray(table.astype(ml_dtypes.bfloat16))


def kernel_call(body, out_shape, scalars, arrays, scratch=(), anchors=(), far=(), limit=8 * MIB):
    specs = {
        space: pl.BlockSpec(memory_space=space)
        for space in (pltpu.VMEM, pltpu.SMEM, pltpu.HBM, pl.ANY)
    }
    far = [pltpu.with_memory_space_constraint(value, pltpu.HBM) for value in far]
    in_specs = [specs[pltpu.SMEM]] * len(scalars) + [specs[pltpu.VMEM]] * len(arrays)
    in_specs += [specs[pltpu.HBM]] * len(far) + [specs[pl.ANY]] * len(anchors)
    is_far = [getattr(shape, "memory_space", None) is pltpu.HBM for shape in out_shape]
    return pl.pallas_call(
        body,
        out_shape=out_shape,
        in_specs=in_specs,
        out_specs=[specs[pltpu.HBM if distant else pltpu.VMEM] for distant in is_far],
        scratch_shapes=list(scratch),
        compiler_params=pltpu.CompilerParams(vmem_limit_bytes=limit),
    )(*[value.reshape(1).astype(jnp.int32) for value in scalars], *arrays, *far, *anchors)


def gate(source, anchors):
    anywhere = pl.BlockSpec(memory_space=pl.ANY)
    return pl.pallas_call(
        lambda *refs: None,
        out_shape=jax.ShapeDtypeStruct(source.shape, source.dtype),
        in_specs=[anywhere] * (1 + len(anchors)),
        out_specs=anywhere,
        input_output_aliases={0: 0},
    )(source, *anchors)


def pack_body(rows_sub, subs, own, source, *rest):
    sent, slots = rest[:-1], rest[-1]
    cols = source.shape[1]
    for sub in range(subs):
        for block in range(NB):
            pieces = []
            for group in range(RQ):
                row = (group * subs + sub) * rows_sub
                piece = source[row : row + rows_sub, :, block * BS : (block + 1) * BS]
                pieces.append(piece.reshape(rows_sub * cols, BS))
            slots[sub * NB + block] = jnp.concatenate(pieces, axis=1)
    deal(sent, slots, own[0])


def unpack_body(rows_sub, subs, own, base, *rest):
    received, (result, slots) = rest[:-2], rest[-2:]
    cols = base.shape[1]
    place(slots, received, own[0])
    for sub in range(subs):
        for group in range(RQ):
            row = (group * subs + sub) * rows_sub
            pieces = [
                slots[sub * NB + block, :, group * BS : (group + 1) * BS] for block in range(NB)
            ]
            update = jnp.concatenate(pieces, axis=1).reshape(rows_sub, cols, NB * BS)
            old = base[row : row + rows_sub]
            result[row : row + rows_sub] = (
                old.astype(jnp.float32) + update.astype(jnp.float32)
            ).astype(jnp.bfloat16)


def product(left, right):
    return jnp.dot(left, right, preferred_element_type=jnp.float32)


def product_back(left, right):
    return lax.dot_general(
        left, right, (((1,), (1,)), ((), ())), preferred_element_type=jnp.float32
    )


def product_outer(left, right):
    return lax.dot_general(
        left, right, (((0,), (0,)), ((), ())), preferred_element_type=jnp.float32
    )


def place(slots, pieces, own):
    if len(pieces) == 1:
        slots[...] = pieces[0][...]
        return
    for offset, piece in enumerate(pieces):
        slots[jnp.bitwise_xor(own, offset)] = piece[...]


def deal(pieces, slots, own):
    if len(pieces) == 1:
        pieces[0][...] = slots[...]
        return
    for offset, piece in enumerate(pieces):
        piece[...] = slots[jnp.bitwise_xor(own, offset)]


def spectra_body(count, extra, cuts, kept, own_in, own_out, table, *rest):
    received, (sent, slots_in, slots_out) = rest[:count], (rest[count + extra : -2], *rest[-2:])
    place(slots_in, received, own_in[0])
    each = slots_in.shape[1] // cuts
    parts = []
    for cut in range(cuts):
        flat = slots_in[:, cut * each : (cut + 1) * each].reshape(-1, PACK)
        parts.append(product(table[...], flat).reshape(slots_out.shape[0] * kept, -1, PACK))
    joined = jnp.stack(parts, axis=1) if cuts > 1 else parts[0]
    slots_out[...] = joined.reshape(slots_out.shape).astype(jnp.bfloat16)
    deal(sent, slots_out, own_out[0])


def columns_body(count, extra, cuts, kept, own_in, table, *rest):
    received, (result, slots_in, slots_out, sems) = rest[:count], rest[count + extra :]
    place(slots_in, received, own_in[0])
    each = slots_out.shape[1] // cuts
    modes = slots_in.shape[0] * kept
    split = slots_in[...].astype(jnp.float32).reshape(modes, cuts, -1, PACK)
    flats = [split[:, cut].reshape(-1, PACK).astype(jnp.bfloat16) for cut in range(cuts)]
    copies = []
    for cut, flat in enumerate(flats):
        part = product(table[...], flat).astype(jnp.bfloat16)
        rows = pl.ds(cut * each, each)
        slots_out[:, rows] = part.reshape(slots_out.shape[0], each, PACK)
        copies.append(
            pltpu.make_async_copy(slots_out.at[:, rows], result.at[:, rows], sems.at[cut])
        )
        copies[-1].start()
    finish(copies)


def finish(copies):
    for copy in copies:
        copy.wait()


def load_weights(block, weights, real_imag, sems):
    copies = [
        pltpu.make_async_copy(source.at[part, block], real_imag.at[slot, part], sems.at[slot, part])
        for slot, source in enumerate(weights)
        for part in range(2)
    ]
    for copy in copies:
        copy.start()
    return copies


def complex_weights(real_imag, full):
    for slot in range(full.shape[0]):
        real, imag = real_imag[slot, 0], real_imag[slot, 1]
        full[slot, :BS] = jnp.concatenate([real, imag], axis=1)
        full[slot, BS:] = jnp.concatenate([-imag, real], axis=1)


def lat_forward(table, slots, tile, deep, rows):
    slab = slots[:, tile * deep : (tile + 1) * deep]
    flat = slab.reshape(slab.shape[0] * deep, PACK)
    stacked = jnp.concatenate(
        [flat[:, group * BS : (group + 1) * BS] for group in range(RQ)], axis=0
    )
    spectrum = product(table, stacked).astype(jnp.bfloat16)
    return [
        jnp.concatenate([spectrum[at : at + rows], spectrum[at + rows : at + 2 * rows]], axis=1)
        for at in range(0, spectrum.shape[0], 2 * rows)
    ]


def lat_inverse(table, values, slots, tile, deep):
    stacked = jnp.concatenate(
        [part for value in values for part in (value[:, :BS], value[:, BS:])], axis=0
    )
    rows = product(table, stacked).astype(jnp.bfloat16)
    each = rows.shape[0] // RQ
    packed = jnp.concatenate([rows[at : at + each] for at in range(0, RQ * each, each)], axis=1)
    slots[:, tile * deep : (tile + 1) * deep] = packed.reshape(slots.shape[0], deep, PACK)


def mode_weight(first_mode, index):
    return jnp.where(first_mode + index == 0, 1.0, 2.0).astype(jnp.float32)


def gelu(pre):
    squared = pre * pre
    tangent = jnp.tanh(gelu_coeff * (pre + 0.044715 * squared * pre))
    act = (0.5 * pre * (1.0 + tangent)).astype(jnp.bfloat16)
    return act, squared, tangent


def forward_body(members, pack_modes, member, first_mode, block, table, *rest):
    received, weights, sent = rest[:members], rest[members : members + 2], rest[members + 2 :]
    sent, rest = sent[:members], sent[members:]
    saved, anchor, slots, spec, real_imag, full, weight_sems, save_sems = rest
    anchor[...] = jnp.zeros_like(anchor)
    loads = load_weights(block[0], weights, real_imag, weight_sems)
    own = member[0]
    kept, rows, _ = spec.shape
    deep = slots.shape[1] * pack_modes // kept
    place(slots, received, own)
    lat = table[...]
    inverse = lat.T
    copies = []
    for tile in range(kept // pack_modes):
        for inner, values in enumerate(lat_forward(lat, slots, tile, deep, rows)):
            index = tile * pack_modes + inner
            spec[index, :, :WIDE] = values
            copies.append(
                pltpu.make_async_copy(spec.at[index], saved.at[index], save_sems.at[index])
            )
            copies[-1].start()
    finish(loads)
    complex_weights(real_imag, full)
    for tile in range(kept // pack_modes):
        outs = []
        for index in range(tile * pack_modes, (tile + 1) * pack_modes):
            act, _, _ = gelu(product(spec[index, :, :WIDE], full[0]))
            post = product(act, full[1])
            weight = mode_weight(first_mode[0], index)
            shrunk = post - shrink_level * jnp.tanh(post / shrink_level)
            outs.append((weight * shrunk).astype(jnp.bfloat16))
        lat_inverse(inverse, outs, slots, tile, deep)
    deal(sent, slots, own)
    finish(copies)


def backward_body(
    members, shares, pack_modes, factor, member, first_mode, lat_own, block, table, *rest
):
    received, rest = rest[:members], rest[members:]
    weights, saved, result, combined, rest = rest[:2], rest[2], rest[3], rest[4], rest[5:]
    parts, (slots, grads, cots, spec, real_imag, full, weight_sems, load_sems) = (
        rest[:shares],
        rest[shares:],
    )
    loads = load_weights(block[0], weights, real_imag, weight_sems)
    kept, rows, _ = spec.shape
    deep = slots.shape[1] * pack_modes // kept
    spec_loads = [
        pltpu.make_async_copy(saved.at[index], spec.at[index], load_sems.at[index])
        for index in range(kept)
    ]
    for copy in spec_loads:
        copy.start()
    place(slots, received, member[0])
    lat = table[...]
    for tile in range(kept // pack_modes):
        for inner, cot in enumerate(lat_forward(lat, slots, tile, deep, rows)):
            cots[tile * pack_modes + inner] = cot
    finish(loads)
    complex_weights(real_imag, full)
    combined[...] = full[0]
    total_first = jnp.zeros((WIDE, WIDE), jnp.float32)
    total_second = jnp.zeros((WIDE, WIDE), jnp.float32)
    for index in range(kept):
        spec_loads[index].wait()
        values = spec[index, :, :WIDE]
        pre = product(values, full[0])
        act, squared, tangent = gelu(pre)
        slope = 0.5 * (1.0 + tangent) + 0.5 * pre * (1.0 - tangent * tangent) * gelu_coeff * (
            1.0 + 3.0 * 0.044715 * squared
        )
        ratio = jnp.tanh(product(act, full[1]) / shrink_level)
        weight = mode_weight(first_mode[0], index)
        cot = cots[index].astype(jnp.float32)
        grad_post = (weight * cot * (ratio * ratio)).astype(jnp.bfloat16)
        grad_pre = (product_back(grad_post, full[1]) * slope).astype(jnp.bfloat16)
        result[index] = grad_pre
        total_second += product_outer(act, grad_post)
        total_first += product_outer(values, grad_pre)
    share = grads.shape[1]
    for slot, total in enumerate((total_first, total_second)):
        real = (total[:BS, :BS] + total[BS:, BS:]) * factor
        imag = (total[:BS, BS:] - total[BS:, :BS]) * factor
        for part, value in enumerate((real, imag)):
            for at in range(0, BS, share):
                piece = ((2 * slot + part) * BS + at) // share
                grads[piece] = value[at : at + share].astype(jnp.bfloat16)
    deal(parts, grads, lat_own[0])


def input_grad_body(pack_modes, extra, member, table, grad_pre, combined, *rest):
    sent, slots = rest[extra:-1], rest[-1]
    kept = grad_pre.shape[0]
    deep = slots.shape[1] * pack_modes // kept
    inverse = table[...].T
    for tile in range(kept // pack_modes):
        backs = [
            product_back(grad_pre[index], combined[...]).astype(jnp.bfloat16)
            for index in range(tile * pack_modes, (tile + 1) * pack_modes)
        ]
        lat_inverse(inverse, backs, slots, tile, deep)
    deal(sent, slots, member[0])


def sum_body(*refs):
    refs[-1][...] = sum(value[...].astype(jnp.float32) for value in refs[:-1]).astype(jnp.bfloat16)


def stack_body(*refs):
    for slot, piece in enumerate(refs[:-1]):
        refs[-1][slot] = piece[...]


def blocks_body(own, near, other, blocks):
    for slot in range(near.shape[0]):
        blocks[jnp.bitwise_xor(own[0], 2 * slot)] = near[slot]
        blocks[jnp.bitwise_xor(own[0], 2 * slot + 1)] = other[slot]


def assemble_body(lat_count, subs, lat_own, *rest):
    gathered, (first, second, slots) = rest[:lat_count], rest[lat_count:]
    rows = gathered[0].shape[1]
    for offset, pieces in enumerate(gathered):
        start = jnp.bitwise_xor(lat_own[0], offset) * rows
        matrix, row = start // BS, pl.multiple_of(start % BS, 16)
        for block in range(NB):
            total = None
            for sub in range(subs):
                value = pieces[sub * NB + block].astype(jnp.float32)
                total = value if total is None else total + value
            slots[matrix, block, pl.ds(row, rows)] = total
    first[...] = slots[:2]
    second[...] = slots[2:]


def exchange(source):
    return lax.all_to_all(source, "lon", split_axis=0, concat_axis=0, tiled=True)


def swap(pieces, axes, partners):
    return [pieces[0]] + [
        lax.ppermute(piece, axes, partners(offset))
        for offset, piece in enumerate(pieces)
        if offset
    ]


def shards(features, cotangent, weight_first, weight_second):
    lat_count = lax.axis_size("lat")
    lon_count = lax.axis_size("lon")
    band_rows, band_cols, channels = features.shape
    rows_total = band_rows * lat_count
    cols_total = band_cols * lon_count
    kept_total = KWD * lat_count * lon_count
    subs = lon_count // NB
    members = lat_count * subs
    rows_sub = band_rows // (RQ * subs)
    rows_cut = min(rows_sub, 4)
    cuts = rows_sub // rows_cut
    kept = kept_total // members
    deep = 2 * rows_sub
    pack_modes = max(1, 16 // deep)
    lat_index = lax.axis_index("lat")
    lon_index = lax.axis_index("lon")
    block = lon_index % NB
    member = lat_index * subs + lon_index // NB
    bf16, f32 = jnp.bfloat16, jnp.float32
    array = jax.ShapeDtypeStruct

    def member_pairs(offset):
        pairs = []
        for lat in range(lat_count):
            for lon in range(lon_count):
                other = (lat * subs + lon // NB) ^ offset
                lon_other = other % subs * NB + lon % NB
                pairs.append((lat * lon_count + lon, other // subs * lon_count + lon_other))
        return pairs

    def line_pairs(count):
        return lambda offset: [(place, place ^ offset) for place in range(count)]

    lon_fwd, lon_inv = map(constant, lon_tables(kept_total, cols_total, lon_count, rows_cut))
    lat_both = constant(lat_table(rows_total, lat_count, subs, rows_sub, rows_cut, pack_modes))
    lon_piece = array((rows_sub * band_cols, PACK), bf16)
    lon_whole = array((lon_count, rows_sub * band_cols, PACK), bf16)
    mid_piece = array((kept * deep, PACK), bf16)
    lon_slots = pltpu.VMEM(lon_whole.shape, bf16)
    mid_slots = pltpu.VMEM((members, kept * deep, PACK), bf16)
    mid_limit = 14 * MIB + 5 * lat_both.size
    share = 4 * BS // lat_count

    def mid_swap(pieces):
        return swap(pieces, ("lat", "lon"), member_pairs)

    def pack(source, sent):
        body = functools.partial(pack_body, rows_sub, subs)
        return kernel_call(body, sent, [lon_index], [source], [lon_slots])

    def unpack(source, base):
        body = functools.partial(unpack_body, rows_sub, subs)
        result = array(base.shape, bf16)
        return kernel_call(body, [result], [lon_index], [base, source], [lon_slots])[0]

    def to_spectra(pieces, anchors=()):
        return kernel_call(
            functools.partial(spectra_body, len(pieces), len(anchors), cuts, kept),
            [mid_piece] * members,
            [lon_index, member],
            [lon_fwd, *pieces],
            [lon_slots, mid_slots],
            anchors,
        )

    def to_columns(pieces, anchors=()):
        return kernel_call(
            functools.partial(columns_body, members, len(anchors), cuts, kept),
            [pltpu.HBM(lon_whole.shape, bf16)],
            [member],
            [lon_inv, *pieces],
            [mid_slots, lon_slots, pltpu.SemaphoreType.DMA((cuts,))],
            anchors,
        )[0]

    modes = (kept, rows_total, STATE)
    weights = [weight_first, weight_second]
    mid_scratch = [
        pltpu.VMEM(modes, bf16),
        pltpu.VMEM((2, 2, BS, BS), bf16),
        pltpu.VMEM((2, WIDE, WIDE), bf16),
        pltpu.SemaphoreType.DMA((2, 2)),
        pltpu.SemaphoreType.DMA((kept,)),
    ]

    field = swap(pack(features, [lon_piece] * lon_count), "lon", line_pairs(lon_count))
    field_cot = exchange(gate(pack(cotangent, [lon_whole])[0], field[1:]))
    results = kernel_call(
        functools.partial(forward_body, members, pack_modes),
        [mid_piece] * members + [pltpu.HBM(modes, bf16), array((8, 128), f32)],
        [member, member * kept, block],
        [lat_both, *mid_swap(to_spectra(field))],
        [mid_slots, *mid_scratch],
        far=weights,
        limit=mid_limit,
    )
    saved, anchor = results[members:]
    spectra_cot = to_spectra([field_cot], [anchor])
    filtered = exchange(to_columns(mid_swap(results[:members]), spectra_cot[:1]))
    wide = (kept, rows_total, WIDE)
    grad_pre, combined, *parts = kernel_call(
        functools.partial(
            backward_body, members, lat_count, pack_modes, 1.0 / math.sqrt(rows_total * kept_total)
        ),
        [array(wide, bf16), array((WIDE, WIDE), bf16)] + [array((share, BS), bf16)] * lat_count,
        [member, member * kept, lat_index, block],
        [lat_both, *mid_swap(spectra_cot)],
        [
            mid_slots,
            pltpu.VMEM((lat_count, share, BS), bf16),
            pltpu.VMEM(wide, bf16),
            *mid_scratch,
        ],
        far=weights + [saved],
        limit=mid_limit,
    )
    shares = swap(parts, "lat", line_pairs(lat_count))
    own_share = kernel_call(sum_body, [array((share, BS), bf16)], [], shares)[0]
    back = kernel_call(
        functools.partial(input_grad_body, pack_modes, 1),
        [mid_piece] * members,
        [member],
        [lat_both, grad_pre, combined],
        [mid_slots],
        shares[1:2],
        limit=mid_limit,
    )
    lon_pairs = line_pairs(lon_count)
    near = kernel_call(
        stack_body,
        [array((lon_count // 2, share, BS), bf16)],
        [],
        [own_share]
        + [lax.ppermute(own_share, "lon", lon_pairs(far)) for far in range(2, lon_count, 2)],
    )[0]
    returned = exchange(gate(to_columns(mid_swap(back)), [near]))
    blocks = kernel_call(
        blocks_body,
        [array((lon_count, share, BS), bf16)],
        [lon_index],
        [near, lax.ppermute(near, "lon", lon_pairs(1))],
    )[0]

    gathered = {0: blocks}
    step = lat_count // 2
    while step:
        for offset in sorted(gathered):
            moved = lax.ppermute(gathered[offset], "lat", line_pairs(lat_count)(step))
            gathered[offset | step] = moved
        step //= 2
    gathered = [gathered[offset] for offset in range(lat_count)]
    full = array((2, NB, BS, BS), f32)
    grad_first, grad_second = kernel_call(
        functools.partial(assemble_body, lat_count, subs),
        [full, full],
        [lat_index],
        gathered,
        [pltpu.VMEM((4, NB, BS, BS), f32)],
    )
    return (unpack(filtered, features), unpack(returned, cotangent), grad_first, grad_second)


def solution(mesh):
    in_specs = (P("lat", "lon", None), P("lat", "lon", None), P(), P())
    out_specs = (P("lat", "lon", None), P("lat", "lon", None), P(), P())
    return jax.shard_map(shards, mesh=mesh, in_specs=in_specs, out_specs=out_specs, check_vma=False)
```

```python
import functools
import math

import jax
import jax.numpy as jnp
import ml_dtypes
import numpy as np
from jax import lax
from jax.experimental import pallas as pl
from jax.experimental.pallas import tpu as pltpu
from jax.sharding import PartitionSpec as P

NB = 8
BS = 96
KWD = 1
RQ = 4
PACK = RQ * BS
WIDE = 2 * BS
STATE = -(-WIDE // 128) * 128
MIB = 1024 * 1024

shrink_level = 0.01
gelu_coeff = 0.7978845608028654


def wave_table(first, second, length):
    product = (first[:, None] * second[None, :]) % length
    angle = np.float32(2.0 * math.pi / length) * product.astype(np.float32)
    scale = np.float32(math.sqrt(length))
    rounded = ml_dtypes.bfloat16
    cos = (np.cos(angle) / scale).astype(rounded).astype(np.float32)
    sin = (np.sin(angle) / scale).astype(rounded).astype(np.float32)
    return cos, sin


def lon_tables(kept, cols, lon_count, rows):
    cos, sin = wave_table(np.arange(kept), np.arange(cols), cols)
    parts = np.stack([cos, -sin], axis=1).reshape(kept, 2, lon_count, cols // lon_count)
    eye = np.eye(rows, dtype=np.float32)
    forward = np.einsum("kpgw,rs->kprgsw", parts, eye).reshape(2 * kept * rows, -1)
    return forward, forward.T


def lat_table(rows, lat_count, subs, rows_sub, rows_cut, pack_modes):
    cos, sin = wave_table(np.arange(rows), np.arange(rows), rows)
    forward = np.stack([np.stack([cos, sin], axis=1), np.stack([-sin, cos], axis=1)])
    split = forward.reshape(2, rows, 2, lat_count, RQ, subs, rows_sub // rows_cut, rows_cut)
    eye = np.eye(pack_modes, dtype=np.float32)
    return np.einsum("aqplgshr,jk->jaqglskhpr", split, eye).reshape(2 * pack_modes * rows, -1)


def constant(table):
    return jnp.asarray(table.astype(ml_dtypes.bfloat16))


def kernel_call(body, out_shape, scalars, arrays, scratch=(), anchors=(), far=(), limit=8 * MIB):
    specs = {
        space: pl.BlockSpec(memory_space=space)
        for space in (pltpu.VMEM, pltpu.SMEM, pltpu.HBM, pl.ANY)
    }
    far = [pltpu.with_memory_space_constraint(value, pltpu.HBM) for value in far]
    in_specs = [specs[pltpu.SMEM]] * len(scalars) + [specs[pltpu.VMEM]] * len(arrays)
    in_specs += [specs[pltpu.HBM]] * len(far) + [specs[pl.ANY]] * len(anchors)
    is_far = [getattr(shape, "memory_space", None) is pltpu.HBM for shape in out_shape]
    return pl.pallas_call(
        body,
        out_shape=out_shape,
        in_specs=in_specs,
        out_specs=[specs[pltpu.HBM if distant else pltpu.VMEM] for distant in is_far],
        scratch_shapes=list(scratch),
        compiler_params=pltpu.CompilerParams(vmem_limit_bytes=limit),
    )(*[value.reshape(1).astype(jnp.int32) for value in scalars], *arrays, *far, *anchors)


def gate(source, anchors):
    anywhere = pl.BlockSpec(memory_space=pl.ANY)
    return pl.pallas_call(
        lambda *refs: None,
        out_shape=jax.ShapeDtypeStruct(source.shape, source.dtype),
        in_specs=[anywhere] * (1 + len(anchors)),
        out_specs=anywhere,
        input_output_aliases={0: 0},
    )(source, *anchors)


def group_copies(source, target, sems):
    rows = target.shape[0] // RQ
    return [
        pltpu.make_async_copy(
            source.at[pl.ds(group * rows, rows)], target.at[pl.ds(group * rows, rows)], sems.at[group]
        )
        for group in range(RQ)
    ]


def pack_body(rows_sub, subs, own, field, *rest):
    sent, (slots, source, sems) = rest[:-3], rest[-3:]
    cols = source.shape[1]
    loads = group_copies(field, source, sems)
    for copy in loads:
        copy.start()
    finish(loads)
    for sub in range(subs):
        for block in range(NB):
            pieces = []
            for group in range(RQ):
                row = (group * subs + sub) * rows_sub
                piece = source[row : row + rows_sub, :, block * BS : (block + 1) * BS]
                pieces.append(piece.reshape(rows_sub * cols, BS))
            slots[sub * NB + block] = jnp.concatenate(pieces, axis=1)
    deal(sent, slots, own[0])


def unpack_body(rows_sub, subs, own, packed, field, result, slots, base, mixed, load_sems, save_sems):
    cols = base.shape[1]
    loads = group_copies(field, base, load_sems)
    saves = group_copies(mixed, result, save_sems)
    for copy in loads:
        copy.start()
    place(slots, [packed], own[0])
    for group in range(RQ):
        loads[group].wait()
        for sub in range(subs):
            row = (group * subs + sub) * rows_sub
            pieces = [
                slots[sub * NB + block, :, group * BS : (group + 1) * BS] for block in range(NB)
            ]
            update = jnp.concatenate(pieces, axis=1).reshape(rows_sub, cols, NB * BS)
            old = base[row : row + rows_sub]
            mixed[row : row + rows_sub] = (
                old.astype(jnp.float32) + update.astype(jnp.float32)
            ).astype(jnp.bfloat16)
        saves[group].start()
    finish(saves)


def product(left, right):
    return jnp.dot(left, right, preferred_element_type=jnp.float32)


def product_back(left, right):
    return lax.dot_general(
        left, right, (((1,), (1,)), ((), ())), preferred_element_type=jnp.float32
    )


def product_outer(left, right):
    return lax.dot_general(
        left, right, (((0,), (0,)), ((), ())), preferred_element_type=jnp.float32
    )


def place(slots, pieces, own):
    if len(pieces) == 1:
        slots[...] = pieces[0][...]
        return
    for offset, piece in enumerate(pieces):
        slots[jnp.bitwise_xor(own, offset)] = piece[...]


def deal(pieces, slots, own):
    if len(pieces) == 1:
        pieces[0][...] = slots[...]
        return
    for offset, piece in enumerate(pieces):
        piece[...] = slots[jnp.bitwise_xor(own, offset)]


def spectra_body(count, extra, cuts, kept, own_in, own_out, table, *rest):
    received, (sent, slots_in, slots_out) = rest[:count], (rest[count + extra : -2], *rest[-2:])
    place(slots_in, received, own_in[0])
    each = slots_in.shape[1] // cuts
    parts = []
    for cut in range(cuts):
        flat = slots_in[:, cut * each : (cut + 1) * each].reshape(-1, PACK)
        parts.append(product(table[...], flat).reshape(slots_out.shape[0] * kept, -1, PACK))
    joined = jnp.stack(parts, axis=1) if cuts > 1 else parts[0]
    slots_out[...] = joined.reshape(slots_out.shape).astype(jnp.bfloat16)
    deal(sent, slots_out, own_out[0])


def columns_body(count, extra, cuts, kept, own_in, table, *rest):
    received, (result, slots_in, slots_out, sems) = rest[:count], rest[count + extra :]
    place(slots_in, received, own_in[0])
    each = slots_out.shape[1] // cuts
    modes = slots_in.shape[0] * kept
    split = slots_in[...].astype(jnp.float32).reshape(modes, cuts, -1, PACK)
    flats = [split[:, cut].reshape(-1, PACK).astype(jnp.bfloat16) for cut in range(cuts)]
    copies = []
    for cut, flat in enumerate(flats):
        part = product(table[...], flat).astype(jnp.bfloat16)
        rows = pl.ds(cut * each, each)
        slots_out[:, rows] = part.reshape(slots_out.shape[0], each, PACK)
        copies.append(
            pltpu.make_async_copy(slots_out.at[:, rows], result.at[:, rows], sems.at[cut])
        )
        copies[-1].start()
    finish(copies)


def finish(copies):
    for copy in copies:
        copy.wait()


def load_weights(block, weights, real_imag, sems):
    copies = [
        pltpu.make_async_copy(source.at[part, block], real_imag.at[slot, part], sems.at[slot, part])
        for slot, source in enumerate(weights)
        for part in range(2)
    ]
    for copy in copies:
        copy.start()
    return copies


def complex_weights(real_imag, full):
    for slot in range(full.shape[0]):
        real, imag = real_imag[slot, 0], real_imag[slot, 1]
        full[slot, :BS] = jnp.concatenate([real, imag], axis=1)
        full[slot, BS:] = jnp.concatenate([-imag, real], axis=1)


def lat_forward(table, slots, tile, deep, rows):
    slab = slots[:, tile * deep : (tile + 1) * deep]
    flat = slab.reshape(slab.shape[0] * deep, PACK)
    stacked = jnp.concatenate(
        [flat[:, group * BS : (group + 1) * BS] for group in range(RQ)], axis=0
    )
    spectrum = product(table, stacked).astype(jnp.bfloat16)
    return [
        jnp.concatenate([spectrum[at : at + rows], spectrum[at + rows : at + 2 * rows]], axis=1)
        for at in range(0, spectrum.shape[0], 2 * rows)
    ]


def lat_inverse(table, values, slots, tile, deep):
    stacked = jnp.concatenate(
        [part for value in values for part in (value[:, :BS], value[:, BS:])], axis=0
    )
    rows = product(table, stacked).astype(jnp.bfloat16)
    each = rows.shape[0] // RQ
    packed = jnp.concatenate([rows[at : at + each] for at in range(0, RQ * each, each)], axis=1)
    slots[:, tile * deep : (tile + 1) * deep] = packed.reshape(slots.shape[0], deep, PACK)


def mode_weight(first_mode, index):
    return jnp.where(first_mode + index == 0, 1.0, 2.0).astype(jnp.float32)


def gelu(pre):
    squared = pre * pre
    tangent = jnp.tanh(gelu_coeff * (pre + 0.044715 * squared * pre))
    act = (0.5 * pre * (1.0 + tangent)).astype(jnp.bfloat16)
    return act, squared, tangent


def forward_body(members, pack_modes, member, first_mode, block, table, *rest):
    received, weights, sent = rest[:members], rest[members : members + 2], rest[members + 2 :]
    sent, rest = sent[:members], sent[members:]
    saved, anchor, slots, spec, real_imag, full, weight_sems, save_sems = rest
    anchor[...] = jnp.zeros_like(anchor)
    loads = load_weights(block[0], weights, real_imag, weight_sems)
    own = member[0]
    kept, rows, _ = spec.shape
    deep = slots.shape[1] * pack_modes // kept
    place(slots, received, own)
    lat = table[...]
    inverse = lat.T
    copies = []
    for tile in range(kept // pack_modes):
        for inner, values in enumerate(lat_forward(lat, slots, tile, deep, rows)):
            index = tile * pack_modes + inner
            spec[index, :, :WIDE] = values
            copies.append(
                pltpu.make_async_copy(spec.at[index], saved.at[index], save_sems.at[index])
            )
            copies[-1].start()
    finish(loads)
    complex_weights(real_imag, full)
    count = max(pack_modes, 2)
    for start in range(0, kept, count):
        values = spec[start : start + count].reshape(count * rows, -1)[:, :WIDE]
        act, _, _ = gelu(product(values, full[0]))
        post = product(act, full[1])
        shrunk = post - shrink_level * jnp.tanh(post / shrink_level)
        outs = [
            (mode_weight(first_mode[0], start + at) * shrunk[at * rows : (at + 1) * rows]).astype(
                jnp.bfloat16
            )
            for at in range(count)
        ]
        for at in range(0, count, pack_modes):
            tile = (start + at) // pack_modes
            lat_inverse(inverse, outs[at : at + pack_modes], slots, tile, deep)
    deal(sent, slots, own)
    finish(copies)


def backward_body(
    members, shares, pack_modes, factor, member, first_mode, lat_own, block, table, *rest
):
    received, rest = rest[:members], rest[members:]
    weights, saved, result, combined, rest = rest[:2], rest[2], rest[3], rest[4], rest[5:]
    parts, (slots, grads, cots, hidden, spec, real_imag, full, weight_sems, load_sems) = (
        rest[:shares],
        rest[shares:],
    )
    loads = load_weights(block[0], weights, real_imag, weight_sems)
    kept, rows, _ = spec.shape
    deep = slots.shape[1] * pack_modes // kept
    spec_loads = [
        pltpu.make_async_copy(saved.at[index], spec.at[index], load_sems.at[index])
        for index in range(kept)
    ]
    for copy in spec_loads:
        copy.start()
    place(slots, received, member[0])
    lat = table[...]
    for tile in range(kept // pack_modes):
        for inner, cot in enumerate(lat_forward(lat, slots, tile, deep, rows)):
            index = tile * pack_modes + inner
            weight = mode_weight(first_mode[0], index)
            cots[index] = (weight * cot.astype(jnp.float32)).astype(jnp.bfloat16)
    finish(loads)
    complex_weights(real_imag, full)
    combined[...] = full[0]
    count = max(pack_modes, 2)
    for start in range(0, kept, count):
        group = pl.ds(start, count)
        finish(spec_loads[start : start + count])
        values = spec[group].reshape(count * rows, -1)[:, :WIDE]
        pre = product(values, full[0])
        act, squared, tangent = gelu(pre)
        slope = 0.5 * (1.0 + tangent) + 0.5 * pre * (1.0 - tangent * tangent) * gelu_coeff * (
            1.0 + 3.0 * 0.044715 * squared
        )
        ratio = jnp.tanh(product(act, full[1]) / shrink_level)
        cot = cots[group].reshape(count * rows, WIDE).astype(jnp.float32)
        grad_post = (cot * (ratio * ratio)).astype(jnp.bfloat16)
        grad_pre = (product_back(grad_post, full[1]) * slope).astype(jnp.bfloat16)
        result[group] = grad_pre.reshape(count, rows, WIDE)
        hidden[group] = act.reshape(count, rows, WIDE)
        cots[group] = grad_post.reshape(count, rows, WIDE)
    modes = kept * rows
    grads_pre = result[...].reshape(modes, WIDE)
    total_first = product_outer(spec[...].reshape(modes, -1)[:, :WIDE], grads_pre)
    total_second = product_outer(
        hidden[...].reshape(modes, WIDE), cots[...].reshape(modes, WIDE)
    )
    share = grads.shape[1]
    for slot, total in enumerate((total_first, total_second)):
        real = (total[:BS, :BS] + total[BS:, BS:]) * factor
        imag = (total[:BS, BS:] - total[BS:, :BS]) * factor
        for part, value in enumerate((real, imag)):
            for at in range(0, BS, share):
                piece = ((2 * slot + part) * BS + at) // share
                grads[piece] = value[at : at + share].astype(jnp.bfloat16)
    deal(parts, grads, lat_own[0])


def input_grad_body(pack_modes, extra, member, table, grad_pre, combined, *rest):
    sent, slots = rest[extra:-1], rest[-1]
    kept = grad_pre.shape[0]
    deep = slots.shape[1] * pack_modes // kept
    inverse = table[...].T
    for tile in range(kept // pack_modes):
        backs = [
            product_back(grad_pre[index], combined[...]).astype(jnp.bfloat16)
            for index in range(tile * pack_modes, (tile + 1) * pack_modes)
        ]
        lat_inverse(inverse, backs, slots, tile, deep)
    deal(sent, slots, member[0])


def sum_body(*refs):
    refs[-1][...] = sum(value[...].astype(jnp.float32) for value in refs[:-1]).astype(jnp.bfloat16)


def stack_body(*refs):
    for slot, piece in enumerate(refs[:-1]):
        refs[-1][slot] = piece[...]


def blocks_body(own, near, other, blocks):
    for slot in range(near.shape[0]):
        blocks[jnp.bitwise_xor(own[0], 2 * slot)] = near[slot]
        blocks[jnp.bitwise_xor(own[0], 2 * slot + 1)] = other[slot]


def assemble_body(lat_count, subs, lat_own, *rest):
    gathered, (first, second, slots) = rest[:lat_count], rest[lat_count:]
    rows = gathered[0].shape[1]
    for offset, pieces in enumerate(gathered):
        start = jnp.bitwise_xor(lat_own[0], offset) * rows
        matrix, row = start // BS, pl.multiple_of(start % BS, 16)
        for block in range(NB):
            total = None
            for sub in range(subs):
                value = pieces[sub * NB + block].astype(jnp.float32)
                total = value if total is None else total + value
            slots[matrix, block, pl.ds(row, rows)] = total
    first[...] = slots[:2]
    second[...] = slots[2:]


def exchange(source):
    return lax.all_to_all(source, "lon", split_axis=0, concat_axis=0, tiled=True)


def swap(pieces, axes, partners):
    return [pieces[0]] + [
        lax.ppermute(piece, axes, partners(offset))
        for offset, piece in enumerate(pieces)
        if offset
    ]


def shards(features, cotangent, weight_first, weight_second):
    lat_count = lax.axis_size("lat")
    lon_count = lax.axis_size("lon")
    band_rows, band_cols, channels = features.shape
    rows_total = band_rows * lat_count
    cols_total = band_cols * lon_count
    kept_total = KWD * lat_count * lon_count
    subs = lon_count // NB
    members = lat_count * subs
    rows_sub = band_rows // (RQ * subs)
    rows_cut = min(rows_sub, 4)
    cuts = rows_sub // rows_cut
    kept = kept_total // members
    deep = 2 * rows_sub
    pack_modes = max(1, 16 // deep)
    lat_index = lax.axis_index("lat")
    lon_index = lax.axis_index("lon")
    block = lon_index % NB
    member = lat_index * subs + lon_index // NB
    bf16, f32 = jnp.bfloat16, jnp.float32
    array = jax.ShapeDtypeStruct

    def member_pairs(offset):
        pairs = []
        for lat in range(lat_count):
            for lon in range(lon_count):
                other = (lat * subs + lon // NB) ^ offset
                lon_other = other % subs * NB + lon % NB
                pairs.append((lat * lon_count + lon, other // subs * lon_count + lon_other))
        return pairs

    def line_pairs(count):
        return lambda offset: [(place, place ^ offset) for place in range(count)]

    lon_fwd, lon_inv = map(constant, lon_tables(kept_total, cols_total, lon_count, rows_cut))
    lat_both = constant(lat_table(rows_total, lat_count, subs, rows_sub, rows_cut, pack_modes))
    lon_piece = array((rows_sub * band_cols, PACK), bf16)
    lon_whole = array((lon_count, rows_sub * band_cols, PACK), bf16)
    mid_piece = array((kept * deep, PACK), bf16)
    lon_slots = pltpu.VMEM(lon_whole.shape, bf16)
    mid_slots = pltpu.VMEM((members, kept * deep, PACK), bf16)
    mid_limit = 14 * MIB + 5 * lat_both.size
    share = 4 * BS // lat_count

    def mid_swap(pieces):
        return swap(pieces, ("lat", "lon"), member_pairs)

    def pack(source, sent):
        body = functools.partial(pack_body, rows_sub, subs)
        scratch = [lon_slots, pltpu.VMEM(source.shape, bf16), pltpu.SemaphoreType.DMA((RQ,))]
        return kernel_call(body, sent, [lon_index], [], scratch, far=[source])

    def unpack(source, base):
        body = functools.partial(unpack_body, rows_sub, subs)
        scratch = [lon_slots] + [pltpu.VMEM(base.shape, bf16)] * 2
        scratch += [pltpu.SemaphoreType.DMA((RQ,))] * 2
        result = pltpu.HBM(base.shape, bf16)
        return kernel_call(body, [result], [lon_index], [source], scratch, far=[base])[0]

    def to_spectra(pieces, anchors=()):
        return kernel_call(
            functools.partial(spectra_body, len(pieces), len(anchors), cuts, kept),
            [mid_piece] * members,
            [lon_index, member],
            [lon_fwd, *pieces],
            [lon_slots, mid_slots],
            anchors,
        )

    def to_columns(pieces, anchors=()):
        return kernel_call(
            functools.partial(columns_body, members, len(anchors), cuts, kept),
            [pltpu.HBM(lon_whole.shape, bf16)],
            [member],
            [lon_inv, *pieces],
            [mid_slots, lon_slots, pltpu.SemaphoreType.DMA((cuts,))],
            anchors,
        )[0]

    modes = (kept, rows_total, STATE)
    weights = [weight_first, weight_second]
    mid_scratch = [
        pltpu.VMEM(modes, bf16),
        pltpu.VMEM((2, 2, BS, BS), bf16),
        pltpu.VMEM((2, WIDE, WIDE), bf16),
        pltpu.SemaphoreType.DMA((2, 2)),
        pltpu.SemaphoreType.DMA((kept,)),
    ]

    field = swap(pack(features, [lon_piece] * lon_count), "lon", line_pairs(lon_count))
    field_cot = exchange(gate(pack(cotangent, [lon_whole])[0], field[1:]))
    results = kernel_call(
        functools.partial(forward_body, members, pack_modes),
        [mid_piece] * members + [pltpu.HBM(modes, bf16), array((8, 128), f32)],
        [member, member * kept, block],
        [lat_both, *mid_swap(to_spectra(field))],
        [mid_slots, *mid_scratch],
        far=weights,
        limit=mid_limit,
    )
    saved, anchor = results[members:]
    spectra_cot = to_spectra([field_cot], [anchor])
    filtered = exchange(to_columns(mid_swap(results[:members]), spectra_cot[:1]))
    wide = (kept, rows_total, WIDE)
    grad_pre, combined, *parts = kernel_call(
        functools.partial(
            backward_body, members, lat_count, pack_modes, 1.0 / math.sqrt(rows_total * kept_total)
        ),
        [array(wide, bf16), array((WIDE, WIDE), bf16)] + [array((share, BS), bf16)] * lat_count,
        [member, member * kept, lat_index, block],
        [lat_both, *mid_swap(spectra_cot)],
        [
            mid_slots,
            pltpu.VMEM((lat_count, share, BS), bf16),
            pltpu.VMEM(wide, bf16),
            pltpu.VMEM(wide, bf16),
            *mid_scratch,
        ],
        far=weights + [saved],
        limit=mid_limit,
    )
    own_share = kernel_call(
        sum_body, [array((share, BS), bf16)], [], swap(parts, "lat", line_pairs(lat_count))
    )[0]
    back = kernel_call(
        functools.partial(input_grad_body, pack_modes, 1),
        [mid_piece] * members,
        [member],
        [lat_both, grad_pre, combined],
        [mid_slots],
        [own_share],
        limit=mid_limit,
    )
    lon_pairs = line_pairs(lon_count)
    near = kernel_call(
        stack_body,
        [array((lon_count // 2, share, BS), bf16)],
        [],
        [own_share]
        + [lax.ppermute(own_share, "lon", lon_pairs(far)) for far in range(2, lon_count, 2)],
    )[0]
    returned = exchange(to_columns(mid_swap(back), [near]))
    blocks = kernel_call(
        blocks_body,
        [array((lon_count, share, BS), bf16)],
        [lon_index],
        [near, lax.ppermute(near, "lon", lon_pairs(1))],
    )[0]

    gathered = {0: blocks}
    step = lat_count // 2
    while step:
        for offset in sorted(gathered):
            moved = lax.ppermute(gathered[offset], "lat", line_pairs(lat_count)(step))
            gathered[offset | step] = moved
        step //= 2
    gathered = [gathered[offset] for offset in range(lat_count)]
    full = array((2, NB, BS, BS), f32)
    grad_first, grad_second = kernel_call(
        functools.partial(assemble_body, lat_count, subs),
        [full, full],
        [lat_index],
        gathered,
        [pltpu.VMEM((4, NB, BS, BS), f32)],
    )
    return (unpack(filtered, features), unpack(returned, cotangent), grad_first, grad_second)


def solution(mesh):
    in_specs = (P("lat", "lon", None), P("lat", "lon", None), P(), P())
    out_specs = (P("lat", "lon", None), P("lat", "lon", None), P(), P())
    return jax.shard_map(shards, mesh=mesh, in_specs=in_specs, out_specs=out_specs, check_vma=False)
```

```python
import functools
import math

import jax
import jax.numpy as jnp
import ml_dtypes
import numpy as np
from jax import lax
from jax.experimental import pallas as pl
from jax.experimental.pallas import tpu as pltpu
from jax.sharding import PartitionSpec as P

NB = 8
BS = 96
KWD = 1
RQ = 4
PACK = RQ * BS
WIDE = 2 * BS
STATE = -(-WIDE // 128) * 128
MIB = 1024 * 1024

shrink_level = 0.01
gelu_coeff = 0.7978845608028654


def wave_table(first, second, length):
    product = (first[:, None] * second[None, :]) % length
    angle = np.float32(2.0 * math.pi / length) * product.astype(np.float32)
    scale = np.float32(math.sqrt(length))
    rounded = ml_dtypes.bfloat16
    cos = (np.cos(angle) / scale).astype(rounded).astype(np.float32)
    sin = (np.sin(angle) / scale).astype(rounded).astype(np.float32)
    return cos, sin


def lon_tables(kept, cols, lon_count, rows):
    cos, sin = wave_table(np.arange(kept), np.arange(cols), cols)
    parts = np.stack([cos, -sin], axis=1).reshape(kept, 2, lon_count, cols // lon_count)
    eye = np.eye(rows, dtype=np.float32)
    forward = np.einsum("kpgw,rs->kprgsw", parts, eye).reshape(2 * kept * rows, -1)
    return forward, forward.T


def lat_table(rows, lat_count, subs, rows_sub, rows_cut, pack_modes):
    cos, sin = wave_table(np.arange(rows), np.arange(rows), rows)
    forward = np.stack([np.stack([cos, sin], axis=1), np.stack([-sin, cos], axis=1)])
    split = forward.reshape(2, rows, 2, lat_count, RQ, subs, rows_sub // rows_cut, rows_cut)
    eye = np.eye(pack_modes, dtype=np.float32)
    return np.einsum("aqplgshr,jk->jaqglskhpr", split, eye).reshape(2 * pack_modes * rows, -1)


def constant(table):
    return jnp.asarray(table.astype(ml_dtypes.bfloat16))


def kernel_call(body, out_shape, scalars, arrays, scratch=(), anchors=(), far=(), limit=8 * MIB):
    specs = {
        space: pl.BlockSpec(memory_space=space)
        for space in (pltpu.VMEM, pltpu.SMEM, pltpu.HBM, pl.ANY)
    }
    far = [pltpu.with_memory_space_constraint(value, pltpu.HBM) for value in far]
    in_specs = [specs[pltpu.SMEM]] * len(scalars) + [specs[pltpu.VMEM]] * len(arrays)
    in_specs += [specs[pltpu.HBM]] * len(far) + [specs[pl.ANY]] * len(anchors)
    is_far = [getattr(shape, "memory_space", None) is pltpu.HBM for shape in out_shape]
    return pl.pallas_call(
        body,
        out_shape=out_shape,
        in_specs=in_specs,
        out_specs=[specs[pltpu.HBM if distant else pltpu.VMEM] for distant in is_far],
        scratch_shapes=list(scratch),
        compiler_params=pltpu.CompilerParams(vmem_limit_bytes=limit),
    )(*[value.reshape(1).astype(jnp.int32) for value in scalars], *arrays, *far, *anchors)


def gate(source, anchors):
    anywhere = pl.BlockSpec(memory_space=pl.ANY)
    return pl.pallas_call(
        lambda *refs: None,
        out_shape=jax.ShapeDtypeStruct(source.shape, source.dtype),
        in_specs=[anywhere] * (1 + len(anchors)),
        out_specs=anywhere,
        input_output_aliases={0: 0},
    )(source, *anchors)


def group_copies(source, target, sems):
    rows = target.shape[0] // RQ
    return [
        pltpu.make_async_copy(
            source.at[pl.ds(group * rows, rows)], target.at[pl.ds(group * rows, rows)], sems.at[group]
        )
        for group in range(RQ)
    ]


def pack_body(rows_sub, subs, own, field, *rest):
    sent, (slots, source, sems) = rest[:-3], rest[-3:]
    cols = source.shape[1]
    loads = group_copies(field, source, sems)
    for copy in loads:
        copy.start()
    finish(loads)
    for sub in range(subs):
        for block in range(NB):
            pieces = []
            for group in range(RQ):
                row = (group * subs + sub) * rows_sub
                piece = source[row : row + rows_sub, :, block * BS : (block + 1) * BS]
                pieces.append(piece.reshape(rows_sub * cols, BS))
            slots[sub * NB + block] = jnp.concatenate(pieces, axis=1)
    deal(sent, slots, own[0])


def unpack_body(rows_sub, subs, packed, base, result, mixed, sems):
    cols = base.shape[1]
    saves = group_copies(mixed, result, sems)
    for group in range(RQ):
        for sub in range(subs):
            row = (group * subs + sub) * rows_sub
            pieces = [
                packed[sub * NB + block, :, group * BS : (group + 1) * BS] for block in range(NB)
            ]
            update = jnp.concatenate(pieces, axis=1).reshape(rows_sub, cols, NB * BS)
            old = base[row : row + rows_sub]
            mixed[row : row + rows_sub] = (
                old.astype(jnp.float32) + update.astype(jnp.float32)
            ).astype(jnp.bfloat16)
        saves[group].start()
    finish(saves)


def product(left, right):
    return jnp.dot(left, right, preferred_element_type=jnp.float32)


def product_back(left, right):
    return lax.dot_general(
        left, right, (((1,), (1,)), ((), ())), preferred_element_type=jnp.float32
    )


def product_outer(left, right):
    return lax.dot_general(
        left, right, (((0,), (0,)), ((), ())), preferred_element_type=jnp.float32
    )


def place(slots, pieces, own):
    if len(pieces) == 1:
        slots[...] = pieces[0][...]
        return
    for offset, piece in enumerate(pieces):
        slots[jnp.bitwise_xor(own, offset)] = piece[...]


def deal(pieces, slots, own):
    if len(pieces) == 1:
        pieces[0][...] = slots[...]
        return
    for offset, piece in enumerate(pieces):
        piece[...] = slots[jnp.bitwise_xor(own, offset)]


def spectra_body(count, extra, cuts, kept, own_in, own_out, table, *rest):
    received, (sent, slots_in, slots_out) = rest[:count], (rest[count + extra : -2], *rest[-2:])
    place(slots_in, received, own_in[0])
    each = slots_in.shape[1] // cuts
    parts = []
    for cut in range(cuts):
        flat = slots_in[:, cut * each : (cut + 1) * each].reshape(-1, PACK)
        parts.append(product(table[...], flat).reshape(slots_out.shape[0] * kept, -1, PACK))
    joined = jnp.stack(parts, axis=1) if cuts > 1 else parts[0]
    slots_out[...] = joined.reshape(slots_out.shape).astype(jnp.bfloat16)
    deal(sent, slots_out, own_out[0])


def columns_body(count, extra, cuts, kept, own_in, table, *rest):
    received, (result, slots_in, slots_out, sems) = rest[:count], rest[count + extra :]
    place(slots_in, received, own_in[0])
    each = slots_out.shape[1] // cuts
    modes = slots_in.shape[0] * kept
    split = slots_in[...].astype(jnp.float32).reshape(modes, cuts, -1, PACK)
    flats = [split[:, cut].reshape(-1, PACK).astype(jnp.bfloat16) for cut in range(cuts)]
    copies = []
    for cut, flat in enumerate(flats):
        part = product(table[...], flat).astype(jnp.bfloat16)
        rows = pl.ds(cut * each, each)
        slots_out[:, rows] = part.reshape(slots_out.shape[0], each, PACK)
        copies.append(
            pltpu.make_async_copy(slots_out.at[:, rows], result.at[:, rows], sems.at[cut])
        )
        copies[-1].start()
    finish(copies)


def finish(copies):
    for copy in copies:
        copy.wait()


def load_weights(block, weights, real_imag, sems):
    copies = [
        pltpu.make_async_copy(source.at[part, block], real_imag.at[slot, part], sems.at[slot, part])
        for slot, source in enumerate(weights)
        for part in range(2)
    ]
    for copy in copies:
        copy.start()
    return copies


def complex_weights(real_imag, full):
    for slot in range(full.shape[0]):
        real, imag = real_imag[slot, 0], real_imag[slot, 1]
        full[slot, :BS] = jnp.concatenate([real, imag], axis=1)
        full[slot, BS:] = jnp.concatenate([-imag, real], axis=1)


def lat_forward(table, slots, tile, deep, rows):
    slab = slots[:, tile * deep : (tile + 1) * deep]
    flat = slab.reshape(slab.shape[0] * deep, PACK)
    stacked = jnp.concatenate(
        [flat[:, group * BS : (group + 1) * BS] for group in range(RQ)], axis=0
    )
    spectrum = product(table, stacked).astype(jnp.bfloat16)
    return [
        jnp.concatenate([spectrum[at : at + rows], spectrum[at + rows : at + 2 * rows]], axis=1)
        for at in range(0, spectrum.shape[0], 2 * rows)
    ]


def lat_inverse(table, values, slots, tile, deep):
    stacked = jnp.concatenate(
        [part for value in values for part in (value[:, :BS], value[:, BS:])], axis=0
    )
    rows = product(table, stacked).astype(jnp.bfloat16)
    each = rows.shape[0] // RQ
    packed = jnp.concatenate([rows[at : at + each] for at in range(0, RQ * each, each)], axis=1)
    slots[:, tile * deep : (tile + 1) * deep] = packed.reshape(slots.shape[0], deep, PACK)


def mode_weight(first_mode, index):
    return jnp.where(first_mode + index == 0, 1.0, 2.0).astype(jnp.float32)


def gelu(pre):
    squared = pre * pre
    tangent = jnp.tanh(gelu_coeff * (pre + 0.044715 * squared * pre))
    act = (0.5 * pre * (1.0 + tangent)).astype(jnp.bfloat16)
    return act, squared, tangent


def forward_body(members, pack_modes, member, first_mode, block, table, *rest):
    received, weights, sent = rest[:members], rest[members : members + 2], rest[members + 2 :]
    sent, rest = sent[:members], sent[members:]
    saved, anchor, slots, spec, real_imag, full, weight_sems, save_sems = rest
    anchor[...] = jnp.zeros_like(anchor)
    loads = load_weights(block[0], weights, real_imag, weight_sems)
    own = member[0]
    kept, rows, _ = spec.shape
    deep = slots.shape[1] * pack_modes // kept
    place(slots, received, own)
    lat = table[...]
    inverse = lat.T
    copies = []
    for tile in range(kept // pack_modes):
        for inner, values in enumerate(lat_forward(lat, slots, tile, deep, rows)):
            index = tile * pack_modes + inner
            spec[index, :, :WIDE] = values
            copies.append(
                pltpu.make_async_copy(spec.at[index], saved.at[index], save_sems.at[index])
            )
            copies[-1].start()
    finish(loads)
    complex_weights(real_imag, full)
    count = max(pack_modes, 2)
    for start in range(0, kept, count):
        values = spec[start : start + count].reshape(count * rows, -1)[:, :WIDE]
        act, _, _ = gelu(product(values, full[0]))
        post = product(act, full[1])
        shrunk = post - shrink_level * jnp.tanh(post / shrink_level)
        outs = [
            (mode_weight(first_mode[0], start + at) * shrunk[at * rows : (at + 1) * rows]).astype(
                jnp.bfloat16
            )
            for at in range(count)
        ]
        for at in range(0, count, pack_modes):
            tile = (start + at) // pack_modes
            lat_inverse(inverse, outs[at : at + pack_modes], slots, tile, deep)
    deal(sent, slots, own)
    finish(copies)


def backward_body(
    members, shares, pack_modes, factor, member, first_mode, lat_own, block, table, *rest
):
    received, rest = rest[:members], rest[members:]
    weights, saved, result, combined, rest = rest[:2], rest[2], rest[3], rest[4], rest[5:]
    parts, (slots, grads, cots, hidden, spec, real_imag, full, weight_sems, load_sems) = (
        rest[:shares],
        rest[shares:],
    )
    loads = load_weights(block[0], weights, real_imag, weight_sems)
    kept, rows, _ = spec.shape
    deep = slots.shape[1] * pack_modes // kept
    spec_loads = [
        pltpu.make_async_copy(saved.at[index], spec.at[index], load_sems.at[index])
        for index in range(kept)
    ]
    for copy in spec_loads:
        copy.start()
    place(slots, received, member[0])
    lat = table[...]
    for tile in range(kept // pack_modes):
        for inner, cot in enumerate(lat_forward(lat, slots, tile, deep, rows)):
            index = tile * pack_modes + inner
            weight = mode_weight(first_mode[0], index)
            cots[index] = (weight * cot.astype(jnp.float32)).astype(jnp.bfloat16)
    finish(loads)
    complex_weights(real_imag, full)
    combined[...] = full[0]
    count = max(pack_modes, 2)
    for start in range(0, kept, count):
        group = pl.ds(start, count)
        finish(spec_loads[start : start + count])
        values = spec[group].reshape(count * rows, -1)[:, :WIDE]
        pre = product(values, full[0])
        act, squared, tangent = gelu(pre)
        slope = 0.5 * (1.0 + tangent) + 0.5 * pre * (1.0 - tangent * tangent) * gelu_coeff * (
            1.0 + 3.0 * 0.044715 * squared
        )
        ratio = jnp.tanh(product(act, full[1]) / shrink_level)
        cot = cots[group].reshape(count * rows, WIDE).astype(jnp.float32)
        grad_post = (cot * (ratio * ratio)).astype(jnp.bfloat16)
        grad_pre = (product_back(grad_post, full[1]) * slope).astype(jnp.bfloat16)
        result[group] = grad_pre.reshape(count, rows, WIDE)
        hidden[group] = act.reshape(count, rows, WIDE)
        cots[group] = grad_post.reshape(count, rows, WIDE)
    modes = kept * rows
    grads_pre = result[...].reshape(modes, WIDE)
    total_first = product_outer(spec[...].reshape(modes, -1)[:, :WIDE], grads_pre)
    total_second = product_outer(
        hidden[...].reshape(modes, WIDE), cots[...].reshape(modes, WIDE)
    )
    share = grads.shape[1]
    for slot, total in enumerate((total_first, total_second)):
        real = (total[:BS, :BS] + total[BS:, BS:]) * factor
        imag = (total[:BS, BS:] - total[BS:, :BS]) * factor
        for part, value in enumerate((real, imag)):
            for at in range(0, BS, share):
                piece = ((2 * slot + part) * BS + at) // share
                grads[piece] = value[at : at + share].astype(jnp.bfloat16)
    deal(parts, grads, lat_own[0])


def input_grad_body(pack_modes, extra, member, table, grad_pre, combined, *rest):
    sent, slots = rest[extra:-1], rest[-1]
    kept = grad_pre.shape[0]
    deep = slots.shape[1] * pack_modes // kept
    inverse = table[...].T
    for tile in range(kept // pack_modes):
        backs = [
            product_back(grad_pre[index], combined[...]).astype(jnp.bfloat16)
            for index in range(tile * pack_modes, (tile + 1) * pack_modes)
        ]
        lat_inverse(inverse, backs, slots, tile, deep)
    deal(sent, slots, member[0])


def sum_body(*refs):
    refs[-1][0] = sum(value[...].astype(jnp.float32) for value in refs[:-1]).astype(jnp.bfloat16)


def join_body(first, second, joined):
    count = first.shape[0]
    joined[:count] = first[...]
    joined[count:] = second[...]


def blocks_body(own, near, other, anchor, blocks):
    for slot in range(near.shape[0]):
        blocks[jnp.bitwise_xor(own[0], 2 * slot)] = near[slot]
        blocks[jnp.bitwise_xor(own[0], 2 * slot + 1)] = other[slot]


def assemble_body(lat_count, subs, lat_own, *rest):
    gathered, (first, second, slots) = rest[:lat_count], rest[lat_count:]
    rows = gathered[0].shape[1]
    for offset, pieces in enumerate(gathered):
        start = jnp.bitwise_xor(lat_own[0], offset) * rows
        matrix, row = start // BS, pl.multiple_of(start % BS, 16)
        for block in range(NB):
            total = None
            for sub in range(subs):
                value = pieces[sub * NB + block].astype(jnp.float32)
                total = value if total is None else total + value
            slots[matrix, block, pl.ds(row, rows)] = total
    first[...] = slots[:2]
    second[...] = slots[2:]


def exchange(source):
    return lax.all_to_all(source, "lon", split_axis=0, concat_axis=0, tiled=True)


def swap(pieces, axes, partners):
    return [pieces[0]] + [
        lax.ppermute(piece, axes, partners(offset))
        for offset, piece in enumerate(pieces)
        if offset
    ]


def shards(features, cotangent, weight_first, weight_second):
    lat_count = lax.axis_size("lat")
    lon_count = lax.axis_size("lon")
    band_rows, band_cols, channels = features.shape
    rows_total = band_rows * lat_count
    cols_total = band_cols * lon_count
    kept_total = KWD * lat_count * lon_count
    subs = lon_count // NB
    members = lat_count * subs
    rows_sub = band_rows // (RQ * subs)
    rows_cut = min(rows_sub, 4)
    cuts = rows_sub // rows_cut
    kept = kept_total // members
    deep = 2 * rows_sub
    pack_modes = max(1, 16 // deep)
    lat_index = lax.axis_index("lat")
    lon_index = lax.axis_index("lon")
    block = lon_index % NB
    member = lat_index * subs + lon_index // NB
    bf16, f32 = jnp.bfloat16, jnp.float32
    array = jax.ShapeDtypeStruct

    def member_pairs(offset):
        pairs = []
        for lat in range(lat_count):
            for lon in range(lon_count):
                other = (lat * subs + lon // NB) ^ offset
                lon_other = other % subs * NB + lon % NB
                pairs.append((lat * lon_count + lon, other // subs * lon_count + lon_other))
        return pairs

    def line_pairs(count):
        return lambda offset: [(place, place ^ offset) for place in range(count)]

    lon_fwd, lon_inv = map(constant, lon_tables(kept_total, cols_total, lon_count, rows_cut))
    lat_both = constant(lat_table(rows_total, lat_count, subs, rows_sub, rows_cut, pack_modes))
    lon_piece = array((rows_sub * band_cols, PACK), bf16)
    lon_whole = array((lon_count, rows_sub * band_cols, PACK), bf16)
    mid_piece = array((kept * deep, PACK), bf16)
    lon_slots = pltpu.VMEM(lon_whole.shape, bf16)
    mid_slots = pltpu.VMEM((members, kept * deep, PACK), bf16)
    mid_limit = 14 * MIB + 5 * lat_both.size
    share = 4 * BS // lat_count

    def mid_swap(pieces):
        return swap(pieces, ("lat", "lon"), member_pairs)

    def pack(source, sent):
        body = functools.partial(pack_body, rows_sub, subs)
        scratch = [lon_slots, pltpu.VMEM(source.shape, bf16), pltpu.SemaphoreType.DMA((RQ,))]
        return kernel_call(body, sent, [lon_index], [], scratch, far=[source])

    def unpack(source, base):
        body = functools.partial(unpack_body, rows_sub, subs)
        scratch = [pltpu.VMEM(base.shape, bf16), pltpu.SemaphoreType.DMA((RQ,))]
        return kernel_call(body, [pltpu.HBM(base.shape, bf16)], [], [source, base], scratch)[0]

    def to_spectra(pieces, anchors=()):
        return kernel_call(
            functools.partial(spectra_body, len(pieces), len(anchors), cuts, kept),
            [mid_piece] * members,
            [lon_index, member],
            [lon_fwd, *pieces],
            [lon_slots, mid_slots],
            anchors,
        )

    def to_columns(pieces, anchors=()):
        return kernel_call(
            functools.partial(columns_body, members, len(anchors), cuts, kept),
            [pltpu.HBM(lon_whole.shape, bf16)],
            [member],
            [lon_inv, *pieces],
            [mid_slots, lon_slots, pltpu.SemaphoreType.DMA((cuts,))],
            anchors,
        )[0]

    modes = (kept, rows_total, STATE)
    weights = [weight_first, weight_second]
    mid_scratch = [
        pltpu.VMEM(modes, bf16),
        pltpu.VMEM((2, 2, BS, BS), bf16),
        pltpu.VMEM((2, WIDE, WIDE), bf16),
        pltpu.SemaphoreType.DMA((2, 2)),
        pltpu.SemaphoreType.DMA((kept,)),
    ]

    field = swap(pack(features, [lon_piece] * lon_count), "lon", line_pairs(lon_count))
    field_cot = exchange(gate(pack(cotangent, [lon_whole])[0], field[1:]))
    results = kernel_call(
        functools.partial(forward_body, members, pack_modes),
        [mid_piece] * members + [pltpu.HBM(modes, bf16), array((8, 128), f32)],
        [member, member * kept, block],
        [lat_both, *mid_swap(to_spectra(field))],
        [mid_slots, *mid_scratch],
        far=weights,
        limit=mid_limit,
    )
    saved, anchor = results[members:]
    spectra_cot = to_spectra([field_cot], [anchor])
    filtered = exchange(to_columns(mid_swap(results[:members]), spectra_cot[:1]))
    wide = (kept, rows_total, WIDE)
    grad_pre, combined, *parts = kernel_call(
        functools.partial(
            backward_body, members, lat_count, pack_modes, 1.0 / math.sqrt(rows_total * kept_total)
        ),
        [array(wide, bf16), array((WIDE, WIDE), bf16)] + [array((share, BS), bf16)] * lat_count,
        [member, member * kept, lat_index, block],
        [lat_both, *mid_swap(spectra_cot)],
        [
            mid_slots,
            pltpu.VMEM((lat_count, share, BS), bf16),
            pltpu.VMEM(wide, bf16),
            pltpu.VMEM(wide, bf16),
            *mid_scratch,
        ],
        far=weights + [saved],
        limit=mid_limit,
    )
    own_share = kernel_call(
        sum_body, [array((1, share, BS), bf16)], [], swap(parts, "lat", line_pairs(lat_count))
    )[0]
    back = kernel_call(
        functools.partial(input_grad_body, pack_modes, 1),
        [mid_piece] * members,
        [member],
        [lat_both, grad_pre, combined],
        [mid_slots],
        [own_share],
        limit=mid_limit,
    )
    lon_pairs = line_pairs(lon_count)
    near, step = own_share, 2
    while step < lon_count:
        joined = array((2 * near.shape[0], share, BS), bf16)
        moved = lax.ppermute(near, "lon", lon_pairs(step))
        near = kernel_call(join_body, [joined], [], [near, moved])[0]
        step *= 2
    returned = exchange(to_columns(mid_swap(back), [near]))
    mixed_field = unpack(filtered, features)
    blocks = kernel_call(
        blocks_body,
        [array((lon_count, share, BS), bf16)],
        [lon_index],
        [near, lax.ppermute(near, "lon", lon_pairs(1))],
        anchors=[mixed_field],
    )[0]

    gathered = {0: blocks}
    step = lat_count // 2
    while step:
        for offset in sorted(gathered):
            moved = lax.ppermute(gathered[offset], "lat", line_pairs(lat_count)(step))
            gathered[offset | step] = moved
        step //= 2
    gathered = [gathered[offset] for offset in range(lat_count)]
    full = array((2, NB, BS, BS), f32)
    grad_first, grad_second = kernel_call(
        functools.partial(assemble_body, lat_count, subs),
        [full, full],
        [lat_index],
        gathered,
        [pltpu.VMEM((4, NB, BS, BS), f32)],
    )
    return (mixed_field, unpack(returned, cotangent), grad_first, grad_second)


def solution(mesh):
    in_specs = (P("lat", "lon", None), P("lat", "lon", None), P(), P())
    out_specs = (P("lat", "lon", None), P("lat", "lon", None), P(), P())
    return jax.shard_map(shards, mesh=mesh, in_specs=in_specs, out_specs=out_specs, check_vma=False)
```

```python
import functools
import math

import jax
import jax.numpy as jnp
import ml_dtypes
import numpy as np
from jax import lax
from jax.experimental import pallas as pl
from jax.experimental.pallas import tpu as pltpu
from jax.sharding import PartitionSpec as P

NB = 8
BS = 96
KWD = 1
RQ = 4
PACK = RQ * BS
WIDE = 2 * BS
STATE = -(-WIDE // 128) * 128
MIB = 1024 * 1024

shrink_level = 0.01
gelu_coeff = 0.7978845608028654


def wave_table(first, second, length):
    product = (first[:, None] * second[None, :]) % length
    angle = np.float32(2.0 * math.pi / length) * product.astype(np.float32)
    scale = np.float32(math.sqrt(length))
    rounded = ml_dtypes.bfloat16
    cos = (np.cos(angle) / scale).astype(rounded).astype(np.float32)
    sin = (np.sin(angle) / scale).astype(rounded).astype(np.float32)
    return cos, sin


def lon_tables(kept, cols, lon_count, rows):
    cos, sin = wave_table(np.arange(kept), np.arange(cols), cols)
    parts = np.stack([cos, -sin], axis=1).reshape(kept, 2, lon_count, cols // lon_count)
    eye = np.eye(rows, dtype=np.float32)
    forward = np.einsum("kpgw,rs->kprgsw", parts, eye).reshape(2 * kept * rows, -1)
    return forward, forward.T


def lat_table(rows, lat_count, subs, rows_sub, rows_cut, pack_modes):
    cos, sin = wave_table(np.arange(rows), np.arange(rows), rows)
    forward = np.stack([np.stack([cos, sin], axis=1), np.stack([-sin, cos], axis=1)])
    split = forward.reshape(2, rows, 2, lat_count, RQ, subs, rows_sub // rows_cut, rows_cut)
    eye = np.eye(pack_modes, dtype=np.float32)
    return np.einsum("aqplgshr,jk->jaqglskhpr", split, eye).reshape(2 * pack_modes * rows, -1)


def constant(table):
    return jnp.asarray(table.astype(ml_dtypes.bfloat16))


def kernel_call(body, out_shape, scalars, arrays, scratch=(), anchors=(), far=(), limit=8 * MIB):
    specs = {
        space: pl.BlockSpec(memory_space=space)
        for space in (pltpu.VMEM, pltpu.SMEM, pltpu.HBM, pl.ANY)
    }
    far = [pltpu.with_memory_space_constraint(value, pltpu.HBM) for value in far]
    in_specs = [specs[pltpu.SMEM]] * len(scalars) + [specs[pltpu.VMEM]] * len(arrays)
    in_specs += [specs[pltpu.HBM]] * len(far) + [specs[pl.ANY]] * len(anchors)
    is_far = [getattr(shape, "memory_space", None) is pltpu.HBM for shape in out_shape]
    return pl.pallas_call(
        body,
        out_shape=out_shape,
        in_specs=in_specs,
        out_specs=[specs[pltpu.HBM if distant else pltpu.VMEM] for distant in is_far],
        scratch_shapes=list(scratch),
        compiler_params=pltpu.CompilerParams(vmem_limit_bytes=limit),
    )(*[value.reshape(1).astype(jnp.int32) for value in scalars], *arrays, *far, *anchors)


def gate(source, anchors):
    anywhere = pl.BlockSpec(memory_space=pl.ANY)
    return pl.pallas_call(
        lambda *refs: None,
        out_shape=jax.ShapeDtypeStruct(source.shape, source.dtype),
        in_specs=[anywhere] * (1 + len(anchors)),
        out_specs=anywhere,
        input_output_aliases={0: 0},
    )(source, *anchors)


def group_copies(source, target, sems):
    rows = target.shape[0] // RQ
    return [
        pltpu.make_async_copy(
            source.at[pl.ds(group * rows, rows)], target.at[pl.ds(group * rows, rows)], sems.at[group]
        )
        for group in range(RQ)
    ]


def join_gate(first, second, source, gated):
    near, anywhere = pl.BlockSpec(memory_space=pltpu.VMEM), pl.BlockSpec(memory_space=pl.ANY)
    joined = jax.ShapeDtypeStruct((2 * first.shape[0],) + first.shape[1:], first.dtype)
    passed = [source] if gated else []
    results = pl.pallas_call(
        join_body,
        out_shape=[joined] + [jax.ShapeDtypeStruct(value.shape, value.dtype) for value in passed],
        in_specs=[near, near] + [anywhere] * len(passed),
        out_specs=[near] + [anywhere] * len(passed),
        input_output_aliases={2: 1} if gated else {},
    )(first, second, *passed)
    return results[0], results[1] if gated else source


def pack_body(rows_sub, subs, own, field, *rest):
    sent, (slots, source, sems) = rest[:-3], rest[-3:]
    cols = source.shape[1]
    loads = group_copies(field, source, sems)
    for copy in loads:
        copy.start()
    finish(loads)
    for sub in range(subs):
        for block in range(NB):
            pieces = []
            for group in range(RQ):
                row = (group * subs + sub) * rows_sub
                piece = source[row : row + rows_sub, :, block * BS : (block + 1) * BS]
                pieces.append(piece.reshape(rows_sub * cols, BS))
            slots[sub * NB + block] = jnp.concatenate(pieces, axis=1)
    deal(sent, slots, own[0])


def unpack_body(rows_sub, subs, extra, packed, base, *rest):
    result, mixed, sems = rest[extra:]
    cols = base.shape[1]
    saves = group_copies(mixed, result, sems)
    for group in range(RQ):
        for sub in range(subs):
            row = (group * subs + sub) * rows_sub
            pieces = [
                packed[sub * NB + block, :, group * BS : (group + 1) * BS] for block in range(NB)
            ]
            update = jnp.concatenate(pieces, axis=1).reshape(rows_sub, cols, NB * BS)
            old = base[row : row + rows_sub]
            mixed[row : row + rows_sub] = (
                old.astype(jnp.float32) + update.astype(jnp.float32)
            ).astype(jnp.bfloat16)
        saves[group].start()
    finish(saves)


def product(left, right):
    return jnp.dot(left, right, preferred_element_type=jnp.float32)


def product_back(left, right):
    return lax.dot_general(
        left, right, (((1,), (1,)), ((), ())), preferred_element_type=jnp.float32
    )


def product_outer(left, right):
    return lax.dot_general(
        left, right, (((0,), (0,)), ((), ())), preferred_element_type=jnp.float32
    )


def place(slots, pieces, own):
    if len(pieces) == 1:
        slots[...] = pieces[0][...]
        return
    for offset, piece in enumerate(pieces):
        slots[jnp.bitwise_xor(own, offset)] = piece[...]


def deal(pieces, slots, own):
    if len(pieces) == 1:
        pieces[0][...] = slots[...]
        return
    for offset, piece in enumerate(pieces):
        piece[...] = slots[jnp.bitwise_xor(own, offset)]


def spectra_body(count, extra, cuts, kept, own_in, own_out, table, *rest):
    received, (sent, slots_in, slots_out) = rest[:count], (rest[count + extra : -2], *rest[-2:])
    place(slots_in, received, own_in[0])
    each = slots_in.shape[1] // cuts
    parts = []
    for cut in range(cuts):
        flat = slots_in[:, cut * each : (cut + 1) * each].reshape(-1, PACK)
        parts.append(product(table[...], flat).reshape(slots_out.shape[0] * kept, -1, PACK))
    joined = jnp.stack(parts, axis=1) if cuts > 1 else parts[0]
    slots_out[...] = joined.reshape(slots_out.shape).astype(jnp.bfloat16)
    deal(sent, slots_out, own_out[0])


def columns_body(count, extra, cuts, kept, own_in, table, *rest):
    received, (result, slots_in, slots_out, sems) = rest[:count], rest[count + extra :]
    place(slots_in, received, own_in[0])
    each = slots_out.shape[1] // cuts
    modes = slots_in.shape[0] * kept
    split = slots_in[...].astype(jnp.float32).reshape(modes, cuts, -1, PACK)
    flats = [split[:, cut].reshape(-1, PACK).astype(jnp.bfloat16) for cut in range(cuts)]
    copies = []
    for cut, flat in enumerate(flats):
        part = product(table[...], flat).astype(jnp.bfloat16)
        rows = pl.ds(cut * each, each)
        slots_out[:, rows] = part.reshape(slots_out.shape[0], each, PACK)
        copies.append(
            pltpu.make_async_copy(slots_out.at[:, rows], result.at[:, rows], sems.at[cut])
        )
        copies[-1].start()
    finish(copies)


def finish(copies):
    for copy in copies:
        copy.wait()


def load_weights(block, weights, real_imag, sems):
    copies = [
        pltpu.make_async_copy(source.at[part, block], real_imag.at[slot, part], sems.at[slot, part])
        for slot, source in enumerate(weights)
        for part in range(2)
    ]
    for copy in copies:
        copy.start()
    return copies


def complex_weights(real_imag, full):
    for slot in range(full.shape[0]):
        real, imag = real_imag[slot, 0], real_imag[slot, 1]
        full[slot, :BS] = jnp.concatenate([real, imag], axis=1)
        full[slot, BS:] = jnp.concatenate([-imag, real], axis=1)


def lat_forward(table, slots, tile, deep, rows):
    slab = slots[:, tile * deep : (tile + 1) * deep]
    flat = slab.reshape(slab.shape[0] * deep, PACK)
    stacked = jnp.concatenate(
        [flat[:, group * BS : (group + 1) * BS] for group in range(RQ)], axis=0
    )
    spectrum = product(table, stacked).astype(jnp.bfloat16)
    return [
        jnp.concatenate([spectrum[at : at + rows], spectrum[at + rows : at + 2 * rows]], axis=1)
        for at in range(0, spectrum.shape[0], 2 * rows)
    ]


def lat_inverse(table, values, slots, tile, deep):
    stacked = jnp.concatenate(
        [part for value in values for part in (value[:, :BS], value[:, BS:])], axis=0
    )
    rows = product(table, stacked).astype(jnp.bfloat16)
    each = rows.shape[0] // RQ
    packed = jnp.concatenate([rows[at : at + each] for at in range(0, RQ * each, each)], axis=1)
    slots[:, tile * deep : (tile + 1) * deep] = packed.reshape(slots.shape[0], deep, PACK)


def mode_weight(first_mode, index):
    return jnp.where(first_mode + index == 0, 1.0, 2.0).astype(jnp.float32)


def gelu(pre):
    squared = pre * pre
    tangent = jnp.tanh(gelu_coeff * (pre + 0.044715 * squared * pre))
    act = (0.5 * pre * (1.0 + tangent)).astype(jnp.bfloat16)
    return act, squared, tangent


def forward_body(members, pack_modes, member, first_mode, block, table, *rest):
    received, weights, sent = rest[:members], rest[members : members + 2], rest[members + 2 :]
    sent, rest = sent[:members], sent[members:]
    saved, anchor, slots, spec, real_imag, full, weight_sems, save_sems = rest
    anchor[...] = jnp.zeros_like(anchor)
    loads = load_weights(block[0], weights, real_imag, weight_sems)
    own = member[0]
    kept, rows, _ = spec.shape
    deep = slots.shape[1] * pack_modes // kept
    place(slots, received, own)
    lat = table[...]
    inverse = lat.T
    copies = []
    for tile in range(kept // pack_modes):
        for inner, values in enumerate(lat_forward(lat, slots, tile, deep, rows)):
            index = tile * pack_modes + inner
            spec[index, :, :WIDE] = values
            copies.append(
                pltpu.make_async_copy(spec.at[index], saved.at[index], save_sems.at[index])
            )
            copies[-1].start()
    finish(loads)
    complex_weights(real_imag, full)
    count = max(pack_modes, 2)
    for start in range(0, kept, count):
        values = spec[start : start + count].reshape(count * rows, -1)[:, :WIDE]
        act, _, _ = gelu(product(values, full[0]))
        post = product(act, full[1])
        shrunk = post - shrink_level * jnp.tanh(post / shrink_level)
        outs = [
            (mode_weight(first_mode[0], start + at) * shrunk[at * rows : (at + 1) * rows]).astype(
                jnp.bfloat16
            )
            for at in range(count)
        ]
        for at in range(0, count, pack_modes):
            tile = (start + at) // pack_modes
            lat_inverse(inverse, outs[at : at + pack_modes], slots, tile, deep)
    deal(sent, slots, own)
    finish(copies)


def backward_body(
    members, shares, pack_modes, factor, member, first_mode, lat_own, block, table, *rest
):
    received, rest = rest[:members], rest[members:]
    weights, saved, result, combined, rest = rest[:2], rest[2], rest[3], rest[4], rest[5:]
    parts, (slots, grads, cots, hidden, spec, real_imag, full, weight_sems, load_sems) = (
        rest[:shares],
        rest[shares:],
    )
    loads = load_weights(block[0], weights, real_imag, weight_sems)
    kept, rows, _ = spec.shape
    deep = slots.shape[1] * pack_modes // kept
    spec_loads = [
        pltpu.make_async_copy(saved.at[index], spec.at[index], load_sems.at[index])
        for index in range(kept)
    ]
    for copy in spec_loads:
        copy.start()
    place(slots, received, member[0])
    lat = table[...]
    for tile in range(kept // pack_modes):
        for inner, cot in enumerate(lat_forward(lat, slots, tile, deep, rows)):
            index = tile * pack_modes + inner
            weight = mode_weight(first_mode[0], index)
            cots[index] = (weight * cot.astype(jnp.float32)).astype(jnp.bfloat16)
    finish(loads)
    complex_weights(real_imag, full)
    combined[...] = full[0]
    count = max(pack_modes, 2)
    for start in range(0, kept, count):
        group = pl.ds(start, count)
        finish(spec_loads[start : start + count])
        values = spec[group].reshape(count * rows, -1)[:, :WIDE]
        pre = product(values, full[0])
        act, squared, tangent = gelu(pre)
        slope = 0.5 * (1.0 + tangent) + 0.5 * pre * (1.0 - tangent * tangent) * gelu_coeff * (
            1.0 + 3.0 * 0.044715 * squared
        )
        ratio = jnp.tanh(product(act, full[1]) / shrink_level)
        cot = cots[group].reshape(count * rows, WIDE).astype(jnp.float32)
        grad_post = (cot * (ratio * ratio)).astype(jnp.bfloat16)
        grad_pre = (product_back(grad_post, full[1]) * slope).astype(jnp.bfloat16)
        result[group] = grad_pre.reshape(count, rows, WIDE)
        hidden[group] = act.reshape(count, rows, WIDE)
        cots[group] = grad_post.reshape(count, rows, WIDE)
    modes = kept * rows
    grads_pre = result[...].reshape(modes, WIDE)
    total_first = product_outer(spec[...].reshape(modes, -1)[:, :WIDE], grads_pre)
    total_second = product_outer(
        hidden[...].reshape(modes, WIDE), cots[...].reshape(modes, WIDE)
    )
    share = grads.shape[1]
    for slot, total in enumerate((total_first, total_second)):
        real = (total[:BS, :BS] + total[BS:, BS:]) * factor
        imag = (total[:BS, BS:] - total[BS:, :BS]) * factor
        for part, value in enumerate((real, imag)):
            for at in range(0, BS, share):
                piece = ((2 * slot + part) * BS + at) // share
                grads[piece] = value[at : at + share].astype(jnp.bfloat16)
    deal(parts, grads, lat_own[0])


def input_grad_body(pack_modes, extra, member, table, grad_pre, combined, *rest):
    sent, slots = rest[extra:-1], rest[-1]
    kept = grad_pre.shape[0]
    deep = slots.shape[1] * pack_modes // kept
    inverse = table[...].T
    for tile in range(kept // pack_modes):
        backs = [
            product_back(grad_pre[index], combined[...]).astype(jnp.bfloat16)
            for index in range(tile * pack_modes, (tile + 1) * pack_modes)
        ]
        lat_inverse(inverse, backs, slots, tile, deep)
    deal(sent, slots, member[0])


def sum_body(*refs):
    refs[-1][0] = sum(value[...].astype(jnp.float32) for value in refs[:-1]).astype(jnp.bfloat16)


def join_body(first, second, *rest):
    joined, count = rest[len(rest) // 2], first.shape[0]
    joined[:count] = first[...]
    joined[count:] = second[...]


def blocks_body(own, near, other, anchor, blocks):
    for slot in range(near.shape[0]):
        blocks[jnp.bitwise_xor(own[0], 2 * slot)] = near[slot]
        blocks[jnp.bitwise_xor(own[0], 2 * slot + 1)] = other[slot]


def assemble_body(lat_count, subs, lat_own, *rest):
    gathered, (first, second, slots) = rest[:lat_count], rest[lat_count:]
    rows = gathered[0].shape[1]
    for offset, pieces in enumerate(gathered):
        start = jnp.bitwise_xor(lat_own[0], offset) * rows
        matrix, row = start // BS, pl.multiple_of(start % BS, 16)
        for block in range(NB):
            total = None
            for sub in range(subs):
                value = pieces[sub * NB + block].astype(jnp.float32)
                total = value if total is None else total + value
            slots[matrix, block, pl.ds(row, rows)] = total
    first[...] = slots[:2]
    second[...] = slots[2:]


def exchange(source):
    return lax.all_to_all(source, "lon", split_axis=0, concat_axis=0, tiled=True)


def swap(pieces, axes, partners):
    return [pieces[0]] + [
        lax.ppermute(piece, axes, partners(offset))
        for offset, piece in enumerate(pieces)
        if offset
    ]


def shards(features, cotangent, weight_first, weight_second):
    lat_count = lax.axis_size("lat")
    lon_count = lax.axis_size("lon")
    band_rows, band_cols, channels = features.shape
    rows_total = band_rows * lat_count
    cols_total = band_cols * lon_count
    kept_total = KWD * lat_count * lon_count
    subs = lon_count // NB
    members = lat_count * subs
    rows_sub = band_rows // (RQ * subs)
    rows_cut = min(rows_sub, 4)
    cuts = rows_sub // rows_cut
    kept = kept_total // members
    deep = 2 * rows_sub
    pack_modes = max(1, 16 // deep)
    lat_index = lax.axis_index("lat")
    lon_index = lax.axis_index("lon")
    block = lon_index % NB
    member = lat_index * subs + lon_index // NB
    bf16, f32 = jnp.bfloat16, jnp.float32
    array = jax.ShapeDtypeStruct

    def member_pairs(offset):
        pairs = []
        for lat in range(lat_count):
            for lon in range(lon_count):
                other = (lat * subs + lon // NB) ^ offset
                lon_other = other % subs * NB + lon % NB
                pairs.append((lat * lon_count + lon, other // subs * lon_count + lon_other))
        return pairs

    def line_pairs(count):
        return lambda offset: [(place, place ^ offset) for place in range(count)]

    lon_fwd, lon_inv = map(constant, lon_tables(kept_total, cols_total, lon_count, rows_cut))
    lat_both = constant(lat_table(rows_total, lat_count, subs, rows_sub, rows_cut, pack_modes))
    lon_piece = array((rows_sub * band_cols, PACK), bf16)
    lon_whole = array((lon_count, rows_sub * band_cols, PACK), bf16)
    mid_piece = array((kept * deep, PACK), bf16)
    lon_slots = pltpu.VMEM(lon_whole.shape, bf16)
    mid_slots = pltpu.VMEM((members, kept * deep, PACK), bf16)
    mid_limit = 14 * MIB + 5 * lat_both.size
    share = 4 * BS // lat_count

    def mid_swap(pieces):
        return swap(pieces, ("lat", "lon"), member_pairs)

    def pack(source, sent):
        body = functools.partial(pack_body, rows_sub, subs)
        scratch = [lon_slots, pltpu.VMEM(source.shape, bf16), pltpu.SemaphoreType.DMA((RQ,))]
        return kernel_call(body, sent, [lon_index], [], scratch, far=[source])

    def unpack(source, base, anchors=()):
        body = functools.partial(unpack_body, rows_sub, subs, len(anchors))
        scratch = [pltpu.VMEM(base.shape, bf16), pltpu.SemaphoreType.DMA((RQ,))]
        return kernel_call(body, [pltpu.HBM(base.shape, bf16)], [], [source, base], scratch, anchors)[0]

    def to_spectra(pieces, anchors=()):
        return kernel_call(
            functools.partial(spectra_body, len(pieces), len(anchors), cuts, kept),
            [mid_piece] * members,
            [lon_index, member],
            [lon_fwd, *pieces],
            [lon_slots, mid_slots],
            anchors,
        )

    def to_columns(pieces, anchors=()):
        return kernel_call(
            functools.partial(columns_body, members, len(anchors), cuts, kept),
            [pltpu.HBM(lon_whole.shape, bf16)],
            [member],
            [lon_inv, *pieces],
            [mid_slots, lon_slots, pltpu.SemaphoreType.DMA((cuts,))],
            anchors,
        )[0]

    modes = (kept, rows_total, STATE)
    weights = [weight_first, weight_second]
    mid_scratch = [
        pltpu.VMEM(modes, bf16),
        pltpu.VMEM((2, 2, BS, BS), bf16),
        pltpu.VMEM((2, WIDE, WIDE), bf16),
        pltpu.SemaphoreType.DMA((2, 2)),
        pltpu.SemaphoreType.DMA((kept,)),
    ]

    field = swap(pack(features, [lon_piece] * lon_count), "lon", line_pairs(lon_count))
    spectra = to_spectra(field)
    field_cot = exchange(gate(pack(cotangent, [lon_whole])[0], spectra[:1]))
    results = kernel_call(
        functools.partial(forward_body, members, pack_modes),
        [mid_piece] * members + [pltpu.HBM(modes, bf16), array((8, 128), f32)],
        [member, member * kept, block],
        [lat_both, *mid_swap(spectra)],
        [mid_slots, *mid_scratch],
        far=weights,
        limit=mid_limit,
    )
    saved, anchor = results[members:]
    spectra_cot = to_spectra([field_cot], [anchor])
    filtered = exchange(to_columns(mid_swap(results[:members]), spectra_cot[:1]))
    wide = (kept, rows_total, WIDE)
    grad_pre, combined, *parts = kernel_call(
        functools.partial(
            backward_body, members, lat_count, pack_modes, 1.0 / math.sqrt(rows_total * kept_total)
        ),
        [array(wide, bf16), array((WIDE, WIDE), bf16)] + [array((share, BS), bf16)] * lat_count,
        [member, member * kept, lat_index, block],
        [lat_both, *mid_swap(spectra_cot)],
        [
            mid_slots,
            pltpu.VMEM((lat_count, share, BS), bf16),
            pltpu.VMEM(wide, bf16),
            pltpu.VMEM(wide, bf16),
            *mid_scratch,
        ],
        far=weights + [saved],
        limit=mid_limit,
    )
    own_share = kernel_call(
        sum_body, [array((1, share, BS), bf16)], [], swap(parts, "lat", line_pairs(lat_count))
    )[0]
    back = kernel_call(
        functools.partial(input_grad_body, pack_modes, 1),
        [mid_piece] * members,
        [member],
        [lat_both, grad_pre, combined],
        [mid_slots],
        [own_share],
        limit=mid_limit,
    )
    lon_pairs = line_pairs(lon_count)
    columns = to_columns(mid_swap(back))
    near, step = own_share, 2
    while step < lon_count:
        moved = lax.ppermute(near, "lon", lon_pairs(step))
        near, columns = join_gate(near, moved, columns, step == lon_count // 2)
        step *= 2
    returned = exchange(columns)
    mixed_field = unpack(filtered, features)
    blocks = kernel_call(
        blocks_body,
        [array((lon_count, share, BS), bf16)],
        [lon_index],
        [near, lax.ppermute(near, "lon", lon_pairs(1))],
        anchors=[mixed_field],
    )[0]

    gathered = {0: blocks}
    step = lat_count // 2
    while step:
        for offset in sorted(gathered):
            moved = lax.ppermute(gathered[offset], "lat", line_pairs(lat_count)(step))
            gathered[offset | step] = moved
        step //= 2
    gathered = [gathered[offset] for offset in range(lat_count)]
    full = array((2, NB, BS, BS), f32)
    grad_first, grad_second = kernel_call(
        functools.partial(assemble_body, lat_count, subs),
        [full, full],
        [lat_index],
        gathered,
        [pltpu.VMEM((4, NB, BS, BS), f32)],
    )
    feature_grad = unpack(returned, cotangent, [grad_first])
    return (mixed_field, feature_grad, grad_first, grad_second)


def solution(mesh):
    in_specs = (P("lat", "lon", None), P("lat", "lon", None), P(), P())
    out_specs = (P("lat", "lon", None), P("lat", "lon", None), P(), P())
    return jax.shard_map(shards, mesh=mesh, in_specs=in_specs, out_specs=out_specs, check_vma=False)
```

```python
import functools
import math

import jax
import jax.numpy as jnp
import ml_dtypes
import numpy as np
from jax import lax
from jax.experimental import pallas as pl
from jax.experimental.pallas import tpu as pltpu
from jax.sharding import PartitionSpec as P

NB = 8
BS = 96
KWD = 1
RQ = 4
PACK = RQ * BS
WIDE = 2 * BS
STATE = -(-WIDE // 128) * 128
MIB = 1024 * 1024

shrink_level = 0.01
gelu_coeff = 0.7978845608028654


def wave_table(first, second, length):
    product = (first[:, None] * second[None, :]) % length
    angle = np.float32(2.0 * math.pi / length) * product.astype(np.float32)
    scale = np.float32(math.sqrt(length))
    rounded = ml_dtypes.bfloat16
    cos = (np.cos(angle) / scale).astype(rounded).astype(np.float32)
    sin = (np.sin(angle) / scale).astype(rounded).astype(np.float32)
    return cos, sin


def lon_tables(kept, cols, lon_count, rows):
    cos, sin = wave_table(np.arange(kept), np.arange(cols), cols)
    parts = np.stack([cos, -sin], axis=1).reshape(kept, 2, lon_count, cols // lon_count)
    eye = np.eye(rows, dtype=np.float32)
    forward = np.einsum("kpgw,rs->kprgsw", parts, eye).reshape(2 * kept * rows, -1)
    return forward, forward.T


def lat_table(rows, lat_count, subs, rows_sub, rows_cut, pack_modes):
    cos, sin = wave_table(np.arange(rows), np.arange(rows), rows)
    forward = np.stack([np.stack([cos, sin], axis=1), np.stack([-sin, cos], axis=1)])
    split = forward.reshape(2, rows, 2, lat_count, RQ, subs, rows_sub // rows_cut, rows_cut)
    eye = np.eye(pack_modes, dtype=np.float32)
    return np.einsum("aqplgshr,jk->jaqglskhpr", split, eye).reshape(2 * pack_modes * rows, -1)


def constant(table):
    return jnp.asarray(table.astype(ml_dtypes.bfloat16))


def kernel_call(body, out_shape, scalars, arrays, scratch=(), anchors=(), far=(), limit=8 * MIB):
    specs = {
        space: pl.BlockSpec(memory_space=space)
        for space in (pltpu.VMEM, pltpu.SMEM, pltpu.HBM, pl.ANY)
    }
    far = [pltpu.with_memory_space_constraint(value, pltpu.HBM) for value in far]
    in_specs = [specs[pltpu.SMEM]] * len(scalars) + [specs[pltpu.VMEM]] * len(arrays)
    in_specs += [specs[pltpu.HBM]] * len(far) + [specs[pl.ANY]] * len(anchors)
    is_far = [getattr(shape, "memory_space", None) is pltpu.HBM for shape in out_shape]
    return pl.pallas_call(
        body,
        out_shape=out_shape,
        in_specs=in_specs,
        out_specs=[specs[pltpu.HBM if distant else pltpu.VMEM] for distant in is_far],
        scratch_shapes=list(scratch),
        compiler_params=pltpu.CompilerParams(vmem_limit_bytes=limit),
    )(*[value.reshape(1).astype(jnp.int32) for value in scalars], *arrays, *far, *anchors)


def gate(source, anchors):
    anywhere = pl.BlockSpec(memory_space=pl.ANY)
    return pl.pallas_call(
        lambda *refs: None,
        out_shape=jax.ShapeDtypeStruct(source.shape, source.dtype),
        in_specs=[anywhere] * (1 + len(anchors)),
        out_specs=anywhere,
        input_output_aliases={0: 0},
        compiler_params=pltpu.CompilerParams(vmem_limit_bytes=8 * MIB),
    )(source, *anchors)


def group_copies(source, target, sems):
    rows = target.shape[0] // RQ
    return [
        pltpu.make_async_copy(
            source.at[pl.ds(group * rows, rows)], target.at[pl.ds(group * rows, rows)], sems.at[group]
        )
        for group in range(RQ)
    ]


def join_gate(first, second, source, gated):
    near, anywhere = pl.BlockSpec(memory_space=pltpu.VMEM), pl.BlockSpec(memory_space=pl.ANY)
    joined = jax.ShapeDtypeStruct((2 * first.shape[0],) + first.shape[1:], first.dtype)
    passed = [source] if gated else []
    results = pl.pallas_call(
        join_body,
        out_shape=[joined] + [jax.ShapeDtypeStruct(value.shape, value.dtype) for value in passed],
        in_specs=[near, near] + [anywhere] * len(passed),
        out_specs=[near] + [anywhere] * len(passed),
        input_output_aliases={2: 1} if gated else {},
        compiler_params=pltpu.CompilerParams(vmem_limit_bytes=8 * MIB),
    )(first, second, *passed)
    return results[0], results[1] if gated else source


def pack_body(rows_sub, subs, own, field, *rest):
    sent, (slots, source, sems) = rest[:-3], rest[-3:]
    cols = source.shape[1]
    loads = group_copies(field, source, sems)
    for copy in loads:
        copy.start()
    finish(loads)
    for sub in range(subs):
        for block in range(NB):
            pieces = []
            for group in range(RQ):
                row = (group * subs + sub) * rows_sub
                piece = source[row : row + rows_sub, :, block * BS : (block + 1) * BS]
                pieces.append(piece.reshape(rows_sub * cols, BS))
            slots[sub * NB + block] = jnp.concatenate(pieces, axis=1)
    deal(sent, slots, own[0])


def unpack_body(rows_sub, subs, extra, packed, base, *rest):
    result, mixed, sems = rest[extra:]
    cols = base.shape[1]
    saves = group_copies(mixed, result, sems)
    for group in range(RQ):
        for sub in range(subs):
            row = (group * subs + sub) * rows_sub
            pieces = [
                packed[sub * NB + block, :, group * BS : (group + 1) * BS] for block in range(NB)
            ]
            update = jnp.concatenate(pieces, axis=1).reshape(rows_sub, cols, NB * BS)
            old = base[row : row + rows_sub]
            mixed[row : row + rows_sub] = (
                old.astype(jnp.float32) + update.astype(jnp.float32)
            ).astype(jnp.bfloat16)
        saves[group].start()
    finish(saves)


def product(left, right):
    return jnp.dot(left, right, preferred_element_type=jnp.float32)


def product_back(left, right):
    return lax.dot_general(
        left, right, (((1,), (1,)), ((), ())), preferred_element_type=jnp.float32
    )


def product_outer(left, right):
    return lax.dot_general(
        left, right, (((0,), (0,)), ((), ())), preferred_element_type=jnp.float32
    )


def place(slots, pieces, own):
    if len(pieces) == 1:
        slots[...] = pieces[0][...]
        return
    for offset, piece in enumerate(pieces):
        slots[jnp.bitwise_xor(own, offset)] = piece[...]


def deal(pieces, slots, own):
    if len(pieces) == 1:
        pieces[0][...] = slots[...]
        return
    for offset, piece in enumerate(pieces):
        piece[...] = slots[jnp.bitwise_xor(own, offset)]


def spectra_body(count, extra, cuts, kept, own_in, own_out, table, *rest):
    received, (sent, slots_in, slots_out) = rest[:count], (rest[count + extra : -2], *rest[-2:])
    place(slots_in, received, own_in[0])
    each = slots_in.shape[1] // cuts
    parts = []
    for cut in range(cuts):
        flat = slots_in[:, cut * each : (cut + 1) * each].reshape(-1, PACK)
        parts.append(product(table[...], flat).reshape(slots_out.shape[0] * kept, -1, PACK))
    joined = jnp.stack(parts, axis=1) if cuts > 1 else parts[0]
    slots_out[...] = joined.reshape(slots_out.shape).astype(jnp.bfloat16)
    deal(sent, slots_out, own_out[0])


def columns_body(count, extra, cuts, kept, own_in, table, *rest):
    received, (result, slots_in, slots_out, sems) = rest[:count], rest[count + extra :]
    place(slots_in, received, own_in[0])
    each = slots_out.shape[1] // cuts
    modes = slots_in.shape[0] * kept
    split = slots_in[...].astype(jnp.float32).reshape(modes, cuts, -1, PACK)
    flats = [split[:, cut].reshape(-1, PACK).astype(jnp.bfloat16) for cut in range(cuts)]
    copies = []
    for cut, flat in enumerate(flats):
        part = product(table[...], flat).astype(jnp.bfloat16)
        rows = pl.ds(cut * each, each)
        slots_out[:, rows] = part.reshape(slots_out.shape[0], each, PACK)
        copies.append(
            pltpu.make_async_copy(slots_out.at[:, rows], result.at[:, rows], sems.at[cut])
        )
        copies[-1].start()
    finish(copies)


def finish(copies):
    for copy in copies:
        copy.wait()


def load_weights(block, weights, real_imag, sems):
    copies = [
        pltpu.make_async_copy(source.at[part, block], real_imag.at[slot, part], sems.at[slot, part])
        for slot, source in enumerate(weights)
        for part in range(2)
    ]
    for copy in copies:
        copy.start()
    return copies


def complex_weights(real_imag, full):
    for slot in range(full.shape[0]):
        real, imag = real_imag[slot, 0], real_imag[slot, 1]
        full[slot, :BS] = jnp.concatenate([real, imag], axis=1)
        full[slot, BS:] = jnp.concatenate([-imag, real], axis=1)


def lat_forward(table, slots, tile, deep, rows):
    slab = slots[:, tile * deep : (tile + 1) * deep]
    flat = slab.reshape(slab.shape[0] * deep, PACK)
    stacked = jnp.concatenate(
        [flat[:, group * BS : (group + 1) * BS] for group in range(RQ)], axis=0
    )
    spectrum = product(table, stacked).astype(jnp.bfloat16)
    return [
        jnp.concatenate([spectrum[at : at + rows], spectrum[at + rows : at + 2 * rows]], axis=1)
        for at in range(0, spectrum.shape[0], 2 * rows)
    ]


def lat_inverse(table, values, slots, tile, deep):
    stacked = jnp.concatenate(
        [part for value in values for part in (value[:, :BS], value[:, BS:])], axis=0
    )
    rows = product(table, stacked).astype(jnp.bfloat16)
    each = rows.shape[0] // RQ
    packed = jnp.concatenate([rows[at : at + each] for at in range(0, RQ * each, each)], axis=1)
    slots[:, tile * deep : (tile + 1) * deep] = packed.reshape(slots.shape[0], deep, PACK)


def mode_weight(first_mode, index):
    return jnp.where(first_mode + index == 0, 1.0, 2.0).astype(jnp.float32)


def gelu(pre):
    squared = pre * pre
    tangent = jnp.tanh(gelu_coeff * (pre + 0.044715 * squared * pre))
    act = (0.5 * pre * (1.0 + tangent)).astype(jnp.bfloat16)
    return act, squared, tangent


def forward_body(members, pack_modes, member, first_mode, block, table, *rest):
    received, weights, sent = rest[:members], rest[members : members + 2], rest[members + 2 :]
    sent, rest = sent[:members], sent[members:]
    saved, anchor, slots, spec, real_imag, full, weight_sems, save_sems = rest
    anchor[...] = jnp.zeros_like(anchor)
    loads = load_weights(block[0], weights, real_imag, weight_sems)
    own = member[0]
    kept, rows, _ = spec.shape
    deep = slots.shape[1] * pack_modes // kept
    place(slots, received, own)
    lat = table[...]
    inverse = lat.T
    copies = []
    for tile in range(kept // pack_modes):
        for inner, values in enumerate(lat_forward(lat, slots, tile, deep, rows)):
            index = tile * pack_modes + inner
            spec[index, :, :WIDE] = values
            copies.append(
                pltpu.make_async_copy(spec.at[index], saved.at[index], save_sems.at[index])
            )
            copies[-1].start()
    finish(loads)
    complex_weights(real_imag, full)
    count = max(pack_modes, 2)
    for start in range(0, kept, count):
        values = spec[start : start + count].reshape(count * rows, -1)[:, :WIDE]
        act, _, _ = gelu(product(values, full[0]))
        post = product(act, full[1])
        shrunk = post - shrink_level * jnp.tanh(post / shrink_level)
        outs = [
            (mode_weight(first_mode[0], start + at) * shrunk[at * rows : (at + 1) * rows]).astype(
                jnp.bfloat16
            )
            for at in range(count)
        ]
        for at in range(0, count, pack_modes):
            tile = (start + at) // pack_modes
            lat_inverse(inverse, outs[at : at + pack_modes], slots, tile, deep)
    deal(sent, slots, own)
    finish(copies)


def backward_body(
    members, shares, pack_modes, factor, member, first_mode, lat_own, block, table, *rest
):
    received, rest = rest[:members], rest[members:]
    weights, saved, result, combined, rest = rest[:2], rest[2], rest[3], rest[4], rest[5:]
    parts, (slots, grads, cots, hidden, spec, real_imag, full, weight_sems, load_sems) = (
        rest[:shares],
        rest[shares:],
    )
    loads = load_weights(block[0], weights, real_imag, weight_sems)
    kept, rows, _ = spec.shape
    deep = slots.shape[1] * pack_modes // kept
    spec_loads = [
        pltpu.make_async_copy(saved.at[index], spec.at[index], load_sems.at[index])
        for index in range(kept)
    ]
    for copy in spec_loads:
        copy.start()
    place(slots, received, member[0])
    lat = table[...]
    for tile in range(kept // pack_modes):
        for inner, cot in enumerate(lat_forward(lat, slots, tile, deep, rows)):
            index = tile * pack_modes + inner
            weight = mode_weight(first_mode[0], index)
            cots[index] = (weight * cot.astype(jnp.float32)).astype(jnp.bfloat16)
    finish(loads)
    complex_weights(real_imag, full)
    combined[...] = full[0]
    count = max(pack_modes, 2)
    for start in range(0, kept, count):
        group = pl.ds(start, count)
        finish(spec_loads[start : start + count])
        values = spec[group].reshape(count * rows, -1)[:, :WIDE]
        pre = product(values, full[0])
        act, squared, tangent = gelu(pre)
        slope = 0.5 * (1.0 + tangent) + 0.5 * pre * (1.0 - tangent * tangent) * gelu_coeff * (
            1.0 + 3.0 * 0.044715 * squared
        )
        ratio = jnp.tanh(product(act, full[1]) / shrink_level)
        cot = cots[group].reshape(count * rows, WIDE).astype(jnp.float32)
        grad_post = (cot * (ratio * ratio)).astype(jnp.bfloat16)
        grad_pre = (product_back(grad_post, full[1]) * slope).astype(jnp.bfloat16)
        result[group] = grad_pre.reshape(count, rows, WIDE)
        hidden[group] = act.reshape(count, rows, WIDE)
        cots[group] = grad_post.reshape(count, rows, WIDE)
    modes = kept * rows
    grads_pre = result[...].reshape(modes, WIDE)
    total_first = product_outer(spec[...].reshape(modes, -1)[:, :WIDE], grads_pre)
    total_second = product_outer(
        hidden[...].reshape(modes, WIDE), cots[...].reshape(modes, WIDE)
    )
    share = grads.shape[1]
    for slot, total in enumerate((total_first, total_second)):
        real = (total[:BS, :BS] + total[BS:, BS:]) * factor
        imag = (total[:BS, BS:] - total[BS:, :BS]) * factor
        for part, value in enumerate((real, imag)):
            for at in range(0, BS, share):
                piece = ((2 * slot + part) * BS + at) // share
                grads[piece] = value[at : at + share].astype(jnp.bfloat16)
    deal(parts, grads, lat_own[0])


def input_grad_body(pack_modes, extra, member, table, grad_pre, combined, *rest):
    sent, slots = rest[extra:-1], rest[-1]
    kept = grad_pre.shape[0]
    deep = slots.shape[1] * pack_modes // kept
    inverse = table[...].T
    for tile in range(kept // pack_modes):
        backs = [
            product_back(grad_pre[index], combined[...]).astype(jnp.bfloat16)
            for index in range(tile * pack_modes, (tile + 1) * pack_modes)
        ]
        lat_inverse(inverse, backs, slots, tile, deep)
    deal(sent, slots, member[0])


def sum_body(*refs):
    refs[-1][0] = sum(value[...].astype(jnp.float32) for value in refs[:-1]).astype(jnp.bfloat16)


def join_body(first, second, *rest):
    joined, count = rest[len(rest) // 2], first.shape[0]
    joined[:count] = first[...]
    joined[count:] = second[...]


def blocks_body(own, near, other, anchor, blocks):
    for slot in range(near.shape[0]):
        blocks[jnp.bitwise_xor(own[0], 2 * slot)] = near[slot]
        blocks[jnp.bitwise_xor(own[0], 2 * slot + 1)] = other[slot]


def assemble_body(lat_count, subs, lat_own, *rest):
    gathered, (first, second, slots) = rest[:lat_count], rest[lat_count:]
    rows = gathered[0].shape[1]
    for offset, pieces in enumerate(gathered):
        start = jnp.bitwise_xor(lat_own[0], offset) * rows
        matrix, row = start // BS, pl.multiple_of(start % BS, 16)
        for block in range(NB):
            total = None
            for sub in range(subs):
                value = pieces[sub * NB + block].astype(jnp.float32)
                total = value if total is None else total + value
            slots[matrix, block, pl.ds(row, rows)] = total
    first[...] = slots[:2]
    second[...] = slots[2:]


def exchange(source):
    return lax.all_to_all(source, "lon", split_axis=0, concat_axis=0, tiled=True)


def swap(pieces, axes, partners):
    return [pieces[0]] + [
        lax.ppermute(piece, axes, partners(offset))
        for offset, piece in enumerate(pieces)
        if offset
    ]


def shards(features, cotangent, weight_first, weight_second):
    lat_count = lax.axis_size("lat")
    lon_count = lax.axis_size("lon")
    band_rows, band_cols, channels = features.shape
    rows_total = band_rows * lat_count
    cols_total = band_cols * lon_count
    kept_total = KWD * lat_count * lon_count
    subs = lon_count // NB
    members = lat_count * subs
    rows_sub = band_rows // (RQ * subs)
    rows_cut = min(rows_sub, 4)
    cuts = rows_sub // rows_cut
    kept = kept_total // members
    deep = 2 * rows_sub
    pack_modes = max(1, 16 // deep)
    lat_index = lax.axis_index("lat")
    lon_index = lax.axis_index("lon")
    block = lon_index % NB
    member = lat_index * subs + lon_index // NB
    bf16, f32 = jnp.bfloat16, jnp.float32
    array = jax.ShapeDtypeStruct

    def member_pairs(offset):
        pairs = []
        for lat in range(lat_count):
            for lon in range(lon_count):
                other = (lat * subs + lon // NB) ^ offset
                lon_other = other % subs * NB + lon % NB
                pairs.append((lat * lon_count + lon, other // subs * lon_count + lon_other))
        return pairs

    def line_pairs(count):
        return lambda offset: [(place, place ^ offset) for place in range(count)]

    lon_fwd, lon_inv = map(constant, lon_tables(kept_total, cols_total, lon_count, rows_cut))
    lat_both = constant(lat_table(rows_total, lat_count, subs, rows_sub, rows_cut, pack_modes))
    lon_piece = array((rows_sub * band_cols, PACK), bf16)
    lon_whole = array((lon_count, rows_sub * band_cols, PACK), bf16)
    mid_piece = array((kept * deep, PACK), bf16)
    lon_slots = pltpu.VMEM(lon_whole.shape, bf16)
    mid_slots = pltpu.VMEM((members, kept * deep, PACK), bf16)
    mid_limit = 14 * MIB + 5 * lat_both.size
    share = 4 * BS // lat_count

    def mid_swap(pieces):
        return swap(pieces, ("lat", "lon"), member_pairs)

    def pack(source, sent):
        body = functools.partial(pack_body, rows_sub, subs)
        scratch = [lon_slots, pltpu.VMEM(source.shape, bf16), pltpu.SemaphoreType.DMA((RQ,))]
        return kernel_call(body, sent, [lon_index], [], scratch, far=[source])

    def unpack(source, base, anchors=()):
        body = functools.partial(unpack_body, rows_sub, subs, len(anchors))
        scratch = [pltpu.VMEM(base.shape, bf16), pltpu.SemaphoreType.DMA((RQ,))]
        return kernel_call(body, [pltpu.HBM(base.shape, bf16)], [], [source, base], scratch, anchors)[0]

    def to_spectra(pieces, anchors=()):
        return kernel_call(
            functools.partial(spectra_body, len(pieces), len(anchors), cuts, kept),
            [mid_piece] * members,
            [lon_index, member],
            [lon_fwd, *pieces],
            [lon_slots, mid_slots],
            anchors,
        )

    def to_columns(pieces, anchors=()):
        return kernel_call(
            functools.partial(columns_body, members, len(anchors), cuts, kept),
            [pltpu.HBM(lon_whole.shape, bf16)],
            [member],
            [lon_inv, *pieces],
            [mid_slots, lon_slots, pltpu.SemaphoreType.DMA((cuts,))],
            anchors,
        )[0]

    modes = (kept, rows_total, STATE)
    weights = [weight_first, weight_second]
    mid_scratch = [
        pltpu.VMEM(modes, bf16),
        pltpu.VMEM((2, 2, BS, BS), bf16),
        pltpu.VMEM((2, WIDE, WIDE), bf16),
        pltpu.SemaphoreType.DMA((2, 2)),
        pltpu.SemaphoreType.DMA((kept,)),
    ]

    field = swap(pack(features, [lon_piece] * lon_count), "lon", line_pairs(lon_count))
    spectra = to_spectra(field)
    field_cot = exchange(gate(pack(cotangent, [lon_whole])[0], spectra[:1]))
    results = kernel_call(
        functools.partial(forward_body, members, pack_modes),
        [mid_piece] * members + [pltpu.HBM(modes, bf16), array((8, 128), f32)],
        [member, member * kept, block],
        [lat_both, *mid_swap(spectra)],
        [mid_slots, *mid_scratch],
        far=weights,
        limit=mid_limit,
    )
    saved, anchor = results[members:]
    spectra_cot = to_spectra([field_cot], [anchor])
    filtered = exchange(to_columns(mid_swap(results[:members]), spectra_cot[:1]))
    wide = (kept, rows_total, WIDE)
    grad_pre, combined, *parts = kernel_call(
        functools.partial(
            backward_body, members, lat_count, pack_modes, 1.0 / math.sqrt(rows_total * kept_total)
        ),
        [array(wide, bf16), array((WIDE, WIDE), bf16)] + [array((share, BS), bf16)] * lat_count,
        [member, member * kept, lat_index, block],
        [lat_both, *mid_swap(spectra_cot)],
        [
            mid_slots,
            pltpu.VMEM((lat_count, share, BS), bf16),
            pltpu.VMEM(wide, bf16),
            pltpu.VMEM(wide, bf16),
            *mid_scratch,
        ],
        far=weights + [saved],
        limit=mid_limit,
    )
    own_share = kernel_call(
        sum_body, [array((1, share, BS), bf16)], [], swap(parts, "lat", line_pairs(lat_count))
    )[0]
    back = kernel_call(
        functools.partial(input_grad_body, pack_modes, 1),
        [mid_piece] * members,
        [member],
        [lat_both, grad_pre, combined],
        [mid_slots],
        [own_share],
        limit=mid_limit,
    )
    lon_pairs = line_pairs(lon_count)
    columns = to_columns(mid_swap(back))
    near, step = own_share, 2
    while step < lon_count:
        moved = lax.ppermute(near, "lon", lon_pairs(step))
        near, columns = join_gate(near, moved, columns, step == lon_count // 2)
        step *= 2
    returned = exchange(columns)
    mixed_field = unpack(filtered, features)
    blocks = kernel_call(
        blocks_body,
        [array((lon_count, share, BS), bf16)],
        [lon_index],
        [near, lax.ppermute(near, "lon", lon_pairs(1))],
        anchors=[mixed_field],
    )[0]

    gathered = {0: blocks}
    step = lat_count // 2
    while step:
        for offset in sorted(gathered):
            moved = lax.ppermute(gathered[offset], "lat", line_pairs(lat_count)(step))
            gathered[offset | step] = moved
        step //= 2
    gathered = [gathered[offset] for offset in range(lat_count)]
    full = array((2, NB, BS, BS), f32)
    grad_first, grad_second = kernel_call(
        functools.partial(assemble_body, lat_count, subs),
        [full, full],
        [lat_index],
        gathered,
        [pltpu.VMEM((4, NB, BS, BS), f32)],
    )
    feature_grad = unpack(returned, cotangent)
    return (mixed_field, feature_grad, grad_first, grad_second)


def solution(mesh):
    in_specs = (P("lat", "lon", None), P("lat", "lon", None), P(), P())
    out_specs = (P("lat", "lon", None), P("lat", "lon", None), P(), P())
    return jax.shard_map(shards, mesh=mesh, in_specs=in_specs, out_specs=out_specs, check_vma=False)
```

```python
import functools
import math

import jax
import jax.numpy as jnp
import ml_dtypes
import numpy as np
from jax import lax
from jax.experimental import pallas as pl
from jax.experimental.pallas import tpu as pltpu
from jax.sharding import PartitionSpec as P

NB = 8
BS = 96
KWD = 1
RQ = 4
PACK = RQ * BS
WIDE = 2 * BS
STATE = -(-WIDE // 128) * 128
MIB = 1024 * 1024

shrink_level = 0.01
gelu_coeff = 0.7978845608028654


def wave_table(first, second, length):
    product = (first[:, None] * second[None, :]) % length
    angle = np.float32(2.0 * math.pi / length) * product.astype(np.float32)
    scale = np.float32(math.sqrt(length))
    rounded = ml_dtypes.bfloat16
    cos = (np.cos(angle) / scale).astype(rounded).astype(np.float32)
    sin = (np.sin(angle) / scale).astype(rounded).astype(np.float32)
    return cos, sin


def lon_tables(kept, cols, lon_count, rows):
    cos, sin = wave_table(np.arange(kept), np.arange(cols), cols)
    parts = np.stack([cos, -sin], axis=1).reshape(kept, 2, lon_count, cols // lon_count)
    eye = np.eye(rows, dtype=np.float32)
    forward = np.einsum("kpgw,rs->kprgsw", parts, eye).reshape(2 * kept * rows, -1)
    return forward, forward.T


def lat_table(rows, lat_count, subs, rows_sub, rows_cut, pack_modes):
    cos, sin = wave_table(np.arange(rows), np.arange(rows), rows)
    forward = np.stack([np.stack([cos, sin], axis=1), np.stack([-sin, cos], axis=1)])
    split = forward.reshape(2, rows, 2, lat_count, RQ, subs, rows_sub // rows_cut, rows_cut)
    eye = np.eye(pack_modes, dtype=np.float32)
    return np.einsum("aqplgshr,jk->jaqglskhpr", split, eye).reshape(2 * pack_modes * rows, -1)


def constant(table):
    return jnp.asarray(table.astype(ml_dtypes.bfloat16))


def kernel_call(body, out_shape, scalars, arrays, scratch=(), anchors=(), far=(), limit=8 * MIB):
    specs = {
        space: pl.BlockSpec(memory_space=space)
        for space in (pltpu.VMEM, pltpu.SMEM, pltpu.HBM, pl.ANY)
    }
    far = [pltpu.with_memory_space_constraint(value, pltpu.HBM) for value in far]
    in_specs = [specs[pltpu.SMEM]] * len(scalars) + [specs[pltpu.VMEM]] * len(arrays)
    in_specs += [specs[pltpu.HBM]] * len(far) + [specs[pl.ANY]] * len(anchors)
    is_far = [getattr(shape, "memory_space", None) is pltpu.HBM for shape in out_shape]
    return pl.pallas_call(
        body,
        out_shape=out_shape,
        in_specs=in_specs,
        out_specs=[specs[pltpu.HBM if distant else pltpu.VMEM] for distant in is_far],
        scratch_shapes=list(scratch),
        compiler_params=pltpu.CompilerParams(vmem_limit_bytes=limit),
    )(*[value.reshape(1).astype(jnp.int32) for value in scalars], *arrays, *far, *anchors)


def gate(source, anchors):
    anywhere, distant = pl.BlockSpec(memory_space=pl.ANY), pl.BlockSpec(memory_space=pltpu.HBM)
    return pl.pallas_call(
        lambda *refs: None,
        out_shape=pltpu.HBM(source.shape, source.dtype),
        in_specs=[distant] + [anywhere] * len(anchors),
        out_specs=distant,
        input_output_aliases={0: 0},
        compiler_params=pltpu.CompilerParams(vmem_limit_bytes=8 * MIB),
    )(pltpu.with_memory_space_constraint(source, pltpu.HBM), *anchors)


def group_copies(source, target, sems):
    rows = target.shape[0] // RQ
    return [
        pltpu.make_async_copy(
            source.at[pl.ds(group * rows, rows)], target.at[pl.ds(group * rows, rows)], sems.at[group]
        )
        for group in range(RQ)
    ]


def join_gate(first, second, source, gated):
    near, distant = pl.BlockSpec(memory_space=pltpu.VMEM), pl.BlockSpec(memory_space=pltpu.HBM)
    joined = jax.ShapeDtypeStruct((2 * first.shape[0],) + first.shape[1:], first.dtype)
    passed = [pltpu.with_memory_space_constraint(source, pltpu.HBM)] if gated else []
    results = pl.pallas_call(
        join_body,
        out_shape=[joined] + [pltpu.HBM(value.shape, value.dtype) for value in passed],
        in_specs=[near, near] + [distant] * len(passed),
        out_specs=[near] + [distant] * len(passed),
        input_output_aliases={2: 1} if gated else {},
        compiler_params=pltpu.CompilerParams(vmem_limit_bytes=8 * MIB),
    )(first, second, *passed)
    return results[0], results[1] if gated else source


def pack_body(rows_sub, subs, own, field, *rest):
    sent, (slots, source, sems) = rest[:-3], rest[-3:]
    cols = source.shape[1]
    loads = group_copies(field, source, sems)
    for copy in loads:
        copy.start()
    finish(loads)
    for sub in range(subs):
        for block in range(NB):
            pieces = []
            for group in range(RQ):
                row = (group * subs + sub) * rows_sub
                piece = source[row : row + rows_sub, :, block * BS : (block + 1) * BS]
                pieces.append(piece.reshape(rows_sub * cols, BS))
            slots[sub * NB + block] = jnp.concatenate(pieces, axis=1)
    deal(sent, slots, own[0])


def unpack_body(rows_sub, subs, extra, packed, base, *rest):
    result, mixed, sems = rest[extra:]
    cols = base.shape[1]
    saves = group_copies(mixed, result, sems)
    for group in range(RQ):
        for sub in range(subs):
            row = (group * subs + sub) * rows_sub
            pieces = [
                packed[sub * NB + block, :, group * BS : (group + 1) * BS] for block in range(NB)
            ]
            update = jnp.concatenate(pieces, axis=1).reshape(rows_sub, cols, NB * BS)
            old = base[row : row + rows_sub]
            mixed[row : row + rows_sub] = (
                old.astype(jnp.float32) + update.astype(jnp.float32)
            ).astype(jnp.bfloat16)
        saves[group].start()
    finish(saves)


def product(left, right):
    return jnp.dot(left, right, preferred_element_type=jnp.float32)


def product_back(left, right):
    return lax.dot_general(
        left, right, (((1,), (1,)), ((), ())), preferred_element_type=jnp.float32
    )


def product_outer(left, right):
    return lax.dot_general(
        left, right, (((0,), (0,)), ((), ())), preferred_element_type=jnp.float32
    )


def place(slots, pieces, own):
    if len(pieces) == 1:
        slots[...] = pieces[0][...]
        return
    for offset, piece in enumerate(pieces):
        slots[jnp.bitwise_xor(own, offset)] = piece[...]


def deal(pieces, slots, own):
    if len(pieces) == 1:
        pieces[0][...] = slots[...]
        return
    for offset, piece in enumerate(pieces):
        piece[...] = slots[jnp.bitwise_xor(own, offset)]


def spectra_body(count, extra, cuts, kept, own_in, own_out, table, *rest):
    received, (sent, slots_in, slots_out) = rest[:count], (rest[count + extra : -2], *rest[-2:])
    place(slots_in, received, own_in[0])
    each = slots_in.shape[1] // cuts
    parts = []
    for cut in range(cuts):
        flat = slots_in[:, cut * each : (cut + 1) * each].reshape(-1, PACK)
        parts.append(product(table[...], flat).reshape(slots_out.shape[0] * kept, -1, PACK))
    joined = jnp.stack(parts, axis=1) if cuts > 1 else parts[0]
    slots_out[...] = joined.reshape(slots_out.shape).astype(jnp.bfloat16)
    deal(sent, slots_out, own_out[0])


def columns_body(count, extra, cuts, kept, own_in, table, *rest):
    received, (result, slots_in, slots_out, sems) = rest[:count], rest[count + extra :]
    place(slots_in, received, own_in[0])
    each = slots_out.shape[1] // cuts
    modes = slots_in.shape[0] * kept
    split = slots_in[...].astype(jnp.float32).reshape(modes, cuts, -1, PACK)
    flats = [split[:, cut].reshape(-1, PACK).astype(jnp.bfloat16) for cut in range(cuts)]
    copies = []
    for cut, flat in enumerate(flats):
        part = product(table[...], flat).astype(jnp.bfloat16)
        rows = pl.ds(cut * each, each)
        slots_out[:, rows] = part.reshape(slots_out.shape[0], each, PACK)
        copies.append(
            pltpu.make_async_copy(slots_out.at[:, rows], result.at[:, rows], sems.at[cut])
        )
        copies[-1].start()
    finish(copies)


def finish(copies):
    for copy in copies:
        copy.wait()


def load_weights(block, weights, real_imag, sems):
    copies = [
        pltpu.make_async_copy(source.at[part, block], real_imag.at[slot, part], sems.at[slot, part])
        for slot, source in enumerate(weights)
        for part in range(2)
    ]
    for copy in copies:
        copy.start()
    return copies


def complex_weights(real_imag, full):
    for slot in range(full.shape[0]):
        real, imag = real_imag[slot, 0], real_imag[slot, 1]
        full[slot, :BS] = jnp.concatenate([real, imag], axis=1)
        full[slot, BS:] = jnp.concatenate([-imag, real], axis=1)


def lat_forward(table, slots, tile, deep, rows):
    slab = slots[:, tile * deep : (tile + 1) * deep]
    flat = slab.reshape(slab.shape[0] * deep, PACK)
    stacked = jnp.concatenate(
        [flat[:, group * BS : (group + 1) * BS] for group in range(RQ)], axis=0
    )
    spectrum = product(table, stacked).astype(jnp.bfloat16)
    return [
        jnp.concatenate([spectrum[at : at + rows], spectrum[at + rows : at + 2 * rows]], axis=1)
        for at in range(0, spectrum.shape[0], 2 * rows)
    ]


def lat_inverse(table, values, slots, tile, deep):
    stacked = jnp.concatenate(
        [part for value in values for part in (value[:, :BS], value[:, BS:])], axis=0
    )
    rows = product(table, stacked).astype(jnp.bfloat16)
    each = rows.shape[0] // RQ
    packed = jnp.concatenate([rows[at : at + each] for at in range(0, RQ * each, each)], axis=1)
    slots[:, tile * deep : (tile + 1) * deep] = packed.reshape(slots.shape[0], deep, PACK)


def mode_weight(first_mode, index):
    return jnp.where(first_mode + index == 0, 1.0, 2.0).astype(jnp.float32)


def gelu(pre):
    squared = pre * pre
    tangent = jnp.tanh(gelu_coeff * (pre + 0.044715 * squared * pre))
    act = (0.5 * pre * (1.0 + tangent)).astype(jnp.bfloat16)
    return act, squared, tangent


def forward_body(members, pack_modes, member, first_mode, block, table, *rest):
    received, weights, sent = rest[:members], rest[members : members + 2], rest[members + 2 :]
    sent, rest = sent[:members], sent[members:]
    saved, anchor, slots, spec, real_imag, full, weight_sems, save_sems = rest
    anchor[...] = jnp.zeros_like(anchor)
    loads = load_weights(block[0], weights, real_imag, weight_sems)
    own = member[0]
    kept, rows, _ = spec.shape
    deep = slots.shape[1] * pack_modes // kept
    place(slots, received, own)
    lat = table[...]
    inverse = lat.T
    copies = []
    for tile in range(kept // pack_modes):
        for inner, values in enumerate(lat_forward(lat, slots, tile, deep, rows)):
            index = tile * pack_modes + inner
            spec[index, :, :WIDE] = values
            copies.append(
                pltpu.make_async_copy(spec.at[index], saved.at[index], save_sems.at[index])
            )
            copies[-1].start()
    finish(loads)
    complex_weights(real_imag, full)
    count = max(pack_modes, 2)
    for start in range(0, kept, count):
        values = spec[start : start + count].reshape(count * rows, -1)[:, :WIDE]
        act, _, _ = gelu(product(values, full[0]))
        post = product(act, full[1])
        shrunk = post - shrink_level * jnp.tanh(post / shrink_level)
        outs = [
            (mode_weight(first_mode[0], start + at) * shrunk[at * rows : (at + 1) * rows]).astype(
                jnp.bfloat16
            )
            for at in range(count)
        ]
        for at in range(0, count, pack_modes):
            tile = (start + at) // pack_modes
            lat_inverse(inverse, outs[at : at + pack_modes], slots, tile, deep)
    deal(sent, slots, own)
    finish(copies)


def backward_body(
    members, shares, pack_modes, factor, member, first_mode, lat_own, block, table, *rest
):
    received, rest = rest[:members], rest[members:]
    weights, saved, result, combined, rest = rest[:2], rest[2], rest[3], rest[4], rest[5:]
    parts, (slots, grads, cots, hidden, spec, real_imag, full, weight_sems, load_sems) = (
        rest[:shares],
        rest[shares:],
    )
    loads = load_weights(block[0], weights, real_imag, weight_sems)
    kept, rows, _ = spec.shape
    deep = slots.shape[1] * pack_modes // kept
    spec_loads = [
        pltpu.make_async_copy(saved.at[index], spec.at[index], load_sems.at[index])
        for index in range(kept)
    ]
    for copy in spec_loads:
        copy.start()
    place(slots, received, member[0])
    lat = table[...]
    for tile in range(kept // pack_modes):
        for inner, cot in enumerate(lat_forward(lat, slots, tile, deep, rows)):
            index = tile * pack_modes + inner
            weight = mode_weight(first_mode[0], index)
            cots[index] = (weight * cot.astype(jnp.float32)).astype(jnp.bfloat16)
    finish(loads)
    complex_weights(real_imag, full)
    combined[...] = full[0]
    count = max(pack_modes, 2)
    for start in range(0, kept, count):
        group = pl.ds(start, count)
        finish(spec_loads[start : start + count])
        values = spec[group].reshape(count * rows, -1)[:, :WIDE]
        pre = product(values, full[0])
        act, squared, tangent = gelu(pre)
        slope = 0.5 * (1.0 + tangent) + 0.5 * pre * (1.0 - tangent * tangent) * gelu_coeff * (
            1.0 + 3.0 * 0.044715 * squared
        )
        ratio = jnp.tanh(product(act, full[1]) / shrink_level)
        cot = cots[group].reshape(count * rows, WIDE).astype(jnp.float32)
        grad_post = (cot * (ratio * ratio)).astype(jnp.bfloat16)
        grad_pre = (product_back(grad_post, full[1]) * slope).astype(jnp.bfloat16)
        result[group] = grad_pre.reshape(count, rows, WIDE)
        hidden[group] = act.reshape(count, rows, WIDE)
        cots[group] = grad_post.reshape(count, rows, WIDE)
    modes = kept * rows
    grads_pre = result[...].reshape(modes, WIDE)
    total_first = product_outer(spec[...].reshape(modes, -1)[:, :WIDE], grads_pre)
    total_second = product_outer(
        hidden[...].reshape(modes, WIDE), cots[...].reshape(modes, WIDE)
    )
    share = grads.shape[1]
    for slot, total in enumerate((total_first, total_second)):
        real = (total[:BS, :BS] + total[BS:, BS:]) * factor
        imag = (total[:BS, BS:] - total[BS:, :BS]) * factor
        for part, value in enumerate((real, imag)):
            for at in range(0, BS, share):
                piece = ((2 * slot + part) * BS + at) // share
                grads[piece] = value[at : at + share].astype(jnp.bfloat16)
    deal(parts, grads, lat_own[0])


def input_grad_body(pack_modes, extra, member, table, grad_pre, combined, *rest):
    sent, slots = rest[extra:-1], rest[-1]
    kept = grad_pre.shape[0]
    deep = slots.shape[1] * pack_modes // kept
    inverse = table[...].T
    for tile in range(kept // pack_modes):
        backs = [
            product_back(grad_pre[index], combined[...]).astype(jnp.bfloat16)
            for index in range(tile * pack_modes, (tile + 1) * pack_modes)
        ]
        lat_inverse(inverse, backs, slots, tile, deep)
    deal(sent, slots, member[0])


def sum_body(*refs):
    refs[-1][0] = sum(value[...].astype(jnp.float32) for value in refs[:-1]).astype(jnp.bfloat16)


def join_body(first, second, *rest):
    joined, count = rest[len(rest) // 2], first.shape[0]
    joined[:count] = first[...]
    joined[count:] = second[...]


def blocks_body(own, near, other, anchor, blocks):
    for slot in range(near.shape[0]):
        blocks[jnp.bitwise_xor(own[0], 2 * slot)] = near[slot]
        blocks[jnp.bitwise_xor(own[0], 2 * slot + 1)] = other[slot]


def assemble_body(lat_count, subs, lat_own, *rest):
    gathered, (first, second, slots) = rest[:lat_count], rest[lat_count:]
    rows = gathered[0].shape[1]
    for offset, pieces in enumerate(gathered):
        start = jnp.bitwise_xor(lat_own[0], offset) * rows
        matrix, row = start // BS, pl.multiple_of(start % BS, 16)
        for block in range(NB):
            total = None
            for sub in range(subs):
                value = pieces[sub * NB + block].astype(jnp.float32)
                total = value if total is None else total + value
            slots[matrix, block, pl.ds(row, rows)] = total
    first[...] = slots[:2]
    second[...] = slots[2:]


def exchange(source):
    return lax.all_to_all(source, "lon", split_axis=0, concat_axis=0, tiled=True)


def swap(pieces, axes, partners):
    return [pieces[0]] + [
        lax.ppermute(piece, axes, partners(offset))
        for offset, piece in enumerate(pieces)
        if offset
    ]


def shards(features, cotangent, weight_first, weight_second):
    lat_count = lax.axis_size("lat")
    lon_count = lax.axis_size("lon")
    band_rows, band_cols, channels = features.shape
    rows_total = band_rows * lat_count
    cols_total = band_cols * lon_count
    kept_total = KWD * lat_count * lon_count
    subs = lon_count // NB
    members = lat_count * subs
    rows_sub = band_rows // (RQ * subs)
    rows_cut = min(rows_sub, 4)
    cuts = rows_sub // rows_cut
    kept = kept_total // members
    deep = 2 * rows_sub
    pack_modes = max(1, 16 // deep)
    lat_index = lax.axis_index("lat")
    lon_index = lax.axis_index("lon")
    block = lon_index % NB
    member = lat_index * subs + lon_index // NB
    bf16, f32 = jnp.bfloat16, jnp.float32
    array = jax.ShapeDtypeStruct

    def member_pairs(offset):
        pairs = []
        for lat in range(lat_count):
            for lon in range(lon_count):
                other = (lat * subs + lon // NB) ^ offset
                lon_other = other % subs * NB + lon % NB
                pairs.append((lat * lon_count + lon, other // subs * lon_count + lon_other))
        return pairs

    def line_pairs(count):
        return lambda offset: [(place, place ^ offset) for place in range(count)]

    lon_fwd, lon_inv = map(constant, lon_tables(kept_total, cols_total, lon_count, rows_cut))
    lat_both = constant(lat_table(rows_total, lat_count, subs, rows_sub, rows_cut, pack_modes))
    lon_piece = array((rows_sub * band_cols, PACK), bf16)
    lon_whole = array((lon_count, rows_sub * band_cols, PACK), bf16)
    mid_piece = array((kept * deep, PACK), bf16)
    lon_slots = pltpu.VMEM(lon_whole.shape, bf16)
    mid_slots = pltpu.VMEM((members, kept * deep, PACK), bf16)
    mid_limit = 14 * MIB + 5 * lat_both.size
    share = 4 * BS // lat_count

    def mid_swap(pieces):
        return swap(pieces, ("lat", "lon"), member_pairs)

    def pack(source, sent):
        body = functools.partial(pack_body, rows_sub, subs)
        scratch = [lon_slots, pltpu.VMEM(source.shape, bf16), pltpu.SemaphoreType.DMA((RQ,))]
        return kernel_call(body, sent, [lon_index], [], scratch, far=[source])

    def unpack(source, base, anchors=()):
        body = functools.partial(unpack_body, rows_sub, subs, len(anchors))
        scratch = [pltpu.VMEM(base.shape, bf16), pltpu.SemaphoreType.DMA((RQ,))]
        return kernel_call(body, [pltpu.HBM(base.shape, bf16)], [], [source, base], scratch, anchors)[0]

    def to_spectra(pieces, anchors=()):
        return kernel_call(
            functools.partial(spectra_body, len(pieces), len(anchors), cuts, kept),
            [mid_piece] * members,
            [lon_index, member],
            [lon_fwd, *pieces],
            [lon_slots, mid_slots],
            anchors,
        )

    def to_columns(pieces, anchors=()):
        return kernel_call(
            functools.partial(columns_body, members, len(anchors), cuts, kept),
            [pltpu.HBM(lon_whole.shape, bf16)],
            [member],
            [lon_inv, *pieces],
            [mid_slots, lon_slots, pltpu.SemaphoreType.DMA((cuts,))],
            anchors,
        )[0]

    modes = (kept, rows_total, STATE)
    weights = [weight_first, weight_second]
    mid_scratch = [
        pltpu.VMEM(modes, bf16),
        pltpu.VMEM((2, 2, BS, BS), bf16),
        pltpu.VMEM((2, WIDE, WIDE), bf16),
        pltpu.SemaphoreType.DMA((2, 2)),
        pltpu.SemaphoreType.DMA((kept,)),
    ]

    field = swap(pack(features, [lon_piece] * lon_count), "lon", line_pairs(lon_count))
    spectra = to_spectra(field)
    field_cot = exchange(gate(pack(cotangent, [lon_whole])[0], spectra[:1]))
    results = kernel_call(
        functools.partial(forward_body, members, pack_modes),
        [mid_piece] * members + [pltpu.HBM(modes, bf16), array((8, 128), f32)],
        [member, member * kept, block],
        [lat_both, *mid_swap(spectra)],
        [mid_slots, *mid_scratch],
        far=weights,
        limit=mid_limit,
    )
    saved, anchor = results[members:]
    spectra_cot = to_spectra([field_cot], [anchor])
    filtered = exchange(to_columns(mid_swap(results[:members]), spectra_cot[:1]))
    wide = (kept, rows_total, WIDE)
    grad_pre, combined, *parts = kernel_call(
        functools.partial(
            backward_body, members, lat_count, pack_modes, 1.0 / math.sqrt(rows_total * kept_total)
        ),
        [array(wide, bf16), array((WIDE, WIDE), bf16)] + [array((share, BS), bf16)] * lat_count,
        [member, member * kept, lat_index, block],
        [lat_both, *mid_swap(spectra_cot)],
        [
            mid_slots,
            pltpu.VMEM((lat_count, share, BS), bf16),
            pltpu.VMEM(wide, bf16),
            pltpu.VMEM(wide, bf16),
            *mid_scratch,
        ],
        far=weights + [saved],
        limit=mid_limit,
    )
    own_share = kernel_call(
        sum_body, [array((1, share, BS), bf16)], [], swap(parts, "lat", line_pairs(lat_count))
    )[0]
    back = kernel_call(
        functools.partial(input_grad_body, pack_modes, 1),
        [mid_piece] * members,
        [member],
        [lat_both, grad_pre, combined],
        [mid_slots],
        [own_share],
        limit=mid_limit,
    )
    lon_pairs = line_pairs(lon_count)
    columns = to_columns(mid_swap(back))
    near, step = own_share, 2
    while step < lon_count:
        moved = lax.ppermute(near, "lon", lon_pairs(step))
        near, columns = join_gate(near, moved, columns, step == lon_count // 2)
        step *= 2
    returned = exchange(columns)
    mixed_field = unpack(filtered, features)
    blocks = kernel_call(
        blocks_body,
        [array((lon_count, share, BS), bf16)],
        [lon_index],
        [near, lax.ppermute(near, "lon", lon_pairs(1))],
        anchors=[mixed_field],
    )[0]

    gathered = {0: blocks}
    step = lat_count // 2
    while step:
        for offset in sorted(gathered):
            moved = lax.ppermute(gathered[offset], "lat", line_pairs(lat_count)(step))
            gathered[offset | step] = moved
        step //= 2
    gathered = [gathered[offset] for offset in range(lat_count)]
    full = array((2, NB, BS, BS), f32)
    grad_first, grad_second = kernel_call(
        functools.partial(assemble_body, lat_count, subs),
        [full, full],
        [lat_index],
        gathered,
        [pltpu.VMEM((4, NB, BS, BS), f32)],
    )
    feature_grad = unpack(returned, cotangent)
    return (mixed_field, feature_grad, grad_first, grad_second)


def solution(mesh):
    in_specs = (P("lat", "lon", None), P("lat", "lon", None), P(), P())
    out_specs = (P("lat", "lon", None), P("lat", "lon", None), P(), P())
    return jax.shard_map(shards, mesh=mesh, in_specs=in_specs, out_specs=out_specs, check_vma=False)
```

```python
import functools
import math

import jax
import jax.numpy as jnp
import ml_dtypes
import numpy as np
from jax import lax
from jax.experimental import pallas as pl
from jax.experimental.pallas import tpu as pltpu
from jax.sharding import PartitionSpec as P

NB = 8
BS = 96
KWD = 1
RQ = 4
PACK = RQ * BS
WIDE = 2 * BS
STATE = -(-WIDE // 128) * 128
MIB = 1024 * 1024

shrink_level = 0.01
gelu_coeff = 0.7978845608028654


def wave_table(first, second, length):
    product = (first[:, None] * second[None, :]) % length
    angle = np.float32(2.0 * math.pi / length) * product.astype(np.float32)
    scale = np.float32(math.sqrt(length))
    rounded = ml_dtypes.bfloat16
    cos = (np.cos(angle) / scale).astype(rounded).astype(np.float32)
    sin = (np.sin(angle) / scale).astype(rounded).astype(np.float32)
    return cos, sin


def lon_tables(kept, cols, lon_count, rows):
    cos, sin = wave_table(np.arange(kept), np.arange(cols), cols)
    parts = np.stack([cos, -sin], axis=1).reshape(kept, 2, lon_count, cols // lon_count)
    eye = np.eye(rows, dtype=np.float32)
    forward = np.einsum("kpgw,rs->kprgsw", parts, eye).reshape(2 * kept * rows, -1)
    return forward, forward.T


def lat_table(rows, lat_count, subs, rows_sub, rows_cut, pack_modes):
    cos, sin = wave_table(np.arange(rows), np.arange(rows), rows)
    forward = np.stack([np.stack([cos, sin], axis=1), np.stack([-sin, cos], axis=1)])
    split = forward.reshape(2, rows, 2, lat_count, RQ, subs, rows_sub // rows_cut, rows_cut)
    eye = np.eye(pack_modes, dtype=np.float32)
    return np.einsum("aqplgshr,jk->jaqglskhpr", split, eye).reshape(2 * pack_modes * rows, -1)


def constant(table):
    return jnp.asarray(table.astype(ml_dtypes.bfloat16))


def kernel_call(body, out_shape, scalars, arrays, scratch=(), anchors=(), far=(), limit=8 * MIB):
    specs = {
        space: pl.BlockSpec(memory_space=space)
        for space in (pltpu.VMEM, pltpu.SMEM, pltpu.HBM, pl.ANY)
    }
    far = [pltpu.with_memory_space_constraint(value, pltpu.HBM) for value in far]
    in_specs = [specs[pltpu.SMEM]] * len(scalars) + [specs[pltpu.VMEM]] * len(arrays)
    in_specs += [specs[pltpu.HBM]] * len(far) + [specs[pl.ANY]] * len(anchors)
    is_far = [getattr(shape, "memory_space", None) is pltpu.HBM for shape in out_shape]
    return pl.pallas_call(
        body,
        out_shape=out_shape,
        in_specs=in_specs,
        out_specs=[specs[pltpu.HBM if distant else pltpu.VMEM] for distant in is_far],
        scratch_shapes=list(scratch),
        compiler_params=pltpu.CompilerParams(vmem_limit_bytes=limit),
    )(*[value.reshape(1).astype(jnp.int32) for value in scalars], *arrays, *far, *anchors)


def gate(source, anchors):
    anywhere, distant = pl.BlockSpec(memory_space=pl.ANY), pl.BlockSpec(memory_space=pltpu.HBM)
    return pl.pallas_call(
        lambda *refs: None,
        out_shape=pltpu.HBM(source.shape, source.dtype),
        in_specs=[distant] + [anywhere] * len(anchors),
        out_specs=distant,
        input_output_aliases={0: 0},
        compiler_params=pltpu.CompilerParams(vmem_limit_bytes=8 * MIB),
    )(pltpu.with_memory_space_constraint(source, pltpu.HBM), *anchors)


def group_copies(source, target, sems):
    rows = target.shape[0] // RQ
    return [
        pltpu.make_async_copy(
            source.at[pl.ds(group * rows, rows)], target.at[pl.ds(group * rows, rows)], sems.at[group]
        )
        for group in range(RQ)
    ]


def join_gate(first, second, source, gated):
    near, distant = pl.BlockSpec(memory_space=pltpu.VMEM), pl.BlockSpec(memory_space=pltpu.HBM)
    joined = jax.ShapeDtypeStruct((2 * first.shape[0],) + first.shape[1:], first.dtype)
    passed = [pltpu.with_memory_space_constraint(source, pltpu.HBM)] if gated else []
    results = pl.pallas_call(
        join_body,
        out_shape=[joined] + [pltpu.HBM(value.shape, value.dtype) for value in passed],
        in_specs=[near, near] + [distant] * len(passed),
        out_specs=[near] + [distant] * len(passed),
        input_output_aliases={2: 1} if gated else {},
        compiler_params=pltpu.CompilerParams(vmem_limit_bytes=8 * MIB),
    )(first, second, *passed)
    return results[0], results[1] if gated else source


def pack_body(rows_sub, subs, own, field, *rest):
    sent, (slots, source, sems) = rest[:-3], rest[-3:]
    cols = source.shape[1]
    loads = group_copies(field, source, sems)
    for copy in loads:
        copy.start()
    finish(loads)
    for sub in range(subs):
        for block in range(NB):
            pieces = []
            for group in range(RQ):
                row = (group * subs + sub) * rows_sub
                piece = source[row : row + rows_sub, :, block * BS : (block + 1) * BS]
                pieces.append(piece.reshape(rows_sub * cols, BS))
            slots[sub * NB + block] = jnp.concatenate(pieces, axis=1)
    deal(sent, slots, own[0])


def unpack_body(rows_sub, subs, packed, base, result, mixed, sems):
    cols = base.shape[1]
    saves = group_copies(mixed, result, sems)
    for group in range(RQ):
        for sub in range(subs):
            row = (group * subs + sub) * rows_sub
            pieces = [
                packed[sub * NB + block, :, group * BS : (group + 1) * BS] for block in range(NB)
            ]
            update = jnp.concatenate(pieces, axis=1).reshape(rows_sub, cols, NB * BS)
            old = base[row : row + rows_sub]
            mixed[row : row + rows_sub] = (
                old.astype(jnp.float32) + update.astype(jnp.float32)
            ).astype(jnp.bfloat16)
        saves[group].start()
    finish(saves)


def product(left, right):
    return jnp.dot(left, right, preferred_element_type=jnp.float32)


def product_back(left, right):
    return lax.dot_general(
        left, right, (((1,), (1,)), ((), ())), preferred_element_type=jnp.float32
    )


def product_outer(left, right):
    return lax.dot_general(
        left, right, (((0,), (0,)), ((), ())), preferred_element_type=jnp.float32
    )


def place(slots, pieces, own):
    if len(pieces) == 1:
        slots[...] = pieces[0][...]
        return
    for offset, piece in enumerate(pieces):
        slots[jnp.bitwise_xor(own, offset)] = piece[...]


def deal(pieces, slots, own):
    if len(pieces) == 1:
        pieces[0][...] = slots[...]
        return
    for offset, piece in enumerate(pieces):
        piece[...] = slots[jnp.bitwise_xor(own, offset)]


def spectra_body(count, extra, cuts, kept, own_in, own_out, table, *rest):
    received, (sent, slots_in, slots_out) = rest[:count], (rest[count + extra : -2], *rest[-2:])
    place(slots_in, received, own_in[0])
    each = slots_in.shape[1] // cuts
    parts = []
    for cut in range(cuts):
        flat = slots_in[:, cut * each : (cut + 1) * each].reshape(-1, PACK)
        parts.append(product(table[...], flat).reshape(slots_out.shape[0] * kept, -1, PACK))
    joined = jnp.stack(parts, axis=1) if cuts > 1 else parts[0]
    slots_out[...] = joined.reshape(slots_out.shape).astype(jnp.bfloat16)
    deal(sent, slots_out, own_out[0])


def columns_body(count, extra, cuts, kept, own_in, table, *rest):
    received, (result, slots_in, slots_out, sems) = rest[:count], rest[count + extra :]
    place(slots_in, received, own_in[0])
    each = slots_out.shape[1] // cuts
    modes = slots_in.shape[0] * kept
    split = slots_in[...].astype(jnp.float32).reshape(modes, cuts, -1, PACK)
    flats = [split[:, cut].reshape(-1, PACK).astype(jnp.bfloat16) for cut in range(cuts)]
    copies = []
    for cut, flat in enumerate(flats):
        part = product(table[...], flat).astype(jnp.bfloat16)
        rows = pl.ds(cut * each, each)
        slots_out[:, rows] = part.reshape(slots_out.shape[0], each, PACK)
        copies.append(
            pltpu.make_async_copy(slots_out.at[:, rows], result.at[:, rows], sems.at[cut])
        )
        copies[-1].start()
    finish(copies)


def finish(copies):
    for copy in copies:
        copy.wait()


def load_weights(block, weights, real_imag, sems):
    copies = [
        pltpu.make_async_copy(source.at[part, block], real_imag.at[slot, part], sems.at[slot, part])
        for slot, source in enumerate(weights)
        for part in range(2)
    ]
    for copy in copies:
        copy.start()
    return copies


def complex_weights(real_imag, full):
    for slot in range(full.shape[0]):
        real, imag = real_imag[slot, 0], real_imag[slot, 1]
        full[slot, :BS] = jnp.concatenate([real, imag], axis=1)
        full[slot, BS:] = jnp.concatenate([-imag, real], axis=1)


def lat_forward(table, slots, tile, deep, rows):
    slab = slots[:, tile * deep : (tile + 1) * deep]
    flat = slab.reshape(slab.shape[0] * deep, PACK)
    stacked = jnp.concatenate(
        [flat[:, group * BS : (group + 1) * BS] for group in range(RQ)], axis=0
    )
    spectrum = product(table, stacked).astype(jnp.bfloat16)
    return [
        jnp.concatenate([spectrum[at : at + rows], spectrum[at + rows : at + 2 * rows]], axis=1)
        for at in range(0, spectrum.shape[0], 2 * rows)
    ]


def lat_inverse(table, values, slots, tile, deep):
    stacked = jnp.concatenate(
        [part for value in values for part in (value[:, :BS], value[:, BS:])], axis=0
    )
    rows = product(table, stacked).astype(jnp.bfloat16)
    each = rows.shape[0] // RQ
    packed = jnp.concatenate([rows[at : at + each] for at in range(0, RQ * each, each)], axis=1)
    slots[:, tile * deep : (tile + 1) * deep] = packed.reshape(slots.shape[0], deep, PACK)


def mode_weight(first_mode, index):
    return jnp.where(first_mode + index == 0, 1.0, 2.0).astype(jnp.float32)


def gelu(pre):
    squared = pre * pre
    tangent = jnp.tanh(gelu_coeff * (pre + 0.044715 * squared * pre))
    act = (0.5 * pre * (1.0 + tangent)).astype(jnp.bfloat16)
    return act, squared, tangent


def forward_body(members, pack_modes, member, first_mode, block, table, *rest):
    received, weights, sent = rest[:members], rest[members : members + 2], rest[members + 2 :]
    sent, rest = sent[:members], sent[members:]
    saved, anchor, slots, spec, real_imag, full, weight_sems, save_sems = rest
    anchor[...] = jnp.zeros_like(anchor)
    loads = load_weights(block[0], weights, real_imag, weight_sems)
    own = member[0]
    kept, rows, _ = spec.shape
    deep = slots.shape[1] * pack_modes // kept
    place(slots, received, own)
    lat = table[...]
    inverse = lat.T
    copies = []
    for tile in range(kept // pack_modes):
        for inner, values in enumerate(lat_forward(lat, slots, tile, deep, rows)):
            index = tile * pack_modes + inner
            spec[index, :, :WIDE] = values
            copies.append(
                pltpu.make_async_copy(spec.at[index], saved.at[index], save_sems.at[index])
            )
            copies[-1].start()
    finish(loads)
    complex_weights(real_imag, full)
    count = max(pack_modes, 2)
    for start in range(0, kept, count):
        values = spec[start : start + count].reshape(count * rows, -1)[:, :WIDE]
        act, _, _ = gelu(product(values, full[0]))
        post = product(act, full[1])
        shrunk = post - shrink_level * jnp.tanh(post / shrink_level)
        outs = [
            (mode_weight(first_mode[0], start + at) * shrunk[at * rows : (at + 1) * rows]).astype(
                jnp.bfloat16
            )
            for at in range(count)
        ]
        for at in range(0, count, pack_modes):
            tile = (start + at) // pack_modes
            lat_inverse(inverse, outs[at : at + pack_modes], slots, tile, deep)
    deal(sent, slots, own)
    finish(copies)


def backward_body(
    members, shares, pack_modes, factor, member, first_mode, lat_own, block, table, *rest
):
    received, rest = rest[:members], rest[members:]
    weights, saved, result, combined, rest = rest[:2], rest[2], rest[3], rest[4], rest[5:]
    parts, (slots, grads, cots, hidden, spec, real_imag, full, weight_sems, load_sems) = (
        rest[:shares],
        rest[shares:],
    )
    loads = load_weights(block[0], weights, real_imag, weight_sems)
    kept, rows, _ = spec.shape
    deep = slots.shape[1] * pack_modes // kept
    spec_loads = [
        pltpu.make_async_copy(saved.at[index], spec.at[index], load_sems.at[index])
        for index in range(kept)
    ]
    for copy in spec_loads:
        copy.start()
    place(slots, received, member[0])
    lat = table[...]
    for tile in range(kept // pack_modes):
        for inner, cot in enumerate(lat_forward(lat, slots, tile, deep, rows)):
            index = tile * pack_modes + inner
            weight = mode_weight(first_mode[0], index)
            cots[index] = (weight * cot.astype(jnp.float32)).astype(jnp.bfloat16)
    finish(loads)
    complex_weights(real_imag, full)
    combined[...] = full[0]
    count = max(pack_modes, 2)
    for start in range(0, kept, count):
        group = pl.ds(start, count)
        finish(spec_loads[start : start + count])
        values = spec[group].reshape(count * rows, -1)[:, :WIDE]
        pre = product(values, full[0])
        act, squared, tangent = gelu(pre)
        slope = 0.5 * (1.0 + tangent) + 0.5 * pre * (1.0 - tangent * tangent) * gelu_coeff * (
            1.0 + 3.0 * 0.044715 * squared
        )
        ratio = jnp.tanh(product(act, full[1]) / shrink_level)
        cot = cots[group].reshape(count * rows, WIDE).astype(jnp.float32)
        grad_post = (cot * (ratio * ratio)).astype(jnp.bfloat16)
        grad_pre = (product_back(grad_post, full[1]) * slope).astype(jnp.bfloat16)
        result[group] = grad_pre.reshape(count, rows, WIDE)
        hidden[group] = act.reshape(count, rows, WIDE)
        cots[group] = grad_post.reshape(count, rows, WIDE)
    modes = kept * rows
    grads_pre = result[...].reshape(modes, WIDE)
    total_first = product_outer(spec[...].reshape(modes, -1)[:, :WIDE], grads_pre)
    total_second = product_outer(
        hidden[...].reshape(modes, WIDE), cots[...].reshape(modes, WIDE)
    )
    share = grads.shape[1]
    for slot, total in enumerate((total_first, total_second)):
        real = (total[:BS, :BS] + total[BS:, BS:]) * factor
        imag = (total[:BS, BS:] - total[BS:, :BS]) * factor
        for part, value in enumerate((real, imag)):
            for at in range(0, BS, share):
                piece = ((2 * slot + part) * BS + at) // share
                grads[piece] = value[at : at + share].astype(jnp.bfloat16)
    deal(parts, grads, lat_own[0])


def input_grad_body(pack_modes, extra, member, table, grad_pre, combined, *rest):
    sent, slots = rest[extra:-1], rest[-1]
    kept = grad_pre.shape[0]
    deep = slots.shape[1] * pack_modes // kept
    inverse = table[...].T
    for tile in range(kept // pack_modes):
        backs = [
            product_back(grad_pre[index], combined[...]).astype(jnp.bfloat16)
            for index in range(tile * pack_modes, (tile + 1) * pack_modes)
        ]
        lat_inverse(inverse, backs, slots, tile, deep)
    deal(sent, slots, member[0])


def sum_body(*refs):
    refs[-1][0] = sum(value[...].astype(jnp.float32) for value in refs[:-1]).astype(jnp.bfloat16)


def join_body(first, second, *rest):
    joined, count = rest[len(rest) // 2], first.shape[0]
    joined[:count] = first[...]
    joined[count:] = second[...]


def blocks_body(own, near, other, anchor, blocks):
    for slot in range(near.shape[0]):
        blocks[jnp.bitwise_xor(own[0], 2 * slot)] = near[slot]
        blocks[jnp.bitwise_xor(own[0], 2 * slot + 1)] = other[slot]


def last_body(lat_count, rows_sub, subs, lat_own, packed, base, *rest):
    gathered, (result, first, second, mixed, sems, slots, grad_sems) = (
        rest[:lat_count],
        rest[lat_count:],
    )
    assemble(lat_own, gathered, slots, subs)
    copies = [
        pltpu.make_async_copy(slots.at[pl.ds(2 * at, 2)], full, grad_sems.at[at])
        for at, full in enumerate((first, second))
    ]
    for copy in copies:
        copy.start()
    unpack_body(rows_sub, subs, packed, base, result, mixed, sems)
    finish(copies)


def assemble(lat_own, gathered, slots, subs):
    rows = gathered[0].shape[1]
    for offset, pieces in enumerate(gathered):
        start = jnp.bitwise_xor(lat_own[0], offset) * rows
        matrix, row = start // BS, pl.multiple_of(start % BS, 16)
        for block in range(NB):
            total = None
            for sub in range(subs):
                value = pieces[sub * NB + block].astype(jnp.float32)
                total = value if total is None else total + value
            slots[matrix, block, pl.ds(row, rows)] = total


def exchange(source):
    return lax.all_to_all(source, "lon", split_axis=0, concat_axis=0, tiled=True)


def swap(pieces, axes, partners):
    return [pieces[0]] + [
        lax.ppermute(piece, axes, partners(offset))
        for offset, piece in enumerate(pieces)
        if offset
    ]


def shards(features, cotangent, weight_first, weight_second):
    lat_count = lax.axis_size("lat")
    lon_count = lax.axis_size("lon")
    band_rows, band_cols, channels = features.shape
    rows_total = band_rows * lat_count
    cols_total = band_cols * lon_count
    kept_total = KWD * lat_count * lon_count
    subs = lon_count // NB
    members = lat_count * subs
    rows_sub = band_rows // (RQ * subs)
    rows_cut = min(rows_sub, 4)
    cuts = rows_sub // rows_cut
    kept = kept_total // members
    deep = 2 * rows_sub
    pack_modes = max(1, 16 // deep)
    lat_index = lax.axis_index("lat")
    lon_index = lax.axis_index("lon")
    block = lon_index % NB
    member = lat_index * subs + lon_index // NB
    bf16, f32 = jnp.bfloat16, jnp.float32
    array = jax.ShapeDtypeStruct

    def member_pairs(offset):
        pairs = []
        for lat in range(lat_count):
            for lon in range(lon_count):
                other = (lat * subs + lon // NB) ^ offset
                lon_other = other % subs * NB + lon % NB
                pairs.append((lat * lon_count + lon, other // subs * lon_count + lon_other))
        return pairs

    def line_pairs(count):
        return lambda offset: [(place, place ^ offset) for place in range(count)]

    lon_fwd, lon_inv = map(constant, lon_tables(kept_total, cols_total, lon_count, rows_cut))
    lat_both = constant(lat_table(rows_total, lat_count, subs, rows_sub, rows_cut, pack_modes))
    lon_piece = array((rows_sub * band_cols, PACK), bf16)
    lon_whole = array((lon_count, rows_sub * band_cols, PACK), bf16)
    mid_piece = array((kept * deep, PACK), bf16)
    lon_slots = pltpu.VMEM(lon_whole.shape, bf16)
    mid_slots = pltpu.VMEM((members, kept * deep, PACK), bf16)
    mid_limit = 14 * MIB + 5 * lat_both.size
    share = 4 * BS // lat_count

    def mid_swap(pieces):
        return swap(pieces, ("lat", "lon"), member_pairs)

    def pack(source, sent):
        body = functools.partial(pack_body, rows_sub, subs)
        scratch = [lon_slots, pltpu.VMEM(source.shape, bf16), pltpu.SemaphoreType.DMA((RQ,))]
        return kernel_call(body, sent, [lon_index], [], scratch, far=[source])

    unpack_scratch = [pltpu.VMEM(features.shape, bf16), pltpu.SemaphoreType.DMA((RQ,))]
    unpacked = pltpu.HBM(features.shape, bf16)

    def to_spectra(pieces, anchors=()):
        return kernel_call(
            functools.partial(spectra_body, len(pieces), len(anchors), cuts, kept),
            [mid_piece] * members,
            [lon_index, member],
            [lon_fwd, *pieces],
            [lon_slots, mid_slots],
            anchors,
        )

    def to_columns(pieces, anchors=()):
        return kernel_call(
            functools.partial(columns_body, members, len(anchors), cuts, kept),
            [pltpu.HBM(lon_whole.shape, bf16)],
            [member],
            [lon_inv, *pieces],
            [mid_slots, lon_slots, pltpu.SemaphoreType.DMA((cuts,))],
            anchors,
        )[0]

    modes = (kept, rows_total, STATE)
    weights = [weight_first, weight_second]
    mid_scratch = [
        pltpu.VMEM(modes, bf16),
        pltpu.VMEM((2, 2, BS, BS), bf16),
        pltpu.VMEM((2, WIDE, WIDE), bf16),
        pltpu.SemaphoreType.DMA((2, 2)),
        pltpu.SemaphoreType.DMA((kept,)),
    ]

    field = swap(pack(features, [lon_piece] * lon_count), "lon", line_pairs(lon_count))
    spectra = to_spectra(field)
    field_cot = exchange(gate(pack(cotangent, [lon_whole])[0], spectra[:1]))
    results = kernel_call(
        functools.partial(forward_body, members, pack_modes),
        [mid_piece] * members + [pltpu.HBM(modes, bf16), array((8, 128), f32)],
        [member, member * kept, block],
        [lat_both, *mid_swap(spectra)],
        [mid_slots, *mid_scratch],
        far=weights,
        limit=mid_limit,
    )
    saved, anchor = results[members:]
    spectra_cot = to_spectra([field_cot], [anchor])
    filtered = exchange(to_columns(mid_swap(results[:members]), spectra_cot[:1]))
    wide = (kept, rows_total, WIDE)
    grad_pre, combined, *parts = kernel_call(
        functools.partial(
            backward_body, members, lat_count, pack_modes, 1.0 / math.sqrt(rows_total * kept_total)
        ),
        [array(wide, bf16), array((WIDE, WIDE), bf16)] + [array((share, BS), bf16)] * lat_count,
        [member, member * kept, lat_index, block],
        [lat_both, *mid_swap(spectra_cot)],
        [
            mid_slots,
            pltpu.VMEM((lat_count, share, BS), bf16),
            pltpu.VMEM(wide, bf16),
            pltpu.VMEM(wide, bf16),
            *mid_scratch,
        ],
        far=weights + [saved],
        limit=mid_limit,
    )
    own_share = kernel_call(
        sum_body, [array((1, share, BS), bf16)], [], swap(parts, "lat", line_pairs(lat_count))
    )[0]
    back = kernel_call(
        functools.partial(input_grad_body, pack_modes, 1),
        [mid_piece] * members,
        [member],
        [lat_both, grad_pre, combined],
        [mid_slots],
        [own_share],
        limit=mid_limit,
    )
    lon_pairs = line_pairs(lon_count)
    columns = to_columns(mid_swap(back))
    near, step = own_share, 2
    while step < lon_count:
        moved = lax.ppermute(near, "lon", lon_pairs(step))
        near, columns = join_gate(near, moved, columns, step == lon_count // 2)
        step *= 2
    returned = exchange(columns)
    mixed_field = kernel_call(
        functools.partial(unpack_body, rows_sub, subs),
        [unpacked],
        [],
        [filtered, features],
        unpack_scratch,
    )[0]
    blocks = kernel_call(
        blocks_body,
        [array((lon_count, share, BS), bf16)],
        [lon_index],
        [near, lax.ppermute(near, "lon", lon_pairs(1))],
        anchors=[mixed_field],
    )[0]

    gathered = {0: blocks}
    step = lat_count // 2
    while step:
        for offset in sorted(gathered):
            moved = lax.ppermute(gathered[offset], "lat", line_pairs(lat_count)(step))
            gathered[offset | step] = moved
        step //= 2
    gathered = [gathered[offset] for offset in range(lat_count)]
    full = pltpu.HBM((2, NB, BS, BS), f32)
    feature_grad, grad_first, grad_second = kernel_call(
        functools.partial(last_body, lat_count, rows_sub, subs),
        [unpacked, full, full],
        [lat_index],
        [returned, cotangent, *gathered],
        [
            *unpack_scratch,
            pltpu.VMEM((4, NB, BS, BS), f32),
            pltpu.SemaphoreType.DMA((2,)),
        ],
    )
    return (mixed_field, feature_grad, grad_first, grad_second)


def solution(mesh):
    in_specs = (P("lat", "lon", None), P("lat", "lon", None), P(), P())
    out_specs = (P("lat", "lon", None), P("lat", "lon", None), P(), P())
    return jax.shard_map(shards, mesh=mesh, in_specs=in_specs, out_specs=out_specs, check_vma=False)
```

```python
import functools
import math

import jax
import jax.numpy as jnp
import ml_dtypes
import numpy as np
from jax import lax
from jax.experimental import pallas as pl
from jax.experimental.pallas import tpu as pltpu
from jax.sharding import PartitionSpec as P

NB = 8
BS = 96
KWD = 1
RQ = 4
PACK = RQ * BS
WIDE = 2 * BS
STATE = -(-WIDE // 128) * 128
MIB = 1024 * 1024

shrink_level = 0.01
gelu_coeff = 0.7978845608028654


def wave_table(first, second, length):
    product = (first[:, None] * second[None, :]) % length
    angle = np.float32(2.0 * math.pi / length) * product.astype(np.float32)
    scale = np.float32(math.sqrt(length))
    rounded = ml_dtypes.bfloat16
    cos = (np.cos(angle) / scale).astype(rounded).astype(np.float32)
    sin = (np.sin(angle) / scale).astype(rounded).astype(np.float32)
    return cos, sin


def lon_table(kept, cols, lon_count, rows):
    cos, sin = wave_table(np.arange(kept), np.arange(cols), cols)
    parts = np.stack([cos, -sin], axis=1).reshape(kept, 2, lon_count, cols // lon_count)
    eye = np.eye(rows, dtype=np.float32)
    return np.einsum("kpgw,rs->kprgsw", parts, eye).reshape(2 * kept * rows, -1)


def lat_table(rows, lat_count, subs, rows_sub, rows_cut, pack_modes):
    cos, sin = wave_table(np.arange(rows), np.arange(rows), rows)
    forward = np.stack([np.stack([cos, sin], axis=1), np.stack([-sin, cos], axis=1)])
    split = forward.reshape(2, rows, 2, lat_count, RQ, subs, rows_sub // rows_cut, rows_cut)
    eye = np.eye(pack_modes, dtype=np.float32)
    return np.einsum("aqplgshr,jk->jaqglskhpr", split, eye).reshape(2 * pack_modes * rows, -1)


def constant(table):
    return jnp.asarray(table.astype(ml_dtypes.bfloat16))


def kernel_call(body, out_shape, scalars, arrays, scratch=(), anchors=(), far=(), limit=8 * MIB):
    specs = {
        space: pl.BlockSpec(memory_space=space)
        for space in (pltpu.VMEM, pltpu.SMEM, pltpu.HBM, pl.ANY)
    }
    far = [pltpu.with_memory_space_constraint(value, pltpu.HBM) for value in far]
    in_specs = [specs[pltpu.SMEM]] * len(scalars) + [specs[pltpu.VMEM]] * len(arrays)
    in_specs += [specs[pltpu.HBM]] * len(far) + [specs[pl.ANY]] * len(anchors)
    is_far = [getattr(shape, "memory_space", None) is pltpu.HBM for shape in out_shape]
    return pl.pallas_call(
        body,
        out_shape=out_shape,
        in_specs=in_specs,
        out_specs=[specs[pltpu.HBM if distant else pltpu.VMEM] for distant in is_far],
        scratch_shapes=list(scratch),
        compiler_params=pltpu.CompilerParams(vmem_limit_bytes=limit),
    )(*[value.reshape(1).astype(jnp.int32) for value in scalars], *arrays, *far, *anchors)


def gate(source, anchors):
    anywhere, distant = pl.BlockSpec(memory_space=pl.ANY), pl.BlockSpec(memory_space=pltpu.HBM)
    return pl.pallas_call(
        lambda *refs: None,
        out_shape=pltpu.HBM(source.shape, source.dtype),
        in_specs=[distant] + [anywhere] * len(anchors),
        out_specs=distant,
        input_output_aliases={0: 0},
        compiler_params=pltpu.CompilerParams(vmem_limit_bytes=8 * MIB),
    )(pltpu.with_memory_space_constraint(source, pltpu.HBM), *anchors)


def group_copies(source, target, sems):
    rows = target.shape[0] // RQ
    return [
        pltpu.make_async_copy(
            source.at[pl.ds(group * rows, rows)], target.at[pl.ds(group * rows, rows)], sems.at[group]
        )
        for group in range(RQ)
    ]


def join_gate(first, second, source, gated):
    near, distant = pl.BlockSpec(memory_space=pltpu.VMEM), pl.BlockSpec(memory_space=pltpu.HBM)
    joined = jax.ShapeDtypeStruct((2 * first.shape[0],) + first.shape[1:], first.dtype)
    passed = [pltpu.with_memory_space_constraint(source, pltpu.HBM)] if gated else []
    results = pl.pallas_call(
        join_body,
        out_shape=[joined] + [pltpu.HBM(value.shape, value.dtype) for value in passed],
        in_specs=[near, near] + [distant] * len(passed),
        out_specs=[near] + [distant] * len(passed),
        input_output_aliases={2: 1} if gated else {},
        compiler_params=pltpu.CompilerParams(vmem_limit_bytes=8 * MIB),
    )(first, second, *passed)
    return results[0], results[1] if gated else source


def pack_body(rows_sub, subs, own, field, *rest):
    sent, (slots, source, sems) = rest[:-3], rest[-3:]
    cols = source.shape[1]
    loads = group_copies(field, source, sems)
    for copy in loads:
        copy.start()
    finish(loads)
    for sub in range(subs):
        for block in range(NB):
            pieces = []
            for group in range(RQ):
                row = (group * subs + sub) * rows_sub
                piece = source[row : row + rows_sub, :, block * BS : (block + 1) * BS]
                pieces.append(piece.reshape(rows_sub * cols, BS))
            slots[sub * NB + block] = jnp.concatenate(pieces, axis=1)
    deal(sent, slots, own[0])


def unpack_body(rows_sub, subs, packed, base, result, mixed, sems):
    cols = base.shape[1]
    saves = group_copies(mixed, result, sems)
    for group in range(RQ):
        for sub in range(subs):
            row = (group * subs + sub) * rows_sub
            pieces = [
                packed[sub * NB + block, :, group * BS : (group + 1) * BS] for block in range(NB)
            ]
            update = jnp.concatenate(pieces, axis=1).reshape(rows_sub, cols, NB * BS)
            old = base[row : row + rows_sub]
            mixed[row : row + rows_sub] = (
                old.astype(jnp.float32) + update.astype(jnp.float32)
            ).astype(jnp.bfloat16)
        saves[group].start()
    finish(saves)


def product(left, right):
    return jnp.dot(left, right, preferred_element_type=jnp.float32)


def product_back(left, right):
    return lax.dot_general(
        left, right, (((1,), (1,)), ((), ())), preferred_element_type=jnp.float32
    )


def product_outer(left, right):
    return lax.dot_general(
        left, right, (((0,), (0,)), ((), ())), preferred_element_type=jnp.float32
    )


def place(slots, pieces, own):
    if len(pieces) == 1:
        slots[...] = pieces[0][...]
        return
    for offset, piece in enumerate(pieces):
        slots[jnp.bitwise_xor(own, offset)] = piece[...]


def deal(pieces, slots, own):
    if len(pieces) == 1:
        pieces[0][...] = slots[...]
        return
    for offset, piece in enumerate(pieces):
        piece[...] = slots[jnp.bitwise_xor(own, offset)]


def spectra_body(count, extra, cuts, kept, own_in, own_out, table, *rest):
    received, (sent, slots_in, slots_out) = rest[:count], (rest[count + extra : -2], *rest[-2:])
    place(slots_in, received, own_in[0])
    each = slots_in.shape[1] // cuts
    parts = []
    for cut in range(cuts):
        flat = slots_in[:, cut * each : (cut + 1) * each].reshape(-1, PACK)
        parts.append(product(table[...], flat).reshape(slots_out.shape[0] * kept, -1, PACK))
    joined = jnp.stack(parts, axis=1) if cuts > 1 else parts[0]
    slots_out[...] = joined.reshape(slots_out.shape).astype(jnp.bfloat16)
    deal(sent, slots_out, own_out[0])


def columns_body(count, extra, cuts, kept, own_in, table, *rest):
    received, (result, slots_in, slots_out, sems) = rest[:count], rest[count + extra :]
    place(slots_in, received, own_in[0])
    each = slots_out.shape[1] // cuts
    modes = slots_in.shape[0] * kept
    split = slots_in[...].astype(jnp.float32).reshape(modes, cuts, -1, PACK)
    flats = [split[:, cut].reshape(-1, PACK).astype(jnp.bfloat16) for cut in range(cuts)]
    inverse = table[...].T
    copies = []
    for cut, flat in enumerate(flats):
        part = product(inverse, flat).astype(jnp.bfloat16)
        rows = pl.ds(cut * each, each)
        slots_out[:, rows] = part.reshape(slots_out.shape[0], each, PACK)
        copies.append(
            pltpu.make_async_copy(slots_out.at[:, rows], result.at[:, rows], sems.at[cut])
        )
        copies[-1].start()
    finish(copies)


def finish(copies):
    for copy in copies:
        copy.wait()


def load_weights(block, weights, real_imag, sems):
    copies = [
        pltpu.make_async_copy(source.at[part, block], real_imag.at[slot, part], sems.at[slot, part])
        for slot, source in enumerate(weights)
        for part in range(2)
    ]
    for copy in copies:
        copy.start()
    return copies


def complex_weights(real_imag, full):
    for slot in range(full.shape[0]):
        real, imag = real_imag[slot, 0], real_imag[slot, 1]
        full[slot, :BS] = jnp.concatenate([real, imag], axis=1)
        full[slot, BS:] = jnp.concatenate([-imag, real], axis=1)


def lat_forward(table, slots, tile, deep, rows):
    slab = slots[:, tile * deep : (tile + 1) * deep]
    flat = slab.reshape(slab.shape[0] * deep, PACK)
    stacked = jnp.concatenate(
        [flat[:, group * BS : (group + 1) * BS] for group in range(RQ)], axis=0
    )
    spectrum = product(table, stacked).astype(jnp.bfloat16)
    return [
        jnp.concatenate([spectrum[at : at + rows], spectrum[at + rows : at + 2 * rows]], axis=1)
        for at in range(0, spectrum.shape[0], 2 * rows)
    ]


def lat_inverse(table, values, slots, tile, deep):
    stacked = jnp.concatenate(
        [part for value in values for part in (value[:, :BS], value[:, BS:])], axis=0
    )
    rows = product(table, stacked).astype(jnp.bfloat16)
    each = rows.shape[0] // RQ
    packed = jnp.concatenate([rows[at : at + each] for at in range(0, RQ * each, each)], axis=1)
    slots[:, tile * deep : (tile + 1) * deep] = packed.reshape(slots.shape[0], deep, PACK)


def mode_weight(first_mode, index):
    return jnp.where(first_mode + index == 0, 1.0, 2.0).astype(jnp.float32)


def gelu(pre):
    squared = pre * pre
    tangent = jnp.tanh(gelu_coeff * (pre + 0.044715 * squared * pre))
    act = (0.5 * pre * (1.0 + tangent)).astype(jnp.bfloat16)
    return act, squared, tangent


def forward_body(members, pack_modes, member, first_mode, block, table, *rest):
    received, weights, sent = rest[:members], rest[members : members + 2], rest[members + 2 :]
    sent, rest = sent[:members], sent[members:]
    saved, anchor, slots, spec, real_imag, full, weight_sems, save_sems = rest
    anchor[...] = jnp.zeros_like(anchor)
    loads = load_weights(block[0], weights, real_imag, weight_sems)
    own = member[0]
    kept, rows, _ = spec.shape
    deep = slots.shape[1] * pack_modes // kept
    place(slots, received, own)
    lat = table[...]
    inverse = lat.T
    copies = []
    for tile in range(kept // pack_modes):
        for inner, values in enumerate(lat_forward(lat, slots, tile, deep, rows)):
            index = tile * pack_modes + inner
            spec[index, :, :WIDE] = values
            copies.append(
                pltpu.make_async_copy(spec.at[index], saved.at[index], save_sems.at[index])
            )
            copies[-1].start()
    finish(loads)
    complex_weights(real_imag, full)
    count = max(pack_modes, 2)
    for start in range(0, kept, count):
        values = spec[start : start + count].reshape(count * rows, -1)[:, :WIDE]
        act, _, _ = gelu(product(values, full[0]))
        post = product(act, full[1])
        shrunk = post - shrink_level * jnp.tanh(post / shrink_level)
        outs = [
            (mode_weight(first_mode[0], start + at) * shrunk[at * rows : (at + 1) * rows]).astype(
                jnp.bfloat16
            )
            for at in range(count)
        ]
        for at in range(0, count, pack_modes):
            tile = (start + at) // pack_modes
            lat_inverse(inverse, outs[at : at + pack_modes], slots, tile, deep)
    deal(sent, slots, own)
    finish(copies)


def backward_body(
    members, shares, pack_modes, factor, member, first_mode, lat_own, block, table, *rest
):
    received, rest = rest[:members], rest[members:]
    weights, saved, result, combined, rest = rest[:2], rest[2], rest[3], rest[4], rest[5:]
    parts, (slots, grads, cots, hidden, spec, real_imag, full, weight_sems, load_sems) = (
        rest[:shares],
        rest[shares:],
    )
    loads = load_weights(block[0], weights, real_imag, weight_sems)
    kept, rows, _ = spec.shape
    deep = slots.shape[1] * pack_modes // kept
    spec_loads = [
        pltpu.make_async_copy(saved.at[index], spec.at[index], load_sems.at[index])
        for index in range(kept)
    ]
    for copy in spec_loads:
        copy.start()
    place(slots, received, member[0])
    lat = table[...]
    for tile in range(kept // pack_modes):
        for inner, cot in enumerate(lat_forward(lat, slots, tile, deep, rows)):
            index = tile * pack_modes + inner
            weight = mode_weight(first_mode[0], index)
            cots[index] = (weight * cot.astype(jnp.float32)).astype(jnp.bfloat16)
    finish(loads)
    complex_weights(real_imag, full)
    combined[...] = full[0]
    count = max(pack_modes, 2)
    for start in range(0, kept, count):
        group = pl.ds(start, count)
        finish(spec_loads[start : start + count])
        values = spec[group].reshape(count * rows, -1)[:, :WIDE]
        pre = product(values, full[0])
        act, squared, tangent = gelu(pre)
        slope = 0.5 * (1.0 + tangent) + 0.5 * pre * (1.0 - tangent * tangent) * gelu_coeff * (
            1.0 + 3.0 * 0.044715 * squared
        )
        ratio = jnp.tanh(product(act, full[1]) / shrink_level)
        cot = cots[group].reshape(count * rows, WIDE).astype(jnp.float32)
        grad_post = (cot * (ratio * ratio)).astype(jnp.bfloat16)
        grad_pre = (product_back(grad_post, full[1]) * slope).astype(jnp.bfloat16)
        result[group] = grad_pre.reshape(count, rows, WIDE)
        hidden[group] = act.reshape(count, rows, WIDE)
        cots[group] = grad_post.reshape(count, rows, WIDE)
    modes = kept * rows
    grads_pre = result[...].reshape(modes, WIDE)
    total_first = product_outer(spec[...].reshape(modes, -1)[:, :WIDE], grads_pre)
    total_second = product_outer(
        hidden[...].reshape(modes, WIDE), cots[...].reshape(modes, WIDE)
    )
    share = grads.shape[1]
    for slot, total in enumerate((total_first, total_second)):
        real = (total[:BS, :BS] + total[BS:, BS:]) * factor
        imag = (total[:BS, BS:] - total[BS:, :BS]) * factor
        for part, value in enumerate((real, imag)):
            for at in range(0, BS, share):
                piece = ((2 * slot + part) * BS + at) // share
                grads[piece] = value[at : at + share].astype(jnp.bfloat16)
    deal(parts, grads, lat_own[0])


def input_grad_body(pack_modes, extra, member, table, grad_pre, combined, *rest):
    sent, slots = rest[extra:-1], rest[-1]
    kept = grad_pre.shape[0]
    deep = slots.shape[1] * pack_modes // kept
    inverse = table[...].T
    for tile in range(kept // pack_modes):
        backs = [
            product_back(grad_pre[index], combined[...]).astype(jnp.bfloat16)
            for index in range(tile * pack_modes, (tile + 1) * pack_modes)
        ]
        lat_inverse(inverse, backs, slots, tile, deep)
    deal(sent, slots, member[0])


def sum_body(*refs):
    refs[-1][0] = sum(value[...].astype(jnp.float32) for value in refs[:-1]).astype(jnp.bfloat16)


def join_body(first, second, *rest):
    joined, count = rest[len(rest) // 2], first.shape[0]
    joined[:count] = first[...]
    joined[count:] = second[...]


def blocks_body(own, near, other, anchor, blocks):
    for slot in range(near.shape[0]):
        blocks[jnp.bitwise_xor(own[0], 2 * slot)] = near[slot]
        blocks[jnp.bitwise_xor(own[0], 2 * slot + 1)] = other[slot]


def last_body(lat_count, rows_sub, subs, lat_own, packed, base, *rest):
    gathered, (result, first, second, mixed, sems, slots, grad_sems) = (
        rest[:lat_count],
        rest[lat_count:],
    )
    assemble(lat_own, gathered, slots, subs)
    copies = [
        pltpu.make_async_copy(slots.at[pl.ds(2 * at, 2)], full, grad_sems.at[at])
        for at, full in enumerate((first, second))
    ]
    for copy in copies:
        copy.start()
    unpack_body(rows_sub, subs, packed, base, result, mixed, sems)
    finish(copies)


def assemble(lat_own, gathered, slots, subs):
    rows = gathered[0].shape[1]
    for offset, pieces in enumerate(gathered):
        start = jnp.bitwise_xor(lat_own[0], offset) * rows
        matrix, row = start // BS, pl.multiple_of(start % BS, 16)
        for block in range(NB):
            total = None
            for sub in range(subs):
                value = pieces[sub * NB + block].astype(jnp.float32)
                total = value if total is None else total + value
            slots[matrix, block, pl.ds(row, rows)] = total


def exchange(source):
    return lax.all_to_all(source, "lon", split_axis=0, concat_axis=0, tiled=True)


def swap(pieces, axes, partners):
    return [pieces[0]] + [
        lax.ppermute(piece, axes, partners(offset))
        for offset, piece in enumerate(pieces)
        if offset
    ]


def shards(features, cotangent, weight_first, weight_second):
    lat_count = lax.axis_size("lat")
    lon_count = lax.axis_size("lon")
    band_rows, band_cols, channels = features.shape
    rows_total = band_rows * lat_count
    cols_total = band_cols * lon_count
    kept_total = KWD * lat_count * lon_count
    subs = lon_count // NB
    members = lat_count * subs
    rows_sub = band_rows // (RQ * subs)
    rows_cut = min(rows_sub, 4)
    cuts = rows_sub // rows_cut
    kept = kept_total // members
    deep = 2 * rows_sub
    pack_modes = max(1, 16 // deep)
    lat_index = lax.axis_index("lat")
    lon_index = lax.axis_index("lon")
    block = lon_index % NB
    member = lat_index * subs + lon_index // NB
    bf16, f32 = jnp.bfloat16, jnp.float32
    array = jax.ShapeDtypeStruct

    def member_pairs(offset):
        pairs = []
        for lat in range(lat_count):
            for lon in range(lon_count):
                other = (lat * subs + lon // NB) ^ offset
                lon_other = other % subs * NB + lon % NB
                pairs.append((lat * lon_count + lon, other // subs * lon_count + lon_other))
        return pairs

    def line_pairs(count):
        return lambda offset: [(place, place ^ offset) for place in range(count)]

    lon_fwd = constant(lon_table(kept_total, cols_total, lon_count, rows_cut))
    lat_both = constant(lat_table(rows_total, lat_count, subs, rows_sub, rows_cut, pack_modes))
    lon_piece = array((rows_sub * band_cols, PACK), bf16)
    lon_whole = array((lon_count, rows_sub * band_cols, PACK), bf16)
    mid_piece = array((kept * deep, PACK), bf16)
    lon_slots = pltpu.VMEM(lon_whole.shape, bf16)
    mid_slots = pltpu.VMEM((members, kept * deep, PACK), bf16)
    mid_limit = 14 * MIB + 5 * lat_both.size
    share = 4 * BS // lat_count

    def mid_swap(pieces):
        return swap(pieces, ("lat", "lon"), member_pairs)

    def pack(source, sent):
        body = functools.partial(pack_body, rows_sub, subs)
        scratch = [lon_slots, pltpu.VMEM(source.shape, bf16), pltpu.SemaphoreType.DMA((RQ,))]
        return kernel_call(body, sent, [lon_index], [], scratch, far=[source])

    unpack_scratch = [pltpu.VMEM(features.shape, bf16), pltpu.SemaphoreType.DMA((RQ,))]
    unpacked = pltpu.HBM(features.shape, bf16)

    def to_spectra(pieces, anchors=()):
        return kernel_call(
            functools.partial(spectra_body, len(pieces), len(anchors), cuts, kept),
            [mid_piece] * members,
            [lon_index, member],
            [lon_fwd, *pieces],
            [lon_slots, mid_slots],
            anchors,
        )

    def to_columns(pieces, anchors=()):
        return kernel_call(
            functools.partial(columns_body, members, len(anchors), cuts, kept),
            [pltpu.HBM(lon_whole.shape, bf16)],
            [member],
            [lon_fwd, *pieces],
            [mid_slots, lon_slots, pltpu.SemaphoreType.DMA((cuts,))],
            anchors,
        )[0]

    modes = (kept, rows_total, STATE)
    weights = [weight_first, weight_second]
    mid_scratch = [
        pltpu.VMEM(modes, bf16),
        pltpu.VMEM((2, 2, BS, BS), bf16),
        pltpu.VMEM((2, WIDE, WIDE), bf16),
        pltpu.SemaphoreType.DMA((2, 2)),
        pltpu.SemaphoreType.DMA((kept,)),
    ]

    field = swap(pack(features, [lon_piece] * lon_count), "lon", line_pairs(lon_count))
    spectra = to_spectra(field)
    field_cot = exchange(gate(pack(cotangent, [lon_whole])[0], spectra[:1]))
    results = kernel_call(
        functools.partial(forward_body, members, pack_modes),
        [mid_piece] * members + [pltpu.HBM(modes, bf16), array((8, 128), f32)],
        [member, member * kept, block],
        [lat_both, *mid_swap(spectra)],
        [mid_slots, *mid_scratch],
        far=weights,
        limit=mid_limit,
    )
    saved, anchor = results[members:]
    spectra_cot = to_spectra([field_cot], [anchor])
    filtered = exchange(to_columns(mid_swap(results[:members]), spectra_cot[:1]))
    wide = (kept, rows_total, WIDE)
    grad_pre, combined, *parts = kernel_call(
        functools.partial(
            backward_body, members, lat_count, pack_modes, 1.0 / math.sqrt(rows_total * kept_total)
        ),
        [array(wide, bf16), array((WIDE, WIDE), bf16)] + [array((share, BS), bf16)] * lat_count,
        [member, member * kept, lat_index, block],
        [lat_both, *mid_swap(spectra_cot)],
        [
            mid_slots,
            pltpu.VMEM((lat_count, share, BS), bf16),
            pltpu.VMEM(wide, bf16),
            pltpu.VMEM(wide, bf16),
            *mid_scratch,
        ],
        far=weights + [saved],
        limit=mid_limit,
    )
    own_share = kernel_call(
        sum_body, [array((1, share, BS), bf16)], [], swap(parts, "lat", line_pairs(lat_count))
    )[0]
    back = kernel_call(
        functools.partial(input_grad_body, pack_modes, 1),
        [mid_piece] * members,
        [member],
        [lat_both, grad_pre, combined],
        [mid_slots],
        [own_share],
        limit=mid_limit,
    )
    lon_pairs = line_pairs(lon_count)
    columns = to_columns(mid_swap(back))
    near, step = own_share, 2
    while step < lon_count:
        moved = lax.ppermute(near, "lon", lon_pairs(step))
        near, columns = join_gate(near, moved, columns, step == lon_count // 2)
        step *= 2
    returned = exchange(columns)
    mixed_field = kernel_call(
        functools.partial(unpack_body, rows_sub, subs),
        [unpacked],
        [],
        [filtered, features],
        unpack_scratch,
    )[0]
    blocks = kernel_call(
        blocks_body,
        [array((lon_count, share, BS), bf16)],
        [lon_index],
        [near, lax.ppermute(near, "lon", lon_pairs(1))],
        anchors=[mixed_field],
    )[0]

    gathered = {0: blocks}
    step = lat_count // 2
    while step:
        for offset in sorted(gathered):
            moved = lax.ppermute(gathered[offset], "lat", line_pairs(lat_count)(step))
            gathered[offset | step] = moved
        step //= 2
    gathered = [gathered[offset] for offset in range(lat_count)]
    full = pltpu.HBM((2, NB, BS, BS), f32)
    feature_grad, grad_first, grad_second = kernel_call(
        functools.partial(last_body, lat_count, rows_sub, subs),
        [unpacked, full, full],
        [lat_index],
        [returned, cotangent, *gathered],
        [
            *unpack_scratch,
            pltpu.VMEM((4, NB, BS, BS), f32),
            pltpu.SemaphoreType.DMA((2,)),
        ],
    )
    return (mixed_field, feature_grad, grad_first, grad_second)


def solution(mesh):
    in_specs = (P("lat", "lon", None), P("lat", "lon", None), P(), P())
    out_specs = (P("lat", "lon", None), P("lat", "lon", None), P(), P())
    return jax.shard_map(shards, mesh=mesh, in_specs=in_specs, out_specs=out_specs, check_vma=False)
```
